32 devices in a mesh: dp: 8 (over y, x, core), space: 4 (over z).
Axes of the slice: x: 2, y: 2, z: 4, core: 2. Of those that a mesh axis runs over, the one named last changes fastest.
Arguments:
- frames: bfloat16 [64, 64, 64, 64], P('dp', 'space'), may hold values from -16 to 16
- cotangent: bfloat16 [64, 64, 64, 64], P('dp', 'space'), may hold values from -5 to 5
- actions: int32 [64], P('dp'), may hold values from 0 to 17
- noise_ids: int32 [64], P('dp'), may hold values from 0 to 63
- games: int32 [64], P('dp'), may hold values from 0 to 25
- live_counts: int32 [8], P('dp'), may hold values from 2 to 8, as said below
- conv_weight: float32 [4032, 64], replicated, may hold values from -0.25 to 0.25
- conv_moment: float32 [4032, 64], replicated
- conv_square: float32 [4032, 64], replicated, as said below
- norm_map: float32 [4, 257, 128], replicated, may hold values from -0.1875 to 0.1875
- norm_moment: float32 [4, 257, 128], replicated
- norm_square: float32 [4, 257, 128], replicated, as said below
- emb_table: float32 [108, 256], replicated, may hold values from -3 to 3
- table_moment: float32 [108, 256], replicated
- table_square: float32 [108, 256], replicated, as said below
Outputs:
- result: bfloat16 [64, 64, 64, 64], P('dp', 'space')
- frames_grad: float32 [64, 64, 64, 64], P('dp', 'space')
- conv_moment_new: float32 [4032, 64], replicated
- conv_square_new: float32 [4032, 64], replicated
- conv_weight_new: float32 [4032, 64], replicated
- conv_weight_low: bfloat16 [4032, 64], replicated
- norm_moment_new: float32 [4, 257, 128], replicated
- norm_square_new: float32 [4, 257, 128], replicated
- norm_map_new: float32 [4, 257, 128], replicated
- norm_map_low: bfloat16 [4, 257, 128], replicated
- table_moment_new: float32 [108, 256], replicated
- table_square_new: float32 [108, 256], replicated
- emb_table_new: float32 [108, 256], replicated
- emb_table_low: bfloat16 [108, 256], replicated
The draws below stay inside these ranges and needn't reach their ends.
Inputs may be any that keep to these rules, and one draw needn't show every extreme that they name: `live_counts`: every group's live frames are its first slots; some group uses all 8 slots. `conv_square`: positive. `norm_square`: positive. `table_square`: positive.
All inputs are finite; a program needn't handle non-finite values.
Results may differ from the reference program's by a relative error of at most 0.0092.
Values may be sent and summed in bfloat16 or wider, within the bound.
A program may use at most 128 MiB of HBM per device.

```python
import math
import jax
import jax.numpy as jnp
from jax import lax

CH = 64
GROUPS = 2
EMB = 256
RES = 64
ACTIONS = 18
GAMES = 26
NOISE_LEVELS = 64
ADAM_STEP = 4
FRAMES_DP = 8
DATA_GROUPS = 8
FRAMES = 64
EMB_ROWS = 108
CONV_ROWS = 4032
N_DP = 8


def draw_frames(key, part):
    first, second = jax.random.split(jax.random.fold_in(key, 11))
    rows = jnp.arange(RES, dtype=jnp.float32) / (RES - 1)
    ramp = (0.6 * jnp.exp(rows * math.log(3.0)))[None, :, None, None]
    chan = jnp.exp(jax.random.uniform(second, (1, 1, 1, CH), jnp.float32, -0.7, 0.7))
    base = jnp.clip(jax.random.normal(first, (FRAMES, RES, RES, CH), jnp.float32), -4.0, 4.0)
    return (base * ramp * chan).astype(jnp.bfloat16)


def draw_live_counts(key, part):
    base = jax.random.randint(jax.random.fold_in(key, 21), (DATA_GROUPS,), FRAMES_DP // 4, FRAMES_DP + 1)
    pick = jax.random.randint(jax.random.fold_in(key, 22), (), 0, DATA_GROUPS)
    return base.at[pick].set(FRAMES_DP).astype(jnp.int32)


def conv_level():
    rows = jnp.arange(CONV_ROWS)
    coarse = (rows >= 18 * CH) & (rows < 45 * CH)
    level = 0.1 * FRAMES * RES * RES * jnp.where(coarse, 0.25, 1.0).astype(jnp.float32)
    return level[:, None] * jnp.ones((1, CH), jnp.float32)


def norm_level():
    level = 0.1 * FRAMES * RES * RES * jnp.array([1.0, 1.0, 0.25, 0.25], jnp.float32)
    return level[:, None, None] * jnp.ones((1, EMB + 1, 2 * CH), jnp.float32)


def table_level():
    rows = jnp.arange(EMB_ROWS)
    kinds = jnp.where(rows < ACTIONS, ACTIONS, jnp.where(rows < ACTIONS + NOISE_LEVELS, NOISE_LEVELS, GAMES)).astype(jnp.float32)
    level = 0.05 * FRAMES * RES * RES / kinds
    return level[:, None] * jnp.ones((1, EMB), jnp.float32)


def second_moment(key, level):
    factor = jnp.exp(jax.random.uniform(key, level.shape, jnp.float32, 0.0, math.log(4.0)))
    return level * factor


def first_moment(key, level):
    noise = jnp.clip(jax.random.normal(key, level.shape, jnp.float32), -4.0, 4.0)
    return jnp.sqrt(level) * noise


def draw_conv_moment(key, part):
    return first_moment(jax.random.fold_in(key, 31), conv_level())


def draw_conv_square(key, part):
    return second_moment(jax.random.fold_in(key, 32), conv_level())


def draw_norm_moment(key, part):
    return first_moment(jax.random.fold_in(key, 33), norm_level())


def draw_norm_square(key, part):
    return second_moment(jax.random.fold_in(key, 34), norm_level())


def draw_table_moment(key, part):
    return first_moment(jax.random.fold_in(key, 35), table_level())


def draw_table_square(key, part):
    return second_moment(jax.random.fold_in(key, 36), table_level())


def place_ends(drawn, rng, least, high):
    spot = [jax.random.randint(jax.random.fold_in(rng, axis), (), 0, length) for axis, length in enumerate(drawn.shape)]
    longest = drawn.shape.index(max(drawn.shape))
    next_to = spot[:longest] + [(spot[longest] + 1) % drawn.shape[longest]] + spot[longest + 1:]
    return drawn.at[tuple(spot)].set(least).at[tuple(next_to)].set(high)


def block_levels(key, shape, cuts, smallest, largest):
    factor_of, own = 1.0, jax.random.fold_in(key, 6)
    for dim, blocks in cuts:
        draws = jnp.exp(jax.random.uniform(jax.random.fold_in(own, dim), (blocks,), jnp.float32, smallest / len(cuts), largest / len(cuts)))
        factor_of = factor_of * jnp.repeat(draws, shape[dim] // blocks).reshape([-1 if axis == dim else 1 for axis in range(len(shape))])
    return factor_of


def bell_draw(stream_key, extent, scale, most, cuts=(), kind=jnp.bfloat16):
    values = jax.random.normal(stream_key, extent, jnp.float32) * scale
    if len(cuts) > 0:
        values = block_levels(stream_key, extent, cuts, -0.22, 0.18) * values
    return jnp.clip(values, min=-most, max=most).astype(kind)


def setup_inputs(seed: int = 0) -> dict:
    key_list = jax.random.split(jax.random.key(seed), 16)
    return {
        "frames": draw_frames(jax.random.fold_in(key_list[15], 71), 0),
        "cotangent": bell_draw(key_list[1], (FRAMES, RES, RES, CH), 1.0, 5.0, ((0, 8), (1, 4))),
        "actions": place_ends(jax.random.randint(key_list[2], (FRAMES,), 0, ACTIONS), jax.random.fold_in(key_list[2], 1), 0, ACTIONS - 1).astype(jnp.int32),
        "noise_ids": place_ends(jax.random.randint(key_list[3], (FRAMES,), 0, NOISE_LEVELS), jax.random.fold_in(key_list[3], 1), 0, NOISE_LEVELS - 1).astype(jnp.int32),
        "games": place_ends(jax.random.randint(key_list[4], (FRAMES,), 0, GAMES), jax.random.fold_in(key_list[4], 1), 0, GAMES - 1).astype(jnp.int32),
        "live_counts": draw_live_counts(jax.random.fold_in(key_list[15], 71), 0),
        "conv_weight": bell_draw(key_list[6], (CONV_ROWS, CH), (9 * CH) ** -0.5, 0.25, (), jnp.float32),
        "conv_moment": draw_conv_moment(jax.random.fold_in(key_list[15], 71), 0),
        "conv_square": draw_conv_square(jax.random.fold_in(key_list[15], 71), 0),
        "norm_map": bell_draw(key_list[9], (4, EMB + 1, 2 * CH), (4 * (EMB + 1)) ** -0.5, 0.1875, (), jnp.float32),
        "norm_moment": draw_norm_moment(jax.random.fold_in(key_list[15], 71), 0),
        "norm_square": draw_norm_square(jax.random.fold_in(key_list[15], 71), 0),
        "emb_table": bell_draw(key_list[12], (EMB_ROWS, EMB), 0.5, 3.0, (), jnp.float32),
        "table_moment": draw_table_moment(jax.random.fold_in(key_list[15], 71), 0),
        "table_square": draw_table_square(jax.random.fold_in(key_list[15], 71), 0),
    }


@jax.custom_vjp
def low(v):
    return lax.optimization_barrier(v.astype(jnp.bfloat16)).astype(jnp.float32)

@jax.custom_vjp
def low_back(v):
    return v

def low_keep(v):
    return (low(v), None)

def low_pass(kept, grad):
    return (grad,)

def back_keep(v):
    return (v, None)

def back_low(kept, grad):
    return (low(grad),)
low.defvjp(low_keep, low_pass)
low_back.defvjp(back_keep, back_low)
NORM_EPSILON = 1e-05
ADAM_EPS = 1e-08
BETA_ONE = 0.5
BETA_TWO = 0.5
DECAY = 0.01
HIGH = lax.Precision.HIGHEST
DIMS = ('NHWC', 'HWIO', 'NHWC')

def kernels(conv_weight):
    channel_width = conv_weight.shape[1]
    pieces = [conv_weight[k * 9 * channel_width:(k + 1) * 9 * channel_width].reshape(3, 3, channel_width, channel_width) for k in range(5)]
    pieces.append(conv_weight[45 * channel_width:].reshape(3, 3, 2 * channel_width, channel_width))
    return pieces

def conv_same(input_value, kernel):
    return lax.conv_general_dilated(input_value, kernel, (1, 1), ((1, 1), (1, 1)), dimension_numbers=DIMS, precision=HIGH)

def conv_down(input_value, kernel):
    return lax.conv_general_dilated(input_value, kernel, (2, 2), ((1, 1), (1, 1)), dimension_numbers=DIMS, precision=HIGH)

def ada_norm(input_value, adaptive_modulation):
    count, height, breadth, channel_width = input_value.shape
    group_split_input = input_value.reshape(count, height, breadth, GROUPS, channel_width // GROUPS)
    group_mean = lax.optimization_barrier(jnp.mean(group_split_input, axis=(1, 2, 4), keepdims=True))
    group_variance = lax.optimization_barrier(jnp.mean(jnp.square(group_split_input - group_mean), axis=(1, 2, 4), keepdims=True))
    centered_normalized = ((group_split_input - group_mean) * lax.rsqrt(group_variance + NORM_EPSILON)).reshape(input_value.shape)
    modulation_scale = adaptive_modulation[:, None, None, :channel_width]
    modulation_shift = adaptive_modulation[:, None, None, channel_width:]
    return centered_normalized * (1.0 + modulation_scale) + modulation_shift

def doubled(input_value):
    return jnp.repeat(jnp.repeat(input_value, 2, 1), 2, 2)

def forward(frames, conv_weight, norm_map, emb_table, multihot):
    kern = [low(k) for k in kernels(conv_weight)]
    embedded = jnp.dot(multihot, emb_table, precision=HIGH)
    augmented = jnp.concatenate([embedded, jnp.ones((embedded.shape[0], 1), jnp.float32)], 1)
    mods = [jnp.dot(augmented, norm_map[k], precision=HIGH) for k in range(4)]
    h_one = low(jax.nn.silu(ada_norm(frames, mods[0])))
    conv_first_output = low_back(conv_same(h_one, kern[0]))
    h_two = low(jax.nn.silu(ada_norm(conv_first_output, mods[1])))
    c_two = low_back(conv_same(h_two, kern[1]))
    y_one = frames + c_two
    skip = low(y_one)
    down_in = low_back(skip)
    down_value = low_back(conv_down(down_in, kern[2]))
    h_three = low(jax.nn.silu(ada_norm(down_value, mods[2])))
    conv_third_output = low_back(conv_same(h_three, kern[3]))
    h_four = low(jax.nn.silu(ada_norm(conv_third_output, mods[3])))
    c_four = low_back(conv_same(h_four, kern[4]))
    y_two = down_value + c_four
    coarse = low(low_back(y_two))
    joined = jnp.concatenate([skip, doubled(coarse)], -1)
    return conv_same(joined, kern[5])

def adamw(weight, moment, square, grad_value, rate):
    fix_one = 1.0 - BETA_ONE ** ADAM_STEP
    fix_two = 1.0 - BETA_TWO ** ADAM_STEP
    moment_new = BETA_ONE * moment + (1.0 - BETA_ONE) * grad_value
    square_new = BETA_TWO * square + (1.0 - BETA_TWO) * grad_value * grad_value
    fixed_m = moment_new / fix_one
    fixed_v = square_new / fix_two
    weight_new = weight - rate * (fixed_m / (jnp.sqrt(fixed_v) + ADAM_EPS) + DECAY * weight)
    return (moment_new, square_new, weight_new, weight_new.astype(jnp.bfloat16))

def reference(frames, cotangent, actions, noise_ids, games, live_counts, conv_weight, conv_moment, conv_square, norm_map, norm_moment, norm_square, emb_table, table_moment, table_square):
    slots = jnp.arange(FRAMES, dtype=jnp.int32)
    live = (slots % FRAMES_DP < live_counts[slots // FRAMES_DP]).astype(jnp.float32)
    entries = jnp.arange(EMB_ROWS, dtype=jnp.int32)[None, :]
    hits = (entries == actions[:, None]) | (entries == noise_ids[:, None] + ACTIONS) | (entries == games[:, None] + ACTIONS + NOISE_LEVELS)
    multihot = hits.astype(jnp.float32)
    input_shape = (N_DP, FRAMES_DP, RES, RES, CH)
    inputs = frames.astype(jnp.float32).reshape(input_shape)
    grads_out = (cotangent.astype(jnp.float32) * live[:, None, None, None]).reshape(input_shape)
    hots = multihot.reshape(N_DP, FRAMES_DP, EMB_ROWS)

    def group_step(carry, item):
        source, pull_in, hot = item

        def local(a_frames, a_conv, a_map, a_table):
            return forward(a_frames, a_conv, a_map, a_table, hot)
        out, pull = jax.vjp(local, source, conv_weight, norm_map, emb_table)
        g_frames, g_conv, g_map, g_table = pull(pull_in)
        return ((carry[0] + g_conv, carry[1] + g_map, carry[2] + g_table), (out.astype(jnp.bfloat16), g_frames))
    start = (jnp.zeros_like(conv_weight), jnp.zeros_like(norm_map), jnp.zeros_like(emb_table))
    (g_conv, g_map, g_table), (outs, g_frames) = lax.scan(group_step, start, (inputs, grads_out, hots))
    result = outs.reshape(FRAMES, RES, RES, CH)
    frames_grad = g_frames.reshape(FRAMES, RES, RES, CH)
    conv_out = adamw(conv_weight, conv_moment, conv_square, g_conv, 0.05)
    norm_out = adamw(norm_map, norm_moment, norm_square, g_map, 0.04)
    table_out = adamw(emb_table, table_moment, table_square, g_table, 0.5)
    return (result, frames_grad, conv_out[0], conv_out[1], conv_out[2], conv_out[3], norm_out[0], norm_out[1], norm_out[2], norm_out[3], table_out[0], table_out[1], table_out[2], table_out[3])
```

```python
import functools

import jax
import jax.numpy as jnp
from jax import lax
from jax.experimental import pallas as pl
from jax.experimental.pallas import tpu as pltpu
from jax.sharding import PartitionSpec as P

ACTIONS = 18
NOISE_LEVELS = 64
ADAM_STEP = 4
NORM_EPSILON = 1e-05
ADAM_EPS = 1e-08
BETA_ONE = 0.5
BETA_TWO = 0.5
DECAY = 0.01
HIGH = lax.Precision.HIGHEST
F32 = jnp.float32
BF16 = jnp.bfloat16
MESH = pl.DeviceIdType.MESH
VM = pltpu.VMEM

ALPHA, BETA, RSTD, NMR, GAIN, SHIFT, COEF, BIAS = range(8)


def dot_nn(a, b):
    return lax.dot_general(a, b, (((1,), (0,)), ((), ())), preferred_element_type=F32)


def dot_nt(a, b):
    return lax.dot_general(a, b, (((1,), (1,)), ((), ())), preferred_element_type=F32)


def dot_tn(a, b):
    return lax.dot_general(a, b, (((0,), (0,)), ((), ())), preferred_element_type=F32)


def dot_high(a, b):
    return lax.dot_general(
        a, b, (((1,), (0,)), ((), ())), precision=HIGH, preferred_element_type=F32
    )


def logistic(z):
    return 0.5 * jnp.tanh(0.5 * z) + 0.5


def lane_iota(shape):
    return lax.broadcasted_iota(jnp.int32, shape, len(shape) - 1)


def swap(v):
    return pltpu.roll(v, 64, len(v.shape) - 1)


def join(lo, hi):
    return jnp.where(lane_iota(lo.shape) < 64, lo, hi)


def twice(row):
    return jnp.concatenate([row, row], axis=-1)


def step_kernel(
    n,
    x_hbm,
    cot_hbm,
    act_ref,
    noise_ref,
    game_ref,
    live_ref,
    cw_ref,
    nm_ref,
    tab_ref,
    res_hbm,
    fg_hbm,
    gt_ref,
    pack_ref,
    raw,
    xh,
    tmp,
    fst,
    xs,
    e1,
    e2,
    esk,
    eg,
    eg2,
    c1,
    gsa,
    gz,
    dv,
    c3,
    gh4,
    gz4,
    gz3,
    gco,
    ec3,
    ec4,
    ecg,
    ecg3,
    ecy,
    ed,
    w1f,
    w1b,
    w2f,
    w2b,
    wsf,
    wsb,
    wup,
    wco,
    wdf,
    wdb,
    w3f,
    w3b,
    w4f,
    w4b,
    acc,
    prm,
    tabp,
    stat,
    hal,
    hout,
    hfull,
    hfout,
    local_sem,
    out_sem,
    fg_sem,
    stat_send,
    stat_recv,
    halo_send,
    halo_recv,
):
    frames, strip = raw.shape[0], raw.shape[1]
    breadth = raw.shape[2]
    half = frames // 2
    rows = strip // 2
    cols = breadth // 2
    me = lax.axis_index("space")
    full_cells = float(strip * n * breadth * 32)
    coarse_cells = full_cells / 4.0
    owned = rows * cols
    ext = (rows + 2) * cols

    barrier = pltpu.get_barrier_semaphore()
    for off in range(1, n):
        pl.semaphore_signal(
            barrier,
            inc=1,
            device_id={"space": lax.rem(me + off, n)},
            device_id_type=MESH,
        )

    x_copy = pltpu.make_async_copy(x_hbm, raw, local_sem.at[0])
    x_copy.start()
    pl.semaphore_wait(barrier, n - 1)

    def halo_copies(k, first, last, to_up, to_down):
        up = pltpu.make_async_remote_copy(
            src_ref=first,
            dst_ref=to_up,
            send_sem=halo_send.at[k, 0],
            recv_sem=halo_recv.at[k, 0],
            device_id={"space": lax.rem(me + n - 1, n)},
            device_id_type=MESH,
        )
        down = pltpu.make_async_remote_copy(
            src_ref=last,
            dst_ref=to_down,
            send_sem=halo_send.at[k, 1],
            recv_sem=halo_recv.at[k, 1],
            device_id={"space": lax.rem(me + 1, n)},
            device_id_type=MESH,
        )
        return up, down

    def halo_start(copies):
        @pl.when(me > 0)
        def _():
            copies[0].start()

        @pl.when(me < n - 1)
        def _():
            copies[1].start()

    def halo_wait(copies):
        @pl.when(me < n - 1)
        def _():
            copies[0].wait_recv()

        @pl.when(me > 0)
        def _():
            copies[1].wait_recv()

    def halo_finish(copies):
        @pl.when(me > 0)
        def _():
            copies[0].wait_send()

        @pl.when(me < n - 1)
        def _():
            copies[1].wait_send()

    def stat_copy(k, off, slot):
        return pltpu.make_async_remote_copy(
            src_ref=stat.at[k, slot],
            dst_ref=stat.at[k, slot],
            send_sem=stat_send.at[k, off - 1],
            recv_sem=stat_recv.at[k, off - 1],
            device_id={"space": lax.rem(me + off, n)},
            device_id_type=MESH,
        )

    def stat_start(k, value):
        stat[k, me] = value
        for off in range(1, n):
            stat_copy(k, off, me).start()

    def stat_total(k):
        for off in range(1, n):
            stat_copy(k, off, lax.rem(me + n - off, n)).wait_recv()
        total = stat[k, 0]
        for i in range(1, n):
            total = total + stat[k, i]
        for off in range(1, n):
            stat_copy(k, off, me).wait_send()
        return total

    x_halo = halo_copies(
        0, x_hbm.at[:, pl.ds(0, 3)], x_hbm.at[:, pl.ds(strip - 3, 3)], xh.at[0, 1], xh.at[0, 0]
    )
    g_halo = halo_copies(
        1, cot_hbm.at[:, pl.ds(0, 3)], cot_hbm.at[:, pl.ds(strip - 3, 3)], xh.at[1, 1], xh.at[1, 0]
    )
    for side in range(2):

        @pl.when((me == 0) if side == 0 else (me == n - 1))
        def _():
            for which in range(2):
                xh[which, side] = jnp.zeros(xh.shape[2:], BF16)
            for which in range(hal.shape[0]):
                hal[which, side] = jnp.zeros(hal.shape[2:], BF16)
            hfull[side] = jnp.zeros(hfull.shape[1:], BF16)

    halo_start(x_halo)

    def coarse_halo(k):
        return halo_copies(
            k, hout.at[k - 2, 0], hout.at[k - 2, 1], hal.at[k - 2, 1], hal.at[k - 2, 0]
        )

    g_h4_halo, d_halo, c3_halo, y_halo, g_h3_halo = [coarse_halo(k) for k in range(2, 7)]
    g_h2_halo = halo_copies(7, hfout.at[0], hfout.at[1], hfull.at[1], hfull.at[0])

    def block_mask(shape, pad):
        blocks = shape[0]
        b = lax.broadcasted_iota(jnp.int32, shape, 0)
        low = jnp.where(me > 0, 0, pad)
        high = jnp.where(me < n - 1, blocks, blocks - pad)
        return (b >= low) & (b < high)

    def param(k, which, f):
        return prm[k * 8 + which, pl.ds(f, 1), :]

    def wide(k, which, f):
        return twice(param(k, which, f))

    def put_row(carry, f, value):
        row = lax.broadcasted_iota(jnp.int32, carry.shape, 0)
        return jnp.where(row == f, value, carry)

    def full_sum(v):
        s = jnp.sum(v.reshape(-1, 256), axis=0, keepdims=True)
        return s[:, :128] + s[:, 128:]

    def paired(raw_rows):
        count = raw_rows.shape[0]
        tmp[0:count, :, 0:64] = raw_rows.astype(F32)
        even = tmp[0:count, pl.ds(0, cols, stride=2), :]
        odd = tmp[0:count, pl.ds(1, cols, stride=2), :]
        return join(even, swap(odd))

    def pair_halves(p):
        count = p.shape[0] // 2
        p = p.reshape(count, 2, cols, 128)
        return p[:, 0], p[:, 1]

    def neighbours(v):
        count = v.shape[0]
        flat = v.reshape(count * cols, 128)
        up = pltpu.roll(flat, count * cols - 1, 0).reshape(v.shape)
        down = pltpu.roll(flat, 1, 0).reshape(v.shape)
        return up, down

    def put_e(e, f, start, h):
        count = h.shape[0]
        for part in range(2):
            v = h[:, :, part * 128 : (part + 1) * 128]
            up, down = neighbours(v)
            lane = lane_iota(v.shape)
            q = lax.broadcasted_iota(jnp.int32, v.shape, 1)
            near = jnp.where(
                lane < 64, jnp.where(q == cols - 1, 0.0, up), jnp.where(q == 0, 0.0, down)
            )
            e[f, start : start + count, :, part * 256 : part * 256 + 128] = v.astype(BF16)
            e[f, start : start + count, :, part * 256 + 128 : part * 256 + 256] = near.astype(BF16)

    def window(e, f, start, count):
        return jnp.concatenate(
            [
                e[f, start - 1 : start - 1 + count, :, 256:512],
                e[f, start : start + count, :, :],
                e[f, start + 1 : start + 1 + count, :, 0:256],
            ],
            axis=-1,
        ).reshape(count * cols, 1024)

    def own_pixels(e, f, start, count):
        return jnp.concatenate(
            [
                e[f, start : start + count, :, 0:128],
                e[f, start : start + count, :, 256:384],
            ],
            axis=-1,
        ).reshape(count * cols, 256)

    def put_ec(ec, hf, v):
        up, down = neighbours(v)
        q = lax.broadcasted_iota(jnp.int32, v.shape, 1)
        ec[hf, :, :, 0:128] = jnp.where(q == 0, 0.0, down).astype(BF16)
        ec[hf, :, :, 128:256] = v.astype(BF16)
        ec[hf, :, :, 256:384] = jnp.where(q == cols - 1, 0.0, up).astype(BF16)

    def coarse_window(ec, hf):
        return jnp.concatenate([ec[hf, a : a + rows] for a in range(3)], axis=-1).reshape(
            owned, 1152
        )

    def coarse_sum(v):
        return jnp.sum(v.reshape(-1, 128), axis=0, keepdims=True)

    def with_halo(ref, hf, k):
        ref[hf, 0] = hal[k, 0, hf].astype(F32)
        ref[hf, rows + 1] = hal[k, 1, hf].astype(F32)

    def border(ref_out, k, hf, v):
        ref_out[k, 0, hf] = v[0].astype(BF16)
        ref_out[k, 1, hf] = v[rows - 1].astype(BF16)

    def group_matrix(coarse):
        r = lax.broadcasted_iota(jnp.int32, (128, 128), 0) // 32
        c = lax.broadcasted_iota(jnp.int32, (128, 128), 1) // 32
        same = (r == c) if coarse else (r % 2 == c % 2)
        return jnp.where(same, 1.0, 0.0)

    def norm_forward(k, total, coarse):
        cells = coarse_cells if coarse else full_cells
        count = half if coarse else frames
        moments = dot_high(total, group_matrix(coarse)) / cells
        mean = moments[0:count]
        var = moments[count : 2 * count] - mean * mean
        rstd = lax.rsqrt(var + NORM_EPSILON)
        gain = prm[k * 8 + GAIN, 0:count, :]
        alpha = rstd * gain
        prm[k * 8 + ALPHA, 0:count, :] = alpha
        prm[k * 8 + BETA, 0:count, :] = prm[k * 8 + SHIFT, 0:count, :] - mean * alpha
        prm[k * 8 + RSTD, 0:count, :] = rstd
        prm[k * 8 + NMR, 0:count, :] = -mean * rstd

    def norm_backward(k, total, coarse):
        cells = coarse_cells if coarse else full_cells
        count = half if coarse else frames
        gain = prm[k * 8 + GAIN, 0:count, :]
        shift_grad = total[0:count]
        scale_grad = total[count : 2 * count]
        means = (
            dot_high(
                jnp.concatenate([shift_grad * gain, scale_grad * gain], axis=0),
                group_matrix(coarse),
            )
            / cells
        )
        rstd = prm[k * 8 + RSTD, 0:count, :]
        factor = -rstd * means[count : 2 * count]
        prm[k * 8 + COEF, 0:count, :] = rstd * factor
        prm[k * 8 + BIAS, 0:count, :] = (
            prm[k * 8 + NMR, 0:count, :] * factor - rstd * means[0:count]
        )
        if coarse:
            scale_all = jnp.concatenate([scale_grad, swap(scale_grad)], axis=0)
            shift_all = jnp.concatenate([shift_grad, swap(shift_grad)], axis=0)
        else:
            scale_all = scale_grad + swap(scale_grad)
            shift_all = shift_grad + swap(shift_grad)
        pack_ref[:, k * 128 : (k + 1) * 128] = join(scale_all, swap(shift_all))

    x_copy.wait()

    def load_x(f, carry):
        total, square = carry
        even, odd = pair_halves(paired(raw[f]))
        both = jnp.concatenate([even, odd], axis=-1)
        xs[f, 2 : 2 + rows] = both.astype(BF16)
        return put_row(total, f, full_sum(both)), put_row(square, f, full_sum(both * both))

    zero_rows = jnp.zeros((frames, 128), F32)
    sums = lax.fori_loop(0, frames, load_x, (zero_rows, zero_rows))
    stat_start(0, jnp.concatenate(sums, axis=0))
    g_copy = pltpu.make_async_copy(cot_hbm, raw, local_sem.at[1])
    g_copy.start()
    halo_start(g_halo)

    def conditioning():
        entry = lax.broadcasted_iota(jnp.int32, (frames, 128), 1)
        row = lax.broadcasted_iota(jnp.int32, (frames, 128), 0)
        hot = jnp.zeros((frames, 128), F32)
        for f in range(frames):
            hit = (
                (entry == act_ref[f])
                | (entry == noise_ref[f] + ACTIONS)
                | (entry == game_ref[f] + ACTIONS + NOISE_LEVELS)
            )
            hot = jnp.where((row == f) & hit, 1.0, hot)
        table_rows = tab_ref.shape[0]
        tabp[...] = jnp.zeros(tabp.shape, F32)
        tabp[0:table_rows, :] = tab_ref[...]
        embedded = dot_high(hot, tabp[...])
        pack_ref[:, 512:768] = embedded
        pack_ref[:, 768:896] = hot
        for k in range(4):
            mod = dot_high(embedded, nm_ref[pl.ds(k, 256, stride=4), :]) + nm_ref[
                1024 + k : 1025 + k, :
            ]
            scale = join(mod, swap(mod)) + 1.0
            shift = join(swap(mod), mod)
            if k < 2:
                prm[k * 8 + GAIN] = scale
                prm[k * 8 + SHIFT] = shift
            else:
                prm[k * 8 + GAIN, 0:half, :] = join(scale[0:half], scale[half:])
                prm[k * 8 + SHIFT, 0:half, :] = join(shift[0:half], shift[half:])

    conditioning()

    def tap(index):
        first = (index // 2) * 128
        last = min(first + 128, cw_ref.shape[1])
        tile = cw_ref[:, first:last].astype(BF16).astype(F32)
        if last - first < 128:
            tile = jnp.concatenate([tile, jnp.zeros((64, 128 - last + first), F32)], axis=-1)
        return tile, index % 2

    def low_half(index):
        tile, odd = tap(index)
        return swap(tile) if odd else tile

    def high_half(index):
        tile, odd = tap(index)
        return tile if odd else swap(tile)

    def lane_pair(low_index, high_index):
        zero = jnp.zeros((64, 128), F32)
        low = zero if low_index is None else low_half(low_index)
        high = zero if high_index is None else high_half(high_index)
        return join(low, high).astype(BF16)

    def fine_weights(index, forward_w, backward_w):
        zero = jnp.zeros((64, 128), BF16)
        pairs = []
        for t in range(3):
            p12 = lane_pair(index(t, 1), index(t, 2))
            p01 = lane_pair(index(t, 0), index(t, 1))
            pz0 = lane_pair(None, index(t, 0))
            p2z = lane_pair(index(t, 2), None)
            pairs.append((p12, p01, pz0, p2z))
        for a in range(4):
            for dr in range(2):
                t = a - dr
                ok = 0 <= t <= 2
                for dq in range(2):
                    r = (dr * 2 + dq) * 64
                    first = pairs[t][0 if dq == 0 else 1] if ok else zero
                    second = pairs[t][2 if dq == 0 else 3] if ok else zero
                    forward_w[r : r + 64, a * 256 : a * 256 + 128] = first
                    forward_w[r : r + 64, a * 256 + 128 : a * 256 + 256] = second
                t = 2 - a + dr
                ok = 0 <= t <= 2
                for g in range(4):
                    r = a * 256 + g * 64
                    backward_w[r : r + 64, dr * 128 : dr * 128 + 128] = (
                        pairs[t][g] if ok else zero
                    )

    def coarse_weights(index, forward_w, backward_w):
        for a in range(3):
            for j in range(3):
                lane = (a * 3 + j) * 128
                low = lane_pair(index(a, j), None)
                high = lane_pair(None, index(a, j))
                forward_w[0:64, lane : lane + 128] = low
                forward_w[64:128, lane : lane + 128] = high
                lane = ((2 - a) * 3 + (2 - j)) * 128
                backward_w[lane : lane + 64, :] = low
                backward_w[lane + 64 : lane + 128, :] = high

    def down_weights(index):
        zero = jnp.zeros((64, 128), BF16)
        wdf[...] = jnp.zeros(wdf.shape, BF16)
        wdb[...] = jnp.zeros(wdb.shape, BF16)
        for t in range(3):
            p12 = lane_pair(index(t, 1), index(t, 2))
            pz0 = lane_pair(None, index(t, 0))
            for hi in range(2):
                lane = hi * 768 + t * 256
                wdf[hi * 64 : hi * 64 + 64, lane : lane + 128] = p12
                wdf[hi * 64 : hi * 64 + 64, lane + 128 : lane + 256] = pz0
                i, dr = ((1, 1), (0, 0), (0, 1))[t]
                lane = hi * 256 + dr * 128
                for j in range(2):
                    r = (i * 2 + j) * 128 + hi * 64
                    wdb[r : r + 64, lane : lane + 128] = p12 if j == 0 else pz0

    def up_weights():
        def up_tap(ta, tb):
            return low_half(45 + (ta * 3 + tb) * 2 + 1)

        taps = [[up_tap(ta, tb) for tb in range(3)] for ta in range(3)]
        members = {(0, 0): (0,), (0, 1): (1, 2), (1, 1): (0, 1), (1, 2): (2,)}
        wup[...] = jnp.zeros(wup.shape, BF16)
        for (dr, i), in_rows in members.items():
            for (dq, j), in_cols in members.items():
                total = sum(taps[ta][tb] for ta in in_rows for tb in in_cols)
                zero = jnp.zeros_like(total)
                r = (dr * 2 + dq) * 64
                lane = (i * 3 + j) * 128
                wup[r : r + 64, lane : lane + 128] = join(total, zero).astype(BF16)
                wup[256 + r : 256 + r + 64, lane : lane + 128] = join(zero, swap(total)).astype(
                    BF16
                )
        for a in range(4):
            for g, off in enumerate((0, 1, 2, -1)):
                chosen = [
                    taps[2 - a + dr][1 - off + dq]
                    for dr in range(2)
                    for dq in range(2)
                    if 0 <= 2 - a + dr <= 2 and 0 <= 1 - off + dq <= 2
                ]
                total = sum(chosen[1:], chosen[0])
                zero = jnp.zeros_like(total)
                r = a * 256 + g * 64
                wco[0, r : r + 64, :] = join(total, zero).astype(BF16)
                wco[1, r : r + 64, :] = join(zero, swap(total)).astype(BF16)

    def stacked(k):
        return lambda t, s: k * 9 + t * 3 + s

    fine_weights(stacked(0), w1f, w1b)
    fine_weights(stacked(1), w2f, w2b)
    fine_weights(lambda t, s: 45 + (t * 3 + s) * 2, wsf, wsb)
    up_weights()
    down_weights(stacked(2))
    coarse_weights(stacked(3), w3f, w3b)
    coarse_weights(stacked(4), w4f, w4b)

    halo_wait(x_halo)

    def load_x_halo(f, carry):
        zero = jnp.zeros((1, cols, 128), F32)
        top = paired(xh[0, 0, f])
        low = paired(xh[0, 1, f])
        xs[f, 0] = jnp.concatenate([zero, top[0:1]], axis=-1)[0].astype(BF16)
        xs[f, 1] = jnp.concatenate([top[1:2], top[2:3]], axis=-1)[0].astype(BF16)
        xs[f, rows + 2] = jnp.concatenate([low[0:1], low[1:2]], axis=-1)[0].astype(BF16)
        xs[f, rows + 3] = jnp.concatenate([low[2:3], zero], axis=-1)[0].astype(BF16)
        return carry

    lax.fori_loop(0, frames, load_x_halo, 0)
    norm_forward(0, stat_total(0), False)

    def first_layer(f, carry):
        total, square = carry
        x = xs[f].astype(F32)
        z = x * wide(0, ALPHA, f) + wide(0, BETA, f)
        h = z * logistic(z)
        h = jnp.where(block_mask(h.shape, 2), h, 0.0)
        put_e(e1, f, 0, h)
        out = dot_nt(window(e1, f, 1, rows + 2), w1f[...]).reshape(rows + 2, cols, 256)
        c1[f] = out
        own = out[1 : rows + 1]
        return put_row(total, f, full_sum(own)), put_row(square, f, full_sum(own * own))

    sums = lax.fori_loop(0, frames, first_layer, (zero_rows, zero_rows))
    stat_start(1, jnp.concatenate(sums, axis=0))

    g_copy.wait()
    halo_wait(g_halo)

    def load_g(f, carry):
        live = jnp.where(f < live_ref[0], 1.0, 0.0)
        even, odd = pair_halves(paired(raw[f]))
        own = jnp.concatenate([even, odd], axis=-1)
        zero = jnp.zeros((1, cols, 128), F32)
        top = paired(xh[1, 0, f])
        low = paired(xh[1, 1, f])
        g = jnp.concatenate(
            [
                jnp.concatenate([zero, top[0:1]], axis=-1),
                jnp.concatenate([top[1:2], top[2:3]], axis=-1),
                own,
                jnp.concatenate([low[0:1], low[1:2]], axis=-1),
                jnp.concatenate([low[2:3], zero], axis=-1),
            ],
            axis=0,
        )
        g = jnp.where(block_mask(g.shape, 2), g * live, 0.0)
        put_e(eg, f, 0, g)
        gsa[f] = dot_nn(window(eg, f, 1, rows + 2), wsb[...]).reshape(rows + 2, cols, 256)
        return carry

    lax.fori_loop(0, frames, load_g, 0)

    def coarse_gradient(hf, carry):
        g = dot_nn(window(eg, hf, 1, rows + 2), wco[0]) + dot_nn(
            window(eg, hf + half, 1, rows + 2), wco[1]
        )
        g = g.reshape(rows + 2, cols, 128)
        g = jnp.where(block_mask(g.shape, 1), g, 0.0).astype(BF16).astype(F32)
        gco[hf] = g
        put_ec(ecg, hf, g)
        back = dot_nn(coarse_window(ecg, hf), w4b[...]).reshape(rows, cols, 128)
        gh4[hf, 1 : rows + 1] = back
        border(hout, 0, hf, back)
        return carry

    lax.fori_loop(0, half, coarse_gradient, 0)
    halo_start(g_h4_halo)

    norm_forward(1, stat_total(1), False)

    def second_layer(f, carry):
        z = c1[f] * wide(1, ALPHA, f) + wide(1, BETA, f)
        h = z * logistic(z)
        h = jnp.where(block_mask(h.shape, 1), h, 0.0)
        edge = jnp.zeros((cols, 512), BF16)
        e2[f, 0] = edge
        e2[f, rows + 3] = edge
        put_e(e2, f, 1, h)
        out = dot_nt(window(e2, f, 1, rows + 2), w2f[...]).reshape(rows + 2, cols, 256)
        skip = out + xs[f, 1 : rows + 3].astype(F32)
        skip = jnp.where(block_mask(skip.shape, 1), skip, 0.0)
        put_e(esk, f, 1, skip)
        return carry

    lax.fori_loop(0, frames, second_layer, 0)

    def down_window(f):
        return jnp.concatenate(
            [esk[f, 1 : 1 + rows, :, 256:512], esk[f, 2 : 2 + rows]], axis=-1
        ).reshape(owned, 768)

    zero_coarse = jnp.zeros((half, 128), F32)
    pad_rows = [jnp.zeros((2 * frames - 2 * half, 128), F32)]

    def down_layer(hf, carry):
        total, square = carry
        d = dot_nt(down_window(hf), wdf[:, 0:768]) + dot_nt(
            down_window(hf + half), wdf[:, 768:1536]
        )
        d = d.reshape(rows, cols, 128)
        dv[hf, 1 : rows + 1] = d
        border(hout, 1, hf, d)
        return put_row(total, hf, coarse_sum(d)), put_row(square, hf, coarse_sum(d * d))

    sums = lax.fori_loop(0, half, down_layer, (zero_coarse, zero_coarse))
    stat_start(2, jnp.concatenate(list(sums) + pad_rows, axis=0))
    halo_start(d_halo)

    def put_half(index, value):
        tile = index // 2
        current = gt_ref[tile].astype(F32)
        value = join(current, swap(value)) if index % 2 else join(value, current)
        gt_ref[tile] = value.astype(BF16)

    gt_ref[...] = jnp.zeros(gt_ref.shape, BF16)

    def fine_kernel_grad(index, e, start, gradient, gradient_start):
        acc[0, :, 0:1024] = jnp.zeros((256, 1024), F32)

        def add(f, carry):
            g = own_pixels(gradient, f, gradient_start, rows)
            acc[0, :, 0:1024] += dot_tn(g, window(e, f, start, rows))
            return carry

        lax.fori_loop(0, frames, add, 0)
        for t in range(3):
            u = []
            for dq in range(2):
                parts = [
                    acc[0, (dr * 2 + dq) * 64 : (dr * 2 + dq) * 64 + 64, pl.ds((t + dr) * 256, 256)]
                    for dr in range(2)
                ]
                u.append(parts[0] + parts[1])
            near, far = [v[:, 0:128] for v in u], [v[:, 128:256] for v in u]
            put_half(index(t, 0), swap(far[0]) + near[1])
            put_half(index(t, 1), near[0] + swap(near[1]))
            put_half(index(t, 2), swap(near[0]) + far[1])

    def coarse_kernel_grad(index, ec, gradient):
        acc[0, 0:128, :] = jnp.zeros((128, 1152), F32)

        def add(hf, carry):
            g = gradient[hf, 1 : rows + 1, :, 128:256].reshape(owned, 128)
            acc[0, 0:128, :] += dot_tn(g, coarse_window(ec, hf))
            return carry

        lax.fori_loop(0, half, add, 0)
        for a in range(3):
            for j in range(3):
                lanes = pl.ds((a * 3 + j) * 128, 128)
                put_half(index(a, j), acc[0, 0:64, lanes] + swap(acc[0, 64:128, lanes]))

    def down_kernel_grad(index):
        acc[:, 0:128, 0:768] = jnp.zeros((2, 128, 768), F32)

        def add(hf, carry):
            g = ed[hf, 1 : rows + 1, :, 0:128].reshape(owned, 128)
            acc[0, 0:128, 0:768] += dot_tn(g, down_window(hf))
            acc[1, 0:128, 0:768] += dot_tn(g, down_window(hf + half))
            return carry

        lax.fori_loop(0, half, add, 0)
        for a in range(3):
            near = acc[0, 0:64, pl.ds(a * 256, 128)] + acc[1, 64:128, pl.ds(a * 256, 128)]
            far = (
                acc[0, 0:64, pl.ds(a * 256 + 128, 128)] + acc[1, 64:128, pl.ds(a * 256 + 128, 128)]
            )
            put_half(index(a, 0), swap(far))
            put_half(index(a, 1), near)
            put_half(index(a, 2), swap(near))

    def up_kernel_grad():
        acc[...] = jnp.zeros(acc.shape, F32)

        def add(hf, carry):
            v = coarse_window(ecy, hf)
            acc[0] += dot_tn(own_pixels(eg, hf, 2, rows), v)
            acc[1] += dot_tn(own_pixels(eg, hf + half, 2, rows), v)
            return carry

        lax.fori_loop(0, half, add, 0)

        def block(dr, dq, i, j):
            r = (dr * 2 + dq) * 64
            lanes = pl.ds((i * 3 + j) * 128, 128)
            return acc[0, r : r + 64, lanes] + swap(acc[1, r : r + 64, lanes])

        place = {(0, 0): 0, (0, 1): 1, (0, 2): 1, (1, 0): 1, (1, 1): 1, (1, 2): 2}
        for ta in range(3):
            for tb in range(3):
                total = sum(
                    block(dr, dq, place[dr, ta], place[dq, tb])
                    for dr in range(2)
                    for dq in range(2)
                )
                put_half(45 + (ta * 3 + tb) * 2 + 1, total)

    fine_kernel_grad(lambda t, s: 45 + (t * 3 + s) * 2, esk, 2, eg, 2)

    halo_wait(d_halo)
    norm_forward(2, stat_total(2), True)

    def third_layer(hf, carry):
        total, square = carry
        with_halo(dv, hf, 1)
        z = dv[hf] * param(2, ALPHA, hf) + param(2, BETA, hf)
        h = z * logistic(z)
        put_ec(ec3, hf, jnp.where(block_mask(h.shape, 1), h, 0.0))
        out = dot_nt(coarse_window(ec3, hf), w3f[...]).reshape(rows, cols, 128)
        c3[hf, 1 : rows + 1] = out
        border(hout, 2, hf, out)
        return put_row(total, hf, coarse_sum(out)), put_row(square, hf, coarse_sum(out * out))

    sums = lax.fori_loop(0, half, third_layer, (zero_coarse, zero_coarse))
    stat_start(3, jnp.concatenate(list(sums) + pad_rows, axis=0))
    halo_start(c3_halo)

    halo_wait(c3_halo)
    halo_wait(g_h4_halo)
    norm_forward(3, stat_total(3), True)

    def fourth_layer(hf, carry):
        shift, scale = carry
        with_halo(c3, hf, 2)
        with_halo(gh4, hf, 0)
        v = c3[hf]
        z = v * param(3, ALPHA, hf) + param(3, BETA, hf)
        gate = logistic(z)
        h = z * gate
        put_ec(ec4, hf, jnp.where(block_mask(h.shape, 1), h, 0.0))
        g = gh4[hf] * (gate + h * (1.0 - gate))
        gz4[hf] = g
        own = g[1 : rows + 1]
        xhat = v[1 : rows + 1] * param(3, RSTD, hf) + param(3, NMR, hf)
        return put_row(shift, hf, coarse_sum(own)), put_row(scale, hf, coarse_sum(own * xhat))

    sums = lax.fori_loop(0, half, fourth_layer, (zero_coarse, zero_coarse))
    stat_start(4, jnp.concatenate(list(sums) + pad_rows, axis=0))

    def coarse_output(hf, carry):
        out = dot_nt(coarse_window(ec4, hf), w4f[...]).reshape(rows, cols, 128)
        y = dv[hf, 1 : rows + 1] + out
        border(hout, 3, hf, y)
        edge = jnp.zeros((1, cols, 128), F32)
        put_ec(ecy, hf, jnp.concatenate([edge, y, edge], axis=0))
        return carry

    lax.fori_loop(0, half, coarse_output, 0)
    halo_start(y_halo)
    coarse_kernel_grad(stacked(4), ec4, ecg)

    norm_backward(3, stat_total(4), True)

    def third_back(hf, carry):
        shift, scale = carry
        g = (
            gz4[hf] * param(3, ALPHA, hf)
            + c3[hf] * param(3, COEF, hf)
            + param(3, BIAS, hf)
        )
        put_ec(ecg3, hf, jnp.where(block_mask(g.shape, 1), g, 0.0))
        back = dot_nn(coarse_window(ecg3, hf), w3b[...]).reshape(rows, cols, 128)
        border(hout, 4, hf, back)
        v = dv[hf, 1 : rows + 1]
        z = v * param(2, ALPHA, hf) + param(2, BETA, hf)
        gate = logistic(z)
        own = back * (gate + z * gate * (1.0 - gate))
        gz3[hf, 1 : rows + 1] = own
        xhat = v * param(2, RSTD, hf) + param(2, NMR, hf)
        return put_row(shift, hf, coarse_sum(own)), put_row(scale, hf, coarse_sum(own * xhat))

    sums = lax.fori_loop(0, half, third_back, (zero_coarse, zero_coarse))
    stat_start(5, jnp.concatenate(list(sums) + pad_rows, axis=0))
    halo_start(g_h3_halo)

    halo_wait(y_halo)

    def result_copy(f):
        return pltpu.make_async_copy(raw.at[f], res_hbm.at[f], out_sem.at[f])

    def unpair(lo, hi):
        count = lo.shape[0]
        both = jnp.stack([lo, hi], axis=1).reshape(count * 2, cols, 128)
        tmp[0 : 2 * count, pl.ds(0, cols, stride=2), :] = both
        tmp[0 : 2 * count, pl.ds(1, cols, stride=2), :] = swap(both)

    def merge(hf, carry):
        for side, row in ((0, 0), (1, rows + 1)):
            line = hal[3, side, hf].astype(F32)[None]
            up, down = neighbours(line)
            q = lax.broadcasted_iota(jnp.int32, line.shape, 1)
            ecy[hf, row, :, 0:128] = jnp.where(q == 0, 0.0, down)[0].astype(BF16)
            ecy[hf, row, :, 128:256] = line[0].astype(BF16)
            ecy[hf, row, :, 256:384] = jnp.where(q == cols - 1, 0.0, up)[0].astype(BF16)
        both = dot_nt(coarse_window(ecy, hf), wup[...])
        for hi in range(2):
            f = hf + hi * half
            out = dot_nt(window(esk, f, 2, rows), wsf[...]) + both[:, hi * 256 : hi * 256 + 256]
            out = out.reshape(rows, cols, 256)
            unpair(out[:, :, 0:128], out[:, :, 128:256])
            raw[f] = tmp[:, :, 0:64].astype(BF16)
            result_copy(f).start()
        return carry

    lax.fori_loop(0, half, merge, 0)
    coarse_kernel_grad(stacked(3), ec3, ecg3)

    halo_wait(g_h3_halo)
    norm_backward(2, stat_total(5), True)

    def down_back(hf, carry):
        for side, row in ((0, 0), (1, rows + 1)):
            v = dv[hf, row]
            z = v * param(2, ALPHA, hf) + param(2, BETA, hf)
            gate = logistic(z)
            gz3[hf, row] = hal[4, side, hf].astype(F32) * (gate + z * gate * (1.0 - gate))
        g = (
            gco[hf]
            + gz3[hf] * param(2, ALPHA, hf)
            + dv[hf] * param(2, COEF, hf)
            + param(2, BIAS, hf)
        )
        g = jnp.where(block_mask(g.shape, 1), g, 0.0)
        up, _ = neighbours(g)
        q = lax.broadcasted_iota(jnp.int32, g.shape, 1)
        ed[hf, 0 : rows + 2, :, 0:128] = g.astype(BF16)
        ed[hf, 0 : rows + 2, :, 128:256] = jnp.where(q == cols - 1, 0.0, up).astype(BF16)
        ed[hf, rows + 2] = jnp.zeros((cols, 256), BF16)
        lhs = jnp.concatenate([ed[hf, 0 : rows + 2], ed[hf, 1 : rows + 3]], axis=-1)
        back = dot_nn(lhs.reshape(ext, 512), wdb[...])
        back = back.astype(BF16).astype(F32).reshape(rows + 2, cols, 512)
        for hi in range(2):
            f = hf + hi * half
            total = gsa[f] + back[:, :, hi * 256 : hi * 256 + 256]
            gsa[f] = total
            put_e(eg2, f, 0, jnp.where(block_mask(total.shape, 1), total, 0.0))
        return carry

    lax.fori_loop(0, half, down_back, 0)

    def second_back(f, carry):
        shift, scale = carry
        back = dot_nn(window(eg2, f, 1, rows), w2b[...]).reshape(rows, cols, 256)
        hfout[0, f] = back[0, :, 0:128].astype(BF16)
        hfout[1, f] = back[rows - 1, :, 128:256].astype(BF16)
        v = c1[f, 1 : rows + 1]
        z = v * wide(1, ALPHA, f) + wide(1, BETA, f)
        gate = logistic(z)
        own = back * (gate + z * gate * (1.0 - gate))
        gz[f, 1 : rows + 1] = own
        xhat = v * wide(1, RSTD, f) + wide(1, NMR, f)
        return put_row(shift, f, full_sum(own)), put_row(scale, f, full_sum(own * xhat))

    sums = lax.fori_loop(0, frames, second_back, (zero_rows, zero_rows))
    stat_start(6, jnp.concatenate(sums, axis=0))
    halo_start(g_h2_halo)
    up_kernel_grad()
    down_kernel_grad(stacked(2))
    fine_kernel_grad(stacked(1), e2, 2, eg2, 1)
    halo_wait(g_h2_halo)
    norm_backward(1, stat_total(6), False)

    def first_back(f, carry):
        shift, scale = carry
        for side, row in ((0, 0), (1, rows + 1)):
            v = c1[f, row]
            lanes = slice(128, 256) if side == 0 else slice(0, 128)
            z = v[:, lanes] * param(1, ALPHA, f) + param(1, BETA, f)
            gate = logistic(z)
            g = hfull[side, f].astype(F32) * (gate + z * gate * (1.0 - gate))
            blank = jnp.zeros_like(g)
            gz[f, row] = jnp.concatenate([blank, g] if side == 0 else [g, blank], axis=-1)
        g = gz[f] * wide(1, ALPHA, f) + c1[f] * wide(1, COEF, f) + wide(1, BIAS, f)
        put_e(eg, f, 0, jnp.where(block_mask(g.shape, 1), g, 0.0))
        back = dot_nn(window(eg, f, 1, rows), w1b[...]).reshape(rows, cols, 256)
        v = xs[f, 2 : rows + 2].astype(F32)
        z = v * wide(0, ALPHA, f) + wide(0, BETA, f)
        gate = logistic(z)
        own = back * (gate + z * gate * (1.0 - gate))
        gz[f, 1 : rows + 1] = own
        xhat = v * wide(0, RSTD, f) + wide(0, NMR, f)
        return put_row(shift, f, full_sum(own)), put_row(scale, f, full_sum(own * xhat))

    sums = lax.fori_loop(0, frames, first_back, (zero_rows, zero_rows))
    stat_start(7, jnp.concatenate(sums, axis=0))
    fine_kernel_grad(stacked(0), e1, 2, eg, 1)
    norm_backward(0, stat_total(7), False)

    def frames_copy(f):
        slot = lax.rem(f, 2)
        return pltpu.make_async_copy(fst.at[slot], fg_hbm.at[f], fg_sem.at[slot])

    def frames_back(f, carry):
        g = (
            gsa[f, 1 : rows + 1]
            + gz[f, 1 : rows + 1] * wide(0, ALPHA, f)
            + xs[f, 2 : rows + 2].astype(F32) * wide(0, COEF, f)
            + wide(0, BIAS, f)
        )
        unpair(g[:, :, 0:128], g[:, :, 128:256])

        @pl.when(f >= 2)
        def _():
            frames_copy(f - 2).wait()

        fst[lax.rem(f, 2)] = tmp[:, :, 0:64]
        frames_copy(f).start()
        return carry

    lax.fori_loop(0, frames, frames_back, 0)

    frames_copy(frames - 2).wait()
    frames_copy(frames - 1).wait()
    for f in range(frames):
        result_copy(f).wait()
    for copies in (x_halo, g_halo, g_h4_halo, d_halo, c3_halo, y_halo, g_h3_halo, g_h2_halo):
        halo_finish(copies)


def run_step(n, frames, cotangent, actions, noise_ids, games, live_counts, cw, nm, table):
    count, strip, breadth, _ = frames.shape
    half, rows, cols = count // 2, strip // 2, breadth // 2
    fine = (count, rows + 4, cols, 512)
    coarse = (half, rows + 2, cols, 128)
    coarse_e = (half, rows + 2, cols, 384)
    scratch = [
        VM((count, strip, breadth, 64), BF16),
        VM((2, 2, count, 3, breadth, 64), BF16),
        VM((strip, breadth, 128), F32),
        VM((2, strip, breadth, 64), F32),
        VM((count, rows + 4, cols, 256), BF16),
        VM(fine, BF16),
        VM(fine, BF16),
        VM(fine, BF16),
        VM(fine, BF16),
        VM((count, rows + 2, cols, 512), BF16),
        VM((count, rows + 2, cols, 256), F32),
        VM((count, rows + 2, cols, 256), F32),
        VM((count, rows + 2, cols, 256), F32),
        VM(coarse, F32),
        VM(coarse, F32),
        VM(coarse, F32),
        VM(coarse, F32),
        VM(coarse, F32),
        VM(coarse, F32),
        VM(coarse_e, BF16),
        VM(coarse_e, BF16),
        VM(coarse_e, BF16),
        VM(coarse_e, BF16),
        VM(coarse_e, BF16),
        VM((half, rows + 3, cols, 256), BF16),
        VM((256, 1024), BF16),
        VM((1024, 256), BF16),
        VM((256, 1024), BF16),
        VM((1024, 256), BF16),
        VM((256, 1024), BF16),
        VM((1024, 256), BF16),
        VM((512, 1152), BF16),
        VM((2, 1024, 128), BF16),
        VM((128, 1536), BF16),
        VM((512, 512), BF16),
        VM((128, 1152), BF16),
        VM((1152, 128), BF16),
        VM((128, 1152), BF16),
        VM((1152, 128), BF16),
        VM((2, 256, 1152), F32),
        VM((32, count, 128), F32),
        VM((128, 256), F32),
        VM((8, n, 2 * count, 128), F32),
        VM((5, 2, half, cols, 128), BF16),
        VM((5, 2, half, cols, 128), BF16),
        VM((2, count, cols, 128), BF16),
        VM((2, count, cols, 128), BF16),
        pltpu.SemaphoreType.DMA((2,)),
        pltpu.SemaphoreType.DMA((count,)),
        pltpu.SemaphoreType.DMA((2,)),
        pltpu.SemaphoreType.DMA((8, n - 1)),
        pltpu.SemaphoreType.DMA((8, n - 1)),
        pltpu.SemaphoreType.DMA((8, 2)),
        pltpu.SemaphoreType.DMA((8, 2)),
    ]
    smem = pl.BlockSpec(memory_space=pltpu.SMEM)
    vmem = pl.BlockSpec(memory_space=pltpu.VMEM)
    hbm = pl.BlockSpec(memory_space=pl.ANY)
    return pl.pallas_call(
        functools.partial(step_kernel, n),
        out_shape=(
            jax.ShapeDtypeStruct(frames.shape, BF16),
            jax.ShapeDtypeStruct(frames.shape, F32),
            jax.ShapeDtypeStruct((32, 64, 128), BF16),
            jax.ShapeDtypeStruct((count, 896), F32),
        ),
        in_specs=[hbm, hbm, smem, smem, smem, smem, vmem, vmem, vmem],
        out_specs=(hbm, hbm, vmem, vmem),
        scratch_shapes=scratch,
        compiler_params=pltpu.CompilerParams(
            collective_id=0, has_side_effects=True, vmem_limit_bytes=62 * 1024 * 1024
        ),
        name="step",
    )(frames, cotangent, actions, noise_ids, games, live_counts, cw, nm, table)


def adamw(weight, moment, square, grad_value, rate):
    fix_one = 1.0 - BETA_ONE**ADAM_STEP
    fix_two = 1.0 - BETA_TWO**ADAM_STEP
    moment_new = BETA_ONE * moment + (1.0 - BETA_ONE) * grad_value
    square_new = BETA_TWO * square + (1.0 - BETA_TWO) * grad_value * grad_value
    fixed_m = moment_new / fix_one
    fixed_v = square_new / fix_two
    weight_new = weight - rate * (fixed_m / (jnp.sqrt(fixed_v) + ADAM_EPS) + DECAY * weight)
    return (moment_new, square_new, weight_new, weight_new.astype(BF16))


def reduce_kernel(
    nd, ns, gt, pk, out, packs, rbuf, part, zbuf, own, sem_a, sem_b, sem_c, sem_d, sem_p, bar_unused
):
    dp = lax.axis_index("dp")
    sp = lax.axis_index("space")
    barrier = pltpu.get_barrier_semaphore()
    for off in range(1, nd):
        pl.semaphore_signal(
            barrier, inc=1, device_id={"dp": lax.rem(dp + off, nd)}, device_id_type=MESH
        )
    for off in range(1, ns):
        pl.semaphore_signal(
            barrier, inc=1, device_id={"space": lax.rem(sp + off, ns)}, device_id_type=MESH
        )
    pl.semaphore_wait(barrier, nd + ns - 2)

    def copy(src, dst, sems, off, axis):
        here, size = (dp, nd) if axis == "dp" else (sp, ns)
        return pltpu.make_async_remote_copy(
            src_ref=src,
            dst_ref=dst,
            send_sem=sems.at[0, off - 1],
            recv_sem=sems.at[1, off - 1],
            device_id={axis: lax.rem(here + off, size)},
            device_id_type=MESH,
        )

    def before(off, axis):
        here, size = (dp, nd) if axis == "dp" else (sp, ns)
        return lax.rem(here + size - off, size)

    def after(off, axis):
        here, size = (dp, nd) if axis == "dp" else (sp, ns)
        return lax.rem(here + off, size)

    packs[dp] = pk[...]
    for off in range(1, nd):
        copy(gt.at[after(off, "dp")], rbuf.at[dp], sem_a, off, "dp").start()
    for off in range(1, nd):
        copy(packs.at[dp], packs.at[dp], sem_p, off, "dp").start()
    rbuf[dp] = gt[dp]
    for off in range(1, nd):
        copy(gt.at[0], rbuf.at[before(off, "dp")], sem_a, off, "dp").wait_recv()
    total = rbuf[0].astype(F32)
    for i in range(1, nd):
        total = total + rbuf[i].astype(F32)
    part[...] = total
    for off in range(1, ns):
        copy(part.at[after(off, "space")], zbuf.at[sp], sem_b, off, "space").start()
    zbuf[sp] = part[sp]
    for off in range(1, ns):
        copy(part.at[0], zbuf.at[before(off, "space")], sem_b, off, "space").wait_recv()
    total = zbuf[0]
    for i in range(1, ns):
        total = total + zbuf[i]
    out[dp, sp] = total.astype(BF16)
    for off in range(1, ns):
        copy(out.at[dp, sp], out.at[dp, sp], sem_c, off, "space").start()
    for off in range(1, ns):
        slot = before(off, "space")
        copy(out.at[dp, slot], out.at[dp, slot], sem_c, off, "space").wait_recv()
    for off in range(1, nd):
        copy(out.at[dp], out.at[dp], sem_d, off, "dp").start()
    for off in range(1, nd):
        slot = before(off, "dp")
        copy(out.at[slot], out.at[slot], sem_d, off, "dp").wait_recv()
        copy(packs.at[slot], packs.at[slot], sem_p, off, "dp").wait_recv()
    for off in range(1, nd):
        copy(gt.at[0], rbuf.at[dp], sem_a, off, "dp").wait_send()
        copy(packs.at[dp], packs.at[dp], sem_p, off, "dp").wait_send()
        copy(out.at[dp], out.at[dp], sem_d, off, "dp").wait_send()
    for off in range(1, ns):
        copy(part.at[0], zbuf.at[sp], sem_b, off, "space").wait_send()
        copy(out.at[dp, sp], out.at[dp, sp], sem_c, off, "space").wait_send()


def run_reduce(nd, ns, gt, pack):
    rpd = 2048 // (nd * ns)
    shape = (nd, ns, rpd, 128)
    vmem = pl.BlockSpec(memory_space=pltpu.VMEM)
    sems = lambda k: pltpu.SemaphoreType.DMA((2, k - 1))
    return pl.pallas_call(
        functools.partial(reduce_kernel, nd, ns),
        out_shape=(
            jax.ShapeDtypeStruct(shape, BF16),
            jax.ShapeDtypeStruct((nd,) + pack.shape, F32),
        ),
        in_specs=[vmem, vmem],
        out_specs=(vmem, vmem),
        scratch_shapes=[
            VM(shape, BF16),
            VM(shape[1:], F32),
            VM(shape[1:], F32),
            VM(shape[2:], F32),
            sems(nd),
            sems(ns),
            sems(ns),
            sems(nd),
            sems(nd),
            pltpu.SemaphoreType.REGULAR,
        ],
        compiler_params=pltpu.CompilerParams(
            collective_id=1, has_side_effects=True, vmem_limit_bytes=32 * 1024 * 1024
        ),
        name="reduce",
    )(gt.reshape(shape), pack)


def local(
    nd,
    ns,
    frames,
    cotangent,
    actions,
    noise_ids,
    games,
    live_counts,
    conv_weight,
    conv_moment,
    conv_square,
    norm_map,
    norm_moment,
    norm_square,
    emb_table,
    table_moment,
    table_square,
):
    cw = conv_weight.T
    nm = jnp.transpose(norm_map, (1, 0, 2)).reshape(-1, 128)
    result, frames_grad, gt, pack = run_step(
        ns, frames, cotangent, actions, noise_ids, games, live_counts, cw, nm, emb_table
    )
    grads, packs = run_reduce(nd, ns, gt, pack)
    conv_rows = conv_weight.shape[0]
    grad_t = (
        grads.reshape(32, 64, 128).transpose(1, 0, 2).reshape(64, 4096)[:, :conv_rows].astype(F32)
    )
    conv_out = [v.T for v in adamw(cw, conv_moment.T, conv_square.T, grad_t, 0.05)]
    packs = packs.reshape(-1, 896)
    dmods = packs[:, 0:512]
    embedded = packs[:, 512:768]
    hot = packs[:, 768 : 768 + emb_table.shape[0]]
    top = jnp.dot(embedded.T, dmods, precision=HIGH).reshape(256, 4, 128)
    last = jnp.sum(dmods, axis=0).reshape(1, 4, 128)
    grad_map = jnp.concatenate([top, last], axis=0).transpose(1, 0, 2)
    norm_out = adamw(norm_map, norm_moment, norm_square, grad_map, 0.04)
    g_embed = jnp.dot(
        dmods, norm_map[:, :-1].transpose(0, 2, 1).reshape(512, 256), precision=HIGH
    )
    grad_table = jnp.dot(hot.T, g_embed, precision=HIGH)
    table_out = adamw(emb_table, table_moment, table_square, grad_table, 0.5)
    return (result, frames_grad, *conv_out, *norm_out, *table_out)


def solution(mesh):
    split = P("dp", "space", None, None)
    in_specs = (split, split) + (P("dp"),) * 4 + (P(),) * 9
    out_specs = (split, split) + (P(),) * 12
    sizes = dict(mesh.shape)
    return jax.shard_map(
        functools.partial(local, sizes["dp"], sizes["space"]),
        mesh=mesh,
        in_specs=in_specs,
        out_specs=out_specs,
        check_vma=False,
    )
```

```python
import functools

import jax
import jax.numpy as jnp
from jax import lax
from jax.experimental import pallas as pl
from jax.experimental.pallas import tpu as pltpu
from jax.sharding import PartitionSpec as P

ACTIONS = 18
NOISE_LEVELS = 64
ADAM_STEP = 4
NORM_EPSILON = 1e-05
ADAM_EPS = 1e-08
BETA_ONE = 0.5
BETA_TWO = 0.5
DECAY = 0.01
HIGH = lax.Precision.HIGHEST
F32 = jnp.float32
BF16 = jnp.bfloat16
MESH = pl.DeviceIdType.MESH
VM = pltpu.VMEM

ALPHA, BETA, RSTD, NMR, GAIN, SHIFT, COEF, BIAS = range(8)


def dot_nn(a, b):
    return lax.dot_general(a, b, (((1,), (0,)), ((), ())), preferred_element_type=F32)


def dot_nt(a, b):
    return lax.dot_general(a, b, (((1,), (1,)), ((), ())), preferred_element_type=F32)


def dot_tn(a, b):
    return lax.dot_general(a, b, (((0,), (0,)), ((), ())), preferred_element_type=F32)


def dot_high(a, b):
    return lax.dot_general(
        a, b, (((1,), (0,)), ((), ())), precision=HIGH, preferred_element_type=F32
    )


def logistic(z):
    return 0.5 * jnp.tanh(0.5 * z) + 0.5


def lane_iota(shape):
    return lax.broadcasted_iota(jnp.int32, shape, len(shape) - 1)


def swap(v):
    return pltpu.roll(v, 64, len(v.shape) - 1)


def join(lo, hi):
    return jnp.where(lane_iota(lo.shape) < 64, lo, hi)


def twice(row):
    return jnp.concatenate([row, row], axis=-1)


def step_kernel(
    nd,
    n,
    x_hbm,
    cot_hbm,
    act_ref,
    noise_ref,
    game_ref,
    live_ref,
    cw_ref,
    nm_hbm,
    tab_ref,
    res_hbm,
    fg_hbm,
    gout_ref,
    packs,
    raw,
    xh,
    tmp,
    fst,
    xs,
    e1,
    e2,
    esk,
    eg,
    eg2,
    c1,
    gsa,
    gz,
    dv,
    c3,
    gh4,
    gz4,
    gz3,
    gco,
    ec3,
    ec4,
    ecg,
    ecg3,
    ecy,
    ed,
    w1f,
    w1b,
    w2f,
    w2b,
    wsf,
    wsb,
    wup,
    wco,
    wdf,
    wdb,
    w3f,
    w3b,
    w4f,
    w4b,
    acc,
    prm,
    tabp,
    stat,
    hal,
    hout,
    hfull,
    hfout,
    nmv,
    nmb,
    gt_ref,
    rbuf,
    part,
    zbuf,
    zfull,
    gall,
    local_sem,
    out_sem,
    fg_sem,
    stat_send,
    stat_recv,
    halo_send,
    halo_recv,
    dp_send,
    dp_recv,
    sp_send,
    sp_recv,
):
    frames, strip = raw.shape[0], raw.shape[1]
    breadth = raw.shape[2]
    half = frames // 2
    rows = strip // 2
    cols = breadth // 2
    me = lax.axis_index("space")
    dp = lax.axis_index("dp")
    full_cells = float(strip * n * breadth * 32)
    coarse_cells = full_cells / 4.0
    owned = rows * cols
    ext = (rows + 2) * cols

    barrier = pltpu.get_barrier_semaphore()
    for off in range(1, n):
        pl.semaphore_signal(
            barrier,
            inc=1,
            device_id={"space": lax.rem(me + off, n)},
            device_id_type=MESH,
        )
    for off in range(1, nd):
        pl.semaphore_signal(
            barrier,
            inc=1,
            device_id={"dp": lax.rem(dp + off, nd)},
            device_id_type=MESH,
        )

    x_copy = pltpu.make_async_copy(x_hbm, raw, local_sem.at[0])
    x_copy.start()
    map_copies = [
        pltpu.make_async_copy(nm_hbm.at[pl.ds(0, 256), k], nmv.at[k], local_sem.at[2 + k])
        for k in range(4)
    ]
    map_copies.append(pltpu.make_async_copy(nm_hbm.at[256], nmb, local_sem.at[6]))
    for copy in map_copies:
        copy.start()
    pl.semaphore_wait(barrier, n + nd - 2)

    def halo_copies(k, first, last, to_up, to_down):
        up = pltpu.make_async_remote_copy(
            src_ref=first,
            dst_ref=to_up,
            send_sem=halo_send.at[k, 0],
            recv_sem=halo_recv.at[k, 0],
            device_id={"space": lax.rem(me + n - 1, n)},
            device_id_type=MESH,
        )
        down = pltpu.make_async_remote_copy(
            src_ref=last,
            dst_ref=to_down,
            send_sem=halo_send.at[k, 1],
            recv_sem=halo_recv.at[k, 1],
            device_id={"space": lax.rem(me + 1, n)},
            device_id_type=MESH,
        )
        return up, down

    def halo_start(copies):
        @pl.when(me > 0)
        def _():
            copies[0].start()

        @pl.when(me < n - 1)
        def _():
            copies[1].start()

    def halo_wait(copies):
        @pl.when(me < n - 1)
        def _():
            copies[0].wait_recv()

        @pl.when(me > 0)
        def _():
            copies[1].wait_recv()

    def halo_finish(copies):
        @pl.when(me > 0)
        def _():
            copies[0].wait_send()

        @pl.when(me < n - 1)
        def _():
            copies[1].wait_send()

    def stat_copy(k, off, slot):
        return pltpu.make_async_remote_copy(
            src_ref=stat.at[k, slot],
            dst_ref=stat.at[k, slot],
            send_sem=stat_send.at[k, off - 1],
            recv_sem=stat_recv.at[k, off - 1],
            device_id={"space": lax.rem(me + off, n)},
            device_id_type=MESH,
        )

    def stat_start(k, value):
        stat[k, me] = value
        for off in range(1, n):
            stat_copy(k, off, me).start()

    def stat_total(k):
        for off in range(1, n):
            stat_copy(k, off, lax.rem(me + n - off, n)).wait_recv()
        total = stat[k, 0]
        for i in range(1, n):
            total = total + stat[k, i]
        for off in range(1, n):
            stat_copy(k, off, me).wait_send()
        return total

    x_halo = halo_copies(
        0, x_hbm.at[:, pl.ds(0, 3)], x_hbm.at[:, pl.ds(strip - 3, 3)], xh.at[0, 1], xh.at[0, 0]
    )
    g_halo = halo_copies(
        1, cot_hbm.at[:, pl.ds(0, 3)], cot_hbm.at[:, pl.ds(strip - 3, 3)], xh.at[1, 1], xh.at[1, 0]
    )
    for side in range(2):

        @pl.when((me == 0) if side == 0 else (me == n - 1))
        def _():
            for which in range(2):
                xh[which, side] = jnp.zeros(xh.shape[2:], BF16)
            for which in range(hal.shape[0]):
                hal[which, side] = jnp.zeros(hal.shape[2:], BF16)
            hfull[side] = jnp.zeros(hfull.shape[1:], BF16)

    halo_start(x_halo)

    def coarse_halo(k):
        return halo_copies(
            k, hout.at[k - 2, 0], hout.at[k - 2, 1], hal.at[k - 2, 1], hal.at[k - 2, 0]
        )

    g_h4_halo, d_halo, c3_halo, y_halo, g_h3_halo = [coarse_halo(k) for k in range(2, 7)]
    g_h2_halo = halo_copies(7, hfout.at[0], hfout.at[1], hfull.at[1], hfull.at[0])

    def block_mask(shape, pad):
        blocks = shape[0]
        b = lax.broadcasted_iota(jnp.int32, shape, 0)
        low = jnp.where(me > 0, 0, pad)
        high = jnp.where(me < n - 1, blocks, blocks - pad)
        return (b >= low) & (b < high)

    def param(k, which, f):
        return prm[k * 8 + which, pl.ds(f, 1), :]

    def wide(k, which, f):
        return twice(param(k, which, f))

    def put_row(carry, f, value):
        row = lax.broadcasted_iota(jnp.int32, carry.shape, 0)
        return jnp.where(row == f, value, carry)

    def full_sum(v):
        s = jnp.sum(v.reshape(-1, 256), axis=0, keepdims=True)
        return s[:, :128] + s[:, 128:]

    def paired(raw_rows):
        count = raw_rows.shape[0]
        tmp[0:count, :, 0:64] = raw_rows.astype(F32)
        even = tmp[0:count, pl.ds(0, cols, stride=2), :]
        odd = tmp[0:count, pl.ds(1, cols, stride=2), :]
        return join(even, swap(odd))

    def pair_halves(p):
        count = p.shape[0] // 2
        p = p.reshape(count, 2, cols, 128)
        return p[:, 0], p[:, 1]

    def neighbours(v):
        count = v.shape[0]
        flat = v.reshape(count * cols, 128)
        up = pltpu.roll(flat, count * cols - 1, 0).reshape(v.shape)
        down = pltpu.roll(flat, 1, 0).reshape(v.shape)
        return up, down

    def put_e(e, f, start, h):
        count = h.shape[0]
        for part in range(2):
            v = h[:, :, part * 128 : (part + 1) * 128]
            up, down = neighbours(v)
            lane = lane_iota(v.shape)
            q = lax.broadcasted_iota(jnp.int32, v.shape, 1)
            near = jnp.where(
                lane < 64, jnp.where(q == cols - 1, 0.0, up), jnp.where(q == 0, 0.0, down)
            )
            e[f, start : start + count, :, part * 256 : part * 256 + 128] = v.astype(BF16)
            e[f, start : start + count, :, part * 256 + 128 : part * 256 + 256] = near.astype(BF16)

    def window(e, f, start, count):
        return jnp.concatenate(
            [
                e[f, start - 1 : start - 1 + count, :, 256:512],
                e[f, start : start + count, :, :],
                e[f, start + 1 : start + 1 + count, :, 0:256],
            ],
            axis=-1,
        ).reshape(count * cols, 1024)

    def own_pixels(e, f, start, count):
        return jnp.concatenate(
            [
                e[f, start : start + count, :, 0:128],
                e[f, start : start + count, :, 256:384],
            ],
            axis=-1,
        ).reshape(count * cols, 256)

    def put_ec(ec, hf, v):
        up, down = neighbours(v)
        q = lax.broadcasted_iota(jnp.int32, v.shape, 1)
        ec[hf, :, :, 0:128] = jnp.where(q == 0, 0.0, down).astype(BF16)
        ec[hf, :, :, 128:256] = v.astype(BF16)
        ec[hf, :, :, 256:384] = jnp.where(q == cols - 1, 0.0, up).astype(BF16)

    def coarse_window(ec, hf):
        return jnp.concatenate([ec[hf, a : a + rows] for a in range(3)], axis=-1).reshape(
            owned, 1152
        )

    def coarse_sum(v):
        return jnp.sum(v.reshape(-1, 128), axis=0, keepdims=True)

    def with_halo(ref, hf, k):
        ref[hf, 0] = hal[k, 0, hf].astype(F32)
        ref[hf, rows + 1] = hal[k, 1, hf].astype(F32)

    def border(ref_out, k, hf, v):
        ref_out[k, 0, hf] = v[0].astype(BF16)
        ref_out[k, 1, hf] = v[rows - 1].astype(BF16)

    def group_matrix(coarse):
        r = lax.broadcasted_iota(jnp.int32, (128, 128), 0) // 32
        c = lax.broadcasted_iota(jnp.int32, (128, 128), 1) // 32
        same = (r == c) if coarse else (r % 2 == c % 2)
        return jnp.where(same, 1.0, 0.0)

    def norm_forward(k, total, coarse):
        cells = coarse_cells if coarse else full_cells
        count = half if coarse else frames
        moments = dot_high(total, group_matrix(coarse)) / cells
        mean = moments[0:count]
        var = moments[count : 2 * count] - mean * mean
        rstd = lax.rsqrt(var + NORM_EPSILON)
        gain = prm[k * 8 + GAIN, 0:count, :]
        alpha = rstd * gain
        prm[k * 8 + ALPHA, 0:count, :] = alpha
        prm[k * 8 + BETA, 0:count, :] = prm[k * 8 + SHIFT, 0:count, :] - mean * alpha
        prm[k * 8 + RSTD, 0:count, :] = rstd
        prm[k * 8 + NMR, 0:count, :] = -mean * rstd

    def norm_backward(k, total, coarse):
        cells = coarse_cells if coarse else full_cells
        count = half if coarse else frames
        gain = prm[k * 8 + GAIN, 0:count, :]
        shift_grad = total[0:count]
        scale_grad = total[count : 2 * count]
        means = (
            dot_high(
                jnp.concatenate([shift_grad * gain, scale_grad * gain], axis=0),
                group_matrix(coarse),
            )
            / cells
        )
        rstd = prm[k * 8 + RSTD, 0:count, :]
        factor = -rstd * means[count : 2 * count]
        prm[k * 8 + COEF, 0:count, :] = rstd * factor
        prm[k * 8 + BIAS, 0:count, :] = (
            prm[k * 8 + NMR, 0:count, :] * factor - rstd * means[0:count]
        )
        if coarse:
            scale_all = jnp.concatenate([scale_grad, swap(scale_grad)], axis=0)
            shift_all = jnp.concatenate([shift_grad, swap(shift_grad)], axis=0)
        else:
            scale_all = scale_grad + swap(scale_grad)
            shift_all = shift_grad + swap(shift_grad)
        packs[dp, :, k * 128 : (k + 1) * 128] = join(scale_all, swap(shift_all))

    slots = 32 // nd
    share = 64 // n
    first_slots = [
        [i for i in range(slots) if i * nd >= 16],
        [i for i in range(slots) if 8 <= i * nd < 16],
        [0],
    ]

    def dp_before(off):
        return lax.rem(dp + nd - off, nd)

    def dp_after(off):
        return lax.rem(dp + off, nd)

    def sp_before(off):
        return lax.rem(me + n - off, n)

    def sp_after(off):
        return lax.rem(me + off, n)

    def stage_slots(stage):
        chosen = first_slots[stage]
        return pl.ds(chosen[0], len(chosen))

    def dp_copy(stage, phase, src, dst, off):
        return pltpu.make_async_remote_copy(
            src_ref=src,
            dst_ref=dst,
            send_sem=dp_send.at[stage, phase, off - 1],
            recv_sem=dp_recv.at[stage, phase, off - 1],
            device_id={"dp": dp_after(off)},
            device_id_type=MESH,
        )

    def sp_copy(stage, phase, src, dst, off):
        return pltpu.make_async_remote_copy(
            src_ref=src,
            dst_ref=dst,
            send_sem=sp_send.at[stage, phase, off - 1],
            recv_sem=sp_recv.at[stage, phase, off - 1],
            device_id={"space": sp_after(off)},
            device_id_type=MESH,
        )

    def first_copy(stage, off, owner, slot):
        where = stage_slots(stage)
        return dp_copy(stage, 0, gt_ref.at[where, owner], rbuf.at[slot, where], off)

    def second_copy(stage, off, row, slot):
        where = stage_slots(stage)
        return sp_copy(stage, 0, part.at[row, where], zbuf.at[slot, where], off)

    def third_copy(stage, off, slot):
        where = stage_slots(stage)
        return sp_copy(stage, 1, zfull.at[slot, where], zfull.at[slot, where], off)

    def fourth_copy(stage, off, slot):
        where = stage_slots(stage)
        return dp_copy(stage, 1, gall.at[slot, where], gall.at[slot, where], off)

    def pack_copy(which, off, slot):
        lanes = pl.ds(0, 128) if which else pl.ds(128, 768)
        return dp_copy(3, which, packs.at[slot, :, lanes], packs.at[slot, :, lanes], off)

    def pack_start(which):
        for off in range(1, nd):
            pack_copy(which, off, dp).start()

    def gather_start(stage):
        if not first_slots[stage]:
            return
        for off in range(1, nd):
            first_copy(stage, off, dp_after(off), dp).start()

    def gather_space(stage):
        if not first_slots[stage]:
            return
        where = stage_slots(stage)
        for off in range(1, nd):
            first_copy(stage, off, dp, dp_before(off)).wait_recv()
        rbuf[dp, where] = gt_ref[where, dp]
        total = rbuf[0, where].astype(F32)
        for i in range(1, nd):
            total = total + rbuf[i, where].astype(F32)
        for z in range(n):
            part[z, where] = total[:, z * share : (z + 1) * share]
        for off in range(1, n):
            second_copy(stage, off, sp_after(off), me).start()

    def gather_spread(stage):
        if not first_slots[stage]:
            return
        where = stage_slots(stage)
        for off in range(1, n):
            second_copy(stage, off, me, sp_before(off)).wait_recv()
        zbuf[me, where] = part[me, where]
        total = zbuf[0, where]
        for i in range(1, n):
            total = total + zbuf[i, where]
        zfull[me, where] = total
        for off in range(1, n):
            third_copy(stage, off, me).start()

    def gather_all(stage):
        if not first_slots[stage]:
            return
        where = stage_slots(stage)
        for off in range(1, n):
            third_copy(stage, off, sp_before(off)).wait_recv()
        whole = jnp.concatenate([zfull[z, where] for z in range(n)], axis=1)
        gall[dp, where] = whole.astype(BF16)
        for off in range(1, nd):
            fourth_copy(stage, off, dp).start()

    def gather_finish(stage):
        if not first_slots[stage]:
            return
        for off in range(1, nd):
            fourth_copy(stage, off, dp_before(off)).wait_recv()
            first_copy(stage, off, dp_after(off), dp).wait_send()
            fourth_copy(stage, off, dp).wait_send()
        for off in range(1, n):
            second_copy(stage, off, sp_after(off), me).wait_send()
            third_copy(stage, off, me).wait_send()

    x_copy.wait()

    def load_x(f, carry):
        total, square = carry
        even, odd = pair_halves(paired(raw[f]))
        both = jnp.concatenate([even, odd], axis=-1)
        xs[f, 2 : 2 + rows] = both.astype(BF16)
        return put_row(total, f, full_sum(both)), put_row(square, f, full_sum(both * both))

    zero_rows = jnp.zeros((frames, 128), F32)
    sums = lax.fori_loop(0, frames, load_x, (zero_rows, zero_rows))
    stat_start(0, jnp.concatenate(sums, axis=0))
    g_copy = pltpu.make_async_copy(cot_hbm, raw, local_sem.at[1])
    g_copy.start()
    halo_start(g_halo)

    def conditioning():
        entry = lax.broadcasted_iota(jnp.int32, (frames, 128), 1)
        row = lax.broadcasted_iota(jnp.int32, (frames, 128), 0)
        hot = jnp.zeros((frames, 128), F32)
        for f in range(frames):
            hit = (
                (entry == act_ref[f])
                | (entry == noise_ref[f] + ACTIONS)
                | (entry == game_ref[f] + ACTIONS + NOISE_LEVELS)
            )
            hot = jnp.where((row == f) & hit, 1.0, hot)
        table_rows = tab_ref.shape[0]
        tabp[...] = jnp.zeros(tabp.shape, F32)
        tabp[0:table_rows, :] = tab_ref[...]
        embedded = dot_high(hot, tabp[...])
        packs[dp, :, 512:768] = embedded
        packs[dp, :, 768:896] = hot
        for copy in map_copies:
            copy.wait()
        for k in range(4):
            mod = dot_high(embedded, nmv[k]) + nmb[k : k + 1, :]
            scale = join(mod, swap(mod)) + 1.0
            shift = join(swap(mod), mod)
            if k < 2:
                prm[k * 8 + GAIN] = scale
                prm[k * 8 + SHIFT] = shift
            else:
                prm[k * 8 + GAIN, 0:half, :] = join(scale[0:half], scale[half:])
                prm[k * 8 + SHIFT, 0:half, :] = join(shift[0:half], shift[half:])

    conditioning()

    def tap(index):
        first = (index // 2) * 128
        last = min(first + 128, cw_ref.shape[1])
        tile = cw_ref[:, first:last].astype(BF16).astype(F32)
        if last - first < 128:
            tile = jnp.concatenate([tile, jnp.zeros((64, 128 - last + first), F32)], axis=-1)
        return tile, index % 2

    def low_half(index):
        tile, odd = tap(index)
        return swap(tile) if odd else tile

    def high_half(index):
        tile, odd = tap(index)
        return tile if odd else swap(tile)

    def lane_pair(low_index, high_index):
        zero = jnp.zeros((64, 128), F32)
        low = zero if low_index is None else low_half(low_index)
        high = zero if high_index is None else high_half(high_index)
        return join(low, high).astype(BF16)

    def fine_weights(index, forward_w, backward_w):
        zero = jnp.zeros((64, 128), BF16)
        pairs = []
        for t in range(3):
            p12 = lane_pair(index(t, 1), index(t, 2))
            p01 = lane_pair(index(t, 0), index(t, 1))
            pz0 = lane_pair(None, index(t, 0))
            p2z = lane_pair(index(t, 2), None)
            pairs.append((p12, p01, pz0, p2z))
        for a in range(4):
            for dr in range(2):
                t = a - dr
                ok = 0 <= t <= 2
                for dq in range(2):
                    r = (dr * 2 + dq) * 64
                    first = pairs[t][0 if dq == 0 else 1] if ok else zero
                    second = pairs[t][2 if dq == 0 else 3] if ok else zero
                    forward_w[r : r + 64, a * 256 : a * 256 + 128] = first
                    forward_w[r : r + 64, a * 256 + 128 : a * 256 + 256] = second
                t = 2 - a + dr
                ok = 0 <= t <= 2
                for g in range(4):
                    r = a * 256 + g * 64
                    backward_w[r : r + 64, dr * 128 : dr * 128 + 128] = (
                        pairs[t][g] if ok else zero
                    )

    def coarse_weights(index, forward_w, backward_w):
        for a in range(3):
            for j in range(3):
                lane = (a * 3 + j) * 128
                low = lane_pair(index(a, j), None)
                high = lane_pair(None, index(a, j))
                forward_w[0:64, lane : lane + 128] = low
                forward_w[64:128, lane : lane + 128] = high
                lane = ((2 - a) * 3 + (2 - j)) * 128
                backward_w[lane : lane + 64, :] = low
                backward_w[lane + 64 : lane + 128, :] = high

    def down_weights(index):
        zero = jnp.zeros((64, 128), BF16)
        wdf[...] = jnp.zeros(wdf.shape, BF16)
        wdb[...] = jnp.zeros(wdb.shape, BF16)
        for t in range(3):
            p12 = lane_pair(index(t, 1), index(t, 2))
            pz0 = lane_pair(None, index(t, 0))
            for hi in range(2):
                lane = hi * 768 + t * 256
                wdf[hi * 64 : hi * 64 + 64, lane : lane + 128] = p12
                wdf[hi * 64 : hi * 64 + 64, lane + 128 : lane + 256] = pz0
                i, dr = ((1, 1), (0, 0), (0, 1))[t]
                lane = hi * 256 + dr * 128
                for j in range(2):
                    r = (i * 2 + j) * 128 + hi * 64
                    wdb[r : r + 64, lane : lane + 128] = p12 if j == 0 else pz0

    def up_weights():
        def up_tap(ta, tb):
            return low_half(45 + (ta * 3 + tb) * 2 + 1)

        taps = [[up_tap(ta, tb) for tb in range(3)] for ta in range(3)]
        members = {(0, 0): (0,), (0, 1): (1, 2), (1, 1): (0, 1), (1, 2): (2,)}
        wup[...] = jnp.zeros(wup.shape, BF16)
        for (dr, i), in_rows in members.items():
            for (dq, j), in_cols in members.items():
                total = sum(taps[ta][tb] for ta in in_rows for tb in in_cols)
                zero = jnp.zeros_like(total)
                r = (dr * 2 + dq) * 64
                lane = (i * 3 + j) * 128
                wup[r : r + 64, lane : lane + 128] = join(total, zero).astype(BF16)
                wup[256 + r : 256 + r + 64, lane : lane + 128] = join(zero, swap(total)).astype(
                    BF16
                )
        for a in range(4):
            for g, off in enumerate((0, 1, 2, -1)):
                chosen = [
                    taps[2 - a + dr][1 - off + dq]
                    for dr in range(2)
                    for dq in range(2)
                    if 0 <= 2 - a + dr <= 2 and 0 <= 1 - off + dq <= 2
                ]
                total = sum(chosen[1:], chosen[0])
                zero = jnp.zeros_like(total)
                r = a * 256 + g * 64
                wco[0, r : r + 64, :] = join(total, zero).astype(BF16)
                wco[1, r : r + 64, :] = join(zero, swap(total)).astype(BF16)

    def stacked(k):
        return lambda t, s: k * 9 + t * 3 + s

    fine_weights(stacked(0), w1f, w1b)
    fine_weights(stacked(1), w2f, w2b)
    fine_weights(lambda t, s: 45 + (t * 3 + s) * 2, wsf, wsb)
    up_weights()
    down_weights(stacked(2))
    coarse_weights(stacked(3), w3f, w3b)
    coarse_weights(stacked(4), w4f, w4b)

    halo_wait(x_halo)

    def load_x_halo(f, carry):
        zero = jnp.zeros((1, cols, 128), F32)
        top = paired(xh[0, 0, f])
        low = paired(xh[0, 1, f])
        xs[f, 0] = jnp.concatenate([zero, top[0:1]], axis=-1)[0].astype(BF16)
        xs[f, 1] = jnp.concatenate([top[1:2], top[2:3]], axis=-1)[0].astype(BF16)
        xs[f, rows + 2] = jnp.concatenate([low[0:1], low[1:2]], axis=-1)[0].astype(BF16)
        xs[f, rows + 3] = jnp.concatenate([low[2:3], zero], axis=-1)[0].astype(BF16)
        return carry

    lax.fori_loop(0, frames, load_x_halo, 0)
    norm_forward(0, stat_total(0), False)

    def first_layer(f, carry):
        total, square = carry
        x = xs[f].astype(F32)
        z = x * wide(0, ALPHA, f) + wide(0, BETA, f)
        h = z * logistic(z)
        h = jnp.where(block_mask(h.shape, 2), h, 0.0)
        put_e(e1, f, 0, h)
        out = dot_nt(window(e1, f, 1, rows + 2), w1f[...]).reshape(rows + 2, cols, 256)
        c1[f] = out
        own = out[1 : rows + 1]
        return put_row(total, f, full_sum(own)), put_row(square, f, full_sum(own * own))

    sums = lax.fori_loop(0, frames, first_layer, (zero_rows, zero_rows))
    stat_start(1, jnp.concatenate(sums, axis=0))

    g_copy.wait()
    halo_wait(g_halo)

    def load_g(f, carry):
        live = jnp.where(f < live_ref[0], 1.0, 0.0)
        even, odd = pair_halves(paired(raw[f]))
        own = jnp.concatenate([even, odd], axis=-1)
        zero = jnp.zeros((1, cols, 128), F32)
        top = paired(xh[1, 0, f])
        low = paired(xh[1, 1, f])
        g = jnp.concatenate(
            [
                jnp.concatenate([zero, top[0:1]], axis=-1),
                jnp.concatenate([top[1:2], top[2:3]], axis=-1),
                own,
                jnp.concatenate([low[0:1], low[1:2]], axis=-1),
                jnp.concatenate([low[2:3], zero], axis=-1),
            ],
            axis=0,
        )
        g = jnp.where(block_mask(g.shape, 2), g * live, 0.0)
        put_e(eg, f, 0, g)
        gsa[f] = dot_nn(window(eg, f, 1, rows + 2), wsb[...]).reshape(rows + 2, cols, 256)
        return carry

    lax.fori_loop(0, frames, load_g, 0)

    norm_forward(1, stat_total(1), False)

    def second_layer(f, carry):
        z = c1[f] * wide(1, ALPHA, f) + wide(1, BETA, f)
        h = z * logistic(z)
        h = jnp.where(block_mask(h.shape, 1), h, 0.0)
        edge = jnp.zeros((cols, 512), BF16)
        e2[f, 0] = edge
        e2[f, rows + 3] = edge
        put_e(e2, f, 1, h)
        out = dot_nt(window(e2, f, 1, rows + 2), w2f[...]).reshape(rows + 2, cols, 256)
        skip = out + xs[f, 1 : rows + 3].astype(F32)
        skip = jnp.where(block_mask(skip.shape, 1), skip, 0.0)
        put_e(esk, f, 1, skip)
        return carry

    lax.fori_loop(0, frames, second_layer, 0)

    def down_window(f):
        return jnp.concatenate(
            [esk[f, 1 : 1 + rows, :, 256:512], esk[f, 2 : 2 + rows]], axis=-1
        ).reshape(owned, 768)

    zero_coarse = jnp.zeros((half, 128), F32)
    pad_rows = [jnp.zeros((2 * frames - 2 * half, 128), F32)]

    def down_layer(hf, carry):
        total, square = carry
        d = dot_nt(down_window(hf), wdf[:, 0:768]) + dot_nt(
            down_window(hf + half), wdf[:, 768:1536]
        )
        d = d.reshape(rows, cols, 128)
        dv[hf, 1 : rows + 1] = d
        border(hout, 1, hf, d)
        return put_row(total, hf, coarse_sum(d)), put_row(square, hf, coarse_sum(d * d))

    sums = lax.fori_loop(0, half, down_layer, (zero_coarse, zero_coarse))
    stat_start(2, jnp.concatenate(list(sums) + pad_rows, axis=0))
    halo_start(d_halo)

    def coarse_gradient(hf, carry):
        g = dot_nn(window(eg, hf, 1, rows + 2), wco[0]) + dot_nn(
            window(eg, hf + half, 1, rows + 2), wco[1]
        )
        g = g.reshape(rows + 2, cols, 128)
        g = jnp.where(block_mask(g.shape, 1), g, 0.0).astype(BF16).astype(F32)
        gco[hf] = g
        put_ec(ecg, hf, g)
        back = dot_nn(coarse_window(ecg, hf), w4b[...]).reshape(rows, cols, 128)
        gh4[hf, 1 : rows + 1] = back
        border(hout, 0, hf, back)
        return carry

    lax.fori_loop(0, half, coarse_gradient, 0)
    halo_start(g_h4_halo)

    def put_half(index, value):
        slot, owner = index // 2 // nd, index // 2 % nd
        current = gt_ref[slot, owner].astype(F32)
        value = join(current, swap(value)) if index % 2 else join(value, current)
        gt_ref[slot, owner] = value.astype(BF16)

    gt_ref[...] = jnp.zeros(gt_ref.shape, BF16)

    def fine_kernel_grad(index, e, start, gradient, gradient_start):
        acc[0, :, 0:1024] = jnp.zeros((256, 1024), F32)

        def add(f, carry):
            g = own_pixels(gradient, f, gradient_start, rows)
            acc[0, :, 0:1024] += dot_tn(g, window(e, f, start, rows))
            return carry

        lax.fori_loop(0, frames, add, 0)
        for t in range(3):
            u = []
            for dq in range(2):
                parts = [
                    acc[0, (dr * 2 + dq) * 64 : (dr * 2 + dq) * 64 + 64, pl.ds((t + dr) * 256, 256)]
                    for dr in range(2)
                ]
                u.append(parts[0] + parts[1])
            near, far = [v[:, 0:128] for v in u], [v[:, 128:256] for v in u]
            put_half(index(t, 0), swap(far[0]) + near[1])
            put_half(index(t, 1), near[0] + swap(near[1]))
            put_half(index(t, 2), swap(near[0]) + far[1])

    def coarse_kernel_grad(index, ec, gradient):
        acc[0, 0:128, :] = jnp.zeros((128, 1152), F32)

        def add(hf, carry):
            g = gradient[hf, 1 : rows + 1, :, 128:256].reshape(owned, 128)
            acc[0, 0:128, :] += dot_tn(g, coarse_window(ec, hf))
            return carry

        lax.fori_loop(0, half, add, 0)
        for a in range(3):
            for j in range(3):
                lanes = pl.ds((a * 3 + j) * 128, 128)
                put_half(index(a, j), acc[0, 0:64, lanes] + swap(acc[0, 64:128, lanes]))

    def down_kernel_grad(index):
        acc[:, 0:128, 0:768] = jnp.zeros((2, 128, 768), F32)

        def add(hf, carry):
            g = ed[hf, 1 : rows + 1, :, 0:128].reshape(owned, 128)
            acc[0, 0:128, 0:768] += dot_tn(g, down_window(hf))
            acc[1, 0:128, 0:768] += dot_tn(g, down_window(hf + half))
            return carry

        lax.fori_loop(0, half, add, 0)
        for a in range(3):
            near = acc[0, 0:64, pl.ds(a * 256, 128)] + acc[1, 64:128, pl.ds(a * 256, 128)]
            far = (
                acc[0, 0:64, pl.ds(a * 256 + 128, 128)] + acc[1, 64:128, pl.ds(a * 256 + 128, 128)]
            )
            put_half(index(a, 0), swap(far))
            put_half(index(a, 1), near)
            put_half(index(a, 2), swap(near))

    def up_kernel_grad():
        acc[...] = jnp.zeros(acc.shape, F32)

        def add(hf, carry):
            v = coarse_window(ecy, hf)
            acc[0] += dot_tn(own_pixels(eg, hf, 2, rows), v)
            acc[1] += dot_tn(own_pixels(eg, hf + half, 2, rows), v)
            return carry

        lax.fori_loop(0, half, add, 0)

        def block(dr, dq, i, j):
            r = (dr * 2 + dq) * 64
            lanes = pl.ds((i * 3 + j) * 128, 128)
            return acc[0, r : r + 64, lanes] + swap(acc[1, r : r + 64, lanes])

        place = {(0, 0): 0, (0, 1): 1, (0, 2): 1, (1, 0): 1, (1, 1): 1, (1, 2): 2}
        for ta in range(3):
            for tb in range(3):
                total = sum(
                    block(dr, dq, place[dr, ta], place[dq, tb])
                    for dr in range(2)
                    for dq in range(2)
                )
                put_half(45 + (ta * 3 + tb) * 2 + 1, total)


    halo_wait(d_halo)
    norm_forward(2, stat_total(2), True)

    def third_layer(hf, carry):
        total, square = carry
        with_halo(dv, hf, 1)
        z = dv[hf] * param(2, ALPHA, hf) + param(2, BETA, hf)
        h = z * logistic(z)
        put_ec(ec3, hf, jnp.where(block_mask(h.shape, 1), h, 0.0))
        out = dot_nt(coarse_window(ec3, hf), w3f[...]).reshape(rows, cols, 128)
        c3[hf, 1 : rows + 1] = out
        border(hout, 2, hf, out)
        return put_row(total, hf, coarse_sum(out)), put_row(square, hf, coarse_sum(out * out))

    sums = lax.fori_loop(0, half, third_layer, (zero_coarse, zero_coarse))
    stat_start(3, jnp.concatenate(list(sums) + pad_rows, axis=0))
    halo_start(c3_halo)
    fine_kernel_grad(lambda t, s: 45 + (t * 3 + s) * 2, esk, 2, eg, 2)

    halo_wait(c3_halo)
    halo_wait(g_h4_halo)
    norm_forward(3, stat_total(3), True)

    def fourth_layer(hf, carry):
        shift, scale = carry
        with_halo(c3, hf, 2)
        with_halo(gh4, hf, 0)
        v = c3[hf]
        z = v * param(3, ALPHA, hf) + param(3, BETA, hf)
        gate = logistic(z)
        h = z * gate
        put_ec(ec4, hf, jnp.where(block_mask(h.shape, 1), h, 0.0))
        g = gh4[hf] * (gate + h * (1.0 - gate))
        gz4[hf] = g
        own = g[1 : rows + 1]
        xhat = v[1 : rows + 1] * param(3, RSTD, hf) + param(3, NMR, hf)
        return put_row(shift, hf, coarse_sum(own)), put_row(scale, hf, coarse_sum(own * xhat))

    sums = lax.fori_loop(0, half, fourth_layer, (zero_coarse, zero_coarse))
    stat_start(4, jnp.concatenate(list(sums) + pad_rows, axis=0))

    def coarse_output(hf, carry):
        out = dot_nt(coarse_window(ec4, hf), w4f[...]).reshape(rows, cols, 128)
        y = dv[hf, 1 : rows + 1] + out
        border(hout, 3, hf, y)
        edge = jnp.zeros((1, cols, 128), F32)
        put_ec(ecy, hf, jnp.concatenate([edge, y, edge], axis=0))
        return carry

    lax.fori_loop(0, half, coarse_output, 0)
    halo_start(y_halo)
    coarse_kernel_grad(stacked(4), ec4, ecg)

    norm_backward(3, stat_total(4), True)

    def third_back(hf, carry):
        shift, scale = carry
        g = (
            gz4[hf] * param(3, ALPHA, hf)
            + c3[hf] * param(3, COEF, hf)
            + param(3, BIAS, hf)
        )
        put_ec(ecg3, hf, jnp.where(block_mask(g.shape, 1), g, 0.0))
        back = dot_nn(coarse_window(ecg3, hf), w3b[...]).reshape(rows, cols, 128)
        border(hout, 4, hf, back)
        v = dv[hf, 1 : rows + 1]
        z = v * param(2, ALPHA, hf) + param(2, BETA, hf)
        gate = logistic(z)
        own = back * (gate + z * gate * (1.0 - gate))
        gz3[hf, 1 : rows + 1] = own
        xhat = v * param(2, RSTD, hf) + param(2, NMR, hf)
        return put_row(shift, hf, coarse_sum(own)), put_row(scale, hf, coarse_sum(own * xhat))

    sums = lax.fori_loop(0, half, third_back, (zero_coarse, zero_coarse))
    stat_start(5, jnp.concatenate(list(sums) + pad_rows, axis=0))
    halo_start(g_h3_halo)

    halo_wait(y_halo)

    def result_copy(f):
        return pltpu.make_async_copy(raw.at[f], res_hbm.at[f], out_sem.at[f])

    def unpair(lo, hi):
        count = lo.shape[0]
        both = jnp.stack([lo, hi], axis=1).reshape(count * 2, cols, 128)
        tmp[0 : 2 * count, pl.ds(0, cols, stride=2), :] = both
        tmp[0 : 2 * count, pl.ds(1, cols, stride=2), :] = swap(both)

    def merge(hf, carry):
        for side, row in ((0, 0), (1, rows + 1)):
            line = hal[3, side, hf].astype(F32)[None]
            up, down = neighbours(line)
            q = lax.broadcasted_iota(jnp.int32, line.shape, 1)
            ecy[hf, row, :, 0:128] = jnp.where(q == 0, 0.0, down)[0].astype(BF16)
            ecy[hf, row, :, 128:256] = line[0].astype(BF16)
            ecy[hf, row, :, 256:384] = jnp.where(q == cols - 1, 0.0, up)[0].astype(BF16)
        both = dot_nt(coarse_window(ecy, hf), wup[...])
        for hi in range(2):
            f = hf + hi * half
            out = dot_nt(window(esk, f, 2, rows), wsf[...]) + both[:, hi * 256 : hi * 256 + 256]
            out = out.reshape(rows, cols, 256)
            unpair(out[:, :, 0:128], out[:, :, 128:256])
            raw[f] = tmp[:, :, 0:64].astype(BF16)
            result_copy(f).start()
        return carry

    lax.fori_loop(0, half, merge, 0)
    coarse_kernel_grad(stacked(3), ec3, ecg3)
    up_kernel_grad()
    gather_start(0)

    halo_wait(g_h3_halo)
    norm_backward(2, stat_total(5), True)

    def down_back(hf, carry):
        for side, row in ((0, 0), (1, rows + 1)):
            v = dv[hf, row]
            z = v * param(2, ALPHA, hf) + param(2, BETA, hf)
            gate = logistic(z)
            gz3[hf, row] = hal[4, side, hf].astype(F32) * (gate + z * gate * (1.0 - gate))
        g = (
            gco[hf]
            + gz3[hf] * param(2, ALPHA, hf)
            + dv[hf] * param(2, COEF, hf)
            + param(2, BIAS, hf)
        )
        g = jnp.where(block_mask(g.shape, 1), g, 0.0)
        up, _ = neighbours(g)
        q = lax.broadcasted_iota(jnp.int32, g.shape, 1)
        ed[hf, 0 : rows + 2, :, 0:128] = g.astype(BF16)
        ed[hf, 0 : rows + 2, :, 128:256] = jnp.where(q == cols - 1, 0.0, up).astype(BF16)
        ed[hf, rows + 2] = jnp.zeros((cols, 256), BF16)
        lhs = jnp.concatenate([ed[hf, 0 : rows + 2], ed[hf, 1 : rows + 3]], axis=-1)
        back = dot_nn(lhs.reshape(ext, 512), wdb[...])
        back = back.astype(BF16).astype(F32).reshape(rows + 2, cols, 512)
        for hi in range(2):
            f = hf + hi * half
            total = gsa[f] + back[:, :, hi * 256 : hi * 256 + 256]
            gsa[f] = total
            put_e(eg2, f, 0, jnp.where(block_mask(total.shape, 1), total, 0.0))
        return carry

    lax.fori_loop(0, half, down_back, 0)

    def second_back(f, carry):
        shift, scale = carry
        back = dot_nn(window(eg2, f, 1, rows), w2b[...]).reshape(rows, cols, 256)
        hfout[0, f] = back[0, :, 0:128].astype(BF16)
        hfout[1, f] = back[rows - 1, :, 128:256].astype(BF16)
        v = c1[f, 1 : rows + 1]
        z = v * wide(1, ALPHA, f) + wide(1, BETA, f)
        gate = logistic(z)
        own = back * (gate + z * gate * (1.0 - gate))
        gz[f, 1 : rows + 1] = own
        xhat = v * wide(1, RSTD, f) + wide(1, NMR, f)
        return put_row(shift, f, full_sum(own)), put_row(scale, f, full_sum(own * xhat))

    sums = lax.fori_loop(0, frames, second_back, (zero_rows, zero_rows))
    stat_start(6, jnp.concatenate(sums, axis=0))
    halo_start(g_h2_halo)
    down_kernel_grad(stacked(2))
    fine_kernel_grad(stacked(1), e2, 2, eg2, 1)
    gather_start(1)
    gather_space(0)
    halo_wait(g_h2_halo)
    norm_backward(1, stat_total(6), False)

    def first_back(f, carry):
        shift, scale = carry
        for side, row in ((0, 0), (1, rows + 1)):
            v = c1[f, row]
            lanes = slice(128, 256) if side == 0 else slice(0, 128)
            z = v[:, lanes] * param(1, ALPHA, f) + param(1, BETA, f)
            gate = logistic(z)
            g = hfull[side, f].astype(F32) * (gate + z * gate * (1.0 - gate))
            blank = jnp.zeros_like(g)
            gz[f, row] = jnp.concatenate([blank, g] if side == 0 else [g, blank], axis=-1)
        g = gz[f] * wide(1, ALPHA, f) + c1[f] * wide(1, COEF, f) + wide(1, BIAS, f)
        put_e(eg, f, 0, jnp.where(block_mask(g.shape, 1), g, 0.0))
        back = dot_nn(window(eg, f, 1, rows), w1b[...]).reshape(rows, cols, 256)
        v = xs[f, 2 : rows + 2].astype(F32)
        z = v * wide(0, ALPHA, f) + wide(0, BETA, f)
        gate = logistic(z)
        own = back * (gate + z * gate * (1.0 - gate))
        gz[f, 1 : rows + 1] = own
        xhat = v * wide(0, RSTD, f) + wide(0, NMR, f)
        return put_row(shift, f, full_sum(own)), put_row(scale, f, full_sum(own * xhat))

    pack_start(0)
    sums = lax.fori_loop(0, frames, first_back, (zero_rows, zero_rows))
    stat_start(7, jnp.concatenate(sums, axis=0))
    gather_spread(0)
    gather_space(1)
    fine_kernel_grad(stacked(0), e1, 2, eg, 1)
    gather_start(2)
    norm_backward(0, stat_total(7), False)
    pack_start(1)
    gather_all(0)
    gather_spread(1)

    def frames_copy(f):
        slot = lax.rem(f, 2)
        return pltpu.make_async_copy(fst.at[slot], fg_hbm.at[f], fg_sem.at[slot])

    def frames_back(f, carry):
        g = (
            gsa[f, 1 : rows + 1]
            + gz[f, 1 : rows + 1] * wide(0, ALPHA, f)
            + xs[f, 2 : rows + 2].astype(F32) * wide(0, COEF, f)
            + wide(0, BIAS, f)
        )
        unpair(g[:, :, 0:128], g[:, :, 128:256])

        @pl.when(f >= 2)
        def _():
            frames_copy(f - 2).wait()

        fst[lax.rem(f, 2)] = tmp[:, :, 0:64]
        frames_copy(f).start()
        return carry

    lax.fori_loop(0, frames, frames_back, 0)
    gather_space(2)
    gather_all(1)
    gather_spread(2)
    gather_all(2)
    for stage in range(3):
        gather_finish(stage)
    for off in range(1, nd):
        for which in range(2):
            pack_copy(which, off, dp_before(off)).wait_recv()
            pack_copy(which, off, dp).wait_send()
    for slot in range(slots):
        for owner in range(nd):
            lane = (slot * nd + owner) * 128
            gout_ref[:, lane : lane + 128] = gall[owner, slot]

    frames_copy(frames - 2).wait()
    frames_copy(frames - 1).wait()
    for f in range(frames):
        result_copy(f).wait()
    for copies in (x_halo, g_halo, g_h4_halo, d_halo, c3_halo, y_halo, g_h3_halo, g_h2_halo):
        halo_finish(copies)


def run_step(nd, n, frames, cotangent, actions, noise_ids, games, live_counts, cw, nm, table):
    count, strip, breadth, _ = frames.shape
    half, rows, cols = count // 2, strip // 2, breadth // 2
    fine = (count, rows + 4, cols, 512)
    coarse = (half, rows + 2, cols, 128)
    coarse_e = (half, rows + 2, cols, 384)
    scratch = [
        VM((count, strip, breadth, 64), BF16),
        VM((2, 2, count, 3, breadth, 64), BF16),
        VM((strip, breadth, 128), F32),
        VM((2, strip, breadth, 64), F32),
        VM((count, rows + 4, cols, 256), BF16),
        VM(fine, BF16),
        VM(fine, BF16),
        VM(fine, BF16),
        VM(fine, BF16),
        VM((count, rows + 2, cols, 512), BF16),
        VM((count, rows + 2, cols, 256), F32),
        VM((count, rows + 2, cols, 256), F32),
        VM((count, rows + 2, cols, 256), F32),
        VM(coarse, F32),
        VM(coarse, F32),
        VM(coarse, F32),
        VM(coarse, F32),
        VM(coarse, F32),
        VM(coarse, F32),
        VM(coarse_e, BF16),
        VM(coarse_e, BF16),
        VM(coarse_e, BF16),
        VM(coarse_e, BF16),
        VM(coarse_e, BF16),
        VM((half, rows + 3, cols, 256), BF16),
        VM((256, 1024), BF16),
        VM((1024, 256), BF16),
        VM((256, 1024), BF16),
        VM((1024, 256), BF16),
        VM((256, 1024), BF16),
        VM((1024, 256), BF16),
        VM((512, 1152), BF16),
        VM((2, 1024, 128), BF16),
        VM((128, 1536), BF16),
        VM((512, 512), BF16),
        VM((128, 1152), BF16),
        VM((1152, 128), BF16),
        VM((128, 1152), BF16),
        VM((1152, 128), BF16),
        VM((2, 256, 1152), F32),
        VM((32, count, 128), F32),
        VM((128, 256), F32),
        VM((8, n, 2 * count, 128), F32),
        VM((5, 2, half, cols, 128), BF16),
        VM((5, 2, half, cols, 128), BF16),
        VM((2, count, cols, 128), BF16),
        VM((2, count, cols, 128), BF16),
        VM((4, 256, 128), F32),
        VM((4, 128), F32),
        VM((32 // nd, nd, 64, 128), BF16),
        VM((nd, 32 // nd, 64, 128), BF16),
        VM((n, 32 // nd, 64 // n, 128), F32),
        VM((n, 32 // nd, 64 // n, 128), F32),
        VM((n, 32 // nd, 64 // n, 128), F32),
        VM((nd, 32 // nd, 64, 128), BF16),
        pltpu.SemaphoreType.DMA((7,)),
        pltpu.SemaphoreType.DMA((count,)),
        pltpu.SemaphoreType.DMA((2,)),
        pltpu.SemaphoreType.DMA((8, n - 1)),
        pltpu.SemaphoreType.DMA((8, n - 1)),
        pltpu.SemaphoreType.DMA((8, 2)),
        pltpu.SemaphoreType.DMA((8, 2)),
        pltpu.SemaphoreType.DMA((4, 2, nd - 1)),
        pltpu.SemaphoreType.DMA((4, 2, nd - 1)),
        pltpu.SemaphoreType.DMA((3, 2, n - 1)),
        pltpu.SemaphoreType.DMA((3, 2, n - 1)),
    ]
    smem = pl.BlockSpec(memory_space=pltpu.SMEM)
    vmem = pl.BlockSpec(memory_space=pltpu.VMEM)
    hbm = pl.BlockSpec(memory_space=pl.ANY)
    return pl.pallas_call(
        functools.partial(step_kernel, nd, n),
        out_shape=(
            jax.ShapeDtypeStruct(frames.shape, BF16),
            jax.ShapeDtypeStruct(frames.shape, F32),
            jax.ShapeDtypeStruct((64, 4096), BF16),
            jax.ShapeDtypeStruct((nd, count, 896), F32),
        ),
        in_specs=[hbm, hbm, smem, smem, smem, smem, vmem, hbm, vmem],
        out_specs=(hbm, hbm, vmem, vmem),
        scratch_shapes=scratch,
        compiler_params=pltpu.CompilerParams(
            collective_id=0, has_side_effects=True, vmem_limit_bytes=62 * 1024 * 1024
        ),
        name="step",
    )(frames, cotangent, actions, noise_ids, games, live_counts, cw, nm, table)


def adamw(weight, moment, square, grad_value, rate):
    fix_one = 1.0 - BETA_ONE**ADAM_STEP
    fix_two = 1.0 - BETA_TWO**ADAM_STEP
    moment_new = BETA_ONE * moment + (1.0 - BETA_ONE) * grad_value
    square_new = BETA_TWO * square + (1.0 - BETA_TWO) * grad_value * grad_value
    fixed_m = moment_new / fix_one
    fixed_v = square_new / fix_two
    weight_new = weight - rate * (fixed_m / (jnp.sqrt(fixed_v) + ADAM_EPS) + DECAY * weight)
    return (moment_new, square_new, weight_new, weight_new.astype(BF16))


def local(
    nd,
    ns,
    frames,
    cotangent,
    actions,
    noise_ids,
    games,
    live_counts,
    conv_weight,
    conv_moment,
    conv_square,
    norm_map,
    norm_moment,
    norm_square,
    emb_table,
    table_moment,
    table_square,
):
    cw = conv_weight.T
    nm = jnp.transpose(norm_map, (1, 0, 2))
    result, frames_grad, grads, packs = run_step(
        nd, ns, frames, cotangent, actions, noise_ids, games, live_counts, cw, nm, emb_table
    )
    grad_t = grads[:, : conv_weight.shape[0]].astype(F32)
    conv_out = [v.T for v in adamw(cw, conv_moment.T, conv_square.T, grad_t, 0.05)]
    packs = packs.reshape(-1, 896)
    dmods = packs[:, 0:512]
    embedded = packs[:, 512:768]
    hot = packs[:, 768 : 768 + emb_table.shape[0]]
    top = jnp.dot(embedded.T, dmods, precision=HIGH).reshape(256, 4, 128)
    last = jnp.sum(dmods, axis=0).reshape(1, 4, 128)
    grad_map = jnp.concatenate([top, last], axis=0).transpose(1, 0, 2)
    norm_out = adamw(norm_map, norm_moment, norm_square, grad_map, 0.04)
    g_embed = jnp.dot(
        dmods, norm_map[:, :-1].transpose(0, 2, 1).reshape(512, 256), precision=HIGH
    )
    grad_table = jnp.dot(hot.T, g_embed, precision=HIGH)
    table_out = adamw(emb_table, table_moment, table_square, grad_table, 0.5)
    return (result, frames_grad, *conv_out, *norm_out, *table_out)


def solution(mesh):
    split = P("dp", "space", None, None)
    in_specs = (split, split) + (P("dp"),) * 4 + (P(),) * 9
    out_specs = (split, split) + (P(),) * 12
    sizes = dict(mesh.shape)
    return jax.shard_map(
        functools.partial(local, sizes["dp"], sizes["space"]),
        mesh=mesh,
        in_specs=in_specs,
        out_specs=out_specs,
        check_vma=False,
    )
```

```python
import functools

import jax
import jax.numpy as jnp
from jax import lax
from jax.experimental import pallas as pl
from jax.experimental.pallas import tpu as pltpu
from jax.sharding import PartitionSpec as P

ACTIONS = 18
NOISE_LEVELS = 64
ADAM_STEP = 4
NORM_EPSILON = 1e-05
ADAM_EPS = 1e-08
BETA_ONE = 0.5
BETA_TWO = 0.5
DECAY = 0.01
HIGH = lax.Precision.HIGHEST
F32 = jnp.float32
BF16 = jnp.bfloat16
MESH = pl.DeviceIdType.MESH
VM = pltpu.VMEM

ALPHA, BETA, RSTD, NMR, GAIN, SHIFT, COEF, BIAS = range(8)


def dot_nn(a, b):
    return lax.dot_general(a, b, (((1,), (0,)), ((), ())), preferred_element_type=F32)


def dot_nt(a, b):
    return lax.dot_general(a, b, (((1,), (1,)), ((), ())), preferred_element_type=F32)


def dot_tn(a, b):
    return lax.dot_general(a, b, (((0,), (0,)), ((), ())), preferred_element_type=F32)


def dot_high(a, b):
    return lax.dot_general(
        a, b, (((1,), (0,)), ((), ())), precision=HIGH, preferred_element_type=F32
    )


def logistic(z):
    return 0.5 * jnp.tanh(0.5 * z) + 0.5


def lane_iota(shape):
    return lax.broadcasted_iota(jnp.int32, shape, len(shape) - 1)


def swap(v):
    return pltpu.roll(v, 64, len(v.shape) - 1)


def join(lo, hi):
    return jnp.where(lane_iota(lo.shape) < 64, lo, hi)


def twice(row):
    return jnp.concatenate([row, row], axis=-1)


def step_kernel(
    nd,
    n,
    x_hbm,
    cot_hbm,
    act_ref,
    noise_ref,
    game_ref,
    live_ref,
    cw_ref,
    nm_hbm,
    tab_ref,
    res_hbm,
    fg_hbm,
    gout_ref,
    packs,
    raw,
    xh,
    tmp,
    fst,
    xs,
    e1,
    e2,
    esk,
    eg,
    eg2,
    c1,
    gsa,
    gz,
    dv,
    c3,
    gh4,
    gz4,
    gz3,
    gco,
    ec3,
    ec4,
    ecg,
    ecg3,
    ecy,
    ed,
    w1f,
    w1b,
    w2f,
    w2b,
    wsf,
    wsb,
    wup,
    wco,
    wdf,
    wdb,
    w3f,
    w3b,
    w4f,
    w4b,
    acc,
    prm,
    tabp,
    stat,
    hal,
    hout,
    hfull,
    hfout,
    nmv,
    nmb,
    gt_ref,
    rbuf,
    part,
    zbuf,
    zfull,
    gall,
    local_sem,
    out_sem,
    fg_sem,
    stat_send,
    stat_recv,
    halo_send,
    halo_recv,
    dp_send,
    dp_recv,
    sp_send,
    sp_recv,
):
    frames, strip = raw.shape[0], raw.shape[1]
    breadth = raw.shape[2]
    half = frames // 2
    rows = strip // 2
    cols = breadth // 2
    me = lax.axis_index("space")
    dp = lax.axis_index("dp")
    full_cells = float(strip * n * breadth * 32)
    coarse_cells = full_cells / 4.0
    owned = rows * cols
    ext = (rows + 2) * cols

    barrier = pltpu.get_barrier_semaphore()
    for off in range(1, n):
        pl.semaphore_signal(
            barrier,
            inc=1,
            device_id={"space": lax.rem(me + off, n)},
            device_id_type=MESH,
        )
    for off in range(1, nd):
        pl.semaphore_signal(
            barrier,
            inc=1,
            device_id={"dp": lax.rem(dp + off, nd)},
            device_id_type=MESH,
        )

    x_copy = pltpu.make_async_copy(x_hbm, raw, local_sem.at[0])
    x_copy.start()
    map_copies = [
        pltpu.make_async_copy(nm_hbm.at[pl.ds(0, 256), k], nmv.at[k], local_sem.at[2 + k])
        for k in range(4)
    ]
    map_copies.append(pltpu.make_async_copy(nm_hbm.at[256], nmb, local_sem.at[6]))
    for copy in map_copies:
        copy.start()
    pl.semaphore_wait(barrier, n + nd - 2)

    def halo_copies(k, first, last, to_up, to_down):
        up = pltpu.make_async_remote_copy(
            src_ref=first,
            dst_ref=to_up,
            send_sem=halo_send.at[k, 0],
            recv_sem=halo_recv.at[k, 0],
            device_id={"space": lax.rem(me + n - 1, n)},
            device_id_type=MESH,
        )
        down = pltpu.make_async_remote_copy(
            src_ref=last,
            dst_ref=to_down,
            send_sem=halo_send.at[k, 1],
            recv_sem=halo_recv.at[k, 1],
            device_id={"space": lax.rem(me + 1, n)},
            device_id_type=MESH,
        )
        return up, down

    def halo_start(copies):
        @pl.when(me > 0)
        def _():
            copies[0].start()

        @pl.when(me < n - 1)
        def _():
            copies[1].start()

    def halo_wait(copies):
        @pl.when(me < n - 1)
        def _():
            copies[0].wait_recv()

        @pl.when(me > 0)
        def _():
            copies[1].wait_recv()

    def halo_finish(copies):
        @pl.when(me > 0)
        def _():
            copies[0].wait_send()

        @pl.when(me < n - 1)
        def _():
            copies[1].wait_send()

    def stat_copy(k, off, slot):
        return pltpu.make_async_remote_copy(
            src_ref=stat.at[k, slot],
            dst_ref=stat.at[k, slot],
            send_sem=stat_send.at[k, off - 1],
            recv_sem=stat_recv.at[k, off - 1],
            device_id={"space": lax.rem(me + off, n)},
            device_id_type=MESH,
        )

    def stat_start(k, value):
        stat[k, me] = value
        for off in range(1, n):
            stat_copy(k, off, me).start()

    def stat_total(k):
        for off in range(1, n):
            stat_copy(k, off, lax.rem(me + n - off, n)).wait_recv()
        total = stat[k, 0]
        for i in range(1, n):
            total = total + stat[k, i]
        for off in range(1, n):
            stat_copy(k, off, me).wait_send()
        return total

    x_halo = halo_copies(
        0, x_hbm.at[:, pl.ds(0, 3)], x_hbm.at[:, pl.ds(strip - 3, 3)], xh.at[0, 1], xh.at[0, 0]
    )
    g_halo = halo_copies(
        1, cot_hbm.at[:, pl.ds(0, 3)], cot_hbm.at[:, pl.ds(strip - 3, 3)], xh.at[1, 1], xh.at[1, 0]
    )
    for side in range(2):

        @pl.when((me == 0) if side == 0 else (me == n - 1))
        def _():
            for which in range(2):
                xh[which, side] = jnp.zeros(xh.shape[2:], BF16)
            for which in range(hal.shape[0]):
                hal[which, side] = jnp.zeros(hal.shape[2:], BF16)
            hfull[side] = jnp.zeros(hfull.shape[1:], BF16)

    halo_start(x_halo)

    def coarse_halo(k):
        return halo_copies(
            k, hout.at[k - 2, 0], hout.at[k - 2, 1], hal.at[k - 2, 1], hal.at[k - 2, 0]
        )

    g_h4_halo, d_halo, c3_halo, y_halo, g_h3_halo = [coarse_halo(k) for k in range(2, 7)]
    g_h2_halo = halo_copies(7, hfout.at[0], hfout.at[1], hfull.at[1], hfull.at[0])

    def block_mask(shape, pad):
        blocks = shape[0]
        b = lax.broadcasted_iota(jnp.int32, shape, 0)
        low = jnp.where(me > 0, 0, pad)
        high = jnp.where(me < n - 1, blocks, blocks - pad)
        return (b >= low) & (b < high)

    def param(k, which, f):
        return prm[k * 8 + which, pl.ds(f, 1), :]

    def wide(k, which, f):
        return twice(param(k, which, f))

    def put_row(carry, f, value):
        row = lax.broadcasted_iota(jnp.int32, carry.shape, 0)
        return jnp.where(row == f, value, carry)

    def full_sum(v):
        s = jnp.sum(v.reshape(-1, 256), axis=0, keepdims=True)
        return s[:, :128] + s[:, 128:]

    def paired(raw_rows):
        count = raw_rows.shape[0]
        tmp[0:count, :, 0:64] = raw_rows.astype(F32)
        even = tmp[0:count, pl.ds(0, cols, stride=2), :]
        odd = tmp[0:count, pl.ds(1, cols, stride=2), :]
        return join(even, swap(odd))

    def pair_halves(p):
        count = p.shape[0] // 2
        p = p.reshape(count, 2, cols, 128)
        return p[:, 0], p[:, 1]

    def neighbours(v):
        count = v.shape[0]
        flat = v.reshape(count * cols, 128)
        up = pltpu.roll(flat, count * cols - 1, 0).reshape(v.shape)
        down = pltpu.roll(flat, 1, 0).reshape(v.shape)
        return up, down

    def put_e(e, f, start, h):
        count = h.shape[0]
        for part in range(2):
            v = h[:, :, part * 128 : (part + 1) * 128]
            up, down = neighbours(v)
            lane = lane_iota(v.shape)
            q = lax.broadcasted_iota(jnp.int32, v.shape, 1)
            near = jnp.where(
                lane < 64, jnp.where(q == cols - 1, 0.0, up), jnp.where(q == 0, 0.0, down)
            )
            e[f, start : start + count, :, part * 256 : part * 256 + 128] = v.astype(BF16)
            e[f, start : start + count, :, part * 256 + 128 : part * 256 + 256] = near.astype(BF16)

    def window(e, f, start, count):
        return jnp.concatenate(
            [
                e[f, start - 1 : start - 1 + count, :, 256:512],
                e[f, start : start + count, :, :],
                e[f, start + 1 : start + 1 + count, :, 0:256],
            ],
            axis=-1,
        ).reshape(count * cols, 1024)

    def own_pixels(e, f, start, count):
        return jnp.concatenate(
            [
                e[f, start : start + count, :, 0:128],
                e[f, start : start + count, :, 256:384],
            ],
            axis=-1,
        ).reshape(count * cols, 256)

    def put_ec(ec, hf, v):
        up, down = neighbours(v)
        q = lax.broadcasted_iota(jnp.int32, v.shape, 1)
        ec[hf, :, :, 0:128] = jnp.where(q == 0, 0.0, down).astype(BF16)
        ec[hf, :, :, 128:256] = v.astype(BF16)
        ec[hf, :, :, 256:384] = jnp.where(q == cols - 1, 0.0, up).astype(BF16)

    def coarse_window(ec, hf):
        return jnp.concatenate([ec[hf, a : a + rows] for a in range(3)], axis=-1).reshape(
            owned, 1152
        )

    def coarse_sum(v):
        return jnp.sum(v.reshape(-1, 128), axis=0, keepdims=True)

    def with_halo(ref, hf, k):
        ref[hf, 0] = hal[k, 0, hf].astype(F32)
        ref[hf, rows + 1] = hal[k, 1, hf].astype(F32)

    def border(ref_out, k, hf, v):
        ref_out[k, 0, hf] = v[0].astype(BF16)
        ref_out[k, 1, hf] = v[rows - 1].astype(BF16)

    def group_matrix(coarse):
        r = lax.broadcasted_iota(jnp.int32, (128, 128), 0) // 32
        c = lax.broadcasted_iota(jnp.int32, (128, 128), 1) // 32
        same = (r == c) if coarse else (r % 2 == c % 2)
        return jnp.where(same, 1.0, 0.0)

    def norm_forward(k, total, coarse):
        cells = coarse_cells if coarse else full_cells
        count = half if coarse else frames
        moments = dot_high(total, group_matrix(coarse)) / cells
        mean = moments[0:count]
        var = moments[count : 2 * count] - mean * mean
        rstd = lax.rsqrt(var + NORM_EPSILON)
        gain = prm[k * 8 + GAIN, 0:count, :]
        alpha = rstd * gain
        prm[k * 8 + ALPHA, 0:count, :] = alpha
        prm[k * 8 + BETA, 0:count, :] = prm[k * 8 + SHIFT, 0:count, :] - mean * alpha
        prm[k * 8 + RSTD, 0:count, :] = rstd
        prm[k * 8 + NMR, 0:count, :] = -mean * rstd

    def norm_backward(k, total, coarse):
        cells = coarse_cells if coarse else full_cells
        count = half if coarse else frames
        gain = prm[k * 8 + GAIN, 0:count, :]
        shift_grad = total[0:count]
        scale_grad = total[count : 2 * count]
        means = (
            dot_high(
                jnp.concatenate([shift_grad * gain, scale_grad * gain], axis=0),
                group_matrix(coarse),
            )
            / cells
        )
        rstd = prm[k * 8 + RSTD, 0:count, :]
        factor = -rstd * means[count : 2 * count]
        prm[k * 8 + COEF, 0:count, :] = rstd * factor
        prm[k * 8 + BIAS, 0:count, :] = (
            prm[k * 8 + NMR, 0:count, :] * factor - rstd * means[0:count]
        )
        if coarse:
            scale_all = jnp.concatenate([scale_grad, swap(scale_grad)], axis=0)
            shift_all = jnp.concatenate([shift_grad, swap(shift_grad)], axis=0)
        else:
            scale_all = scale_grad + swap(scale_grad)
            shift_all = shift_grad + swap(shift_grad)
        packs[dp, :, k * 128 : (k + 1) * 128] = join(scale_all, swap(shift_all))

    slots = 32 // nd
    share = 64 // n
    first_slots = [
        [i for i in range(slots) if i * nd >= 16],
        [i for i in range(slots) if 8 <= i * nd < 16],
        [0],
    ]

    def dp_before(off):
        return lax.rem(dp + nd - off, nd)

    def dp_after(off):
        return lax.rem(dp + off, nd)

    def sp_before(off):
        return lax.rem(me + n - off, n)

    def sp_after(off):
        return lax.rem(me + off, n)

    def stage_slots(stage):
        chosen = first_slots[stage]
        return pl.ds(chosen[0], len(chosen))

    def dp_copy(stage, phase, src, dst, off):
        return pltpu.make_async_remote_copy(
            src_ref=src,
            dst_ref=dst,
            send_sem=dp_send.at[stage, phase, off - 1],
            recv_sem=dp_recv.at[stage, phase, off - 1],
            device_id={"dp": dp_after(off)},
            device_id_type=MESH,
        )

    def sp_copy(stage, phase, src, dst, off):
        return pltpu.make_async_remote_copy(
            src_ref=src,
            dst_ref=dst,
            send_sem=sp_send.at[stage, phase, off - 1],
            recv_sem=sp_recv.at[stage, phase, off - 1],
            device_id={"space": sp_after(off)},
            device_id_type=MESH,
        )

    def first_copy(stage, off, owner, slot):
        where = stage_slots(stage)
        return dp_copy(stage, 0, gt_ref.at[where, owner], rbuf.at[slot, where], off)

    def second_copy(stage, off, row, slot):
        where = stage_slots(stage)
        return sp_copy(stage, 0, part.at[row, where], zbuf.at[slot, where], off)

    def third_copy(stage, off, slot):
        where = stage_slots(stage)
        return sp_copy(stage, 1, zfull.at[slot, where], zfull.at[slot, where], off)

    def fourth_copy(stage, off, slot):
        where = stage_slots(stage)
        return dp_copy(stage, 1, gall.at[slot, where], gall.at[slot, where], off)

    def pack_copy(which, off, slot):
        lanes = pl.ds(0, 128) if which else pl.ds(128, 768)
        return dp_copy(3, which, packs.at[slot, :, lanes], packs.at[slot, :, lanes], off)

    def pack_start(which):
        for off in range(1, nd):
            pack_copy(which, off, dp).start()

    def gather_start(stage):
        if not first_slots[stage]:
            return
        for off in range(1, nd):
            first_copy(stage, off, dp_after(off), dp).start()

    def gather_space(stage):
        if not first_slots[stage]:
            return
        where = stage_slots(stage)
        for off in range(1, nd):
            first_copy(stage, off, dp, dp_before(off)).wait_recv()
        rbuf[dp, where] = gt_ref[where, dp]
        total = rbuf[0, where].astype(F32)
        for i in range(1, nd):
            total = total + rbuf[i, where].astype(F32)
        for z in range(n):
            part[z, where] = total[:, z * share : (z + 1) * share]
        for off in range(1, n):
            second_copy(stage, off, sp_after(off), me).start()

    def gather_spread(stage):
        if not first_slots[stage]:
            return
        where = stage_slots(stage)
        for off in range(1, n):
            second_copy(stage, off, me, sp_before(off)).wait_recv()
        zbuf[me, where] = part[me, where]
        total = zbuf[0, where]
        for i in range(1, n):
            total = total + zbuf[i, where]
        zfull[me, where] = total
        for off in range(1, n):
            third_copy(stage, off, me).start()

    def gather_all(stage):
        if not first_slots[stage]:
            return
        where = stage_slots(stage)
        for off in range(1, n):
            third_copy(stage, off, sp_before(off)).wait_recv()
        whole = jnp.concatenate([zfull[z, where] for z in range(n)], axis=1)
        gall[dp, where] = whole.astype(BF16)
        for off in range(1, nd):
            fourth_copy(stage, off, dp).start()

    def gather_finish(stage):
        if not first_slots[stage]:
            return
        for off in range(1, nd):
            fourth_copy(stage, off, dp_before(off)).wait_recv()
            first_copy(stage, off, dp_after(off), dp).wait_send()
            fourth_copy(stage, off, dp).wait_send()
        for off in range(1, n):
            second_copy(stage, off, sp_after(off), me).wait_send()
            third_copy(stage, off, me).wait_send()

    x_copy.wait()

    def load_x(f, carry):
        total, square = carry
        even, odd = pair_halves(paired(raw[f]))
        both = jnp.concatenate([even, odd], axis=-1)
        xs[f, 2 : 2 + rows] = both.astype(BF16)
        return put_row(total, f, full_sum(both)), put_row(square, f, full_sum(both * both))

    zero_rows = jnp.zeros((frames, 128), F32)
    sums = lax.fori_loop(0, frames, load_x, (zero_rows, zero_rows), unroll=4)
    stat_start(0, jnp.concatenate(sums, axis=0))
    g_copy = pltpu.make_async_copy(cot_hbm, raw, local_sem.at[1])
    g_copy.start()
    halo_start(g_halo)

    def conditioning():
        entry = lax.broadcasted_iota(jnp.int32, (frames, 128), 1)
        row = lax.broadcasted_iota(jnp.int32, (frames, 128), 0)
        hot = jnp.zeros((frames, 128), F32)
        for f in range(frames):
            hit = (
                (entry == act_ref[f])
                | (entry == noise_ref[f] + ACTIONS)
                | (entry == game_ref[f] + ACTIONS + NOISE_LEVELS)
            )
            hot = jnp.where((row == f) & hit, 1.0, hot)
        table_rows = tab_ref.shape[0]
        tabp[...] = jnp.zeros(tabp.shape, F32)
        tabp[0:table_rows, :] = tab_ref[...]
        embedded = dot_high(hot, tabp[...])
        packs[dp, :, 512:768] = embedded
        packs[dp, :, 768:896] = hot
        for copy in map_copies:
            copy.wait()
        for k in range(4):
            mod = dot_high(embedded, nmv[k]) + nmb[k : k + 1, :]
            scale = join(mod, swap(mod)) + 1.0
            shift = join(swap(mod), mod)
            if k < 2:
                prm[k * 8 + GAIN] = scale
                prm[k * 8 + SHIFT] = shift
            else:
                prm[k * 8 + GAIN, 0:half, :] = join(scale[0:half], scale[half:])
                prm[k * 8 + SHIFT, 0:half, :] = join(shift[0:half], shift[half:])

    conditioning()

    def tap(index):
        first = (index // 2) * 128
        last = min(first + 128, cw_ref.shape[1])
        tile = cw_ref[:, first:last].astype(BF16).astype(F32)
        if last - first < 128:
            tile = jnp.concatenate([tile, jnp.zeros((64, 128 - last + first), F32)], axis=-1)
        return tile, index % 2

    def low_half(index):
        tile, odd = tap(index)
        return swap(tile) if odd else tile

    def high_half(index):
        tile, odd = tap(index)
        return tile if odd else swap(tile)

    def lane_pair(low_index, high_index):
        zero = jnp.zeros((64, 128), F32)
        low = zero if low_index is None else low_half(low_index)
        high = zero if high_index is None else high_half(high_index)
        return join(low, high).astype(BF16)

    def fine_weights(index, forward_w, backward_w):
        zero = jnp.zeros((64, 128), BF16)
        pairs = []
        for t in range(3):
            p12 = lane_pair(index(t, 1), index(t, 2))
            p01 = lane_pair(index(t, 0), index(t, 1))
            pz0 = lane_pair(None, index(t, 0))
            p2z = lane_pair(index(t, 2), None)
            pairs.append((p12, p01, pz0, p2z))
        for a in range(4):
            for dr in range(2):
                t = a - dr
                ok = 0 <= t <= 2
                for dq in range(2):
                    r = (dr * 2 + dq) * 64
                    first = pairs[t][0 if dq == 0 else 1] if ok else zero
                    second = pairs[t][2 if dq == 0 else 3] if ok else zero
                    forward_w[r : r + 64, a * 256 : a * 256 + 128] = first
                    forward_w[r : r + 64, a * 256 + 128 : a * 256 + 256] = second
                t = 2 - a + dr
                ok = 0 <= t <= 2
                for g in range(4):
                    r = a * 256 + g * 64
                    backward_w[r : r + 64, dr * 128 : dr * 128 + 128] = (
                        pairs[t][g] if ok else zero
                    )

    def coarse_weights(index, forward_w, backward_w):
        for a in range(3):
            for j in range(3):
                lane = (a * 3 + j) * 128
                low = lane_pair(index(a, j), None)
                high = lane_pair(None, index(a, j))
                forward_w[0:64, lane : lane + 128] = low
                forward_w[64:128, lane : lane + 128] = high
                lane = ((2 - a) * 3 + (2 - j)) * 128
                backward_w[lane : lane + 64, :] = low
                backward_w[lane + 64 : lane + 128, :] = high

    def down_weights(index):
        zero = jnp.zeros((64, 128), BF16)
        wdf[...] = jnp.zeros(wdf.shape, BF16)
        wdb[...] = jnp.zeros(wdb.shape, BF16)
        for t in range(3):
            p12 = lane_pair(index(t, 1), index(t, 2))
            pz0 = lane_pair(None, index(t, 0))
            for hi in range(2):
                lane = hi * 768 + t * 256
                wdf[hi * 64 : hi * 64 + 64, lane : lane + 128] = p12
                wdf[hi * 64 : hi * 64 + 64, lane + 128 : lane + 256] = pz0
                i, dr = ((1, 1), (0, 0), (0, 1))[t]
                lane = hi * 256 + dr * 128
                for j in range(2):
                    r = (i * 2 + j) * 128 + hi * 64
                    wdb[r : r + 64, lane : lane + 128] = p12 if j == 0 else pz0

    def up_weights():
        def up_tap(ta, tb):
            return low_half(45 + (ta * 3 + tb) * 2 + 1)

        taps = [[up_tap(ta, tb) for tb in range(3)] for ta in range(3)]
        members = {(0, 0): (0,), (0, 1): (1, 2), (1, 1): (0, 1), (1, 2): (2,)}
        wup[...] = jnp.zeros(wup.shape, BF16)
        for (dr, i), in_rows in members.items():
            for (dq, j), in_cols in members.items():
                total = sum(taps[ta][tb] for ta in in_rows for tb in in_cols)
                zero = jnp.zeros_like(total)
                r = (dr * 2 + dq) * 64
                lane = (i * 3 + j) * 128
                wup[r : r + 64, lane : lane + 128] = join(total, zero).astype(BF16)
                wup[256 + r : 256 + r + 64, lane : lane + 128] = join(zero, swap(total)).astype(
                    BF16
                )
        for a in range(4):
            for g, off in enumerate((0, 1, 2, -1)):
                chosen = [
                    taps[2 - a + dr][1 - off + dq]
                    for dr in range(2)
                    for dq in range(2)
                    if 0 <= 2 - a + dr <= 2 and 0 <= 1 - off + dq <= 2
                ]
                total = sum(chosen[1:], chosen[0])
                zero = jnp.zeros_like(total)
                r = a * 256 + g * 64
                wco[0, r : r + 64, :] = join(total, zero).astype(BF16)
                wco[1, r : r + 64, :] = join(zero, swap(total)).astype(BF16)

    def stacked(k):
        return lambda t, s: k * 9 + t * 3 + s

    fine_weights(stacked(0), w1f, w1b)
    fine_weights(stacked(1), w2f, w2b)
    fine_weights(lambda t, s: 45 + (t * 3 + s) * 2, wsf, wsb)
    up_weights()
    down_weights(stacked(2))
    coarse_weights(stacked(3), w3f, w3b)
    coarse_weights(stacked(4), w4f, w4b)

    halo_wait(x_halo)

    def load_x_halo(f, carry):
        zero = jnp.zeros((1, cols, 128), F32)
        top = paired(xh[0, 0, f])
        low = paired(xh[0, 1, f])
        xs[f, 0] = jnp.concatenate([zero, top[0:1]], axis=-1)[0].astype(BF16)
        xs[f, 1] = jnp.concatenate([top[1:2], top[2:3]], axis=-1)[0].astype(BF16)
        xs[f, rows + 2] = jnp.concatenate([low[0:1], low[1:2]], axis=-1)[0].astype(BF16)
        xs[f, rows + 3] = jnp.concatenate([low[2:3], zero], axis=-1)[0].astype(BF16)
        return carry

    lax.fori_loop(0, frames, load_x_halo, 0, unroll=4)
    norm_forward(0, stat_total(0), False)

    def first_layer(f, carry):
        total, square = carry
        x = xs[f].astype(F32)
        z = x * wide(0, ALPHA, f) + wide(0, BETA, f)
        h = z * logistic(z)
        h = jnp.where(block_mask(h.shape, 2), h, 0.0)
        put_e(e1, f, 0, h)
        out = dot_nt(window(e1, f, 1, rows + 2), w1f[...]).reshape(rows + 2, cols, 256)
        c1[f] = out
        own = out[1 : rows + 1]
        return put_row(total, f, full_sum(own)), put_row(square, f, full_sum(own * own))

    sums = lax.fori_loop(0, frames, first_layer, (zero_rows, zero_rows), unroll=4)
    stat_start(1, jnp.concatenate(sums, axis=0))

    g_copy.wait()
    halo_wait(g_halo)

    def load_g(f, carry):
        live = jnp.where(f < live_ref[0], 1.0, 0.0)
        even, odd = pair_halves(paired(raw[f]))
        own = jnp.concatenate([even, odd], axis=-1)
        zero = jnp.zeros((1, cols, 128), F32)
        top = paired(xh[1, 0, f])
        low = paired(xh[1, 1, f])
        g = jnp.concatenate(
            [
                jnp.concatenate([zero, top[0:1]], axis=-1),
                jnp.concatenate([top[1:2], top[2:3]], axis=-1),
                own,
                jnp.concatenate([low[0:1], low[1:2]], axis=-1),
                jnp.concatenate([low[2:3], zero], axis=-1),
            ],
            axis=0,
        )
        g = jnp.where(block_mask(g.shape, 2), g * live, 0.0)
        put_e(eg, f, 0, g)
        gsa[f] = dot_nn(window(eg, f, 1, rows + 2), wsb[...]).reshape(rows + 2, cols, 256)
        return carry

    lax.fori_loop(0, frames, load_g, 0, unroll=4)

    norm_forward(1, stat_total(1), False)

    def second_layer(f, carry):
        z = c1[f] * wide(1, ALPHA, f) + wide(1, BETA, f)
        h = z * logistic(z)
        h = jnp.where(block_mask(h.shape, 1), h, 0.0)
        edge = jnp.zeros((cols, 512), BF16)
        e2[f, 0] = edge
        e2[f, rows + 3] = edge
        put_e(e2, f, 1, h)
        out = dot_nt(window(e2, f, 1, rows + 2), w2f[...]).reshape(rows + 2, cols, 256)
        skip = out + xs[f, 1 : rows + 3].astype(F32)
        skip = jnp.where(block_mask(skip.shape, 1), skip, 0.0)
        put_e(esk, f, 1, skip)
        return carry

    lax.fori_loop(0, frames, second_layer, 0, unroll=4)

    def down_window(f):
        return jnp.concatenate(
            [esk[f, 1 : 1 + rows, :, 256:512], esk[f, 2 : 2 + rows]], axis=-1
        ).reshape(owned, 768)

    zero_coarse = jnp.zeros((half, 128), F32)
    pad_rows = [jnp.zeros((2 * frames - 2 * half, 128), F32)]

    def down_layer(hf, carry):
        total, square = carry
        d = dot_nt(down_window(hf), wdf[:, 0:768]) + dot_nt(
            down_window(hf + half), wdf[:, 768:1536]
        )
        d = d.reshape(rows, cols, 128)
        dv[hf, 1 : rows + 1] = d
        border(hout, 1, hf, d)
        return put_row(total, hf, coarse_sum(d)), put_row(square, hf, coarse_sum(d * d))

    sums = lax.fori_loop(0, half, down_layer, (zero_coarse, zero_coarse), unroll=4)
    stat_start(2, jnp.concatenate(list(sums) + pad_rows, axis=0))
    halo_start(d_halo)

    def coarse_gradient(hf, carry):
        g = dot_nn(window(eg, hf, 1, rows + 2), wco[0]) + dot_nn(
            window(eg, hf + half, 1, rows + 2), wco[1]
        )
        g = g.reshape(rows + 2, cols, 128)
        g = jnp.where(block_mask(g.shape, 1), g, 0.0).astype(BF16).astype(F32)
        gco[hf] = g
        put_ec(ecg, hf, g)
        back = dot_nn(coarse_window(ecg, hf), w4b[...]).reshape(rows, cols, 128)
        gh4[hf, 1 : rows + 1] = back
        border(hout, 0, hf, back)
        return carry

    lax.fori_loop(0, half, coarse_gradient, 0, unroll=4)
    halo_start(g_h4_halo)

    def put_half(index, value):
        slot, owner = index // 2 // nd, index // 2 % nd
        current = gt_ref[slot, owner].astype(F32)
        value = join(current, swap(value)) if index % 2 else join(value, current)
        gt_ref[slot, owner] = value.astype(BF16)

    gt_ref[...] = jnp.zeros(gt_ref.shape, BF16)

    def fine_kernel_grad(index, e, start, gradient, gradient_start):
        acc[0, :, 0:1024] = jnp.zeros((256, 1024), F32)

        def add(f, carry):
            g = own_pixels(gradient, f, gradient_start, rows)
            acc[0, :, 0:1024] += dot_tn(g, window(e, f, start, rows))
            return carry

        lax.fori_loop(0, frames, add, 0, unroll=4)
        for t in range(3):
            u = []
            for dq in range(2):
                parts = [
                    acc[0, (dr * 2 + dq) * 64 : (dr * 2 + dq) * 64 + 64, pl.ds((t + dr) * 256, 256)]
                    for dr in range(2)
                ]
                u.append(parts[0] + parts[1])
            near, far = [v[:, 0:128] for v in u], [v[:, 128:256] for v in u]
            put_half(index(t, 0), swap(far[0]) + near[1])
            put_half(index(t, 1), near[0] + swap(near[1]))
            put_half(index(t, 2), swap(near[0]) + far[1])

    def coarse_kernel_grad(index, ec, gradient):
        acc[0, 0:128, :] = jnp.zeros((128, 1152), F32)

        def add(hf, carry):
            g = gradient[hf, 1 : rows + 1, :, 128:256].reshape(owned, 128)
            acc[0, 0:128, :] += dot_tn(g, coarse_window(ec, hf))
            return carry

        lax.fori_loop(0, half, add, 0, unroll=4)
        for a in range(3):
            for j in range(3):
                lanes = pl.ds((a * 3 + j) * 128, 128)
                put_half(index(a, j), acc[0, 0:64, lanes] + swap(acc[0, 64:128, lanes]))

    def down_kernel_grad(index):
        acc[:, 0:128, 0:768] = jnp.zeros((2, 128, 768), F32)

        def add(hf, carry):
            g = ed[hf, 1 : rows + 1, :, 0:128].reshape(owned, 128)
            acc[0, 0:128, 0:768] += dot_tn(g, down_window(hf))
            acc[1, 0:128, 0:768] += dot_tn(g, down_window(hf + half))
            return carry

        lax.fori_loop(0, half, add, 0, unroll=4)
        for a in range(3):
            near = acc[0, 0:64, pl.ds(a * 256, 128)] + acc[1, 64:128, pl.ds(a * 256, 128)]
            far = (
                acc[0, 0:64, pl.ds(a * 256 + 128, 128)] + acc[1, 64:128, pl.ds(a * 256 + 128, 128)]
            )
            put_half(index(a, 0), swap(far))
            put_half(index(a, 1), near)
            put_half(index(a, 2), swap(near))

    def up_kernel_grad():
        acc[...] = jnp.zeros(acc.shape, F32)

        def add(hf, carry):
            v = coarse_window(ecy, hf)
            acc[0] += dot_tn(own_pixels(eg, hf, 2, rows), v)
            acc[1] += dot_tn(own_pixels(eg, hf + half, 2, rows), v)
            return carry

        lax.fori_loop(0, half, add, 0, unroll=4)

        def block(dr, dq, i, j):
            r = (dr * 2 + dq) * 64
            lanes = pl.ds((i * 3 + j) * 128, 128)
            return acc[0, r : r + 64, lanes] + swap(acc[1, r : r + 64, lanes])

        place = {(0, 0): 0, (0, 1): 1, (0, 2): 1, (1, 0): 1, (1, 1): 1, (1, 2): 2}
        for ta in range(3):
            for tb in range(3):
                total = sum(
                    block(dr, dq, place[dr, ta], place[dq, tb])
                    for dr in range(2)
                    for dq in range(2)
                )
                put_half(45 + (ta * 3 + tb) * 2 + 1, total)


    halo_wait(d_halo)
    norm_forward(2, stat_total(2), True)

    def third_layer(hf, carry):
        total, square = carry
        with_halo(dv, hf, 1)
        z = dv[hf] * param(2, ALPHA, hf) + param(2, BETA, hf)
        h = z * logistic(z)
        put_ec(ec3, hf, jnp.where(block_mask(h.shape, 1), h, 0.0))
        out = dot_nt(coarse_window(ec3, hf), w3f[...]).reshape(rows, cols, 128)
        c3[hf, 1 : rows + 1] = out
        border(hout, 2, hf, out)
        return put_row(total, hf, coarse_sum(out)), put_row(square, hf, coarse_sum(out * out))

    sums = lax.fori_loop(0, half, third_layer, (zero_coarse, zero_coarse), unroll=4)
    stat_start(3, jnp.concatenate(list(sums) + pad_rows, axis=0))
    halo_start(c3_halo)
    fine_kernel_grad(lambda t, s: 45 + (t * 3 + s) * 2, esk, 2, eg, 2)

    halo_wait(c3_halo)
    halo_wait(g_h4_halo)
    norm_forward(3, stat_total(3), True)

    def fourth_layer(hf, carry):
        shift, scale = carry
        with_halo(c3, hf, 2)
        with_halo(gh4, hf, 0)
        v = c3[hf]
        z = v * param(3, ALPHA, hf) + param(3, BETA, hf)
        gate = logistic(z)
        h = z * gate
        put_ec(ec4, hf, jnp.where(block_mask(h.shape, 1), h, 0.0))
        g = gh4[hf] * (gate + h * (1.0 - gate))
        gz4[hf] = g
        own = g[1 : rows + 1]
        xhat = v[1 : rows + 1] * param(3, RSTD, hf) + param(3, NMR, hf)
        return put_row(shift, hf, coarse_sum(own)), put_row(scale, hf, coarse_sum(own * xhat))

    sums = lax.fori_loop(0, half, fourth_layer, (zero_coarse, zero_coarse), unroll=4)
    stat_start(4, jnp.concatenate(list(sums) + pad_rows, axis=0))

    def coarse_output(hf, carry):
        out = dot_nt(coarse_window(ec4, hf), w4f[...]).reshape(rows, cols, 128)
        y = dv[hf, 1 : rows + 1] + out
        border(hout, 3, hf, y)
        edge = jnp.zeros((1, cols, 128), F32)
        put_ec(ecy, hf, jnp.concatenate([edge, y, edge], axis=0))
        return carry

    lax.fori_loop(0, half, coarse_output, 0, unroll=4)
    halo_start(y_halo)
    coarse_kernel_grad(stacked(4), ec4, ecg)

    norm_backward(3, stat_total(4), True)

    def third_back(hf, carry):
        shift, scale = carry
        g = (
            gz4[hf] * param(3, ALPHA, hf)
            + c3[hf] * param(3, COEF, hf)
            + param(3, BIAS, hf)
        )
        put_ec(ecg3, hf, jnp.where(block_mask(g.shape, 1), g, 0.0))
        back = dot_nn(coarse_window(ecg3, hf), w3b[...]).reshape(rows, cols, 128)
        border(hout, 4, hf, back)
        v = dv[hf, 1 : rows + 1]
        z = v * param(2, ALPHA, hf) + param(2, BETA, hf)
        gate = logistic(z)
        own = back * (gate + z * gate * (1.0 - gate))
        gz3[hf, 1 : rows + 1] = own
        xhat = v * param(2, RSTD, hf) + param(2, NMR, hf)
        return put_row(shift, hf, coarse_sum(own)), put_row(scale, hf, coarse_sum(own * xhat))

    sums = lax.fori_loop(0, half, third_back, (zero_coarse, zero_coarse), unroll=4)
    stat_start(5, jnp.concatenate(list(sums) + pad_rows, axis=0))
    halo_start(g_h3_halo)

    halo_wait(y_halo)

    def result_copy(f):
        return pltpu.make_async_copy(raw.at[f], res_hbm.at[f], out_sem.at[f])

    def unpair(lo, hi):
        count = lo.shape[0]
        both = jnp.stack([lo, hi], axis=1).reshape(count * 2, cols, 128)
        tmp[0 : 2 * count, pl.ds(0, cols, stride=2), :] = both
        tmp[0 : 2 * count, pl.ds(1, cols, stride=2), :] = swap(both)

    def merge(hf, carry):
        for side, row in ((0, 0), (1, rows + 1)):
            line = hal[3, side, hf].astype(F32)[None]
            up, down = neighbours(line)
            q = lax.broadcasted_iota(jnp.int32, line.shape, 1)
            ecy[hf, row, :, 0:128] = jnp.where(q == 0, 0.0, down)[0].astype(BF16)
            ecy[hf, row, :, 128:256] = line[0].astype(BF16)
            ecy[hf, row, :, 256:384] = jnp.where(q == cols - 1, 0.0, up)[0].astype(BF16)
        both = dot_nt(coarse_window(ecy, hf), wup[...])
        for hi in range(2):
            f = hf + hi * half
            out = dot_nt(window(esk, f, 2, rows), wsf[...]) + both[:, hi * 256 : hi * 256 + 256]
            out = out.reshape(rows, cols, 256)
            unpair(out[:, :, 0:128], out[:, :, 128:256])
            raw[f] = tmp[:, :, 0:64].astype(BF16)
            result_copy(f).start()
        return carry

    lax.fori_loop(0, half, merge, 0, unroll=4)
    coarse_kernel_grad(stacked(3), ec3, ecg3)
    up_kernel_grad()
    gather_start(0)

    halo_wait(g_h3_halo)
    norm_backward(2, stat_total(5), True)

    def down_back(hf, carry):
        for side, row in ((0, 0), (1, rows + 1)):
            v = dv[hf, row]
            z = v * param(2, ALPHA, hf) + param(2, BETA, hf)
            gate = logistic(z)
            gz3[hf, row] = hal[4, side, hf].astype(F32) * (gate + z * gate * (1.0 - gate))
        g = (
            gco[hf]
            + gz3[hf] * param(2, ALPHA, hf)
            + dv[hf] * param(2, COEF, hf)
            + param(2, BIAS, hf)
        )
        g = jnp.where(block_mask(g.shape, 1), g, 0.0)
        up, _ = neighbours(g)
        q = lax.broadcasted_iota(jnp.int32, g.shape, 1)
        ed[hf, 0 : rows + 2, :, 0:128] = g.astype(BF16)
        ed[hf, 0 : rows + 2, :, 128:256] = jnp.where(q == cols - 1, 0.0, up).astype(BF16)
        ed[hf, rows + 2] = jnp.zeros((cols, 256), BF16)
        lhs = jnp.concatenate([ed[hf, 0 : rows + 2], ed[hf, 1 : rows + 3]], axis=-1)
        back = dot_nn(lhs.reshape(ext, 512), wdb[...])
        back = back.astype(BF16).astype(F32).reshape(rows + 2, cols, 512)
        for hi in range(2):
            f = hf + hi * half
            total = gsa[f] + back[:, :, hi * 256 : hi * 256 + 256]
            gsa[f] = total
            put_e(eg2, f, 0, jnp.where(block_mask(total.shape, 1), total, 0.0))
        return carry

    lax.fori_loop(0, half, down_back, 0, unroll=4)

    def second_back(f, carry):
        shift, scale = carry
        back = dot_nn(window(eg2, f, 1, rows), w2b[...]).reshape(rows, cols, 256)
        hfout[0, f] = back[0, :, 0:128].astype(BF16)
        hfout[1, f] = back[rows - 1, :, 128:256].astype(BF16)
        v = c1[f, 1 : rows + 1]
        z = v * wide(1, ALPHA, f) + wide(1, BETA, f)
        gate = logistic(z)
        own = back * (gate + z * gate * (1.0 - gate))
        gz[f, 1 : rows + 1] = own
        xhat = v * wide(1, RSTD, f) + wide(1, NMR, f)
        return put_row(shift, f, full_sum(own)), put_row(scale, f, full_sum(own * xhat))

    sums = lax.fori_loop(0, frames, second_back, (zero_rows, zero_rows), unroll=4)
    stat_start(6, jnp.concatenate(sums, axis=0))
    halo_start(g_h2_halo)
    down_kernel_grad(stacked(2))
    fine_kernel_grad(stacked(1), e2, 2, eg2, 1)
    gather_start(1)
    gather_space(0)
    halo_wait(g_h2_halo)
    norm_backward(1, stat_total(6), False)

    def first_back(f, carry):
        shift, scale = carry
        for side, row in ((0, 0), (1, rows + 1)):
            v = c1[f, row]
            lanes = slice(128, 256) if side == 0 else slice(0, 128)
            z = v[:, lanes] * param(1, ALPHA, f) + param(1, BETA, f)
            gate = logistic(z)
            g = hfull[side, f].astype(F32) * (gate + z * gate * (1.0 - gate))
            blank = jnp.zeros_like(g)
            gz[f, row] = jnp.concatenate([blank, g] if side == 0 else [g, blank], axis=-1)
        g = gz[f] * wide(1, ALPHA, f) + c1[f] * wide(1, COEF, f) + wide(1, BIAS, f)
        put_e(eg, f, 0, jnp.where(block_mask(g.shape, 1), g, 0.0))
        back = dot_nn(window(eg, f, 1, rows), w1b[...]).reshape(rows, cols, 256)
        v = xs[f, 2 : rows + 2].astype(F32)
        z = v * wide(0, ALPHA, f) + wide(0, BETA, f)
        gate = logistic(z)
        own = back * (gate + z * gate * (1.0 - gate))
        gz[f, 1 : rows + 1] = own
        xhat = v * wide(0, RSTD, f) + wide(0, NMR, f)
        return put_row(shift, f, full_sum(own)), put_row(scale, f, full_sum(own * xhat))

    pack_start(0)
    sums = lax.fori_loop(0, frames, first_back, (zero_rows, zero_rows), unroll=4)
    stat_start(7, jnp.concatenate(sums, axis=0))
    gather_spread(0)
    gather_space(1)
    fine_kernel_grad(stacked(0), e1, 2, eg, 1)
    gather_start(2)
    norm_backward(0, stat_total(7), False)
    pack_start(1)
    gather_all(0)
    gather_spread(1)

    def frames_copy(f):
        slot = lax.rem(f, 2)
        return pltpu.make_async_copy(fst.at[slot], fg_hbm.at[f], fg_sem.at[slot])

    def frames_back(f, carry):
        g = (
            gsa[f, 1 : rows + 1]
            + gz[f, 1 : rows + 1] * wide(0, ALPHA, f)
            + xs[f, 2 : rows + 2].astype(F32) * wide(0, COEF, f)
            + wide(0, BIAS, f)
        )
        unpair(g[:, :, 0:128], g[:, :, 128:256])

        @pl.when(f >= 2)
        def _():
            frames_copy(f - 2).wait()

        fst[lax.rem(f, 2)] = tmp[:, :, 0:64]
        frames_copy(f).start()
        return carry

    lax.fori_loop(0, frames, frames_back, 0, unroll=4)
    gather_space(2)
    gather_all(1)
    gather_spread(2)
    gather_all(2)
    for stage in range(3):
        gather_finish(stage)
    for off in range(1, nd):
        for which in range(2):
            pack_copy(which, off, dp_before(off)).wait_recv()
            pack_copy(which, off, dp).wait_send()
    for slot in range(slots):
        for owner in range(nd):
            lane = (slot * nd + owner) * 128
            gout_ref[:, lane : lane + 128] = gall[owner, slot]

    frames_copy(frames - 2).wait()
    frames_copy(frames - 1).wait()
    for f in range(frames):
        result_copy(f).wait()
    for copies in (x_halo, g_halo, g_h4_halo, d_halo, c3_halo, y_halo, g_h3_halo, g_h2_halo):
        halo_finish(copies)


def run_step(nd, n, frames, cotangent, actions, noise_ids, games, live_counts, cw, nm, table):
    count, strip, breadth, _ = frames.shape
    half, rows, cols = count // 2, strip // 2, breadth // 2
    fine = (count, rows + 4, cols, 512)
    coarse = (half, rows + 2, cols, 128)
    coarse_e = (half, rows + 2, cols, 384)
    scratch = [
        VM((count, strip, breadth, 64), BF16),
        VM((2, 2, count, 3, breadth, 64), BF16),
        VM((strip, breadth, 128), F32),
        VM((2, strip, breadth, 64), F32),
        VM((count, rows + 4, cols, 256), BF16),
        VM(fine, BF16),
        VM(fine, BF16),
        VM(fine, BF16),
        VM(fine, BF16),
        VM((count, rows + 2, cols, 512), BF16),
        VM((count, rows + 2, cols, 256), F32),
        VM((count, rows + 2, cols, 256), F32),
        VM((count, rows + 2, cols, 256), F32),
        VM(coarse, F32),
        VM(coarse, F32),
        VM(coarse, F32),
        VM(coarse, F32),
        VM(coarse, F32),
        VM(coarse, F32),
        VM(coarse_e, BF16),
        VM(coarse_e, BF16),
        VM(coarse_e, BF16),
        VM(coarse_e, BF16),
        VM(coarse_e, BF16),
        VM((half, rows + 3, cols, 256), BF16),
        VM((256, 1024), BF16),
        VM((1024, 256), BF16),
        VM((256, 1024), BF16),
        VM((1024, 256), BF16),
        VM((256, 1024), BF16),
        VM((1024, 256), BF16),
        VM((512, 1152), BF16),
        VM((2, 1024, 128), BF16),
        VM((128, 1536), BF16),
        VM((512, 512), BF16),
        VM((128, 1152), BF16),
        VM((1152, 128), BF16),
        VM((128, 1152), BF16),
        VM((1152, 128), BF16),
        VM((2, 256, 1152), F32),
        VM((32, count, 128), F32),
        VM((128, 256), F32),
        VM((8, n, 2 * count, 128), F32),
        VM((5, 2, half, cols, 128), BF16),
        VM((5, 2, half, cols, 128), BF16),
        VM((2, count, cols, 128), BF16),
        VM((2, count, cols, 128), BF16),
        VM((4, 256, 128), F32),
        VM((4, 128), F32),
        VM((32 // nd, nd, 64, 128), BF16),
        VM((nd, 32 // nd, 64, 128), BF16),
        VM((n, 32 // nd, 64 // n, 128), F32),
        VM((n, 32 // nd, 64 // n, 128), F32),
        VM((n, 32 // nd, 64 // n, 128), F32),
        VM((nd, 32 // nd, 64, 128), BF16),
        pltpu.SemaphoreType.DMA((7,)),
        pltpu.SemaphoreType.DMA((count,)),
        pltpu.SemaphoreType.DMA((2,)),
        pltpu.SemaphoreType.DMA((8, n - 1)),
        pltpu.SemaphoreType.DMA((8, n - 1)),
        pltpu.SemaphoreType.DMA((8, 2)),
        pltpu.SemaphoreType.DMA((8, 2)),
        pltpu.SemaphoreType.DMA((4, 2, nd - 1)),
        pltpu.SemaphoreType.DMA((4, 2, nd - 1)),
        pltpu.SemaphoreType.DMA((3, 2, n - 1)),
        pltpu.SemaphoreType.DMA((3, 2, n - 1)),
    ]
    smem = pl.BlockSpec(memory_space=pltpu.SMEM)
    vmem = pl.BlockSpec(memory_space=pltpu.VMEM)
    hbm = pl.BlockSpec(memory_space=pl.ANY)
    return pl.pallas_call(
        functools.partial(step_kernel, nd, n),
        out_shape=(
            jax.ShapeDtypeStruct(frames.shape, BF16),
            jax.ShapeDtypeStruct(frames.shape, F32),
            jax.ShapeDtypeStruct((64, 4096), BF16),
            jax.ShapeDtypeStruct((nd, count, 896), F32),
        ),
        in_specs=[hbm, hbm, smem, smem, smem, smem, vmem, hbm, vmem],
        out_specs=(hbm, hbm, vmem, vmem),
        scratch_shapes=scratch,
        compiler_params=pltpu.CompilerParams(
            collective_id=0, has_side_effects=True, vmem_limit_bytes=62 * 1024 * 1024
        ),
        name="step",
    )(frames, cotangent, actions, noise_ids, games, live_counts, cw, nm, table)


def adamw(weight, moment, square, grad_value, rate):
    fix_one = 1.0 - BETA_ONE**ADAM_STEP
    fix_two = 1.0 - BETA_TWO**ADAM_STEP
    moment_new = BETA_ONE * moment + (1.0 - BETA_ONE) * grad_value
    square_new = BETA_TWO * square + (1.0 - BETA_TWO) * grad_value * grad_value
    fixed_m = moment_new / fix_one
    fixed_v = square_new / fix_two
    weight_new = weight - rate * (fixed_m / (jnp.sqrt(fixed_v) + ADAM_EPS) + DECAY * weight)
    return (moment_new, square_new, weight_new, weight_new.astype(BF16))


def local(
    nd,
    ns,
    frames,
    cotangent,
    actions,
    noise_ids,
    games,
    live_counts,
    conv_weight,
    conv_moment,
    conv_square,
    norm_map,
    norm_moment,
    norm_square,
    emb_table,
    table_moment,
    table_square,
):
    cw = conv_weight.T
    nm = jnp.transpose(norm_map, (1, 0, 2))
    result, frames_grad, grads, packs = run_step(
        nd, ns, frames, cotangent, actions, noise_ids, games, live_counts, cw, nm, emb_table
    )
    grad_t = grads[:, : conv_weight.shape[0]].astype(F32)
    conv_out = [v.T for v in adamw(cw, conv_moment.T, conv_square.T, grad_t, 0.05)]
    packs = packs.reshape(-1, 896)
    dmods = packs[:, 0:512]
    embedded = packs[:, 512:768]
    hot = packs[:, 768 : 768 + emb_table.shape[0]]
    top = jnp.dot(embedded.T, dmods, precision=HIGH).reshape(256, 4, 128)
    last = jnp.sum(dmods, axis=0).reshape(1, 4, 128)
    grad_map = jnp.concatenate([top, last], axis=0).transpose(1, 0, 2)
    norm_out = adamw(norm_map, norm_moment, norm_square, grad_map, 0.04)
    g_embed = jnp.dot(
        dmods, norm_map[:, :-1].transpose(0, 2, 1).reshape(512, 256), precision=HIGH
    )
    grad_table = jnp.dot(hot.T, g_embed, precision=HIGH)
    table_out = adamw(emb_table, table_moment, table_square, grad_table, 0.5)
    return (result, frames_grad, *conv_out, *norm_out, *table_out)


def solution(mesh):
    split = P("dp", "space", None, None)
    in_specs = (split, split) + (P("dp"),) * 4 + (P(),) * 9
    out_specs = (split, split) + (P(),) * 12
    sizes = dict(mesh.shape)
    return jax.shard_map(
        functools.partial(local, sizes["dp"], sizes["space"]),
        mesh=mesh,
        in_specs=in_specs,
        out_specs=out_specs,
        check_vma=False,
    )
```

```python
import functools

import jax
import jax.numpy as jnp
from jax import lax
from jax.experimental import pallas as pl
from jax.experimental.pallas import tpu as pltpu
from jax.sharding import PartitionSpec as P

ACTIONS = 18
NOISE_LEVELS = 64
ADAM_STEP = 4
NORM_EPSILON = 1e-05
ADAM_EPS = 1e-08
BETA_ONE = 0.5
BETA_TWO = 0.5
DECAY = 0.01
HIGH = lax.Precision.HIGHEST
F32 = jnp.float32
BF16 = jnp.bfloat16
MESH = pl.DeviceIdType.MESH
VM = pltpu.VMEM

ALPHA, BETA, RSTD, NMR, GAIN, SHIFT, COEF, BIAS = range(8)


def dot_nn(a, b):
    return lax.dot_general(a, b, (((1,), (0,)), ((), ())), preferred_element_type=F32)


def dot_nt(a, b):
    return lax.dot_general(a, b, (((1,), (1,)), ((), ())), preferred_element_type=F32)


def dot_tn(a, b):
    return lax.dot_general(a, b, (((0,), (0,)), ((), ())), preferred_element_type=F32)


def dot_high(a, b):
    return lax.dot_general(
        a, b, (((1,), (0,)), ((), ())), precision=HIGH, preferred_element_type=F32
    )


def logistic(z):
    return 0.5 * jnp.tanh(0.5 * z) + 0.5


def lane_iota(shape):
    return lax.broadcasted_iota(jnp.int32, shape, len(shape) - 1)


def swap(v):
    return pltpu.roll(v, 64, len(v.shape) - 1)


def join(lo, hi):
    return jnp.where(lane_iota(lo.shape) < 64, lo, hi)


def twice(row):
    return jnp.concatenate([row, row], axis=-1)


def step_kernel(
    nd,
    n,
    x_hbm,
    cot_hbm,
    act_ref,
    noise_ref,
    game_ref,
    live_ref,
    cw_ref,
    nm_hbm,
    tab_ref,
    io_hbm,
    par_hbm,
    raw,
    tmp,
    xs,
    gs,
    e1,
    e2,
    esk,
    eg,
    c1,
    gsa,
    gz,
    dv,
    c3,
    gh4,
    gzc,
    gco,
    ec3,
    ec4,
    ecg,
    ecg3,
    ecy,
    ed,
    w1f,
    w1b,
    w2f,
    w2b,
    wsf,
    wsb,
    wup,
    wco,
    wdf,
    wdb,
    w3f,
    w3b,
    w4f,
    w4b,
    acc,
    prm,
    tabp,
    stat,
    hal,
    hout,
    hfull,
    hfout,
    nmv,
    nmb,
    gt_ref,
    rbuf,
    part,
    zbuf,
    zfull,
    gall,
    packs,
    local_sem,
    out_sem,
    fg_sem,
    stat_send,
    stat_recv,
    halo_send,
    halo_recv,
    dp_send,
    dp_recv,
    sp_send,
    sp_recv,
):
    frames, strip = raw.shape[0], raw.shape[1]
    breadth = raw.shape[2]
    half = frames // 2
    rows = strip // 2
    cols = breadth // 2
    me = lax.axis_index("space")
    dp = lax.axis_index("dp")
    full_cells = float(strip * n * breadth * 32)
    coarse_cells = full_cells / 4.0
    owned = rows * cols
    ext = (rows + 2) * cols

    x_copy = pltpu.make_async_copy(x_hbm, raw, local_sem.at[0])
    x_copy.start()
    g_copy = pltpu.make_async_copy(cot_hbm, raw, local_sem.at[1])
    map_copies = [
        pltpu.make_async_copy(nm_hbm.at[pl.ds(0, 256), k], nmv.at[k], local_sem.at[2 + k])
        for k in range(4)
    ]
    map_copies.append(pltpu.make_async_copy(nm_hbm.at[256], nmb, local_sem.at[6]))
    for copy in map_copies:
        copy.start()

    barrier = pltpu.get_barrier_semaphore()
    for off in range(1, n):
        pl.semaphore_signal(
            barrier,
            inc=1,
            device_id={"space": lax.rem(me + off, n)},
            device_id_type=MESH,
        )
    for off in range(1, nd):
        pl.semaphore_signal(
            barrier,
            inc=1,
            device_id={"dp": lax.rem(dp + off, nd)},
            device_id_type=MESH,
        )

    def halo_copies(k, first, last, to_up, to_down):
        up = pltpu.make_async_remote_copy(
            src_ref=first,
            dst_ref=to_up,
            send_sem=halo_send.at[k, 0],
            recv_sem=halo_recv.at[k, 0],
            device_id={"space": lax.rem(me + n - 1, n)},
            device_id_type=MESH,
        )
        down = pltpu.make_async_remote_copy(
            src_ref=last,
            dst_ref=to_down,
            send_sem=halo_send.at[k, 1],
            recv_sem=halo_recv.at[k, 1],
            device_id={"space": lax.rem(me + 1, n)},
            device_id_type=MESH,
        )
        return up, down

    def halo_start(copies):
        @pl.when(me > 0)
        def _():
            copies[0].start()

        @pl.when(me < n - 1)
        def _():
            copies[1].start()

    def halo_wait(copies):
        @pl.when(me < n - 1)
        def _():
            copies[0].wait_recv()

        @pl.when(me > 0)
        def _():
            copies[1].wait_recv()

    def halo_finish(copies):
        @pl.when(me > 0)
        def _():
            copies[0].wait_send()

        @pl.when(me < n - 1)
        def _():
            copies[1].wait_send()

    def stat_copy(k, off, slot):
        return pltpu.make_async_remote_copy(
            src_ref=stat.at[k, slot],
            dst_ref=stat.at[k, slot],
            send_sem=stat_send.at[k, off - 1],
            recv_sem=stat_recv.at[k, off - 1],
            device_id={"space": lax.rem(me + off, n)},
            device_id_type=MESH,
        )

    def stat_start(k, value):
        stat[k, me] = value
        for off in range(1, n):
            stat_copy(k, off, me).start()

    def stat_total(k):
        for off in range(1, n):
            stat_copy(k, off, lax.rem(me + n - off, n)).wait_recv()
        total = stat[k, 0]
        for i in range(1, n):
            total = total + stat[k, i]
        for off in range(1, n):
            stat_copy(k, off, me).wait_send()
        return total

    def wide_halos(k, v):
        both = halo_copies(
            k, v.at[:, 2], v.at[:, rows + 1], v.at[:, rows + 2], v.at[:, 1]
        )
        third = halo_copies(
            k + 1,
            v.at[:, 3, :, pl.ds(0, 128)],
            v.at[:, rows, :, pl.ds(128, 128)],
            v.at[:, rows + 3, :, pl.ds(0, 128)],
            v.at[:, 0, :, pl.ds(128, 128)],
        )
        return both, third

    x_halos = wide_halos(0, xs)
    g_halos = wide_halos(8, gs)

    def coarse_halo(k):
        return halo_copies(
            k, hout.at[k - 2, 0], hout.at[k - 2, 1], hal.at[k - 2, 1], hal.at[k - 2, 0]
        )

    g_h4_halo, d_halo, c3_halo, y_halo, g_h3_halo = [coarse_halo(k) for k in range(2, 7)]
    g_h2_halo = halo_copies(7, hfout.at[0], hfout.at[1], hfull.at[1], hfull.at[0])

    def block_mask(shape, pad):
        blocks = shape[0]
        b = lax.broadcasted_iota(jnp.int32, shape, 0)
        low = jnp.where(me > 0, 0, pad)
        high = jnp.where(me < n - 1, blocks, blocks - pad)
        return (b >= low) & (b < high)

    def param(k, which, f):
        return prm[k * 8 + which, pl.ds(f, 1), :]

    def wide(k, which, f):
        return twice(param(k, which, f))

    def put_row(carry, f, value):
        row = lax.broadcasted_iota(jnp.int32, carry.shape, 0)
        return jnp.where(row == f, value, carry)

    def full_sum(v):
        s = jnp.sum(v.reshape(-1, 256), axis=0, keepdims=True)
        return s[:, :128] + s[:, 128:]

    def paired(raw_rows):
        count = raw_rows.shape[0]
        tmp[0:count, :, 0:64] = raw_rows.astype(F32)
        even = tmp[0:count, pl.ds(0, cols, stride=2), :]
        odd = tmp[0:count, pl.ds(1, cols, stride=2), :]
        return join(even, swap(odd))

    def pair_halves(p):
        count = p.shape[0] // 2
        p = p.reshape(count, 2, cols, 128)
        return p[:, 0], p[:, 1]

    def neighbours(v):
        count = v.shape[0]
        flat = v.reshape(count * cols, 128)
        up = pltpu.roll(flat, count * cols - 1, 0).reshape(v.shape)
        down = pltpu.roll(flat, 1, 0).reshape(v.shape)
        return up, down

    def put_e(e, f, start, h):
        count = h.shape[0]
        for part in range(2):
            v = h[:, :, part * 128 : (part + 1) * 128]
            up, down = neighbours(v)
            lane = lane_iota(v.shape)
            q = lax.broadcasted_iota(jnp.int32, v.shape, 1)
            near = jnp.where(
                lane < 64, jnp.where(q == cols - 1, 0.0, up), jnp.where(q == 0, 0.0, down)
            )
            e[f, start : start + count, :, part * 256 : part * 256 + 128] = v.astype(BF16)
            e[f, start : start + count, :, part * 256 + 128 : part * 256 + 256] = near.astype(BF16)

    def window(e, f, start, count):
        return jnp.concatenate(
            [
                e[f, start - 1 : start - 1 + count, :, 256:512],
                e[f, start : start + count, :, :],
                e[f, start + 1 : start + 1 + count, :, 0:256],
            ],
            axis=-1,
        ).reshape(count * cols, 1024)

    def own_pixels(e, f, start, count):
        return jnp.concatenate(
            [
                e[f, start : start + count, :, 0:128],
                e[f, start : start + count, :, 256:384],
            ],
            axis=-1,
        ).reshape(count * cols, 256)

    def put_ec(ec, hf, v):
        up, down = neighbours(v)
        q = lax.broadcasted_iota(jnp.int32, v.shape, 1)
        ec[hf, :, :, 0:128] = jnp.where(q == 0, 0.0, down).astype(BF16)
        ec[hf, :, :, 128:256] = v.astype(BF16)
        ec[hf, :, :, 256:384] = jnp.where(q == cols - 1, 0.0, up).astype(BF16)

    def coarse_window(ec, hf):
        return jnp.concatenate([ec[hf, a : a + rows] for a in range(3)], axis=-1).reshape(
            owned, 1152
        )

    def coarse_sum(v):
        return jnp.sum(v.reshape(-1, 128), axis=0, keepdims=True)

    def with_halo(ref, hf, k):
        ref[hf, 0] = hal[k, 0, hf].astype(F32)
        ref[hf, rows + 1] = hal[k, 1, hf].astype(F32)

    def border(ref_out, k, hf, v):
        ref_out[k, 0, hf] = v[0].astype(BF16)
        ref_out[k, 1, hf] = v[rows - 1].astype(BF16)

    def group_matrix(coarse):
        r = lax.broadcasted_iota(jnp.int32, (128, 128), 0) // 32
        c = lax.broadcasted_iota(jnp.int32, (128, 128), 1) // 32
        same = (r == c) if coarse else (r % 2 == c % 2)
        return jnp.where(same, 1.0, 0.0)

    def norm_forward(k, total, coarse):
        cells = coarse_cells if coarse else full_cells
        count = half if coarse else frames
        moments = dot_high(total, group_matrix(coarse)) / cells
        mean = moments[0:count]
        var = moments[count : 2 * count] - mean * mean
        rstd = lax.rsqrt(var + NORM_EPSILON)
        gain = prm[k * 8 + GAIN, 0:count, :]
        alpha = rstd * gain
        prm[k * 8 + ALPHA, 0:count, :] = alpha
        prm[k * 8 + BETA, 0:count, :] = prm[k * 8 + SHIFT, 0:count, :] - mean * alpha
        prm[k * 8 + RSTD, 0:count, :] = rstd
        prm[k * 8 + NMR, 0:count, :] = -mean * rstd

    def norm_backward(k, total, coarse):
        cells = coarse_cells if coarse else full_cells
        count = half if coarse else frames
        gain = prm[k * 8 + GAIN, 0:count, :]
        shift_grad = total[0:count]
        scale_grad = total[count : 2 * count]
        means = (
            dot_high(
                jnp.concatenate([shift_grad * gain, scale_grad * gain], axis=0),
                group_matrix(coarse),
            )
            / cells
        )
        rstd = prm[k * 8 + RSTD, 0:count, :]
        factor = -rstd * means[count : 2 * count]
        prm[k * 8 + COEF, 0:count, :] = rstd * factor
        prm[k * 8 + BIAS, 0:count, :] = (
            prm[k * 8 + NMR, 0:count, :] * factor - rstd * means[0:count]
        )
        if coarse:
            scale_all = jnp.concatenate([scale_grad, swap(scale_grad)], axis=0)
            shift_all = jnp.concatenate([shift_grad, swap(shift_grad)], axis=0)
        else:
            scale_all = scale_grad + swap(scale_grad)
            shift_all = shift_grad + swap(shift_grad)
        packs[dp, :, k * 128 : (k + 1) * 128] = join(scale_all, swap(shift_all))

    slots = 32 // nd
    share = 64 // n
    first_slots = [
        [i for i in range(slots) if i * nd >= 16],
        [i for i in range(slots) if 8 <= i * nd < 16],
        [0],
    ]

    def dp_before(off):
        return lax.rem(dp + nd - off, nd)

    def dp_after(off):
        return lax.rem(dp + off, nd)

    def sp_before(off):
        return lax.rem(me + n - off, n)

    def sp_after(off):
        return lax.rem(me + off, n)

    def stage_slots(stage):
        chosen = first_slots[stage]
        return pl.ds(chosen[0], len(chosen))

    def dp_copy(stage, phase, src, dst, off):
        return pltpu.make_async_remote_copy(
            src_ref=src,
            dst_ref=dst,
            send_sem=dp_send.at[stage, phase, off - 1],
            recv_sem=dp_recv.at[stage, phase, off - 1],
            device_id={"dp": dp_after(off)},
            device_id_type=MESH,
        )

    def sp_copy(stage, phase, src, dst, off):
        return pltpu.make_async_remote_copy(
            src_ref=src,
            dst_ref=dst,
            send_sem=sp_send.at[stage, phase, off - 1],
            recv_sem=sp_recv.at[stage, phase, off - 1],
            device_id={"space": sp_after(off)},
            device_id_type=MESH,
        )

    def first_copy(stage, off, owner, slot):
        where = stage_slots(stage)
        return dp_copy(stage, 0, gt_ref.at[where, owner], rbuf.at[slot, where], off)

    def second_copy(stage, off, row, slot):
        where = stage_slots(stage)
        return sp_copy(stage, 0, part.at[row, where], zbuf.at[slot, where], off)

    def third_copy(stage, off, slot):
        where = stage_slots(stage)
        return sp_copy(stage, 1, zfull.at[slot, where], zfull.at[slot, where], off)

    def fourth_copy(stage, off, slot):
        where = stage_slots(stage)
        return dp_copy(stage, 1, gall.at[slot, where], gall.at[slot, where], off)

    def pack_copy(which, off, slot):
        lanes = pl.ds(0, 128) if which else pl.ds(128, 768)
        return dp_copy(3, which, packs.at[slot, :, lanes], packs.at[slot, :, lanes], off)

    def pack_start(which):
        for off in range(1, nd):
            pack_copy(which, off, dp).start()

    def gather_start(stage):
        if not first_slots[stage]:
            return
        for off in range(1, nd):
            first_copy(stage, off, dp_after(off), dp).start()

    def gather_space(stage):
        if not first_slots[stage]:
            return
        where = stage_slots(stage)
        for off in range(1, nd):
            first_copy(stage, off, dp, dp_before(off)).wait_recv()
        rbuf[dp, where] = gt_ref[where, dp]
        total = rbuf[0, where].astype(F32)
        for i in range(1, nd):
            total = total + rbuf[i, where].astype(F32)
        for z in range(n):
            part[z, where] = total[:, z * share : (z + 1) * share]
        for off in range(1, n):
            second_copy(stage, off, sp_after(off), me).start()

    def gather_spread(stage):
        if not first_slots[stage]:
            return
        where = stage_slots(stage)
        for off in range(1, n):
            second_copy(stage, off, me, sp_before(off)).wait_recv()
        zbuf[me, where] = part[me, where]
        total = zbuf[0, where]
        for i in range(1, n):
            total = total + zbuf[i, where]
        zfull[me, where] = total
        for off in range(1, n):
            third_copy(stage, off, me).start()

    def gather_all(stage):
        if not first_slots[stage]:
            return
        where = stage_slots(stage)
        for off in range(1, n):
            third_copy(stage, off, sp_before(off)).wait_recv()
        whole = jnp.concatenate([zfull[z, where] for z in range(n)], axis=1)
        gall[dp, where] = whole.astype(BF16)
        for off in range(1, nd):
            fourth_copy(stage, off, dp).start()

    def gather_finish(stage):
        if not first_slots[stage]:
            return
        for off in range(1, nd):
            fourth_copy(stage, off, dp_before(off)).wait_recv()
            first_copy(stage, off, dp_after(off), dp).wait_send()
            fourth_copy(stage, off, dp).wait_send()
        for off in range(1, n):
            second_copy(stage, off, sp_after(off), me).wait_send()
            third_copy(stage, off, me).wait_send()

    x_copy.wait()

    def load_x(f, carry):
        total, square = carry
        even, odd = pair_halves(paired(raw[f]))
        both = jnp.concatenate([even, odd], axis=-1)
        xs[f, 2 : 2 + rows] = both.astype(BF16)
        return put_row(total, f, full_sum(both)), put_row(square, f, full_sum(both * both))

    zero_rows = jnp.zeros((frames, 128), F32)
    sums = lax.fori_loop(0, frames, load_x, (zero_rows, zero_rows), unroll=4)
    g_copy.start()
    pl.semaphore_wait(barrier, n + nd - 2)
    stat_start(0, jnp.concatenate(sums, axis=0))
    for copies in x_halos:
        halo_start(copies)

    @pl.when(me == 0)
    def _():
        for v in (xs, gs):
            v[:, 0:2] = jnp.zeros((frames, 2, cols, 256), BF16)
        for which in range(hal.shape[0]):
            hal[which, 0] = jnp.zeros(hal.shape[2:], BF16)
        hfull[0] = jnp.zeros(hfull.shape[1:], BF16)

    @pl.when(me == n - 1)
    def _():
        for v in (xs, gs):
            v[:, rows + 2 : rows + 4] = jnp.zeros((frames, 2, cols, 256), BF16)
        for which in range(hal.shape[0]):
            hal[which, 1] = jnp.zeros(hal.shape[2:], BF16)
        hfull[1] = jnp.zeros(hfull.shape[1:], BF16)

    for v in (xs, gs):
        v[:, 0, :, 0:128] = jnp.zeros((frames, cols, 128), BF16)
        v[:, rows + 3, :, 128:256] = jnp.zeros((frames, cols, 128), BF16)

    def conditioning():
        entry = lax.broadcasted_iota(jnp.int32, (frames, 128), 1)
        row = lax.broadcasted_iota(jnp.int32, (frames, 128), 0)
        hot = jnp.zeros((frames, 128), F32)
        for f in range(frames):
            hit = (
                (entry == act_ref[f])
                | (entry == noise_ref[f] + ACTIONS)
                | (entry == game_ref[f] + ACTIONS + NOISE_LEVELS)
            )
            hot = jnp.where((row == f) & hit, 1.0, hot)
        table_rows = tab_ref.shape[0]
        tabp[...] = jnp.zeros(tabp.shape, F32)
        tabp[0:table_rows, :] = tab_ref[...]
        embedded = dot_high(hot, tabp[...])
        packs[dp, :, 512:768] = embedded
        packs[dp, :, 768:896] = hot
        for copy in map_copies:
            copy.wait()
        for k in range(4):
            mod = dot_high(embedded, nmv[k]) + nmb[k : k + 1, :]
            scale = join(mod, swap(mod)) + 1.0
            shift = join(swap(mod), mod)
            if k < 2:
                prm[k * 8 + GAIN] = scale
                prm[k * 8 + SHIFT] = shift
            else:
                prm[k * 8 + GAIN, 0:half, :] = join(scale[0:half], scale[half:])
                prm[k * 8 + SHIFT, 0:half, :] = join(shift[0:half], shift[half:])

    conditioning()

    g_copy.wait()

    def load_cotangent(f, carry):
        live = jnp.where(f < live_ref[0], 1.0, 0.0)
        even, odd = pair_halves(paired(raw[f]))
        both = jnp.concatenate([even, odd], axis=-1)
        gs[f, 2 : 2 + rows] = (both * live).astype(BF16)
        return carry

    lax.fori_loop(0, frames, load_cotangent, 0, unroll=4)
    for copies in g_halos:
        halo_start(copies)


    def tap(index):
        first = (index // 2) * 128
        last = min(first + 128, cw_ref.shape[1])
        tile = cw_ref[:, first:last].astype(BF16).astype(F32)
        if last - first < 128:
            tile = jnp.concatenate([tile, jnp.zeros((64, 128 - last + first), F32)], axis=-1)
        return tile, index % 2

    def low_half(index):
        tile, odd = tap(index)
        return swap(tile) if odd else tile

    def high_half(index):
        tile, odd = tap(index)
        return tile if odd else swap(tile)

    def lane_pair(low_index, high_index):
        zero = jnp.zeros((64, 128), F32)
        low = zero if low_index is None else low_half(low_index)
        high = zero if high_index is None else high_half(high_index)
        return join(low, high).astype(BF16)

    def fine_weights(index, forward_w, backward_w):
        zero = jnp.zeros((64, 128), BF16)
        pairs = []
        for t in range(3):
            p12 = lane_pair(index(t, 1), index(t, 2))
            p01 = lane_pair(index(t, 0), index(t, 1))
            pz0 = lane_pair(None, index(t, 0))
            p2z = lane_pair(index(t, 2), None)
            pairs.append((p12, p01, pz0, p2z))
        for a in range(4):
            for dr in range(2):
                t = a - dr
                ok = 0 <= t <= 2
                for dq in range(2):
                    r = (dr * 2 + dq) * 64
                    first = pairs[t][0 if dq == 0 else 1] if ok else zero
                    second = pairs[t][2 if dq == 0 else 3] if ok else zero
                    forward_w[r : r + 64, a * 256 : a * 256 + 128] = first
                    forward_w[r : r + 64, a * 256 + 128 : a * 256 + 256] = second
                t = 2 - a + dr
                ok = 0 <= t <= 2
                for g in range(4):
                    r = a * 256 + g * 64
                    backward_w[r : r + 64, dr * 128 : dr * 128 + 128] = (
                        pairs[t][g] if ok else zero
                    )

    def coarse_weights(index, forward_w, backward_w):
        for a in range(3):
            for j in range(3):
                lane = (a * 3 + j) * 128
                low = lane_pair(index(a, j), None)
                high = lane_pair(None, index(a, j))
                forward_w[0:64, lane : lane + 128] = low
                forward_w[64:128, lane : lane + 128] = high
                lane = ((2 - a) * 3 + (2 - j)) * 128
                backward_w[lane : lane + 64, :] = low
                backward_w[lane + 64 : lane + 128, :] = high

    def down_weights(index):
        zero = jnp.zeros((64, 128), BF16)
        wdf[...] = jnp.zeros(wdf.shape, BF16)
        wdb[...] = jnp.zeros(wdb.shape, BF16)
        for t in range(3):
            p12 = lane_pair(index(t, 1), index(t, 2))
            pz0 = lane_pair(None, index(t, 0))
            for hi in range(2):
                lane = hi * 768 + t * 256
                wdf[hi * 64 : hi * 64 + 64, lane : lane + 128] = p12
                wdf[hi * 64 : hi * 64 + 64, lane + 128 : lane + 256] = pz0
                i, dr = ((1, 1), (0, 0), (0, 1))[t]
                lane = hi * 256 + dr * 128
                for j in range(2):
                    r = (i * 2 + j) * 128 + hi * 64
                    wdb[r : r + 64, lane : lane + 128] = p12 if j == 0 else pz0

    def up_weights():
        def up_tap(ta, tb):
            return low_half(45 + (ta * 3 + tb) * 2 + 1)

        taps = [[up_tap(ta, tb) for tb in range(3)] for ta in range(3)]
        members = {(0, 0): (0,), (0, 1): (1, 2), (1, 1): (0, 1), (1, 2): (2,)}
        wup[...] = jnp.zeros(wup.shape, BF16)
        for (dr, i), in_rows in members.items():
            for (dq, j), in_cols in members.items():
                total = sum(taps[ta][tb] for ta in in_rows for tb in in_cols)
                zero = jnp.zeros_like(total)
                r = (dr * 2 + dq) * 64
                lane = (i * 3 + j) * 128
                wup[r : r + 64, lane : lane + 128] = join(total, zero).astype(BF16)
                wup[256 + r : 256 + r + 64, lane : lane + 128] = join(zero, swap(total)).astype(
                    BF16
                )
        for a in range(4):
            for g, off in enumerate((0, 1, 2, -1)):
                chosen = [
                    taps[2 - a + dr][1 - off + dq]
                    for dr in range(2)
                    for dq in range(2)
                    if 0 <= 2 - a + dr <= 2 and 0 <= 1 - off + dq <= 2
                ]
                total = sum(chosen[1:], chosen[0])
                zero = jnp.zeros_like(total)
                r = a * 256 + g * 64
                wco[0, r : r + 64, :] = join(total, zero).astype(BF16)
                wco[1, r : r + 64, :] = join(zero, swap(total)).astype(BF16)

    def stacked(k):
        return lambda t, s: k * 9 + t * 3 + s

    fine_weights(stacked(0), w1f, w1b)
    fine_weights(stacked(1), w2f, w2b)
    fine_weights(lambda t, s: 45 + (t * 3 + s) * 2, wsf, wsb)
    up_weights()
    down_weights(stacked(2))
    coarse_weights(stacked(3), w3f, w3b)
    coarse_weights(stacked(4), w4f, w4b)

    for copies in x_halos:
        halo_wait(copies)
    norm_forward(0, stat_total(0), False)

    def first_layer(f, carry):
        total, square = carry
        x = xs[f].astype(F32)
        z = x * wide(0, ALPHA, f) + wide(0, BETA, f)
        h = z * logistic(z)
        h = jnp.where(block_mask(h.shape, 2), h, 0.0)
        put_e(e1, f, 0, h)
        out = dot_nt(window(e1, f, 1, rows + 2), w1f[...]).reshape(rows + 2, cols, 256)
        c1[f] = out
        own = out[1 : rows + 1]
        return put_row(total, f, full_sum(own)), put_row(square, f, full_sum(own * own))

    sums = lax.fori_loop(0, frames, first_layer, (zero_rows, zero_rows), unroll=4)
    stat_start(1, jnp.concatenate(sums, axis=0))

    for copies in g_halos:
        halo_wait(copies)

    def load_g(f, carry):
        g = gs[f].astype(F32)
        put_e(eg, f, 0, jnp.where(block_mask(g.shape, 2), g, 0.0))
        gsa[f] = dot_nn(window(eg, f, 1, rows + 2), wsb[...]).reshape(rows + 2, cols, 256)
        return carry

    lax.fori_loop(0, frames, load_g, 0, unroll=4)

    norm_forward(1, stat_total(1), False)

    def second_layer(f, carry):
        z = c1[f] * wide(1, ALPHA, f) + wide(1, BETA, f)
        h = z * logistic(z)
        h = jnp.where(block_mask(h.shape, 1), h, 0.0)
        edge = jnp.zeros((cols, 512), BF16)
        e2[f, 0] = edge
        e2[f, rows + 3] = edge
        put_e(e2, f, 1, h)
        out = dot_nt(window(e2, f, 1, rows + 2), w2f[...]).reshape(rows + 2, cols, 256)
        skip = out + xs[f, 1 : rows + 3].astype(F32)
        skip = jnp.where(block_mask(skip.shape, 1), skip, 0.0)
        put_e(esk, f, 1, skip)
        return carry

    lax.fori_loop(0, frames, second_layer, 0, unroll=4)

    def down_window(f):
        return jnp.concatenate(
            [esk[f, 1 : 1 + rows, :, 256:512], esk[f, 2 : 2 + rows]], axis=-1
        ).reshape(owned, 768)

    zero_coarse = jnp.zeros((half, 128), F32)
    pad_rows = [jnp.zeros((2 * frames - 2 * half, 128), F32)]

    def down_layer(hf, carry):
        total, square = carry
        d = dot_nt(down_window(hf), wdf[:, 0:768]) + dot_nt(
            down_window(hf + half), wdf[:, 768:1536]
        )
        d = d.reshape(rows, cols, 128)
        dv[hf, 1 : rows + 1] = d
        border(hout, 1, hf, d)
        return put_row(total, hf, coarse_sum(d)), put_row(square, hf, coarse_sum(d * d))

    sums = lax.fori_loop(0, half, down_layer, (zero_coarse, zero_coarse), unroll=4)
    stat_start(2, jnp.concatenate(list(sums) + pad_rows, axis=0))
    halo_start(d_halo)

    def coarse_gradient(hf, carry):
        g = dot_nn(window(eg, hf, 1, rows + 2), wco[0]) + dot_nn(
            window(eg, hf + half, 1, rows + 2), wco[1]
        )
        g = g.reshape(rows + 2, cols, 128)
        g = jnp.where(block_mask(g.shape, 1), g, 0.0).astype(BF16).astype(F32)
        gco[hf] = g
        put_ec(ecg, hf, g)
        back = dot_nn(coarse_window(ecg, hf), w4b[...]).reshape(rows, cols, 128)
        gh4[hf, 1 : rows + 1] = back
        border(hout, 0, hf, back)
        return carry

    lax.fori_loop(0, half, coarse_gradient, 0, unroll=4)
    halo_start(g_h4_halo)

    def put_half(index, value):
        slot, owner = index // 2 // nd, index // 2 % nd
        current = gt_ref[slot, owner].astype(F32)
        value = join(current, swap(value)) if index % 2 else join(value, current)
        gt_ref[slot, owner] = value.astype(BF16)

    gt_ref[...] = jnp.zeros(gt_ref.shape, BF16)

    def fine_kernel_grad(index, e, start, gradient, gradient_start):
        acc[0, :, 0:1024] = jnp.zeros((256, 1024), F32)

        def add(f, carry):
            g = own_pixels(gradient, f, gradient_start, rows)
            acc[0, :, 0:1024] += dot_tn(g, window(e, f, start, rows))
            return carry

        lax.fori_loop(0, frames, add, 0, unroll=4)
        for t in range(3):
            u = []
            for dq in range(2):
                parts = [
                    acc[0, (dr * 2 + dq) * 64 : (dr * 2 + dq) * 64 + 64, pl.ds((t + dr) * 256, 256)]
                    for dr in range(2)
                ]
                u.append(parts[0] + parts[1])
            near, far = [v[:, 0:128] for v in u], [v[:, 128:256] for v in u]
            put_half(index(t, 0), swap(far[0]) + near[1])
            put_half(index(t, 1), near[0] + swap(near[1]))
            put_half(index(t, 2), swap(near[0]) + far[1])

    def coarse_kernel_grad(index, ec, gradient):
        acc[0, 0:128, :] = jnp.zeros((128, 1152), F32)

        def add(hf, carry):
            g = gradient[hf, 1 : rows + 1, :, 128:256].reshape(owned, 128)
            acc[0, 0:128, :] += dot_tn(g, coarse_window(ec, hf))
            return carry

        lax.fori_loop(0, half, add, 0, unroll=4)
        for a in range(3):
            for j in range(3):
                lanes = pl.ds((a * 3 + j) * 128, 128)
                put_half(index(a, j), acc[0, 0:64, lanes] + swap(acc[0, 64:128, lanes]))

    def down_kernel_grad(index):
        acc[:, 0:128, 0:768] = jnp.zeros((2, 128, 768), F32)

        def add(hf, carry):
            g = ed[hf, 1 : rows + 1, :, 0:128].reshape(owned, 128)
            acc[0, 0:128, 0:768] += dot_tn(g, down_window(hf))
            acc[1, 0:128, 0:768] += dot_tn(g, down_window(hf + half))
            return carry

        lax.fori_loop(0, half, add, 0, unroll=4)
        for a in range(3):
            near = acc[0, 0:64, pl.ds(a * 256, 128)] + acc[1, 64:128, pl.ds(a * 256, 128)]
            far = (
                acc[0, 0:64, pl.ds(a * 256 + 128, 128)] + acc[1, 64:128, pl.ds(a * 256 + 128, 128)]
            )
            put_half(index(a, 0), swap(far))
            put_half(index(a, 1), near)
            put_half(index(a, 2), swap(near))

    def up_kernel_grad():
        acc[...] = jnp.zeros(acc.shape, F32)

        def add(hf, carry):
            v = coarse_window(ecy, hf)
            acc[0] += dot_tn(own_pixels(eg, hf, 2, rows), v)
            acc[1] += dot_tn(own_pixels(eg, hf + half, 2, rows), v)
            return carry

        lax.fori_loop(0, half, add, 0, unroll=4)

        def block(dr, dq, i, j):
            r = (dr * 2 + dq) * 64
            lanes = pl.ds((i * 3 + j) * 128, 128)
            return acc[0, r : r + 64, lanes] + swap(acc[1, r : r + 64, lanes])

        place = {(0, 0): 0, (0, 1): 1, (0, 2): 1, (1, 0): 1, (1, 1): 1, (1, 2): 2}
        for ta in range(3):
            for tb in range(3):
                total = sum(
                    block(dr, dq, place[dr, ta], place[dq, tb])
                    for dr in range(2)
                    for dq in range(2)
                )
                put_half(45 + (ta * 3 + tb) * 2 + 1, total)


    halo_wait(d_halo)
    norm_forward(2, stat_total(2), True)

    def third_layer(hf, carry):
        total, square = carry
        with_halo(dv, hf, 1)
        z = dv[hf] * param(2, ALPHA, hf) + param(2, BETA, hf)
        h = z * logistic(z)
        put_ec(ec3, hf, jnp.where(block_mask(h.shape, 1), h, 0.0))
        out = dot_nt(coarse_window(ec3, hf), w3f[...]).reshape(rows, cols, 128)
        c3[hf, 1 : rows + 1] = out
        border(hout, 2, hf, out)
        return put_row(total, hf, coarse_sum(out)), put_row(square, hf, coarse_sum(out * out))

    sums = lax.fori_loop(0, half, third_layer, (zero_coarse, zero_coarse), unroll=4)
    stat_start(3, jnp.concatenate(list(sums) + pad_rows, axis=0))
    halo_start(c3_halo)
    fine_kernel_grad(lambda t, s: 45 + (t * 3 + s) * 2, esk, 2, eg, 2)

    halo_wait(c3_halo)
    halo_wait(g_h4_halo)
    norm_forward(3, stat_total(3), True)

    def fourth_layer(hf, carry):
        shift, scale = carry
        with_halo(c3, hf, 2)
        with_halo(gh4, hf, 0)
        v = c3[hf]
        z = v * param(3, ALPHA, hf) + param(3, BETA, hf)
        gate = logistic(z)
        h = z * gate
        put_ec(ec4, hf, jnp.where(block_mask(h.shape, 1), h, 0.0))
        g = gh4[hf] * (gate + h * (1.0 - gate))
        gzc[hf] = g
        own = g[1 : rows + 1]
        xhat = v[1 : rows + 1] * param(3, RSTD, hf) + param(3, NMR, hf)
        return put_row(shift, hf, coarse_sum(own)), put_row(scale, hf, coarse_sum(own * xhat))

    sums = lax.fori_loop(0, half, fourth_layer, (zero_coarse, zero_coarse), unroll=4)
    stat_start(4, jnp.concatenate(list(sums) + pad_rows, axis=0))

    def coarse_output(hf, carry):
        out = dot_nt(coarse_window(ec4, hf), w4f[...]).reshape(rows, cols, 128)
        y = dv[hf, 1 : rows + 1] + out
        border(hout, 3, hf, y)
        edge = jnp.zeros((1, cols, 128), F32)
        put_ec(ecy, hf, jnp.concatenate([edge, y, edge], axis=0))
        return carry

    lax.fori_loop(0, half, coarse_output, 0, unroll=4)
    halo_start(y_halo)
    coarse_kernel_grad(stacked(4), ec4, ecg)

    norm_backward(3, stat_total(4), True)

    def third_back(hf, carry):
        shift, scale = carry
        g = (
            gzc[hf] * param(3, ALPHA, hf)
            + c3[hf] * param(3, COEF, hf)
            + param(3, BIAS, hf)
        )
        put_ec(ecg3, hf, jnp.where(block_mask(g.shape, 1), g, 0.0))
        back = dot_nn(coarse_window(ecg3, hf), w3b[...]).reshape(rows, cols, 128)
        border(hout, 4, hf, back)
        v = dv[hf, 1 : rows + 1]
        z = v * param(2, ALPHA, hf) + param(2, BETA, hf)
        gate = logistic(z)
        own = back * (gate + z * gate * (1.0 - gate))
        gzc[hf, 1 : rows + 1] = own
        xhat = v * param(2, RSTD, hf) + param(2, NMR, hf)
        return put_row(shift, hf, coarse_sum(own)), put_row(scale, hf, coarse_sum(own * xhat))

    sums = lax.fori_loop(0, half, third_back, (zero_coarse, zero_coarse), unroll=4)
    stat_start(5, jnp.concatenate(list(sums) + pad_rows, axis=0))
    halo_start(g_h3_halo)

    halo_wait(y_halo)

    def result_copy(f):
        return pltpu.make_async_copy(gz.at[f, pl.ds(1, rows)], io_hbm.at[f], out_sem.at[f])

    def merge(hf, carry):
        for side, row in ((0, 0), (1, rows + 1)):
            line = hal[3, side, hf].astype(F32)[None]
            up, down = neighbours(line)
            q = lax.broadcasted_iota(jnp.int32, line.shape, 1)
            ecy[hf, row, :, 0:128] = jnp.where(q == 0, 0.0, down)[0].astype(BF16)
            ecy[hf, row, :, 128:256] = line[0].astype(BF16)
            ecy[hf, row, :, 256:384] = jnp.where(q == cols - 1, 0.0, up)[0].astype(BF16)
        both = dot_nt(coarse_window(ecy, hf), wup[...])
        for hi in range(2):
            f = hf + hi * half
            out = dot_nt(window(esk, f, 2, rows), wsf[...]) + both[:, hi * 256 : hi * 256 + 256]
            gz[f, 1 : rows + 1] = out.reshape(rows, cols, 256)
            result_copy(f).start()
        return carry

    lax.fori_loop(0, half, merge, 0, unroll=4)
    coarse_kernel_grad(stacked(3), ec3, ecg3)
    up_kernel_grad()
    gather_start(0)

    halo_wait(g_h3_halo)
    norm_backward(2, stat_total(5), True)

    def down_back(hf, carry):
        for side, row in ((0, 0), (1, rows + 1)):
            v = dv[hf, row]
            z = v * param(2, ALPHA, hf) + param(2, BETA, hf)
            gate = logistic(z)
            gzc[hf, row] = hal[4, side, hf].astype(F32) * (gate + z * gate * (1.0 - gate))
        g = (
            gco[hf]
            + gzc[hf] * param(2, ALPHA, hf)
            + dv[hf] * param(2, COEF, hf)
            + param(2, BIAS, hf)
        )
        g = jnp.where(block_mask(g.shape, 1), g, 0.0)
        up, _ = neighbours(g)
        q = lax.broadcasted_iota(jnp.int32, g.shape, 1)
        ed[hf, 0 : rows + 2, :, 0:128] = g.astype(BF16)
        ed[hf, 0 : rows + 2, :, 128:256] = jnp.where(q == cols - 1, 0.0, up).astype(BF16)
        ed[hf, rows + 2] = jnp.zeros((cols, 256), BF16)
        lhs = jnp.concatenate([ed[hf, 0 : rows + 2], ed[hf, 1 : rows + 3]], axis=-1)
        back = dot_nn(lhs.reshape(ext, 512), wdb[...])
        back = back.astype(BF16).astype(F32).reshape(rows + 2, cols, 512)
        for hi in range(2):
            f = hf + hi * half
            total = gsa[f] + back[:, :, hi * 256 : hi * 256 + 256]
            gsa[f] = total
            put_e(eg, f, 0, jnp.where(block_mask(total.shape, 1), total, 0.0))
        return carry

    lax.fori_loop(0, half, down_back, 0, unroll=4)

    def second_back(f, carry):
        shift, scale = carry
        back = dot_nn(window(eg, f, 1, rows), w2b[...]).reshape(rows, cols, 256)
        hfout[0, f] = back[0, :, 0:128].astype(BF16)
        hfout[1, f] = back[rows - 1, :, 128:256].astype(BF16)
        v = c1[f, 1 : rows + 1]
        z = v * wide(1, ALPHA, f) + wide(1, BETA, f)
        gate = logistic(z)
        own = back * (gate + z * gate * (1.0 - gate))
        gz[f, 1 : rows + 1] = own
        xhat = v * wide(1, RSTD, f) + wide(1, NMR, f)
        return put_row(shift, f, full_sum(own)), put_row(scale, f, full_sum(own * xhat))

    for f in range(frames):
        result_copy(f).wait()
    sums = lax.fori_loop(0, frames, second_back, (zero_rows, zero_rows), unroll=4)
    stat_start(6, jnp.concatenate(sums, axis=0))
    halo_start(g_h2_halo)
    down_kernel_grad(stacked(2))
    fine_kernel_grad(stacked(1), e2, 2, eg, 1)
    gather_start(1)
    gather_space(0)
    halo_wait(g_h2_halo)
    norm_backward(1, stat_total(6), False)

    def first_back(f, carry):
        shift, scale = carry
        for side, row in ((0, 0), (1, rows + 1)):
            v = c1[f, row]
            lanes = slice(128, 256) if side == 0 else slice(0, 128)
            z = v[:, lanes] * param(1, ALPHA, f) + param(1, BETA, f)
            gate = logistic(z)
            g = hfull[side, f].astype(F32) * (gate + z * gate * (1.0 - gate))
            blank = jnp.zeros_like(g)
            gz[f, row] = jnp.concatenate([blank, g] if side == 0 else [g, blank], axis=-1)
        g = gz[f] * wide(1, ALPHA, f) + c1[f] * wide(1, COEF, f) + wide(1, BIAS, f)
        put_e(eg, f, 0, jnp.where(block_mask(g.shape, 1), g, 0.0))
        back = dot_nn(window(eg, f, 1, rows), w1b[...]).reshape(rows, cols, 256)
        v = xs[f, 2 : rows + 2].astype(F32)
        z = v * wide(0, ALPHA, f) + wide(0, BETA, f)
        gate = logistic(z)
        own = back * (gate + z * gate * (1.0 - gate))
        gz[f, 1 : rows + 1] = own
        xhat = v * wide(0, RSTD, f) + wide(0, NMR, f)
        return put_row(shift, f, full_sum(own)), put_row(scale, f, full_sum(own * xhat))

    pack_start(0)
    sums = lax.fori_loop(0, frames, first_back, (zero_rows, zero_rows), unroll=4)
    stat_start(7, jnp.concatenate(sums, axis=0))
    gather_spread(0)
    gather_space(1)
    fine_kernel_grad(stacked(0), e1, 2, eg, 1)
    gather_start(2)
    norm_backward(0, stat_total(7), False)
    pack_start(1)
    gather_all(0)
    gather_spread(1)
    gather_space(2)

    def frames_copy(f):
        return pltpu.make_async_copy(
            gz.at[f, pl.ds(1, rows)], io_hbm.at[frames + f], fg_sem.at[f]
        )

    def frames_back(f, carry):
        gz[f, 1 : rows + 1] = (
            gsa[f, 1 : rows + 1]
            + gz[f, 1 : rows + 1] * wide(0, ALPHA, f)
            + xs[f, 2 : rows + 2].astype(F32) * wide(0, COEF, f)
            + wide(0, BIAS, f)
        )
        frames_copy(f).start()
        return carry

    lax.fori_loop(0, half, frames_back, 0, unroll=4)
    gather_all(1)
    gather_spread(2)
    lax.fori_loop(half, frames, frames_back, 0, unroll=4)
    gather_all(2)
    for off in range(1, nd):
        for which in range(2):
            pack_copy(which, off, dp_before(off)).wait_recv()
            pack_copy(which, off, dp).wait_send()
    total_frames = nd * frames
    every = packs[...].reshape(total_frames, 896)
    embedded, hot = every[:, 512:768], every[:, 768:896]
    g_embed = 0.0
    for k in range(4):
        dmod = every[:, k * 128 : (k + 1) * 128]
        acc[1, :, k * 128 : k * 128 + 128] = lax.dot_general(
            embedded, dmod, (((0,), (0,)), ((), ())), precision=HIGH, preferred_element_type=F32
        )
        lane = 512 + k % 2 * 128
        acc[1, 128 + k // 2 : 129 + k // 2, lane : lane + 128] = jnp.sum(
            dmod, axis=0, keepdims=True
        )
        g_embed = g_embed + lax.dot_general(
            dmod, nmv[k], (((1,), (1,)), ((), ())), precision=HIGH, preferred_element_type=F32
        )
    acc[1, 0:128, 512:768] = lax.dot_general(
        hot, g_embed, (((0,), (0,)), ((), ())), precision=HIGH, preferred_element_type=F32
    )

    def par_copy(e):
        return pltpu.make_async_copy(
            acc.at[e // 4, :, pl.ds(e % 4 * 256, 256)], par_hbm.at[e], local_sem.at[e]
        )

    for e in range(4, 7):
        par_copy(e).start()
    for stage in range(3):
        gather_finish(stage)
    for tile in range(32):
        row, lane = tile // 2 % 4 * 64, tile // 8 * 256 + tile % 2 * 128
        acc[0, row : row + 64, lane : lane + 128] = gall[tile % nd, tile // nd].astype(F32)
    for e in range(4):
        par_copy(e).start()

    for e in range(7):
        par_copy(e).wait()
    for f in range(frames):
        frames_copy(f).wait()
    for copies in (*x_halos, *g_halos, g_h4_halo, d_halo, c3_halo, y_halo, g_h3_halo, g_h2_halo):
        halo_finish(copies)


def run_step(nd, n, frames, cotangent, actions, noise_ids, games, live_counts, cw, nm, table):
    count, strip, breadth, _ = frames.shape
    half, rows, cols = count // 2, strip // 2, breadth // 2
    fine = (count, rows + 4, cols, 512)
    coarse = (half, rows + 2, cols, 128)
    coarse_e = (half, rows + 2, cols, 384)
    scratch = [
        VM((count, strip, breadth, 64), BF16),
        VM((strip, breadth, 128), F32),
        VM((count, rows + 4, cols, 256), BF16),
        VM((count, rows + 4, cols, 256), BF16),
        VM(fine, BF16),
        VM(fine, BF16),
        VM(fine, BF16),
        VM(fine, BF16),
        VM((count, rows + 2, cols, 256), F32),
        VM((count, rows + 2, cols, 256), F32),
        VM((count, rows + 2, cols, 256), F32),
        VM(coarse, F32),
        VM(coarse, F32),
        VM(coarse, F32),
        VM(coarse, F32),
        VM(coarse, F32),
        VM(coarse_e, BF16),
        VM(coarse_e, BF16),
        VM(coarse_e, BF16),
        VM(coarse_e, BF16),
        VM(coarse_e, BF16),
        VM((half, rows + 3, cols, 256), BF16),
        VM((256, 1024), BF16),
        VM((1024, 256), BF16),
        VM((256, 1024), BF16),
        VM((1024, 256), BF16),
        VM((256, 1024), BF16),
        VM((1024, 256), BF16),
        VM((512, 1152), BF16),
        VM((2, 1024, 128), BF16),
        VM((128, 1536), BF16),
        VM((512, 512), BF16),
        VM((128, 1152), BF16),
        VM((1152, 128), BF16),
        VM((128, 1152), BF16),
        VM((1152, 128), BF16),
        VM((2, 256, 1152), F32),
        VM((32, count, 128), F32),
        VM((128, 256), F32),
        VM((8, n, 2 * count, 128), F32),
        VM((5, 2, half, cols, 128), BF16),
        VM((5, 2, half, cols, 128), BF16),
        VM((2, count, cols, 128), BF16),
        VM((2, count, cols, 128), BF16),
        VM((4, 256, 128), F32),
        VM((4, 128), F32),
        VM((32 // nd, nd, 64, 128), BF16),
        VM((nd, 32 // nd, 64, 128), BF16),
        VM((n, 32 // nd, 64 // n, 128), F32),
        VM((n, 32 // nd, 64 // n, 128), F32),
        VM((n, 32 // nd, 64 // n, 128), F32),
        VM((nd, 32 // nd, 64, 128), BF16),
        VM((nd, count, 896), F32),
        pltpu.SemaphoreType.DMA((7,)),
        pltpu.SemaphoreType.DMA((count,)),
        pltpu.SemaphoreType.DMA((count,)),
        pltpu.SemaphoreType.DMA((8, n - 1)),
        pltpu.SemaphoreType.DMA((8, n - 1)),
        pltpu.SemaphoreType.DMA((10, 2)),
        pltpu.SemaphoreType.DMA((10, 2)),
        pltpu.SemaphoreType.DMA((4, 2, nd - 1)),
        pltpu.SemaphoreType.DMA((4, 2, nd - 1)),
        pltpu.SemaphoreType.DMA((3, 2, n - 1)),
        pltpu.SemaphoreType.DMA((3, 2, n - 1)),
    ]
    smem = pl.BlockSpec(memory_space=pltpu.SMEM)
    vmem = pl.BlockSpec(memory_space=pltpu.VMEM)
    hbm = pl.BlockSpec(memory_space=pltpu.HBM)
    return pl.pallas_call(
        functools.partial(step_kernel, nd, n),
        out_shape=(
            jax.ShapeDtypeStruct((2 * count, rows, cols, 256), F32),
            jax.ShapeDtypeStruct((7, 256, 256), F32),
        ),
        in_specs=[hbm, hbm, smem, smem, smem, smem, vmem, hbm, vmem],
        out_specs=(hbm, hbm),
        scratch_shapes=scratch,
        compiler_params=pltpu.CompilerParams(
            collective_id=0, has_side_effects=True, vmem_limit_bytes=55 * 1024 * 1024
        ),
        name="step",
    )(frames, cotangent, actions, noise_ids, games, live_counts, cw, nm, table)


def adamw(weight, moment, square, grad_value, rate):
    fix_one = 1.0 - BETA_ONE**ADAM_STEP
    fix_two = 1.0 - BETA_TWO**ADAM_STEP
    moment_new = BETA_ONE * moment + (1.0 - BETA_ONE) * grad_value
    square_new = BETA_TWO * square + (1.0 - BETA_TWO) * grad_value * grad_value
    fixed_m = moment_new / fix_one
    fixed_v = square_new / fix_two
    weight_new = weight - rate * (fixed_m / (jnp.sqrt(fixed_v) + ADAM_EPS) + DECAY * weight)
    return (moment_new, square_new, weight_new, weight_new.astype(BF16))


def finish_kernel(
    io_hbm,
    par_hbm,
    cw,
    cm,
    cv,
    nm,
    nmo,
    nsq,
    tab,
    tmo,
    tsq,
    res_out,
    fg_out,
    *refs,
):
    outs, refs = refs[:12], refs[12:]
    stages, refs = refs[:12], refs[12:]
    io, par, tmp, rs, fs, gmap, in_sem, pin_sem, fg_sem, out_sem, par_sem = refs
    frames, rows, cols = rs.shape[0], io.shape[1], io.shape[2]

    def frame_in(f):
        return pltpu.make_async_copy(io_hbm.at[f], io.at[f], in_sem.at[f])

    def par_in(e):
        return pltpu.make_async_copy(par_hbm.at[e], par.at[e], pin_sem.at[e])

    for e in range(7):
        par_in(e).start()
    for f in range(2 * frames):
        frame_in((f + frames) % (2 * frames)).start()
    out_copies = [
        pltpu.make_async_copy(stages[i], outs[i], par_sem.at[i]) for i in range(12)
    ]

    def update(first, at, weight, moment, square, grad, rate):
        new = adamw(weight, moment, square, grad, rate)
        for i in range(4):
            stages[first + i][at] = new[i]

    wide = cw.shape[1]
    for c in range(16):
        if c % 4 == 0:
            par_in(c // 4).wait()
        lanes = slice(c * 256, min(c * 256 + 256, wide))
        at = (slice(None), lanes)
        grad = par[c // 4, c % 4 * 64 : c % 4 * 64 + 64, 0 : lanes.stop - lanes.start]
        update(0, at, cw[at], cm[at], cv[at], grad, 0.05)
    for i in range(4):
        out_copies[i].start()

    def unpair(v):
        both = jnp.stack([v[:, :, 0:128], v[:, :, 128:256]], axis=1).reshape(rows * 2, cols, 128)
        tmp[:, pl.ds(0, cols, stride=2), :] = both
        tmp[:, pl.ds(1, cols, stride=2), :] = swap(both)
        return tmp[:, :, 0:64]

    def frame_copies(f):
        return (
            pltpu.make_async_copy(fs.at[f], fg_out.at[f], fg_sem.at[f]),
            pltpu.make_async_copy(rs.at[f], res_out.at[f], out_sem.at[f]),
        )

    def put_frames(f, carry):
        frame_in(frames + f).wait()
        fs[f] = unpair(io[frames + f])
        frame_copies(f)[0].start()
        return carry

    lax.fori_loop(0, frames, put_frames, 0)

    def put_result(f, carry):
        frame_in(f).wait()
        rs[f] = unpair(io[f]).astype(BF16)
        frame_copies(f)[1].start()
        return carry

    lax.fori_loop(0, frames, put_result, 0)

    for e in range(4, 7):
        par_in(e).wait()
    for k in range(4):
        lane = k % 2 * 128
        gmap[0:256, k, :] = par[4 + k // 2, :, lane : lane + 128]
        gmap[256, k : k + 1, :] = par[6, 128 + k // 2 : 129 + k // 2, lane : lane + 128]
    at = slice(None)
    update(4, at, nm[...], nmo[...], nsq[...], gmap[...], 0.04)
    for i in range(4, 8):
        out_copies[i].start()
    update(8, at, tab[...], tmo[...], tsq[...], par[6, 0 : tab.shape[0]], 0.5)
    for i in range(8, 12):
        out_copies[i].start()
    for f in range(frames):
        for copy in frame_copies(f):
            copy.wait()
    for copy in out_copies:
        copy.wait()


def run_finish(shape, io, par, conv, norm, table):
    count, strip, breadth, _ = shape
    hbm = pl.BlockSpec(memory_space=pl.ANY)
    vmem = pl.BlockSpec(memory_space=pltpu.VMEM)
    params = [
        jax.ShapeDtypeStruct(v[0].shape, dtype)
        for v in (conv, norm, table)
        for dtype in (F32, F32, F32, BF16)
    ]
    return pl.pallas_call(
        finish_kernel,
        out_shape=(
            jax.ShapeDtypeStruct(shape, BF16),
            jax.ShapeDtypeStruct(shape, F32),
            *params,
        ),
        in_specs=[hbm, hbm] + [vmem] * 9,
        out_specs=(hbm,) * 14,
        scratch_shapes=[VM(v.shape, v.dtype) for v in params]
        + [
            VM(io.shape, F32),
            VM(par.shape, F32),
            VM((strip, breadth, 128), F32),
            VM(shape, BF16),
            VM(shape, F32),
            VM(norm[0].shape, F32),
            pltpu.SemaphoreType.DMA((2 * count,)),
            pltpu.SemaphoreType.DMA((7,)),
            pltpu.SemaphoreType.DMA((count,)),
            pltpu.SemaphoreType.DMA((count,)),
            pltpu.SemaphoreType.DMA((12,)),
        ],
        compiler_params=pltpu.CompilerParams(vmem_limit_bytes=48 * 1024 * 1024),
        name="finish",
    )(io, par, *conv, *norm, *table)


def local(
    nd,
    ns,
    frames,
    cotangent,
    actions,
    noise_ids,
    games,
    live_counts,
    conv_weight,
    conv_moment,
    conv_square,
    norm_map,
    norm_moment,
    norm_square,
    emb_table,
    table_moment,
    table_square,
):
    conv = [v.T for v in (conv_weight, conv_moment, conv_square)]
    norm = [jnp.transpose(v, (1, 0, 2)) for v in (norm_map, norm_moment, norm_square)]
    table = (emb_table, table_moment, table_square)
    io, par = run_step(
        nd,
        ns,
        frames,
        cotangent,
        actions,
        noise_ids,
        games,
        live_counts,
        conv[0],
        norm[0],
        emb_table,
    )
    result, frames_grad, *new = run_finish(
        frames.shape, io, par, conv, norm, table
    )
    conv_out = [v.T for v in new[0:4]]
    norm_out = [jnp.transpose(v, (1, 0, 2)) for v in new[4:8]]
    return (result, frames_grad, *conv_out, *norm_out, *new[8:12])


def solution(mesh):
    split = P("dp", "space", None, None)
    in_specs = (split, split) + (P("dp"),) * 4 + (P(),) * 9
    out_specs = (split, split) + (P(),) * 12
    sizes = dict(mesh.shape)
    return jax.shard_map(
        functools.partial(local, sizes["dp"], sizes["space"]),
        mesh=mesh,
        in_specs=in_specs,
        out_specs=out_specs,
        check_vma=False,
    )
```

```python
import functools

import jax
import jax.numpy as jnp
from jax import lax
from jax.experimental import pallas as pl
from jax.experimental.pallas import tpu as pltpu
from jax.sharding import PartitionSpec as P

ACTIONS = 18
NOISE_LEVELS = 64
ADAM_STEP = 4
NORM_EPSILON = 1e-05
ADAM_EPS = 1e-08
BETA_ONE = 0.5
BETA_TWO = 0.5
DECAY = 0.01
HIGH = lax.Precision.HIGHEST
F32 = jnp.float32
BF16 = jnp.bfloat16
MESH = pl.DeviceIdType.MESH
VM = pltpu.VMEM

ALPHA, BETA, RSTD, NMR, GAIN, SHIFT, COEF, BIAS = range(8)


def dot_nn(a, b):
    return lax.dot_general(a, b, (((1,), (0,)), ((), ())), preferred_element_type=F32)


def dot_nt(a, b):
    return lax.dot_general(a, b, (((1,), (1,)), ((), ())), preferred_element_type=F32)


def dot_tn(a, b):
    return lax.dot_general(a, b, (((0,), (0,)), ((), ())), preferred_element_type=F32)


def dot_high(a, b):
    return lax.dot_general(
        a, b, (((1,), (0,)), ((), ())), precision=HIGH, preferred_element_type=F32
    )


def logistic(z):
    return 0.5 * jnp.tanh(0.5 * z) + 0.5


def lane_iota(shape):
    return lax.broadcasted_iota(jnp.int32, shape, len(shape) - 1)


def swap(v):
    return pltpu.roll(v, 64, len(v.shape) - 1)


def join(lo, hi):
    return jnp.where(lane_iota(lo.shape) < 64, lo, hi)


def twice(row):
    return jnp.concatenate([row, row], axis=-1)


def step_kernel(
    nd,
    n,
    x_hbm,
    cot_hbm,
    act_ref,
    noise_ref,
    game_ref,
    live_ref,
    cw_ref,
    nm_hbm,
    tab_ref,
    io_hbm,
    par_hbm,
    raw,
    tmp,
    xs,
    gs,
    e1,
    e2,
    esk,
    eg,
    c1,
    gsa,
    gz,
    dv,
    c3,
    gh4,
    gzc,
    gco,
    ec3,
    ec4,
    ecg,
    ecg3,
    ecy,
    ed,
    w1f,
    w1b,
    w2f,
    w2b,
    wsf,
    wsb,
    wup,
    wco,
    wdf,
    wdb,
    w3f,
    w3b,
    w4f,
    w4b,
    acc,
    prm,
    tabp,
    stat,
    hal,
    hout,
    hfull,
    hfout,
    nmv,
    nmb,
    gt_ref,
    rbuf,
    part,
    zbuf,
    zfull,
    zwhole,
    gall,
    packs,
    local_sem,
    out_sem,
    fg_sem,
    stat_send,
    stat_recv,
    halo_send,
    halo_recv,
    dp_send,
    dp_recv,
    sp_send,
    sp_recv,
):
    frames, strip = raw.shape[0], raw.shape[1]
    breadth = raw.shape[2]
    half = frames // 2
    rows = strip // 2
    cols = breadth // 2
    me = lax.axis_index("space")
    dp = lax.axis_index("dp")
    full_cells = float(strip * n * breadth * 32)
    coarse_cells = full_cells / 4.0
    owned = rows * cols
    ext = (rows + 2) * cols

    x_copy = pltpu.make_async_copy(x_hbm, raw, local_sem.at[0])
    x_copy.start()
    g_copy = pltpu.make_async_copy(cot_hbm, raw, local_sem.at[1])
    map_copies = [
        pltpu.make_async_copy(nm_hbm.at[pl.ds(0, 256), k], nmv.at[k], local_sem.at[2 + k])
        for k in range(4)
    ]
    map_copies.append(pltpu.make_async_copy(nm_hbm.at[256], nmb, local_sem.at[6]))
    for copy in map_copies:
        copy.start()

    barrier = pltpu.get_barrier_semaphore()
    for off in range(1, n):
        pl.semaphore_signal(
            barrier,
            inc=1,
            device_id={"space": lax.rem(me + off, n)},
            device_id_type=MESH,
        )
    for off in range(1, nd):
        pl.semaphore_signal(
            barrier,
            inc=1,
            device_id={"dp": lax.rem(dp + off, nd)},
            device_id_type=MESH,
        )

    def halo_copies(k, first, last, to_up, to_down):
        up = pltpu.make_async_remote_copy(
            src_ref=first,
            dst_ref=to_up,
            send_sem=halo_send.at[k, 0],
            recv_sem=halo_recv.at[k, 0],
            device_id={"space": lax.rem(me + n - 1, n)},
            device_id_type=MESH,
        )
        down = pltpu.make_async_remote_copy(
            src_ref=last,
            dst_ref=to_down,
            send_sem=halo_send.at[k, 1],
            recv_sem=halo_recv.at[k, 1],
            device_id={"space": lax.rem(me + 1, n)},
            device_id_type=MESH,
        )
        return up, down

    def halo_start(copies):
        @pl.when(me > 0)
        def _():
            copies[0].start()

        @pl.when(me < n - 1)
        def _():
            copies[1].start()

    def halo_wait(copies):
        @pl.when(me < n - 1)
        def _():
            copies[0].wait_recv()

        @pl.when(me > 0)
        def _():
            copies[1].wait_recv()

    def halo_finish(copies):
        @pl.when(me > 0)
        def _():
            copies[0].wait_send()

        @pl.when(me < n - 1)
        def _():
            copies[1].wait_send()

    def stat_copy(k, off, slots):
        return pltpu.make_async_remote_copy(
            src_ref=stat.at[k, slots],
            dst_ref=stat.at[k, slots],
            send_sem=stat_send.at[k],
            recv_sem=stat_recv.at[k],
            device_id={"space": lax.rem(me + off, n)},
            device_id_type=MESH,
        )

    def stat_start(k, value):
        stat[k, me] = value
        for off in range(1, n):
            stat_copy(k, off, me).start()

    def stat_total(k):
        peers = stat_copy(k, 1, pl.ds(0, n - 1))
        peers.wait_recv()
        total = stat[k, 0]
        for i in range(1, n):
            total = total + stat[k, i]
        peers.wait_send()
        return total

    def wide_halos(k, v):
        both = halo_copies(
            k, v.at[:, 2], v.at[:, rows + 1], v.at[:, rows + 2], v.at[:, 1]
        )
        third = halo_copies(
            k + 1,
            v.at[:, 3, :, pl.ds(0, 128)],
            v.at[:, rows, :, pl.ds(128, 128)],
            v.at[:, rows + 3, :, pl.ds(0, 128)],
            v.at[:, 0, :, pl.ds(128, 128)],
        )
        return both, third

    x_halos = wide_halos(0, xs)
    g_halos = wide_halos(8, gs)

    def coarse_halo(k):
        return halo_copies(
            k, hout.at[k - 2, 0], hout.at[k - 2, 1], hal.at[k - 2, 1], hal.at[k - 2, 0]
        )

    g_h4_halo, d_halo, c3_halo, y_halo, g_h3_halo = [coarse_halo(k) for k in range(2, 7)]
    g_h2_halo = halo_copies(7, hfout.at[0], hfout.at[1], hfull.at[1], hfull.at[0])

    def block_mask(shape, pad):
        blocks = shape[0]
        b = lax.broadcasted_iota(jnp.int32, shape, 0)
        low = jnp.where(me > 0, 0, pad)
        high = jnp.where(me < n - 1, blocks, blocks - pad)
        return (b >= low) & (b < high)

    def param(k, which, f):
        return prm[k * 8 + which, pl.ds(f, 1), :]

    def wide(k, which, f):
        return twice(param(k, which, f))

    def put_row(carry, f, value):
        row = lax.broadcasted_iota(jnp.int32, carry.shape, 0)
        return jnp.where(row == f, value, carry)

    def full_sum(v):
        s = jnp.sum(v.reshape(-1, 256), axis=0, keepdims=True)
        return s[:, :128] + s[:, 128:]

    def paired(raw_rows):
        count = raw_rows.shape[0]
        tmp[0:count, :, 0:64] = raw_rows.astype(F32)
        even = tmp[0:count, pl.ds(0, cols, stride=2), :]
        odd = tmp[0:count, pl.ds(1, cols, stride=2), :]
        return join(even, swap(odd))

    def pair_halves(p):
        count = p.shape[0] // 2
        p = p.reshape(count, 2, cols, 128)
        return p[:, 0], p[:, 1]

    def neighbours(v):
        count = v.shape[0]
        flat = v.reshape(count * cols, 128)
        up = pltpu.roll(flat, count * cols - 1, 0).reshape(v.shape)
        down = pltpu.roll(flat, 1, 0).reshape(v.shape)
        return up, down

    def put_e(e, f, start, h):
        count = h.shape[0]
        for part in range(2):
            v = h[:, :, part * 128 : (part + 1) * 128]
            up, down = neighbours(v)
            lane = lane_iota(v.shape)
            q = lax.broadcasted_iota(jnp.int32, v.shape, 1)
            near = jnp.where(
                lane < 64, jnp.where(q == cols - 1, 0.0, up), jnp.where(q == 0, 0.0, down)
            )
            e[f, start : start + count, :, part * 256 : part * 256 + 128] = v.astype(BF16)
            e[f, start : start + count, :, part * 256 + 128 : part * 256 + 256] = near.astype(BF16)

    def window(e, f, start, count):
        return jnp.concatenate(
            [
                e[f, start - 1 : start - 1 + count, :, 256:512],
                e[f, start : start + count, :, :],
                e[f, start + 1 : start + 1 + count, :, 0:256],
            ],
            axis=-1,
        ).reshape(count * cols, 1024)

    def own_pixels(e, f, start, count):
        return jnp.concatenate(
            [
                e[f, start : start + count, :, 0:128],
                e[f, start : start + count, :, 256:384],
            ],
            axis=-1,
        ).reshape(count * cols, 256)

    def put_ec(ec, hf, v):
        up, down = neighbours(v)
        q = lax.broadcasted_iota(jnp.int32, v.shape, 1)
        ec[hf, :, :, 0:128] = jnp.where(q == 0, 0.0, down).astype(BF16)
        ec[hf, :, :, 128:256] = v.astype(BF16)
        ec[hf, :, :, 256:384] = jnp.where(q == cols - 1, 0.0, up).astype(BF16)

    def coarse_window(ec, hf):
        return jnp.concatenate([ec[hf, a : a + rows] for a in range(3)], axis=-1).reshape(
            owned, 1152
        )

    def coarse_sum(v):
        return jnp.sum(v.reshape(-1, 128), axis=0, keepdims=True)

    def with_halo(ref, hf, k):
        ref[hf, 0] = hal[k, 0, hf].astype(F32)
        ref[hf, rows + 1] = hal[k, 1, hf].astype(F32)

    def border(ref_out, k, hf, v):
        ref_out[k, 0, hf] = v[0].astype(BF16)
        ref_out[k, 1, hf] = v[rows - 1].astype(BF16)

    def group_matrix(coarse):
        r = lax.broadcasted_iota(jnp.int32, (128, 128), 0) // 32
        c = lax.broadcasted_iota(jnp.int32, (128, 128), 1) // 32
        same = (r == c) if coarse else (r % 2 == c % 2)
        return jnp.where(same, 1.0, 0.0)

    def norm_forward(k, total, coarse):
        cells = coarse_cells if coarse else full_cells
        count = half if coarse else frames
        moments = dot_high(total, group_matrix(coarse)) / cells
        mean = moments[0:count]
        var = moments[count : 2 * count] - mean * mean
        rstd = lax.rsqrt(var + NORM_EPSILON)
        gain = prm[k * 8 + GAIN, 0:count, :]
        alpha = rstd * gain
        prm[k * 8 + ALPHA, 0:count, :] = alpha
        prm[k * 8 + BETA, 0:count, :] = prm[k * 8 + SHIFT, 0:count, :] - mean * alpha
        prm[k * 8 + RSTD, 0:count, :] = rstd
        prm[k * 8 + NMR, 0:count, :] = -mean * rstd

    def norm_backward(k, total, coarse):
        cells = coarse_cells if coarse else full_cells
        count = half if coarse else frames
        gain = prm[k * 8 + GAIN, 0:count, :]
        shift_grad = total[0:count]
        scale_grad = total[count : 2 * count]
        means = (
            dot_high(
                jnp.concatenate([shift_grad * gain, scale_grad * gain], axis=0),
                group_matrix(coarse),
            )
            / cells
        )
        rstd = prm[k * 8 + RSTD, 0:count, :]
        factor = -rstd * means[count : 2 * count]
        prm[k * 8 + COEF, 0:count, :] = rstd * factor
        prm[k * 8 + BIAS, 0:count, :] = (
            prm[k * 8 + NMR, 0:count, :] * factor - rstd * means[0:count]
        )
        if coarse:
            scale_all = jnp.concatenate([scale_grad, swap(scale_grad)], axis=0)
            shift_all = jnp.concatenate([shift_grad, swap(shift_grad)], axis=0)
        else:
            scale_all = scale_grad + swap(scale_grad)
            shift_all = shift_grad + swap(shift_grad)
        packs[dp, :, k * 128 : (k + 1) * 128] = join(scale_all, swap(shift_all))

    slots = 32 // nd
    share = 64 // n
    stage_slots = [pl.ds(1, slots - 1), pl.ds(0, 1)]

    def dp_copy(which, src, dst, off):
        return pltpu.make_async_remote_copy(
            src_ref=src,
            dst_ref=dst,
            send_sem=dp_send.at[which],
            recv_sem=dp_recv.at[which],
            device_id={"dp": lax.rem(dp + off, nd)},
            device_id_type=MESH,
        )

    def sp_copy(which, src, dst, off):
        return pltpu.make_async_remote_copy(
            src_ref=src,
            dst_ref=dst,
            send_sem=sp_send.at[which],
            recv_sem=sp_recv.at[which],
            device_id={"space": lax.rem(me + off, n)},
            device_id_type=MESH,
        )

    dp_peers, sp_peers = pl.ds(0, nd - 1), pl.ds(0, n - 1)

    def first_all(stage):
        where = stage_slots[stage]
        return dp_copy(stage, rbuf.at[dp_peers, where], rbuf.at[dp_peers, where], 1)

    def last_all(stage):
        where = stage_slots[stage]
        return dp_copy(2 + stage, gall.at[dp_peers, where], gall.at[dp_peers, where], 1)

    def pack_all(which):
        lanes = pl.ds(0, 128) if which else pl.ds(128, 768)
        ref = packs.at[dp_peers, :, lanes]
        return dp_copy(4 + which, ref, ref, 1)

    def space_all(which):
        where = stage_slots[1 if which == 2 else 0]
        ref = zwhole.at[sp_peers] if which == 2 else zbuf.at[sp_peers, where]
        return sp_copy(which, ref, ref, 1)

    def pack_start(which):
        lanes = pl.ds(0, 128) if which else pl.ds(128, 768)
        for off in range(1, nd):
            ref = packs.at[dp, :, lanes]
            dp_copy(4 + which, ref, ref, off).start()

    def gather_start(stage):
        where = stage_slots[stage]
        for off in range(1, nd):
            owner = lax.rem(dp + off, nd)
            dp_copy(stage, gt_ref.at[where, owner], rbuf.at[dp, where], off).start()

    def gather_dp(stage):
        where = stage_slots[stage]
        first_all(stage).wait_recv()
        rbuf[dp, where] = gt_ref[where, dp]
        total = rbuf[0, where].astype(F32)
        for i in range(1, nd):
            total = total + rbuf[i, where].astype(F32)
        return total

    def gather_space(stage):
        where = stage_slots[stage]
        total = gather_dp(stage)
        if stage == 1:
            zwhole[me] = total[0]
            for off in range(1, n):
                sp_copy(2, zwhole.at[me], zwhole.at[me], off).start()
            return
        for z in range(n):
            part[z, where] = total[:, z * share : (z + 1) * share]
        for off in range(1, n):
            row = lax.rem(me + off, n)
            sp_copy(0, part.at[row, where], zbuf.at[me, where], off).start()

    def gather_spread():
        where = stage_slots[0]
        space_all(0).wait_recv()
        zbuf[me, where] = part[me, where]
        total = zbuf[0, where]
        for i in range(1, n):
            total = total + zbuf[i, where]
        zfull[me, where] = total
        for off in range(1, n):
            sp_copy(1, zfull.at[me, where], zfull.at[me, where], off).start()

    def gather_all(stage):
        where = stage_slots[stage]
        if stage == 1:
            space_all(2).wait_recv()
            total = zwhole[0]
            for i in range(1, n):
                total = total + zwhole[i]
            gall[dp, 0] = total.astype(BF16)
        else:
            space_all(1).wait_recv()
            whole = jnp.concatenate([zfull[z, where] for z in range(n)], axis=1)
            gall[dp, where] = whole.astype(BF16)
        for off in range(1, nd):
            dp_copy(2 + stage, gall.at[dp, where], gall.at[dp, where], off).start()

    def gather_finish(stage):
        last_all(stage).wait_recv()
        first_all(stage).wait_send()
        last_all(stage).wait_send()
        for which in (2,) if stage else (0, 1):
            space_all(which).wait_send()

    x_copy.wait()

    def load_x(f, carry):
        total, square = carry
        even, odd = pair_halves(paired(raw[f]))
        both = jnp.concatenate([even, odd], axis=-1)
        xs[f, 2 : 2 + rows] = both.astype(BF16)
        return put_row(total, f, full_sum(both)), put_row(square, f, full_sum(both * both))

    zero_rows = jnp.zeros((frames, 128), F32)
    sums = lax.fori_loop(0, frames, load_x, (zero_rows, zero_rows), unroll=4)
    g_copy.start()
    pl.semaphore_wait(barrier, n + nd - 2)
    stat_start(0, jnp.concatenate(sums, axis=0))
    for copies in x_halos:
        halo_start(copies)

    @pl.when(me == 0)
    def _():
        for v in (xs, gs):
            v[:, 0:2] = jnp.zeros((frames, 2, cols, 256), BF16)
        for which in range(hal.shape[0]):
            hal[which, 0] = jnp.zeros(hal.shape[2:], BF16)
        hfull[0] = jnp.zeros(hfull.shape[1:], BF16)

    @pl.when(me == n - 1)
    def _():
        for v in (xs, gs):
            v[:, rows + 2 : rows + 4] = jnp.zeros((frames, 2, cols, 256), BF16)
        for which in range(hal.shape[0]):
            hal[which, 1] = jnp.zeros(hal.shape[2:], BF16)
        hfull[1] = jnp.zeros(hfull.shape[1:], BF16)

    for v in (xs, gs):
        v[:, 0, :, 0:128] = jnp.zeros((frames, cols, 128), BF16)
        v[:, rows + 3, :, 128:256] = jnp.zeros((frames, cols, 128), BF16)

    def conditioning():
        entry = lax.broadcasted_iota(jnp.int32, (frames, 128), 1)
        row = lax.broadcasted_iota(jnp.int32, (frames, 128), 0)
        hot = jnp.zeros((frames, 128), F32)
        for f in range(frames):
            hit = (
                (entry == act_ref[f])
                | (entry == noise_ref[f] + ACTIONS)
                | (entry == game_ref[f] + ACTIONS + NOISE_LEVELS)
            )
            hot = jnp.where((row == f) & hit, 1.0, hot)
        table_rows = tab_ref.shape[0]
        tabp[...] = jnp.zeros(tabp.shape, F32)
        tabp[0:table_rows, :] = tab_ref[...]
        embedded = dot_high(hot, tabp[...])
        packs[dp, :, 512:768] = embedded
        packs[dp, :, 768:896] = hot
        for copy in map_copies:
            copy.wait()
        for k in range(4):
            mod = dot_high(embedded, nmv[k]) + nmb[k : k + 1, :]
            scale = join(mod, swap(mod)) + 1.0
            shift = join(swap(mod), mod)
            if k < 2:
                prm[k * 8 + GAIN] = scale
                prm[k * 8 + SHIFT] = shift
            else:
                prm[k * 8 + GAIN, 0:half, :] = join(scale[0:half], scale[half:])
                prm[k * 8 + SHIFT, 0:half, :] = join(shift[0:half], shift[half:])

    conditioning()

    g_copy.wait()

    def load_cotangent(f, carry):
        live = jnp.where(f < live_ref[0], 1.0, 0.0)
        even, odd = pair_halves(paired(raw[f]))
        both = jnp.concatenate([even, odd], axis=-1)
        gs[f, 2 : 2 + rows] = (both * live).astype(BF16)
        return carry

    lax.fori_loop(0, frames, load_cotangent, 0, unroll=4)
    for copies in g_halos:
        halo_start(copies)


    def tap(index):
        first = (index // 2) * 128
        last = min(first + 128, cw_ref.shape[1])
        tile = cw_ref[:, first:last].astype(BF16).astype(F32)
        if last - first < 128:
            tile = jnp.concatenate([tile, jnp.zeros((64, 128 - last + first), F32)], axis=-1)
        return tile, index % 2

    def low_half(index):
        tile, odd = tap(index)
        return swap(tile) if odd else tile

    def high_half(index):
        tile, odd = tap(index)
        return tile if odd else swap(tile)

    def lane_pair(low_index, high_index):
        zero = jnp.zeros((64, 128), F32)
        low = zero if low_index is None else low_half(low_index)
        high = zero if high_index is None else high_half(high_index)
        return join(low, high).astype(BF16)

    def fine_weights(index, forward_w, backward_w):
        zero = jnp.zeros((64, 128), BF16)
        pairs = []
        for t in range(3):
            p12 = lane_pair(index(t, 1), index(t, 2))
            p01 = lane_pair(index(t, 0), index(t, 1))
            pz0 = lane_pair(None, index(t, 0))
            p2z = lane_pair(index(t, 2), None)
            pairs.append((p12, p01, pz0, p2z))
        for a in range(4):
            for dr in range(2):
                t = a - dr
                ok = 0 <= t <= 2
                for dq in range(2):
                    r = (dr * 2 + dq) * 64
                    first = pairs[t][0 if dq == 0 else 1] if ok else zero
                    second = pairs[t][2 if dq == 0 else 3] if ok else zero
                    forward_w[r : r + 64, a * 256 : a * 256 + 128] = first
                    forward_w[r : r + 64, a * 256 + 128 : a * 256 + 256] = second
                t = 2 - a + dr
                ok = 0 <= t <= 2
                for g in range(4):
                    r = a * 256 + g * 64
                    backward_w[r : r + 64, dr * 128 : dr * 128 + 128] = (
                        pairs[t][g] if ok else zero
                    )

    def coarse_weights(index, forward_w, backward_w):
        for a in range(3):
            for j in range(3):
                lane = (a * 3 + j) * 128
                low = lane_pair(index(a, j), None)
                high = lane_pair(None, index(a, j))
                forward_w[0:64, lane : lane + 128] = low
                forward_w[64:128, lane : lane + 128] = high
                lane = ((2 - a) * 3 + (2 - j)) * 128
                backward_w[lane : lane + 64, :] = low
                backward_w[lane + 64 : lane + 128, :] = high

    def down_weights(index):
        zero = jnp.zeros((64, 128), BF16)
        wdf[...] = jnp.zeros(wdf.shape, BF16)
        wdb[...] = jnp.zeros(wdb.shape, BF16)
        for t in range(3):
            p12 = lane_pair(index(t, 1), index(t, 2))
            pz0 = lane_pair(None, index(t, 0))
            for hi in range(2):
                lane = hi * 768 + t * 256
                wdf[hi * 64 : hi * 64 + 64, lane : lane + 128] = p12
                wdf[hi * 64 : hi * 64 + 64, lane + 128 : lane + 256] = pz0
                i, dr = ((1, 1), (0, 0), (0, 1))[t]
                lane = hi * 256 + dr * 128
                for j in range(2):
                    r = (i * 2 + j) * 128 + hi * 64
                    wdb[r : r + 64, lane : lane + 128] = p12 if j == 0 else pz0

    def up_weights():
        def up_tap(ta, tb):
            return low_half(45 + (ta * 3 + tb) * 2 + 1)

        taps = [[up_tap(ta, tb) for tb in range(3)] for ta in range(3)]
        members = {(0, 0): (0,), (0, 1): (1, 2), (1, 1): (0, 1), (1, 2): (2,)}
        wup[...] = jnp.zeros(wup.shape, BF16)
        for (dr, i), in_rows in members.items():
            for (dq, j), in_cols in members.items():
                total = sum(taps[ta][tb] for ta in in_rows for tb in in_cols)
                zero = jnp.zeros_like(total)
                r = (dr * 2 + dq) * 64
                lane = (i * 3 + j) * 128
                wup[r : r + 64, lane : lane + 128] = join(total, zero).astype(BF16)
                wup[256 + r : 256 + r + 64, lane : lane + 128] = join(zero, swap(total)).astype(
                    BF16
                )
        for a in range(4):
            for g, off in enumerate((0, 1, 2, -1)):
                chosen = [
                    taps[2 - a + dr][1 - off + dq]
                    for dr in range(2)
                    for dq in range(2)
                    if 0 <= 2 - a + dr <= 2 and 0 <= 1 - off + dq <= 2
                ]
                total = sum(chosen[1:], chosen[0])
                zero = jnp.zeros_like(total)
                r = a * 256 + g * 64
                wco[0, r : r + 64, :] = join(total, zero).astype(BF16)
                wco[1, r : r + 64, :] = join(zero, swap(total)).astype(BF16)

    def stacked(k):
        return lambda t, s: k * 9 + t * 3 + s

    fine_weights(stacked(0), w1f, w1b)
    fine_weights(stacked(1), w2f, w2b)
    fine_weights(lambda t, s: 45 + (t * 3 + s) * 2, wsf, wsb)
    up_weights()
    down_weights(stacked(2))
    coarse_weights(stacked(3), w3f, w3b)
    coarse_weights(stacked(4), w4f, w4b)

    for copies in x_halos:
        halo_wait(copies)
    norm_forward(0, stat_total(0), False)

    def first_layer(f, carry):
        total, square = carry
        x = xs[f].astype(F32)
        z = x * wide(0, ALPHA, f) + wide(0, BETA, f)
        h = z * logistic(z)
        h = jnp.where(block_mask(h.shape, 2), h, 0.0)
        put_e(e1, f, 0, h)
        out = dot_nt(window(e1, f, 1, rows + 2), w1f[...]).reshape(rows + 2, cols, 256)
        c1[f] = out
        own = out[1 : rows + 1]
        return put_row(total, f, full_sum(own)), put_row(square, f, full_sum(own * own))

    sums = lax.fori_loop(0, frames, first_layer, (zero_rows, zero_rows), unroll=4)
    stat_start(1, jnp.concatenate(sums, axis=0))

    for copies in g_halos:
        halo_wait(copies)

    def load_g(f, carry):
        g = gs[f].astype(F32)
        put_e(eg, f, 0, jnp.where(block_mask(g.shape, 2), g, 0.0))
        gsa[f] = dot_nn(window(eg, f, 1, rows + 2), wsb[...]).reshape(rows + 2, cols, 256)
        return carry

    lax.fori_loop(0, frames, load_g, 0, unroll=4)

    norm_forward(1, stat_total(1), False)

    def second_layer(f, carry):
        z = c1[f] * wide(1, ALPHA, f) + wide(1, BETA, f)
        h = z * logistic(z)
        h = jnp.where(block_mask(h.shape, 1), h, 0.0)
        edge = jnp.zeros((cols, 512), BF16)
        e2[f, 0] = edge
        e2[f, rows + 3] = edge
        put_e(e2, f, 1, h)
        out = dot_nt(window(e2, f, 1, rows + 2), w2f[...]).reshape(rows + 2, cols, 256)
        skip = out + xs[f, 1 : rows + 3].astype(F32)
        skip = jnp.where(block_mask(skip.shape, 1), skip, 0.0)
        put_e(esk, f, 1, skip)
        return carry

    lax.fori_loop(0, frames, second_layer, 0, unroll=4)

    def down_window(f):
        return jnp.concatenate(
            [esk[f, 1 : 1 + rows, :, 256:512], esk[f, 2 : 2 + rows]], axis=-1
        ).reshape(owned, 768)

    zero_coarse = jnp.zeros((half, 128), F32)
    pad_rows = [jnp.zeros((2 * frames - 2 * half, 128), F32)]

    def down_layer(hf, carry):
        total, square = carry
        d = dot_nt(down_window(hf), wdf[:, 0:768]) + dot_nt(
            down_window(hf + half), wdf[:, 768:1536]
        )
        d = d.reshape(rows, cols, 128)
        dv[hf, 1 : rows + 1] = d
        border(hout, 1, hf, d)
        return put_row(total, hf, coarse_sum(d)), put_row(square, hf, coarse_sum(d * d))

    sums = lax.fori_loop(0, half, down_layer, (zero_coarse, zero_coarse), unroll=4)
    stat_start(2, jnp.concatenate(list(sums) + pad_rows, axis=0))
    halo_start(d_halo)

    def coarse_gradient(hf, carry):
        g = dot_nn(window(eg, hf, 1, rows + 2), wco[0]) + dot_nn(
            window(eg, hf + half, 1, rows + 2), wco[1]
        )
        g = g.reshape(rows + 2, cols, 128)
        g = jnp.where(block_mask(g.shape, 1), g, 0.0).astype(BF16).astype(F32)
        gco[hf] = g
        put_ec(ecg, hf, g)
        back = dot_nn(coarse_window(ecg, hf), w4b[...]).reshape(rows, cols, 128)
        gh4[hf, 1 : rows + 1] = back
        border(hout, 0, hf, back)
        return carry

    lax.fori_loop(0, half, coarse_gradient, 0, unroll=4)
    halo_start(g_h4_halo)

    def put_half(index, value):
        slot, owner = index // 2 // nd, index // 2 % nd
        current = gt_ref[slot, owner].astype(F32)
        value = join(current, swap(value)) if index % 2 else join(value, current)
        gt_ref[slot, owner] = value.astype(BF16)

    gt_ref[...] = jnp.zeros(gt_ref.shape, BF16)

    def fine_kernel_grad(index, e, start, gradient, gradient_start):
        acc[0, :, 0:1024] = jnp.zeros((256, 1024), F32)

        def add(f, carry):
            g = own_pixels(gradient, f, gradient_start, rows)
            acc[0, :, 0:1024] += dot_tn(g, window(e, f, start, rows))
            return carry

        lax.fori_loop(0, frames, add, 0, unroll=4)
        for t in range(3):
            u = []
            for dq in range(2):
                parts = [
                    acc[0, (dr * 2 + dq) * 64 : (dr * 2 + dq) * 64 + 64, pl.ds((t + dr) * 256, 256)]
                    for dr in range(2)
                ]
                u.append(parts[0] + parts[1])
            near, far = [v[:, 0:128] for v in u], [v[:, 128:256] for v in u]
            put_half(index(t, 0), swap(far[0]) + near[1])
            put_half(index(t, 1), near[0] + swap(near[1]))
            put_half(index(t, 2), swap(near[0]) + far[1])

    def coarse_kernel_grad(index, ec, gradient):
        acc[0, 0:128, :] = jnp.zeros((128, 1152), F32)

        def add(hf, carry):
            g = gradient[hf, 1 : rows + 1, :, 128:256].reshape(owned, 128)
            acc[0, 0:128, :] += dot_tn(g, coarse_window(ec, hf))
            return carry

        lax.fori_loop(0, half, add, 0, unroll=4)
        for a in range(3):
            for j in range(3):
                lanes = pl.ds((a * 3 + j) * 128, 128)
                put_half(index(a, j), acc[0, 0:64, lanes] + swap(acc[0, 64:128, lanes]))

    def down_kernel_grad(index):
        acc[:, 0:128, 0:768] = jnp.zeros((2, 128, 768), F32)

        def add(hf, carry):
            g = ed[hf, 1 : rows + 1, :, 0:128].reshape(owned, 128)
            acc[0, 0:128, 0:768] += dot_tn(g, down_window(hf))
            acc[1, 0:128, 0:768] += dot_tn(g, down_window(hf + half))
            return carry

        lax.fori_loop(0, half, add, 0, unroll=4)
        for a in range(3):
            near = acc[0, 0:64, pl.ds(a * 256, 128)] + acc[1, 64:128, pl.ds(a * 256, 128)]
            far = (
                acc[0, 0:64, pl.ds(a * 256 + 128, 128)] + acc[1, 64:128, pl.ds(a * 256 + 128, 128)]
            )
            put_half(index(a, 0), swap(far))
            put_half(index(a, 1), near)
            put_half(index(a, 2), swap(near))

    def up_kernel_grad():
        acc[...] = jnp.zeros(acc.shape, F32)

        def add(hf, carry):
            v = coarse_window(ecy, hf)
            acc[0] += dot_tn(own_pixels(eg, hf, 2, rows), v)
            acc[1] += dot_tn(own_pixels(eg, hf + half, 2, rows), v)
            return carry

        lax.fori_loop(0, half, add, 0, unroll=4)

        def block(dr, dq, i, j):
            r = (dr * 2 + dq) * 64
            lanes = pl.ds((i * 3 + j) * 128, 128)
            return acc[0, r : r + 64, lanes] + swap(acc[1, r : r + 64, lanes])

        place = {(0, 0): 0, (0, 1): 1, (0, 2): 1, (1, 0): 1, (1, 1): 1, (1, 2): 2}
        for ta in range(3):
            for tb in range(3):
                total = sum(
                    block(dr, dq, place[dr, ta], place[dq, tb])
                    for dr in range(2)
                    for dq in range(2)
                )
                put_half(45 + (ta * 3 + tb) * 2 + 1, total)


    halo_wait(d_halo)
    norm_forward(2, stat_total(2), True)

    def third_layer(hf, carry):
        total, square = carry
        with_halo(dv, hf, 1)
        z = dv[hf] * param(2, ALPHA, hf) + param(2, BETA, hf)
        h = z * logistic(z)
        put_ec(ec3, hf, jnp.where(block_mask(h.shape, 1), h, 0.0))
        out = dot_nt(coarse_window(ec3, hf), w3f[...]).reshape(rows, cols, 128)
        c3[hf, 1 : rows + 1] = out
        border(hout, 2, hf, out)
        return put_row(total, hf, coarse_sum(out)), put_row(square, hf, coarse_sum(out * out))

    sums = lax.fori_loop(0, half, third_layer, (zero_coarse, zero_coarse), unroll=4)
    stat_start(3, jnp.concatenate(list(sums) + pad_rows, axis=0))
    halo_start(c3_halo)

    def result_copy(f):
        return pltpu.make_async_copy(gz.at[f, pl.ds(1, rows)], io_hbm.at[f], out_sem.at[f])

    def merge_skip(f, carry):
        out = dot_nt(window(esk, f, 2, rows), wsf[...])
        gz[f, 1 : rows + 1] = out.reshape(rows, cols, 256)
        return carry

    lax.fori_loop(0, half, merge_skip, 0, unroll=4)
    fine_kernel_grad(lambda t, s: 45 + (t * 3 + s) * 2, esk, 2, eg, 2)

    halo_wait(c3_halo)
    halo_wait(g_h4_halo)
    norm_forward(3, stat_total(3), True)

    def fourth_layer(hf, carry):
        shift, scale = carry
        with_halo(c3, hf, 2)
        with_halo(gh4, hf, 0)
        v = c3[hf]
        z = v * param(3, ALPHA, hf) + param(3, BETA, hf)
        gate = logistic(z)
        h = z * gate
        put_ec(ec4, hf, jnp.where(block_mask(h.shape, 1), h, 0.0))
        g = gh4[hf] * (gate + h * (1.0 - gate))
        gzc[hf] = g
        own = g[1 : rows + 1]
        xhat = v[1 : rows + 1] * param(3, RSTD, hf) + param(3, NMR, hf)
        return put_row(shift, hf, coarse_sum(own)), put_row(scale, hf, coarse_sum(own * xhat))

    sums = lax.fori_loop(0, half, fourth_layer, (zero_coarse, zero_coarse), unroll=4)
    stat_start(4, jnp.concatenate(list(sums) + pad_rows, axis=0))

    def coarse_output(hf, carry):
        out = dot_nt(coarse_window(ec4, hf), w4f[...]).reshape(rows, cols, 128)
        y = dv[hf, 1 : rows + 1] + out
        border(hout, 3, hf, y)
        edge = jnp.zeros((1, cols, 128), F32)
        put_ec(ecy, hf, jnp.concatenate([edge, y, edge], axis=0))
        return carry

    lax.fori_loop(0, half, coarse_output, 0, unroll=4)
    halo_start(y_halo)
    coarse_kernel_grad(stacked(4), ec4, ecg)
    lax.fori_loop(half, frames, merge_skip, 0, unroll=4)

    norm_backward(3, stat_total(4), True)

    def third_back(hf, carry):
        shift, scale = carry
        g = (
            gzc[hf] * param(3, ALPHA, hf)
            + c3[hf] * param(3, COEF, hf)
            + param(3, BIAS, hf)
        )
        put_ec(ecg3, hf, jnp.where(block_mask(g.shape, 1), g, 0.0))
        back = dot_nn(coarse_window(ecg3, hf), w3b[...]).reshape(rows, cols, 128)
        border(hout, 4, hf, back)
        v = dv[hf, 1 : rows + 1]
        z = v * param(2, ALPHA, hf) + param(2, BETA, hf)
        gate = logistic(z)
        own = back * (gate + z * gate * (1.0 - gate))
        gzc[hf, 1 : rows + 1] = own
        xhat = v * param(2, RSTD, hf) + param(2, NMR, hf)
        return put_row(shift, hf, coarse_sum(own)), put_row(scale, hf, coarse_sum(own * xhat))

    sums = lax.fori_loop(0, half, third_back, (zero_coarse, zero_coarse), unroll=4)
    stat_start(5, jnp.concatenate(list(sums) + pad_rows, axis=0))
    halo_start(g_h3_halo)

    halo_wait(y_halo)

    def merge(hf, carry):
        for side, row in ((0, 0), (1, rows + 1)):
            line = hal[3, side, hf].astype(F32)[None]
            up, down = neighbours(line)
            q = lax.broadcasted_iota(jnp.int32, line.shape, 1)
            ecy[hf, row, :, 0:128] = jnp.where(q == 0, 0.0, down)[0].astype(BF16)
            ecy[hf, row, :, 128:256] = line[0].astype(BF16)
            ecy[hf, row, :, 256:384] = jnp.where(q == cols - 1, 0.0, up)[0].astype(BF16)
        both = dot_nt(coarse_window(ecy, hf), wup[...])
        for hi in range(2):
            f = hf + hi * half
            up = both[:, hi * 256 : hi * 256 + 256].reshape(rows, cols, 256)
            gz[f, 1 : rows + 1] = gz[f, 1 : rows + 1] + up
            result_copy(f).start()
        return carry

    lax.fori_loop(0, half, merge, 0, unroll=4)
    coarse_kernel_grad(stacked(3), ec3, ecg3)
    up_kernel_grad()

    halo_wait(g_h3_halo)
    norm_backward(2, stat_total(5), True)

    def down_back(hf, carry):
        for side, row in ((0, 0), (1, rows + 1)):
            v = dv[hf, row]
            z = v * param(2, ALPHA, hf) + param(2, BETA, hf)
            gate = logistic(z)
            gzc[hf, row] = hal[4, side, hf].astype(F32) * (gate + z * gate * (1.0 - gate))
        g = (
            gco[hf]
            + gzc[hf] * param(2, ALPHA, hf)
            + dv[hf] * param(2, COEF, hf)
            + param(2, BIAS, hf)
        )
        g = jnp.where(block_mask(g.shape, 1), g, 0.0)
        up, _ = neighbours(g)
        q = lax.broadcasted_iota(jnp.int32, g.shape, 1)
        ed[hf, 0 : rows + 2, :, 0:128] = g.astype(BF16)
        ed[hf, 0 : rows + 2, :, 128:256] = jnp.where(q == cols - 1, 0.0, up).astype(BF16)
        ed[hf, rows + 2] = jnp.zeros((cols, 256), BF16)
        lhs = jnp.concatenate([ed[hf, 0 : rows + 2], ed[hf, 1 : rows + 3]], axis=-1)
        back = dot_nn(lhs.reshape(ext, 512), wdb[...])
        back = back.astype(BF16).astype(F32).reshape(rows + 2, cols, 512)
        for hi in range(2):
            f = hf + hi * half
            total = gsa[f] + back[:, :, hi * 256 : hi * 256 + 256]
            gsa[f] = total
            put_e(eg, f, 0, jnp.where(block_mask(total.shape, 1), total, 0.0))
        return carry

    lax.fori_loop(0, half, down_back, 0, unroll=4)

    def second_back(f, carry):
        shift, scale = carry
        back = dot_nn(window(eg, f, 1, rows), w2b[...]).reshape(rows, cols, 256)
        hfout[0, f] = back[0, :, 0:128].astype(BF16)
        hfout[1, f] = back[rows - 1, :, 128:256].astype(BF16)
        v = c1[f, 1 : rows + 1]
        z = v * wide(1, ALPHA, f) + wide(1, BETA, f)
        gate = logistic(z)
        own = back * (gate + z * gate * (1.0 - gate))
        gz[f, 1 : rows + 1] = own
        xhat = v * wide(1, RSTD, f) + wide(1, NMR, f)
        return put_row(shift, f, full_sum(own)), put_row(scale, f, full_sum(own * xhat))

    for f in range(frames):
        result_copy(f).wait()
    sums = lax.fori_loop(0, frames, second_back, (zero_rows, zero_rows), unroll=4)
    stat_start(6, jnp.concatenate(sums, axis=0))
    halo_start(g_h2_halo)
    down_kernel_grad(stacked(2))
    fine_kernel_grad(stacked(1), e2, 2, eg, 1)
    gather_start(0)
    halo_wait(g_h2_halo)
    norm_backward(1, stat_total(6), False)

    def first_gradient(f, carry):
        for side, row in ((0, 0), (1, rows + 1)):
            v = c1[f, row]
            lanes = slice(128, 256) if side == 0 else slice(0, 128)
            z = v[:, lanes] * param(1, ALPHA, f) + param(1, BETA, f)
            gate = logistic(z)
            g = hfull[side, f].astype(F32) * (gate + z * gate * (1.0 - gate))
            blank = jnp.zeros_like(g)
            gz[f, row] = jnp.concatenate([blank, g] if side == 0 else [g, blank], axis=-1)
        g = gz[f] * wide(1, ALPHA, f) + c1[f] * wide(1, COEF, f) + wide(1, BIAS, f)
        put_e(eg, f, 0, jnp.where(block_mask(g.shape, 1), g, 0.0))
        return carry

    lax.fori_loop(0, frames, first_gradient, 0, unroll=4)
    fine_kernel_grad(stacked(0), e1, 2, eg, 1)
    gather_start(1)
    gather_space(0)

    def first_back(f, carry):
        shift, scale = carry
        back = dot_nn(window(eg, f, 1, rows), w1b[...]).reshape(rows, cols, 256)
        v = xs[f, 2 : rows + 2].astype(F32)
        z = v * wide(0, ALPHA, f) + wide(0, BETA, f)
        gate = logistic(z)
        own = back * (gate + z * gate * (1.0 - gate))
        gz[f, 1 : rows + 1] = own
        xhat = v * wide(0, RSTD, f) + wide(0, NMR, f)
        return put_row(shift, f, full_sum(own)), put_row(scale, f, full_sum(own * xhat))

    pack_start(0)
    sums = lax.fori_loop(0, frames, first_back, (zero_rows, zero_rows), unroll=4)
    stat_start(7, jnp.concatenate(sums, axis=0))
    gather_spread()
    gather_space(1)
    norm_backward(0, stat_total(7), False)
    pack_start(1)
    gather_all(0)

    def frames_copy(f):
        return pltpu.make_async_copy(
            gz.at[f, pl.ds(1, rows)], io_hbm.at[frames + f], fg_sem.at[f]
        )

    def frames_back(f, carry):
        gz[f, 1 : rows + 1] = (
            gsa[f, 1 : rows + 1]
            + gz[f, 1 : rows + 1] * wide(0, ALPHA, f)
            + xs[f, 2 : rows + 2].astype(F32) * wide(0, COEF, f)
            + wide(0, BIAS, f)
        )
        frames_copy(f).start()
        return carry

    lax.fori_loop(0, half, frames_back, 0, unroll=4)
    gather_all(1)
    lax.fori_loop(half, frames, frames_back, 0, unroll=4)
    for which in range(2):
        pack_all(which).wait_recv()
        pack_all(which).wait_send()
    total_frames = nd * frames
    every = packs[...].reshape(total_frames, 896)
    embedded, hot = every[:, 512:768], every[:, 768:896]
    g_embed = 0.0
    for k in range(4):
        dmod = every[:, k * 128 : (k + 1) * 128]
        acc[1, :, k * 128 : k * 128 + 128] = lax.dot_general(
            embedded, dmod, (((0,), (0,)), ((), ())), precision=HIGH, preferred_element_type=F32
        )
        lane = 512 + k % 2 * 128
        acc[1, 128 + k // 2 : 129 + k // 2, lane : lane + 128] = jnp.sum(
            dmod, axis=0, keepdims=True
        )
        g_embed = g_embed + lax.dot_general(
            dmod, nmv[k], (((1,), (1,)), ((), ())), precision=HIGH, preferred_element_type=F32
        )
    acc[1, 0:128, 512:768] = lax.dot_general(
        hot, g_embed, (((0,), (0,)), ((), ())), precision=HIGH, preferred_element_type=F32
    )

    def par_copy(e):
        return pltpu.make_async_copy(
            acc.at[e // 4, :, pl.ds(e % 4 * 256, 256)], par_hbm.at[e], local_sem.at[e]
        )

    for e in range(4, 7):
        par_copy(e).start()
    for stage in range(2):
        gather_finish(stage)
    for tile in range(32):
        row, lane = tile // 2 % 4 * 64, tile // 8 * 256 + tile % 2 * 128
        acc[0, row : row + 64, lane : lane + 128] = gall[tile % nd, tile // nd].astype(F32)
    for e in range(4):
        par_copy(e).start()

    for e in range(7):
        par_copy(e).wait()
    for f in range(frames):
        frames_copy(f).wait()
    for copies in (*x_halos, *g_halos, g_h4_halo, d_halo, c3_halo, y_halo, g_h3_halo, g_h2_halo):
        halo_finish(copies)


def run_step(nd, n, frames, cotangent, actions, noise_ids, games, live_counts, cw, nm, table):
    count, strip, breadth, _ = frames.shape
    half, rows, cols = count // 2, strip // 2, breadth // 2
    fine = (count, rows + 4, cols, 512)
    coarse = (half, rows + 2, cols, 128)
    coarse_e = (half, rows + 2, cols, 384)
    scratch = [
        VM((count, strip, breadth, 64), BF16),
        VM((strip, breadth, 128), F32),
        VM((count, rows + 4, cols, 256), BF16),
        VM((count, rows + 4, cols, 256), BF16),
        VM(fine, BF16),
        VM(fine, BF16),
        VM(fine, BF16),
        VM(fine, BF16),
        VM((count, rows + 2, cols, 256), F32),
        VM((count, rows + 2, cols, 256), F32),
        VM((count, rows + 2, cols, 256), F32),
        VM(coarse, F32),
        VM(coarse, F32),
        VM(coarse, F32),
        VM(coarse, F32),
        VM(coarse, F32),
        VM(coarse_e, BF16),
        VM(coarse_e, BF16),
        VM(coarse_e, BF16),
        VM(coarse_e, BF16),
        VM(coarse_e, BF16),
        VM((half, rows + 3, cols, 256), BF16),
        VM((256, 1024), BF16),
        VM((1024, 256), BF16),
        VM((256, 1024), BF16),
        VM((1024, 256), BF16),
        VM((256, 1024), BF16),
        VM((1024, 256), BF16),
        VM((512, 1152), BF16),
        VM((2, 1024, 128), BF16),
        VM((128, 1536), BF16),
        VM((512, 512), BF16),
        VM((128, 1152), BF16),
        VM((1152, 128), BF16),
        VM((128, 1152), BF16),
        VM((1152, 128), BF16),
        VM((2, 256, 1152), F32),
        VM((32, count, 128), F32),
        VM((128, 256), F32),
        VM((8, n, 2 * count, 128), F32),
        VM((5, 2, half, cols, 128), BF16),
        VM((5, 2, half, cols, 128), BF16),
        VM((2, count, cols, 128), BF16),
        VM((2, count, cols, 128), BF16),
        VM((4, 256, 128), F32),
        VM((4, 128), F32),
        VM((32 // nd, nd, 64, 128), BF16),
        VM((nd, 32 // nd, 64, 128), BF16),
        VM((n, 32 // nd, 64 // n, 128), F32),
        VM((n, 32 // nd, 64 // n, 128), F32),
        VM((n, 32 // nd, 64 // n, 128), F32),
        VM((n, 64, 128), F32),
        VM((nd, 32 // nd, 64, 128), BF16),
        VM((nd, count, 896), F32),
        pltpu.SemaphoreType.DMA((7,)),
        pltpu.SemaphoreType.DMA((count,)),
        pltpu.SemaphoreType.DMA((count,)),
        pltpu.SemaphoreType.DMA((8,)),
        pltpu.SemaphoreType.DMA((8,)),
        pltpu.SemaphoreType.DMA((10, 2)),
        pltpu.SemaphoreType.DMA((10, 2)),
        pltpu.SemaphoreType.DMA((6,)),
        pltpu.SemaphoreType.DMA((6,)),
        pltpu.SemaphoreType.DMA((3,)),
        pltpu.SemaphoreType.DMA((3,)),
    ]
    smem = pl.BlockSpec(memory_space=pltpu.SMEM)
    vmem = pl.BlockSpec(memory_space=pltpu.VMEM)
    hbm = pl.BlockSpec(memory_space=pltpu.HBM)
    return pl.pallas_call(
        functools.partial(step_kernel, nd, n),
        out_shape=(
            jax.ShapeDtypeStruct((2 * count, rows, cols, 256), F32),
            jax.ShapeDtypeStruct((7, 256, 256), F32),
        ),
        in_specs=[hbm, hbm, smem, smem, smem, smem, vmem, hbm, vmem],
        out_specs=(hbm, hbm),
        scratch_shapes=scratch,
        compiler_params=pltpu.CompilerParams(
            collective_id=0, has_side_effects=True, vmem_limit_bytes=55 * 1024 * 1024
        ),
        name="step",
    )(frames, cotangent, actions, noise_ids, games, live_counts, cw, nm, table)


def adamw(weight, moment, square, grad_value, rate):
    fix_one = 1.0 - BETA_ONE**ADAM_STEP
    fix_two = 1.0 - BETA_TWO**ADAM_STEP
    moment_new = BETA_ONE * moment + (1.0 - BETA_ONE) * grad_value
    square_new = BETA_TWO * square + (1.0 - BETA_TWO) * grad_value * grad_value
    fixed_m = moment_new / fix_one
    fixed_v = square_new / fix_two
    weight_new = weight - rate * (fixed_m / (jnp.sqrt(fixed_v) + ADAM_EPS) + DECAY * weight)
    return (moment_new, square_new, weight_new, weight_new.astype(BF16))


def finish_kernel(
    io_hbm,
    par_hbm,
    cw,
    cm,
    cv,
    nm,
    nmo,
    nsq,
    tab,
    tmo,
    tsq,
    res_out,
    fg_out,
    *refs,
):
    outs, refs = refs[:12], refs[12:]
    stages, refs = refs[:12], refs[12:]
    io, par, tmp, rs, fs, gmap, in_sem, pin_sem, fg_sem, out_sem, par_sem = refs
    frames, rows, cols = rs.shape[0], io.shape[1], io.shape[2]

    def frame_in(f):
        return pltpu.make_async_copy(io_hbm.at[f], io.at[f], in_sem.at[f])

    def par_in(e):
        return pltpu.make_async_copy(par_hbm.at[e], par.at[e], pin_sem.at[e])

    for e in range(7):
        par_in(e).start()
    for f in range(2 * frames):
        frame_in((f + frames) % (2 * frames)).start()
    out_copies = [
        pltpu.make_async_copy(stages[i], outs[i], par_sem.at[i]) for i in range(12)
    ]

    def update(first, at, weight, moment, square, grad, rate):
        new = adamw(weight, moment, square, grad, rate)
        for i in range(4):
            stages[first + i][at] = new[i]

    wide = cw.shape[1]
    for c in range(16):
        if c % 4 == 0:
            par_in(c // 4).wait()
        lanes = slice(c * 256, min(c * 256 + 256, wide))
        at = (slice(None), lanes)
        grad = par[c // 4, c % 4 * 64 : c % 4 * 64 + 64, 0 : lanes.stop - lanes.start]
        update(0, at, cw[at], cm[at], cv[at], grad, 0.05)
    for i in range(4):
        out_copies[i].start()

    def unpair(v):
        both = jnp.stack([v[:, :, 0:128], v[:, :, 128:256]], axis=1).reshape(rows * 2, cols, 128)
        tmp[:, pl.ds(0, cols, stride=2), :] = both
        tmp[:, pl.ds(1, cols, stride=2), :] = swap(both)
        return tmp[:, :, 0:64]

    def frame_copies(f):
        return (
            pltpu.make_async_copy(fs.at[f], fg_out.at[f], fg_sem.at[f]),
            pltpu.make_async_copy(rs.at[f], res_out.at[f], out_sem.at[f]),
        )

    def put_frames(f, carry):
        frame_in(frames + f).wait()
        fs[f] = unpair(io[frames + f])
        frame_copies(f)[0].start()
        return carry

    lax.fori_loop(0, frames, put_frames, 0)

    def put_result(f, carry):
        frame_in(f).wait()
        rs[f] = unpair(io[f]).astype(BF16)
        frame_copies(f)[1].start()
        return carry

    lax.fori_loop(0, frames, put_result, 0)

    for e in range(4, 7):
        par_in(e).wait()
    for k in range(4):
        lane = k % 2 * 128
        gmap[0:256, k, :] = par[4 + k // 2, :, lane : lane + 128]
        gmap[256, k : k + 1, :] = par[6, 128 + k // 2 : 129 + k // 2, lane : lane + 128]
    at = slice(None)
    update(4, at, nm[...], nmo[...], nsq[...], gmap[...], 0.04)
    for i in range(4, 8):
        out_copies[i].start()
    update(8, at, tab[...], tmo[...], tsq[...], par[6, 0 : tab.shape[0]], 0.5)
    for i in range(8, 12):
        out_copies[i].start()
    for f in range(frames):
        for copy in frame_copies(f):
            copy.wait()
    for copy in out_copies:
        copy.wait()


def run_finish(shape, io, par, conv, norm, table):
    count, strip, breadth, _ = shape
    hbm = pl.BlockSpec(memory_space=pl.ANY)
    vmem = pl.BlockSpec(memory_space=pltpu.VMEM)
    params = [
        jax.ShapeDtypeStruct(v[0].shape, dtype)
        for v in (conv, norm, table)
        for dtype in (F32, F32, F32, BF16)
    ]
    return pl.pallas_call(
        finish_kernel,
        out_shape=(
            jax.ShapeDtypeStruct(shape, BF16),
            jax.ShapeDtypeStruct(shape, F32),
            *params,
        ),
        in_specs=[hbm, hbm] + [vmem] * 9,
        out_specs=(hbm,) * 14,
        scratch_shapes=[VM(v.shape, v.dtype) for v in params]
        + [
            VM(io.shape, F32),
            VM(par.shape, F32),
            VM((strip, breadth, 128), F32),
            VM(shape, BF16),
            VM(shape, F32),
            VM(norm[0].shape, F32),
            pltpu.SemaphoreType.DMA((2 * count,)),
            pltpu.SemaphoreType.DMA((7,)),
            pltpu.SemaphoreType.DMA((count,)),
            pltpu.SemaphoreType.DMA((count,)),
            pltpu.SemaphoreType.DMA((12,)),
        ],
        compiler_params=pltpu.CompilerParams(vmem_limit_bytes=48 * 1024 * 1024),
        name="finish",
    )(io, par, *conv, *norm, *table)


def local(
    nd,
    ns,
    frames,
    cotangent,
    actions,
    noise_ids,
    games,
    live_counts,
    conv_weight,
    conv_moment,
    conv_square,
    norm_map,
    norm_moment,
    norm_square,
    emb_table,
    table_moment,
    table_square,
):
    conv = [v.T for v in (conv_weight, conv_moment, conv_square)]
    norm = [jnp.transpose(v, (1, 0, 2)) for v in (norm_map, norm_moment, norm_square)]
    table = (emb_table, table_moment, table_square)
    io, par = run_step(
        nd,
        ns,
        frames,
        cotangent,
        actions,
        noise_ids,
        games,
        live_counts,
        conv[0],
        norm[0],
        emb_table,
    )
    result, frames_grad, *new = run_finish(
        frames.shape, io, par, conv, norm, table
    )
    conv_out = [v.T for v in new[0:4]]
    norm_out = [jnp.transpose(v, (1, 0, 2)) for v in new[4:8]]
    return (result, frames_grad, *conv_out, *norm_out, *new[8:12])


def solution(mesh):
    split = P("dp", "space", None, None)
    in_specs = (split, split) + (P("dp"),) * 4 + (P(),) * 9
    out_specs = (split, split) + (P(),) * 12
    sizes = dict(mesh.shape)
    return jax.shard_map(
        functools.partial(local, sizes["dp"], sizes["space"]),
        mesh=mesh,
        in_specs=in_specs,
        out_specs=out_specs,
        check_vma=False,
    )
```

```python
import functools

import jax
import jax.numpy as jnp
from jax import lax
from jax.experimental import pallas as pl
from jax.experimental.pallas import tpu as pltpu
from jax.sharding import PartitionSpec as P

ACTIONS = 18
NOISE_LEVELS = 64
ADAM_STEP = 4
NORM_EPSILON = 1e-05
ADAM_EPS = 1e-08
BETA_ONE = 0.5
BETA_TWO = 0.5
DECAY = 0.01
HIGH = lax.Precision.HIGHEST
F32 = jnp.float32
BF16 = jnp.bfloat16
MESH = pl.DeviceIdType.MESH
VM = pltpu.VMEM

ALPHA, BETA, RSTD, NMR, GAIN, SHIFT, COEF, BIAS = range(8)


def dot_nn(a, b):
    return lax.dot_general(a, b, (((1,), (0,)), ((), ())), preferred_element_type=F32)


def dot_nt(a, b):
    return lax.dot_general(a, b, (((1,), (1,)), ((), ())), preferred_element_type=F32)


def dot_tn(a, b):
    return lax.dot_general(a, b, (((0,), (0,)), ((), ())), preferred_element_type=F32)


def dot_high(a, b):
    return lax.dot_general(
        a, b, (((1,), (0,)), ((), ())), precision=HIGH, preferred_element_type=F32
    )


def logistic(z):
    return 0.5 * jnp.tanh(0.5 * z) + 0.5


def lane_iota(shape):
    return lax.broadcasted_iota(jnp.int32, shape, len(shape) - 1)


def swap(v):
    return pltpu.roll(v, 64, len(v.shape) - 1)


def join(lo, hi):
    return jnp.where(lane_iota(lo.shape) < 64, lo, hi)


def twice(row):
    return jnp.concatenate([row, row], axis=-1)


def step_kernel(
    nd,
    n,
    x_hbm,
    cot_hbm,
    act_ref,
    noise_ref,
    game_ref,
    live_ref,
    cw_hbm,
    nm_hbm,
    tab_hbm,
    io_hbm,
    par_hbm,
    raw,
    cw_ref,
    tab_ref,
    tmp,
    xs,
    gs,
    e1,
    e2,
    esk,
    eg,
    c1,
    gsa,
    gz,
    dv,
    c3,
    gh4,
    gzc,
    gco,
    ec3,
    ec4,
    ecg,
    ecg3,
    ecy,
    ed,
    w1f,
    w1b,
    w2f,
    w2b,
    wsf,
    wsb,
    wup,
    wco,
    wdf,
    wdb,
    w3f,
    w3b,
    w4f,
    w4b,
    acc,
    prm,
    tabp,
    stat,
    hal,
    hout,
    hfull,
    hfout,
    nmv,
    nmb,
    gt_ref,
    rbuf,
    part,
    zbuf,
    zfull,
    zwhole,
    gall,
    packs,
    local_sem,
    out_sem,
    fg_sem,
    stat_send,
    stat_recv,
    halo_send,
    halo_recv,
    dp_send,
    dp_recv,
    sp_send,
    sp_recv,
):
    frames, strip = raw.shape[0], raw.shape[1]
    breadth = raw.shape[2]
    half = frames // 2
    rows = strip // 2
    cols = breadth // 2
    me = lax.axis_index("space")
    dp = lax.axis_index("dp")
    full_cells = float(strip * n * breadth * 32)
    coarse_cells = full_cells / 4.0
    owned = rows * cols
    ext = (rows + 2) * cols

    x_copy = pltpu.make_async_copy(x_hbm, raw, local_sem.at[0])
    x_copy.start()
    g_copy = pltpu.make_async_copy(cot_hbm, raw, local_sem.at[1])
    map_copies = [
        pltpu.make_async_copy(nm_hbm.at[pl.ds(0, 256), k], nmv.at[k], local_sem.at[2 + k])
        for k in range(4)
    ]
    map_copies.append(pltpu.make_async_copy(nm_hbm.at[256], nmb, local_sem.at[6]))
    map_copies.append(pltpu.make_async_copy(tab_hbm, tab_ref, local_sem.at[7]))
    weight_copy = pltpu.make_async_copy(cw_hbm, cw_ref, local_sem.at[8])
    weight_copy.start()
    for copy in map_copies:
        copy.start()

    barrier = pltpu.get_barrier_semaphore()
    for off in range(1, n):
        pl.semaphore_signal(
            barrier,
            inc=1,
            device_id={"space": lax.rem(me + off, n)},
            device_id_type=MESH,
        )
    for off in range(1, nd):
        pl.semaphore_signal(
            barrier,
            inc=1,
            device_id={"dp": lax.rem(dp + off, nd)},
            device_id_type=MESH,
        )

    def halo_copies(k, first, last, to_up, to_down):
        up = pltpu.make_async_remote_copy(
            src_ref=first,
            dst_ref=to_up,
            send_sem=halo_send.at[k, 0],
            recv_sem=halo_recv.at[k, 0],
            device_id={"space": lax.rem(me + n - 1, n)},
            device_id_type=MESH,
        )
        down = pltpu.make_async_remote_copy(
            src_ref=last,
            dst_ref=to_down,
            send_sem=halo_send.at[k, 1],
            recv_sem=halo_recv.at[k, 1],
            device_id={"space": lax.rem(me + 1, n)},
            device_id_type=MESH,
        )
        return up, down

    def halo_start(copies):
        @pl.when(me > 0)
        def _():
            copies[0].start()

        @pl.when(me < n - 1)
        def _():
            copies[1].start()

    def halo_wait(copies):
        @pl.when(me < n - 1)
        def _():
            copies[0].wait_recv()

        @pl.when(me > 0)
        def _():
            copies[1].wait_recv()

    def halo_finish(copies):
        @pl.when(me > 0)
        def _():
            copies[0].wait_send()

        @pl.when(me < n - 1)
        def _():
            copies[1].wait_send()

    def stat_copy(k, off, slots):
        return pltpu.make_async_remote_copy(
            src_ref=stat.at[k, slots],
            dst_ref=stat.at[k, slots],
            send_sem=stat_send.at[k],
            recv_sem=stat_recv.at[k],
            device_id={"space": lax.rem(me + off, n)},
            device_id_type=MESH,
        )

    def stat_start(k, value):
        stat[k, me] = value
        for off in range(1, n):
            stat_copy(k, off, me).start()

    def stat_total(k):
        peers = stat_copy(k, 1, pl.ds(0, n - 1))
        peers.wait_recv()
        total = stat[k, 0]
        for i in range(1, n):
            total = total + stat[k, i]
        peers.wait_send()
        return total

    def wide_halos(k, v):
        both = halo_copies(
            k, v.at[:, 2], v.at[:, rows + 1], v.at[:, rows + 2], v.at[:, 1]
        )
        third = halo_copies(
            k + 1,
            v.at[:, 3, :, pl.ds(0, 128)],
            v.at[:, rows, :, pl.ds(128, 128)],
            v.at[:, rows + 3, :, pl.ds(0, 128)],
            v.at[:, 0, :, pl.ds(128, 128)],
        )
        return both, third

    x_halos = wide_halos(0, xs)
    g_halos = wide_halos(8, gs)

    def coarse_halo(k):
        return halo_copies(
            k, hout.at[k - 2, 0], hout.at[k - 2, 1], hal.at[k - 2, 1], hal.at[k - 2, 0]
        )

    g_h4_halo, d_halo, c3_halo, y_halo, g_h3_halo = [coarse_halo(k) for k in range(2, 7)]
    g_h2_halos = []
    for piece in range(2):
        at = pl.ds(piece * half, half)
        g_h2_halos.append(
            halo_copies(
                7 + 3 * piece, hfout.at[0, at], hfout.at[1, at], hfull.at[1, at], hfull.at[0, at]
            )
        )

    def block_mask(shape, pad):
        blocks = shape[0]
        b = lax.broadcasted_iota(jnp.int32, shape, 0)
        low = jnp.where(me > 0, 0, pad)
        high = jnp.where(me < n - 1, blocks, blocks - pad)
        return (b >= low) & (b < high)

    def param(k, which, f):
        return prm[k * 8 + which, pl.ds(f, 1), :]

    def wide(k, which, f):
        return twice(param(k, which, f))

    def put_row(carry, f, value):
        row = lax.broadcasted_iota(jnp.int32, carry.shape, 0)
        return jnp.where(row == lax.rem(f, half), value, carry)

    def full_sum(v):
        s = jnp.sum(v.reshape(-1, 256), axis=0, keepdims=True)
        return s[:, :128] + s[:, 128:]

    def paired(raw_rows):
        count = raw_rows.shape[0]
        tmp[0:count, :, 0:64] = raw_rows.astype(F32)
        even = tmp[0:count, pl.ds(0, cols, stride=2), :]
        odd = tmp[0:count, pl.ds(1, cols, stride=2), :]
        return join(even, swap(odd))

    def pair_halves(p):
        count = p.shape[0] // 2
        p = p.reshape(count, 2, cols, 128)
        return p[:, 0], p[:, 1]

    def neighbours(v):
        count = v.shape[0]
        flat = v.reshape(count * cols, 128)
        up = pltpu.roll(flat, count * cols - 1, 0).reshape(v.shape)
        down = pltpu.roll(flat, 1, 0).reshape(v.shape)
        return up, down

    def put_e(e, f, start, h):
        count = h.shape[0]
        for part in range(2):
            v = h[:, :, part * 128 : (part + 1) * 128]
            up, down = neighbours(v)
            lane = lane_iota(v.shape)
            q = lax.broadcasted_iota(jnp.int32, v.shape, 1)
            near = jnp.where(
                lane < 64, jnp.where(q == cols - 1, 0.0, up), jnp.where(q == 0, 0.0, down)
            )
            e[f, start : start + count, :, part * 256 : part * 256 + 128] = v.astype(BF16)
            e[f, start : start + count, :, part * 256 + 128 : part * 256 + 256] = near.astype(BF16)

    def window(e, f, start, count):
        return jnp.concatenate(
            [
                e[f, start - 1 : start - 1 + count, :, 256:512],
                e[f, start : start + count, :, :],
                e[f, start + 1 : start + 1 + count, :, 0:256],
            ],
            axis=-1,
        ).reshape(count * cols, 1024)

    def own_pixels(e, f, start, count):
        return jnp.concatenate(
            [
                e[f, start : start + count, :, 0:128],
                e[f, start : start + count, :, 256:384],
            ],
            axis=-1,
        ).reshape(count * cols, 256)

    def put_ec(ec, hf, v):
        up, down = neighbours(v)
        q = lax.broadcasted_iota(jnp.int32, v.shape, 1)
        ec[hf, :, :, 0:128] = jnp.where(q == 0, 0.0, down).astype(BF16)
        ec[hf, :, :, 128:256] = v.astype(BF16)
        ec[hf, :, :, 256:384] = jnp.where(q == cols - 1, 0.0, up).astype(BF16)

    def coarse_window(ec, hf):
        return jnp.concatenate([ec[hf, a : a + rows] for a in range(3)], axis=-1).reshape(
            owned, 1152
        )

    def coarse_sum(v):
        return jnp.sum(v.reshape(-1, 128), axis=0, keepdims=True)

    def with_halo(ref, hf, k):
        ref[hf, 0] = hal[k, 0, hf].astype(F32)
        ref[hf, rows + 1] = hal[k, 1, hf].astype(F32)

    def border(ref_out, k, hf, v):
        ref_out[k, 0, hf] = v[0].astype(BF16)
        ref_out[k, 1, hf] = v[rows - 1].astype(BF16)

    def group_matrix(coarse):
        r = lax.broadcasted_iota(jnp.int32, (128, 128), 0) // 32
        c = lax.broadcasted_iota(jnp.int32, (128, 128), 1) // 32
        same = (r == c) if coarse else (r % 2 == c % 2)
        return jnp.where(same, 1.0, 0.0)

    def norm_forward(k, total, coarse, first=0):
        cells = coarse_cells if coarse else full_cells
        at = pl.ds(first, half)
        moments = dot_high(total, group_matrix(coarse)) / cells
        mean = moments[0:half]
        var = moments[half : 2 * half] - mean * mean
        rstd = lax.rsqrt(var + NORM_EPSILON)
        alpha = rstd * prm[k * 8 + GAIN, at, :]
        prm[k * 8 + ALPHA, at, :] = alpha
        prm[k * 8 + BETA, at, :] = prm[k * 8 + SHIFT, at, :] - mean * alpha
        prm[k * 8 + RSTD, at, :] = rstd
        prm[k * 8 + NMR, at, :] = -mean * rstd

    def norm_backward(k, total, coarse, first=0):
        cells = coarse_cells if coarse else full_cells
        at = pl.ds(first, half)
        gain = prm[k * 8 + GAIN, at, :]
        shift_grad = total[0:half]
        scale_grad = total[half : 2 * half]
        means = (
            dot_high(
                jnp.concatenate([shift_grad * gain, scale_grad * gain], axis=0),
                group_matrix(coarse),
            )
            / cells
        )
        rstd = prm[k * 8 + RSTD, at, :]
        factor = -rstd * means[half : 2 * half]
        prm[k * 8 + COEF, at, :] = rstd * factor
        prm[k * 8 + BIAS, at, :] = prm[k * 8 + NMR, at, :] * factor - rstd * means[0:half]
        lanes = slice(k * 128, (k + 1) * 128)
        if coarse:
            packs[dp, 0:half, lanes] = join(scale_grad, swap(shift_grad))
            packs[dp, half:frames, lanes] = join(swap(scale_grad), shift_grad)
        else:
            scale_all = scale_grad + swap(scale_grad)
            shift_all = shift_grad + swap(shift_grad)
            packs[dp, first : first + half, lanes] = join(scale_all, swap(shift_all))

    def both_halves(k, body, after=None):
        for first in (0, half):
            sums = lax.fori_loop(
                first, first + half, body, (zero_coarse, zero_coarse), unroll=4
            )
            stat_start(k + first // half, jnp.concatenate(sums, axis=0))
            if after is not None:
                after(first)

    zero_coarse = jnp.zeros((half, 128), F32)

    slots = 32 // nd
    share = 64 // n
    early = max(1, 16 // nd)
    stages = (0, 1, 2) if early > 1 else (0, 2)
    stage_slots = [pl.ds(early, slots - early), pl.ds(1, 1), pl.ds(0, 1)]

    def dp_copy(which, src, dst, off):
        return pltpu.make_async_remote_copy(
            src_ref=src,
            dst_ref=dst,
            send_sem=dp_send.at[which],
            recv_sem=dp_recv.at[which],
            device_id={"dp": lax.rem(dp + off, nd)},
            device_id_type=MESH,
        )

    def sp_copy(which, src, dst, off):
        return pltpu.make_async_remote_copy(
            src_ref=src,
            dst_ref=dst,
            send_sem=sp_send.at[which],
            recv_sem=sp_recv.at[which],
            device_id={"space": lax.rem(me + off, n)},
            device_id_type=MESH,
        )

    dp_peers, sp_peers = pl.ds(0, nd - 1), pl.ds(0, n - 1)

    def first_all(stage):
        ref = rbuf.at[dp_peers, stage_slots[stage]]
        return dp_copy(stage, ref, ref, 1)

    def last_all(stage):
        ref = gall.at[dp_peers, stage_slots[stage]]
        return dp_copy(3 + stage, ref, ref, 1)

    def pack_lanes(which):
        return pl.ds(0, 128) if which else pl.ds(128, 768)

    def pack_all(which):
        ref = packs.at[dp_peers, :, pack_lanes(which)]
        return dp_copy(6 + which, ref, ref, 1)

    def pack_start(which):
        ref = packs.at[dp, :, pack_lanes(which)]
        for off in range(1, nd):
            dp_copy(6 + which, ref, ref, off).start()

    def space_all(which):
        if which >= 2:
            ref = zwhole.at[which - 2, sp_peers]
        else:
            ref = zbuf.at[sp_peers, stage_slots[0]]
        return sp_copy(which, ref, ref, 1)

    def gather_start(stage):
        if stage not in stages:
            return
        where = stage_slots[stage]
        for off in range(1, nd):
            owner = lax.rem(dp + off, nd)
            dp_copy(stage, gt_ref.at[where, owner], rbuf.at[dp, where], off).start()

    def gather_space(stage):
        if stage not in stages:
            return
        where = stage_slots[stage]
        first_all(stage).wait_recv()
        rbuf[dp, where] = gt_ref[where, dp]
        total = rbuf[0, where].astype(F32)
        for i in range(1, nd):
            total = total + rbuf[i, where].astype(F32)
        if stage > 0:
            zwhole[stage - 1, me] = total[0]
            ref = zwhole.at[stage - 1, me]
            for off in range(1, n):
                sp_copy(stage + 1, ref, ref, off).start()
            return
        for z in range(n):
            part[z, where] = total[:, z * share : (z + 1) * share]
        for off in range(1, n):
            row = lax.rem(me + off, n)
            sp_copy(0, part.at[row, where], zbuf.at[me, where], off).start()

    def gather_spread():
        where = stage_slots[0]
        space_all(0).wait_recv()
        zbuf[me, where] = part[me, where]
        total = zbuf[0, where]
        for i in range(1, n):
            total = total + zbuf[i, where]
        zfull[me, where] = total
        for off in range(1, n):
            sp_copy(1, zfull.at[me, where], zfull.at[me, where], off).start()

    def gather_all(stage):
        if stage not in stages:
            return
        where = stage_slots[stage]
        if stage > 0:
            space_all(stage + 1).wait_recv()
            total = zwhole[stage - 1, 0]
            for i in range(1, n):
                total = total + zwhole[stage - 1, i]
            gall[dp, where] = total[None].astype(BF16)
        else:
            space_all(1).wait_recv()
            whole = jnp.concatenate([zfull[z, where] for z in range(n)], axis=1)
            gall[dp, where] = whole.astype(BF16)
        for off in range(1, nd):
            dp_copy(3 + stage, gall.at[dp, where], gall.at[dp, where], off).start()

    def gather_finish(stage):
        last_all(stage).wait_recv()
        first_all(stage).wait_send()
        last_all(stage).wait_send()
        for which in (stage + 1,) if stage > 0 else (0, 1):
            space_all(which).wait_send()

    x_copy.wait()

    def load_x(f, carry):
        total, square = carry
        even, odd = pair_halves(paired(raw[f]))
        both = jnp.concatenate([even, odd], axis=-1)
        xs[f, 2 : 2 + rows] = both.astype(BF16)
        return put_row(total, f, full_sum(both)), put_row(square, f, full_sum(both * both))

    sums = [
        lax.fori_loop(first, first + half, load_x, (zero_coarse, zero_coarse), unroll=4)
        for first in (0, half)
    ]
    g_copy.start()
    pl.semaphore_wait(barrier, n + nd - 2)
    for piece in range(2):
        stat_start(piece, jnp.concatenate(sums[piece], axis=0))
    for copies in x_halos:
        halo_start(copies)

    @pl.when(me == 0)
    def _():
        for v in (xs, gs):
            v[:, 0:2] = jnp.zeros((frames, 2, cols, 256), BF16)
        for which in range(hal.shape[0]):
            hal[which, 0] = jnp.zeros(hal.shape[2:], BF16)
        hfull[0] = jnp.zeros(hfull.shape[1:], BF16)

    @pl.when(me == n - 1)
    def _():
        for v in (xs, gs):
            v[:, rows + 2 : rows + 4] = jnp.zeros((frames, 2, cols, 256), BF16)
        for which in range(hal.shape[0]):
            hal[which, 1] = jnp.zeros(hal.shape[2:], BF16)
        hfull[1] = jnp.zeros(hfull.shape[1:], BF16)

    for v in (xs, gs):
        v[:, 0, :, 0:128] = jnp.zeros((frames, cols, 128), BF16)
        v[:, rows + 3, :, 128:256] = jnp.zeros((frames, cols, 128), BF16)

    def conditioning():
        entry = lax.broadcasted_iota(jnp.int32, (frames, 128), 1)
        row = lax.broadcasted_iota(jnp.int32, (frames, 128), 0)
        hot = jnp.zeros((frames, 128), F32)
        for f in range(frames):
            hit = (
                (entry == act_ref[f])
                | (entry == noise_ref[f] + ACTIONS)
                | (entry == game_ref[f] + ACTIONS + NOISE_LEVELS)
            )
            hot = jnp.where((row == f) & hit, 1.0, hot)
        for copy in map_copies:
            copy.wait()
        table_rows = tab_ref.shape[0]
        tabp[...] = jnp.zeros(tabp.shape, F32)
        tabp[0:table_rows, :] = tab_ref[...]
        embedded = dot_high(hot, tabp[...])
        packs[dp, :, 512:768] = embedded
        packs[dp, :, 768:896] = hot
        for k in range(4):
            mod = dot_high(embedded, nmv[k]) + nmb[k : k + 1, :]
            scale = join(mod, swap(mod)) + 1.0
            shift = join(swap(mod), mod)
            if k < 2:
                prm[k * 8 + GAIN] = scale
                prm[k * 8 + SHIFT] = shift
            else:
                prm[k * 8 + GAIN, 0:half, :] = join(scale[0:half], scale[half:])
                prm[k * 8 + SHIFT, 0:half, :] = join(shift[0:half], shift[half:])

    conditioning()

    g_copy.wait()

    def load_cotangent(f, carry):
        live = jnp.where(f < live_ref[0], 1.0, 0.0)
        even, odd = pair_halves(paired(raw[f]))
        both = jnp.concatenate([even, odd], axis=-1)
        gs[f, 2 : 2 + rows] = (both * live).astype(BF16)
        return carry

    lax.fori_loop(0, frames, load_cotangent, 0, unroll=4)
    for copies in g_halos:
        halo_start(copies)


    def tap(index):
        first = (index // 2) * 128
        last = min(first + 128, cw_ref.shape[1])
        tile = cw_ref[:, first:last].astype(BF16).astype(F32)
        if last - first < 128:
            tile = jnp.concatenate([tile, jnp.zeros((64, 128 - last + first), F32)], axis=-1)
        return tile, index % 2

    def low_half(index):
        tile, odd = tap(index)
        return swap(tile) if odd else tile

    def high_half(index):
        tile, odd = tap(index)
        return tile if odd else swap(tile)

    def lane_pair(low_index, high_index):
        zero = jnp.zeros((64, 128), F32)
        low = zero if low_index is None else low_half(low_index)
        high = zero if high_index is None else high_half(high_index)
        return join(low, high).astype(BF16)

    def fine_weights(index, forward_w, backward_w):
        zero = jnp.zeros((64, 128), BF16)
        pairs = []
        for t in range(3):
            p12 = lane_pair(index(t, 1), index(t, 2))
            p01 = lane_pair(index(t, 0), index(t, 1))
            pz0 = lane_pair(None, index(t, 0))
            p2z = lane_pair(index(t, 2), None)
            pairs.append((p12, p01, pz0, p2z))
        for a in range(4):
            for dr in range(2):
                t = a - dr
                ok = 0 <= t <= 2
                for dq in range(2):
                    r = (dr * 2 + dq) * 64
                    first = pairs[t][0 if dq == 0 else 1] if ok else zero
                    second = pairs[t][2 if dq == 0 else 3] if ok else zero
                    forward_w[r : r + 64, a * 256 : a * 256 + 128] = first
                    forward_w[r : r + 64, a * 256 + 128 : a * 256 + 256] = second
                t = 2 - a + dr
                ok = 0 <= t <= 2
                for g in range(4):
                    r = a * 256 + g * 64
                    backward_w[r : r + 64, dr * 128 : dr * 128 + 128] = (
                        pairs[t][g] if ok else zero
                    )

    def coarse_weights(index, forward_w, backward_w):
        for a in range(3):
            for j in range(3):
                lane = (a * 3 + j) * 128
                low = lane_pair(index(a, j), None)
                high = lane_pair(None, index(a, j))
                forward_w[0:64, lane : lane + 128] = low
                forward_w[64:128, lane : lane + 128] = high
                lane = ((2 - a) * 3 + (2 - j)) * 128
                backward_w[lane : lane + 64, :] = low
                backward_w[lane + 64 : lane + 128, :] = high

    def down_weights(index):
        zero = jnp.zeros((64, 128), BF16)
        wdf[...] = jnp.zeros(wdf.shape, BF16)
        wdb[...] = jnp.zeros(wdb.shape, BF16)
        for t in range(3):
            p12 = lane_pair(index(t, 1), index(t, 2))
            pz0 = lane_pair(None, index(t, 0))
            for hi in range(2):
                lane = hi * 768 + t * 256
                wdf[hi * 64 : hi * 64 + 64, lane : lane + 128] = p12
                wdf[hi * 64 : hi * 64 + 64, lane + 128 : lane + 256] = pz0
                i, dr = ((1, 1), (0, 0), (0, 1))[t]
                lane = hi * 256 + dr * 128
                for j in range(2):
                    r = (i * 2 + j) * 128 + hi * 64
                    wdb[r : r + 64, lane : lane + 128] = p12 if j == 0 else pz0

    def up_weights():
        def up_tap(ta, tb):
            return low_half(45 + (ta * 3 + tb) * 2 + 1)

        taps = [[up_tap(ta, tb) for tb in range(3)] for ta in range(3)]
        members = {(0, 0): (0,), (0, 1): (1, 2), (1, 1): (0, 1), (1, 2): (2,)}
        wup[...] = jnp.zeros(wup.shape, BF16)
        for (dr, i), in_rows in members.items():
            for (dq, j), in_cols in members.items():
                total = sum(taps[ta][tb] for ta in in_rows for tb in in_cols)
                zero = jnp.zeros_like(total)
                r = (dr * 2 + dq) * 64
                lane = (i * 3 + j) * 128
                wup[r : r + 64, lane : lane + 128] = join(total, zero).astype(BF16)
                wup[256 + r : 256 + r + 64, lane : lane + 128] = join(zero, swap(total)).astype(
                    BF16
                )
        for a in range(4):
            for g, off in enumerate((0, 1, 2, -1)):
                chosen = [
                    taps[2 - a + dr][1 - off + dq]
                    for dr in range(2)
                    for dq in range(2)
                    if 0 <= 2 - a + dr <= 2 and 0 <= 1 - off + dq <= 2
                ]
                total = sum(chosen[1:], chosen[0])
                zero = jnp.zeros_like(total)
                r = a * 256 + g * 64
                wco[0, r : r + 64, :] = join(total, zero).astype(BF16)
                wco[1, r : r + 64, :] = join(zero, swap(total)).astype(BF16)

    def stacked(k):
        return lambda t, s: k * 9 + t * 3 + s

    weight_copy.wait()
    fine_weights(stacked(0), w1f, w1b)
    fine_weights(stacked(1), w2f, w2b)
    fine_weights(lambda t, s: 45 + (t * 3 + s) * 2, wsf, wsb)
    up_weights()
    down_weights(stacked(2))
    coarse_weights(stacked(3), w3f, w3b)
    coarse_weights(stacked(4), w4f, w4b)

    for copies in x_halos:
        halo_wait(copies)
    for piece in range(2):
        norm_forward(0, stat_total(piece), False, piece * half)

    def first_layer(f, carry):
        total, square = carry
        x = xs[f].astype(F32)
        z = x * wide(0, ALPHA, f) + wide(0, BETA, f)
        h = z * logistic(z)
        h = jnp.where(block_mask(h.shape, 2), h, 0.0)
        put_e(e1, f, 0, h)
        out = dot_nt(window(e1, f, 1, rows + 2), w1f[...]).reshape(rows + 2, cols, 256)
        c1[f] = out
        own = out[1 : rows + 1]
        return put_row(total, f, full_sum(own)), put_row(square, f, full_sum(own * own))

    both_halves(2, first_layer)

    for copies in g_halos:
        halo_wait(copies)

    def load_g(f, carry):
        g = gs[f].astype(F32)
        put_e(eg, f, 0, jnp.where(block_mask(g.shape, 2), g, 0.0))
        gsa[f] = dot_nn(window(eg, f, 1, rows + 2), wsb[...]).reshape(rows + 2, cols, 256)
        return carry

    lax.fori_loop(0, frames, load_g, 0, unroll=4)

    def second_layer(f, carry):
        z = c1[f] * wide(1, ALPHA, f) + wide(1, BETA, f)
        h = z * logistic(z)
        h = jnp.where(block_mask(h.shape, 1), h, 0.0)
        edge = jnp.zeros((cols, 512), BF16)
        e2[f, 0] = edge
        e2[f, rows + 3] = edge
        put_e(e2, f, 1, h)
        out = dot_nt(window(e2, f, 1, rows + 2), w2f[...]).reshape(rows + 2, cols, 256)
        skip = out + xs[f, 1 : rows + 3].astype(F32)
        skip = jnp.where(block_mask(skip.shape, 1), skip, 0.0)
        put_e(esk, f, 1, skip)
        return carry

    for first in (0, half):
        norm_forward(1, stat_total(2 + first // half), False, first)
        lax.fori_loop(first, first + half, second_layer, 0, unroll=4)

    def down_window(f):
        return jnp.concatenate(
            [esk[f, 1 : 1 + rows, :, 256:512], esk[f, 2 : 2 + rows]], axis=-1
        ).reshape(owned, 768)

    def down_layer(hf, carry):
        total, square = carry
        d = dot_nt(down_window(hf), wdf[:, 0:768]) + dot_nt(
            down_window(hf + half), wdf[:, 768:1536]
        )
        d = d.reshape(rows, cols, 128)
        dv[hf, 1 : rows + 1] = d
        border(hout, 1, hf, d)
        return put_row(total, hf, coarse_sum(d)), put_row(square, hf, coarse_sum(d * d))

    sums = lax.fori_loop(0, half, down_layer, (zero_coarse, zero_coarse), unroll=4)
    stat_start(8, jnp.concatenate(sums, axis=0))
    halo_start(d_halo)

    def coarse_gradient(hf, carry):
        g = dot_nn(window(eg, hf, 1, rows + 2), wco[0]) + dot_nn(
            window(eg, hf + half, 1, rows + 2), wco[1]
        )
        g = g.reshape(rows + 2, cols, 128)
        g = jnp.where(block_mask(g.shape, 1), g, 0.0).astype(BF16).astype(F32)
        gco[hf] = g
        put_ec(ecg, hf, g)
        back = dot_nn(coarse_window(ecg, hf), w4b[...]).reshape(rows, cols, 128)
        gh4[hf, 1 : rows + 1] = back
        border(hout, 0, hf, back)
        return carry

    lax.fori_loop(0, half, coarse_gradient, 0, unroll=4)
    halo_start(g_h4_halo)

    def put_half(index, value):
        slot, owner = index // 2 // nd, index // 2 % nd
        current = gt_ref[slot, owner].astype(F32)
        value = join(current, swap(value)) if index % 2 else join(value, current)
        gt_ref[slot, owner] = value.astype(BF16)

    gt_ref[...] = jnp.zeros(gt_ref.shape, BF16)

    def fine_kernel_grad(index, e, start, gradient, gradient_start):
        acc[0, :, 0:1024] = jnp.zeros((256, 1024), F32)

        def add(f, carry):
            g = own_pixels(gradient, f, gradient_start, rows)
            acc[0, :, 0:1024] += dot_tn(g, window(e, f, start, rows))
            return carry

        lax.fori_loop(0, frames, add, 0, unroll=4)
        for t in range(3):
            u = []
            for dq in range(2):
                parts = [
                    acc[0, (dr * 2 + dq) * 64 : (dr * 2 + dq) * 64 + 64, pl.ds((t + dr) * 256, 256)]
                    for dr in range(2)
                ]
                u.append(parts[0] + parts[1])
            near, far = [v[:, 0:128] for v in u], [v[:, 128:256] for v in u]
            put_half(index(t, 0), swap(far[0]) + near[1])
            put_half(index(t, 1), near[0] + swap(near[1]))
            put_half(index(t, 2), swap(near[0]) + far[1])

    def coarse_kernel_grad(index, ec, gradient):
        acc[0, 0:128, :] = jnp.zeros((128, 1152), F32)

        def add(hf, carry):
            g = gradient[hf, 1 : rows + 1, :, 128:256].reshape(owned, 128)
            acc[0, 0:128, :] += dot_tn(g, coarse_window(ec, hf))
            return carry

        lax.fori_loop(0, half, add, 0, unroll=4)
        for a in range(3):
            for j in range(3):
                lanes = pl.ds((a * 3 + j) * 128, 128)
                put_half(index(a, j), acc[0, 0:64, lanes] + swap(acc[0, 64:128, lanes]))

    def down_kernel_grad(index):
        acc[:, 0:128, 0:768] = jnp.zeros((2, 128, 768), F32)

        def add(hf, carry):
            g = ed[hf, 1 : rows + 1, :, 0:128].reshape(owned, 128)
            acc[0, 0:128, 0:768] += dot_tn(g, down_window(hf))
            acc[1, 0:128, 0:768] += dot_tn(g, down_window(hf + half))
            return carry

        lax.fori_loop(0, half, add, 0, unroll=4)
        for a in range(3):
            near = acc[0, 0:64, pl.ds(a * 256, 128)] + acc[1, 64:128, pl.ds(a * 256, 128)]
            far = (
                acc[0, 0:64, pl.ds(a * 256 + 128, 128)] + acc[1, 64:128, pl.ds(a * 256 + 128, 128)]
            )
            put_half(index(a, 0), swap(far))
            put_half(index(a, 1), near)
            put_half(index(a, 2), swap(near))

    def up_kernel_grad():
        acc[...] = jnp.zeros(acc.shape, F32)

        def add(hf, carry):
            v = coarse_window(ecy, hf)
            acc[0] += dot_tn(own_pixels(eg, hf, 2, rows), v)
            acc[1] += dot_tn(own_pixels(eg, hf + half, 2, rows), v)
            return carry

        lax.fori_loop(0, half, add, 0, unroll=4)

        def block(dr, dq, i, j):
            r = (dr * 2 + dq) * 64
            lanes = pl.ds((i * 3 + j) * 128, 128)
            return acc[0, r : r + 64, lanes] + swap(acc[1, r : r + 64, lanes])

        place = {(0, 0): 0, (0, 1): 1, (0, 2): 1, (1, 0): 1, (1, 1): 1, (1, 2): 2}
        for ta in range(3):
            for tb in range(3):
                total = sum(
                    block(dr, dq, place[dr, ta], place[dq, tb])
                    for dr in range(2)
                    for dq in range(2)
                )
                put_half(45 + (ta * 3 + tb) * 2 + 1, total)


    halo_wait(d_halo)
    norm_forward(2, stat_total(8), True)

    def third_layer(hf, carry):
        total, square = carry
        with_halo(dv, hf, 1)
        z = dv[hf] * param(2, ALPHA, hf) + param(2, BETA, hf)
        h = z * logistic(z)
        put_ec(ec3, hf, jnp.where(block_mask(h.shape, 1), h, 0.0))
        out = dot_nt(coarse_window(ec3, hf), w3f[...]).reshape(rows, cols, 128)
        c3[hf, 1 : rows + 1] = out
        border(hout, 2, hf, out)
        return put_row(total, hf, coarse_sum(out)), put_row(square, hf, coarse_sum(out * out))

    sums = lax.fori_loop(0, half, third_layer, (zero_coarse, zero_coarse), unroll=4)
    stat_start(9, jnp.concatenate(sums, axis=0))
    halo_start(c3_halo)

    def result_copy(f):
        return pltpu.make_async_copy(gz.at[f, pl.ds(1, rows)], io_hbm.at[f], out_sem.at[f])

    def merge_skip(f, carry):
        out = dot_nt(window(esk, f, 2, rows), wsf[...])
        gz[f, 1 : rows + 1] = out.reshape(rows, cols, 256)
        return carry

    lax.fori_loop(0, half, merge_skip, 0, unroll=4)
    fine_kernel_grad(lambda t, s: 45 + (t * 3 + s) * 2, esk, 2, eg, 2)

    halo_wait(c3_halo)
    halo_wait(g_h4_halo)
    norm_forward(3, stat_total(9), True)

    def fourth_layer(hf, carry):
        shift, scale = carry
        with_halo(c3, hf, 2)
        with_halo(gh4, hf, 0)
        v = c3[hf]
        z = v * param(3, ALPHA, hf) + param(3, BETA, hf)
        gate = logistic(z)
        h = z * gate
        put_ec(ec4, hf, jnp.where(block_mask(h.shape, 1), h, 0.0))
        g = gh4[hf] * (gate + h * (1.0 - gate))
        gzc[hf] = g
        own = g[1 : rows + 1]
        xhat = v[1 : rows + 1] * param(3, RSTD, hf) + param(3, NMR, hf)
        return put_row(shift, hf, coarse_sum(own)), put_row(scale, hf, coarse_sum(own * xhat))

    sums = lax.fori_loop(0, half, fourth_layer, (zero_coarse, zero_coarse), unroll=4)
    stat_start(10, jnp.concatenate(sums, axis=0))

    def coarse_output(hf, carry):
        out = dot_nt(coarse_window(ec4, hf), w4f[...]).reshape(rows, cols, 128)
        y = dv[hf, 1 : rows + 1] + out
        border(hout, 3, hf, y)
        edge = jnp.zeros((1, cols, 128), F32)
        put_ec(ecy, hf, jnp.concatenate([edge, y, edge], axis=0))
        return carry

    lax.fori_loop(0, half, coarse_output, 0, unroll=4)
    halo_start(y_halo)
    coarse_kernel_grad(stacked(4), ec4, ecg)
    lax.fori_loop(half, frames, merge_skip, 0, unroll=4)

    norm_backward(3, stat_total(10), True)

    def third_back(hf, carry):
        shift, scale = carry
        g = (
            gzc[hf] * param(3, ALPHA, hf)
            + c3[hf] * param(3, COEF, hf)
            + param(3, BIAS, hf)
        )
        put_ec(ecg3, hf, jnp.where(block_mask(g.shape, 1), g, 0.0))
        back = dot_nn(coarse_window(ecg3, hf), w3b[...]).reshape(rows, cols, 128)
        border(hout, 4, hf, back)
        v = dv[hf, 1 : rows + 1]
        z = v * param(2, ALPHA, hf) + param(2, BETA, hf)
        gate = logistic(z)
        own = back * (gate + z * gate * (1.0 - gate))
        gzc[hf, 1 : rows + 1] = own
        xhat = v * param(2, RSTD, hf) + param(2, NMR, hf)
        return put_row(shift, hf, coarse_sum(own)), put_row(scale, hf, coarse_sum(own * xhat))

    sums = lax.fori_loop(0, half, third_back, (zero_coarse, zero_coarse), unroll=4)
    stat_start(11, jnp.concatenate(sums, axis=0))
    halo_start(g_h3_halo)

    halo_wait(y_halo)

    def merge(hf, carry):
        for side, row in ((0, 0), (1, rows + 1)):
            line = hal[3, side, hf].astype(F32)[None]
            up, down = neighbours(line)
            q = lax.broadcasted_iota(jnp.int32, line.shape, 1)
            ecy[hf, row, :, 0:128] = jnp.where(q == 0, 0.0, down)[0].astype(BF16)
            ecy[hf, row, :, 128:256] = line[0].astype(BF16)
            ecy[hf, row, :, 256:384] = jnp.where(q == cols - 1, 0.0, up)[0].astype(BF16)
        both = dot_nt(coarse_window(ecy, hf), wup[...])
        for hi in range(2):
            f = hf + hi * half
            up = both[:, hi * 256 : hi * 256 + 256].reshape(rows, cols, 256)
            gz[f, 1 : rows + 1] = gz[f, 1 : rows + 1] + up
            result_copy(f).start()
        return carry

    lax.fori_loop(0, half, merge, 0, unroll=4)
    coarse_kernel_grad(stacked(3), ec3, ecg3)
    up_kernel_grad()
    gather_start(0)

    halo_wait(g_h3_halo)
    norm_backward(2, stat_total(11), True)

    def down_back(hf, carry):
        for side, row in ((0, 0), (1, rows + 1)):
            v = dv[hf, row]
            z = v * param(2, ALPHA, hf) + param(2, BETA, hf)
            gate = logistic(z)
            gzc[hf, row] = hal[4, side, hf].astype(F32) * (gate + z * gate * (1.0 - gate))
        g = (
            gco[hf]
            + gzc[hf] * param(2, ALPHA, hf)
            + dv[hf] * param(2, COEF, hf)
            + param(2, BIAS, hf)
        )
        g = jnp.where(block_mask(g.shape, 1), g, 0.0)
        up, _ = neighbours(g)
        q = lax.broadcasted_iota(jnp.int32, g.shape, 1)
        ed[hf, 0 : rows + 2, :, 0:128] = g.astype(BF16)
        ed[hf, 0 : rows + 2, :, 128:256] = jnp.where(q == cols - 1, 0.0, up).astype(BF16)
        ed[hf, rows + 2] = jnp.zeros((cols, 256), BF16)
        lhs = jnp.concatenate([ed[hf, 0 : rows + 2], ed[hf, 1 : rows + 3]], axis=-1)
        back = dot_nn(lhs.reshape(ext, 512), wdb[...])
        back = back.astype(BF16).astype(F32).reshape(rows + 2, cols, 512)
        for hi in range(2):
            f = hf + hi * half
            total = gsa[f] + back[:, :, hi * 256 : hi * 256 + 256]
            gsa[f] = total
            put_e(eg, f, 0, jnp.where(block_mask(total.shape, 1), total, 0.0))
        return carry

    lax.fori_loop(0, half, down_back, 0, unroll=4)

    def second_back(f, carry):
        shift, scale = carry
        back = dot_nn(window(eg, f, 1, rows), w2b[...]).reshape(rows, cols, 256)
        hfout[0, f] = back[0, :, 0:128].astype(BF16)
        hfout[1, f] = back[rows - 1, :, 128:256].astype(BF16)
        v = c1[f, 1 : rows + 1]
        z = v * wide(1, ALPHA, f) + wide(1, BETA, f)
        gate = logistic(z)
        own = back * (gate + z * gate * (1.0 - gate))
        gz[f, 1 : rows + 1] = own
        xhat = v * wide(1, RSTD, f) + wide(1, NMR, f)
        return put_row(shift, f, full_sum(own)), put_row(scale, f, full_sum(own * xhat))

    for f in range(frames):
        result_copy(f).wait()
    both_halves(4, second_back, lambda first: halo_start(g_h2_halos[first // half]))
    down_kernel_grad(stacked(2))
    gather_space(0)
    fine_kernel_grad(stacked(1), e2, 2, eg, 1)
    gather_start(1)
    gather_spread()

    def first_gradient(f, carry):
        for side, row in ((0, 0), (1, rows + 1)):
            v = c1[f, row]
            lanes = slice(128, 256) if side == 0 else slice(0, 128)
            z = v[:, lanes] * param(1, ALPHA, f) + param(1, BETA, f)
            gate = logistic(z)
            g = hfull[side, f].astype(F32) * (gate + z * gate * (1.0 - gate))
            blank = jnp.zeros_like(g)
            gz[f, row] = jnp.concatenate([blank, g] if side == 0 else [g, blank], axis=-1)
        g = gz[f] * wide(1, ALPHA, f) + c1[f] * wide(1, COEF, f) + wide(1, BIAS, f)
        put_e(eg, f, 0, jnp.where(block_mask(g.shape, 1), g, 0.0))
        return carry

    for first in (0, half):
        halo_wait(g_h2_halos[first // half])
        norm_backward(1, stat_total(4 + first // half), False, first)
        lax.fori_loop(first, first + half, first_gradient, 0, unroll=4)
    fine_kernel_grad(stacked(0), e1, 2, eg, 1)
    gather_start(2)
    gather_all(0)
    gather_space(1)

    def first_back(f, carry):
        shift, scale = carry
        back = dot_nn(window(eg, f, 1, rows), w1b[...]).reshape(rows, cols, 256)
        v = xs[f, 2 : rows + 2].astype(F32)
        z = v * wide(0, ALPHA, f) + wide(0, BETA, f)
        gate = logistic(z)
        own = back * (gate + z * gate * (1.0 - gate))
        gz[f, 1 : rows + 1] = own
        xhat = v * wide(0, RSTD, f) + wide(0, NMR, f)
        return put_row(shift, f, full_sum(own)), put_row(scale, f, full_sum(own * xhat))

    pack_start(0)
    both_halves(6, first_back)
    gather_all(1)
    gather_space(2)

    def frames_copy(f):
        return pltpu.make_async_copy(
            gz.at[f, pl.ds(1, rows)], io_hbm.at[frames + f], fg_sem.at[f]
        )

    def frames_back(f, carry):
        gz[f, 1 : rows + 1] = (
            gsa[f, 1 : rows + 1]
            + gz[f, 1 : rows + 1] * wide(0, ALPHA, f)
            + xs[f, 2 : rows + 2].astype(F32) * wide(0, COEF, f)
            + wide(0, BIAS, f)
        )
        frames_copy(f).start()
        return carry

    norm_backward(0, stat_total(6), False)
    lax.fori_loop(0, half, frames_back, 0, unroll=4)
    norm_backward(0, stat_total(7), False, half)
    pack_start(1)
    gather_all(2)
    lax.fori_loop(half, frames, frames_back, 0, unroll=4)
    for which in range(2):
        pack_all(which).wait_recv()
        pack_all(which).wait_send()
    total_frames = nd * frames
    every = packs[...].reshape(total_frames, 896)
    embedded, hot = every[:, 512:768], every[:, 768:896]
    g_embed = 0.0
    for k in range(4):
        dmod = every[:, k * 128 : (k + 1) * 128]
        acc[1, :, k * 128 : k * 128 + 128] = lax.dot_general(
            embedded, dmod, (((0,), (0,)), ((), ())), precision=HIGH, preferred_element_type=F32
        )
        lane = 512 + k % 2 * 128
        acc[1, 128 + k // 2 : 129 + k // 2, lane : lane + 128] = jnp.sum(
            dmod, axis=0, keepdims=True
        )
        g_embed = g_embed + lax.dot_general(
            dmod, nmv[k], (((1,), (1,)), ((), ())), precision=HIGH, preferred_element_type=F32
        )
    acc[1, 0:128, 512:768] = lax.dot_general(
        hot, g_embed, (((0,), (0,)), ((), ())), precision=HIGH, preferred_element_type=F32
    )

    def par_copy(e):
        return pltpu.make_async_copy(
            acc.at[e // 4, :, pl.ds(e % 4 * 256, 256)], par_hbm.at[e], local_sem.at[e]
        )

    for e in range(4, 7):
        par_copy(e).start()
    for stage in stages:
        gather_finish(stage)
    for tile in range(32):
        row, lane = tile // 2 % 4 * 64, tile // 8 * 256 + tile % 2 * 128
        acc[0, row : row + 64, lane : lane + 128] = gall[tile % nd, tile // nd].astype(F32)
    for e in range(4):
        par_copy(e).start()

    for e in range(7):
        par_copy(e).wait()
    for f in range(frames):
        frames_copy(f).wait()
    for copies in (*x_halos, *g_halos, g_h4_halo, d_halo, c3_halo, y_halo, g_h3_halo, *g_h2_halos):
        halo_finish(copies)


def run_step(nd, n, frames, cotangent, actions, noise_ids, games, live_counts, cw, nm, table):
    count, strip, breadth, _ = frames.shape
    half, rows, cols = count // 2, strip // 2, breadth // 2
    fine = (count, rows + 4, cols, 512)
    coarse = (half, rows + 2, cols, 128)
    coarse_e = (half, rows + 2, cols, 384)
    scratch = [
        VM((count, strip, breadth, 64), BF16),
        VM(cw.shape, F32),
        VM(table.shape, F32),
        VM((strip, breadth, 128), F32),
        VM((count, rows + 4, cols, 256), BF16),
        VM((count, rows + 4, cols, 256), BF16),
        VM(fine, BF16),
        VM(fine, BF16),
        VM(fine, BF16),
        VM(fine, BF16),
        VM((count, rows + 2, cols, 256), F32),
        VM((count, rows + 2, cols, 256), F32),
        VM((count, rows + 2, cols, 256), F32),
        VM(coarse, F32),
        VM(coarse, F32),
        VM(coarse, F32),
        VM(coarse, F32),
        VM(coarse, F32),
        VM(coarse_e, BF16),
        VM(coarse_e, BF16),
        VM(coarse_e, BF16),
        VM(coarse_e, BF16),
        VM(coarse_e, BF16),
        VM((half, rows + 3, cols, 256), BF16),
        VM((256, 1024), BF16),
        VM((1024, 256), BF16),
        VM((256, 1024), BF16),
        VM((1024, 256), BF16),
        VM((256, 1024), BF16),
        VM((1024, 256), BF16),
        VM((512, 1152), BF16),
        VM((2, 1024, 128), BF16),
        VM((128, 1536), BF16),
        VM((512, 512), BF16),
        VM((128, 1152), BF16),
        VM((1152, 128), BF16),
        VM((128, 1152), BF16),
        VM((1152, 128), BF16),
        VM((2, 256, 1152), F32),
        VM((32, count, 128), F32),
        VM((128, 256), F32),
        VM((12, n, 2 * half, 128), F32),
        VM((5, 2, half, cols, 128), BF16),
        VM((5, 2, half, cols, 128), BF16),
        VM((2, count, cols, 128), BF16),
        VM((2, count, cols, 128), BF16),
        VM((4, 256, 128), F32),
        VM((4, 128), F32),
        VM((32 // nd, nd, 64, 128), BF16),
        VM((nd, 32 // nd, 64, 128), BF16),
        VM((n, 32 // nd, 64 // n, 128), F32),
        VM((n, 32 // nd, 64 // n, 128), F32),
        VM((n, 32 // nd, 64 // n, 128), F32),
        VM((2, n, 64, 128), F32),
        VM((nd, 32 // nd, 64, 128), BF16),
        VM((nd, count, 896), F32),
        pltpu.SemaphoreType.DMA((9,)),
        pltpu.SemaphoreType.DMA((count,)),
        pltpu.SemaphoreType.DMA((count,)),
        pltpu.SemaphoreType.DMA((12,)),
        pltpu.SemaphoreType.DMA((12,)),
        pltpu.SemaphoreType.DMA((11, 2)),
        pltpu.SemaphoreType.DMA((11, 2)),
        pltpu.SemaphoreType.DMA((8,)),
        pltpu.SemaphoreType.DMA((8,)),
        pltpu.SemaphoreType.DMA((4,)),
        pltpu.SemaphoreType.DMA((4,)),
    ]
    smem = pl.BlockSpec(memory_space=pltpu.SMEM)
    vmem = pl.BlockSpec(memory_space=pltpu.VMEM)
    hbm = pl.BlockSpec(memory_space=pltpu.HBM)
    return pl.pallas_call(
        functools.partial(step_kernel, nd, n),
        out_shape=(
            jax.ShapeDtypeStruct((2 * count, rows, cols, 256), F32),
            jax.ShapeDtypeStruct((7, 256, 256), F32),
        ),
        in_specs=[hbm, hbm, smem, smem, smem, smem, hbm, hbm, hbm],
        out_specs=(hbm, hbm),
        scratch_shapes=scratch,
        compiler_params=pltpu.CompilerParams(
            collective_id=0, has_side_effects=True, vmem_limit_bytes=55 * 1024 * 1024
        ),
        name="step",
    )(frames, cotangent, actions, noise_ids, games, live_counts, cw, nm, table)


def adamw(weight, moment, square, grad_value, rate):
    fix_one = 1.0 - BETA_ONE**ADAM_STEP
    fix_two = 1.0 - BETA_TWO**ADAM_STEP
    moment_new = BETA_ONE * moment + (1.0 - BETA_ONE) * grad_value
    square_new = BETA_TWO * square + (1.0 - BETA_TWO) * grad_value * grad_value
    fixed_m = moment_new / fix_one
    fixed_v = square_new / fix_two
    weight_new = weight - rate * (fixed_m / (jnp.sqrt(fixed_v) + ADAM_EPS) + DECAY * weight)
    return (moment_new, square_new, weight_new, weight_new.astype(BF16))


def finish_kernel(
    io_hbm,
    par_hbm,
    cw,
    cm,
    cv,
    nm,
    nmo,
    nsq,
    tab,
    tmo,
    tsq,
    res_out,
    fg_out,
    *refs,
):
    outs, refs = refs[:12], refs[12:]
    stages, refs = refs[:12], refs[12:]
    io, par, tmp, rs, fs, gmap, in_sem, pin_sem, fg_sem, out_sem, par_sem = refs
    frames, rows, cols = rs.shape[0], io.shape[1], io.shape[2]

    def frame_in(f):
        return pltpu.make_async_copy(io_hbm.at[f], io.at[f], in_sem.at[f])

    def par_in(e):
        return pltpu.make_async_copy(par_hbm.at[e], par.at[e], pin_sem.at[e])

    for e in range(7):
        par_in(e).start()
    for f in range(2 * frames):
        frame_in((f + frames) % (2 * frames)).start()
    out_copies = [
        pltpu.make_async_copy(stages[i], outs[i], par_sem.at[i]) for i in range(12)
    ]

    def update(first, at, weight, moment, square, grad, rate):
        new = adamw(weight, moment, square, grad, rate)
        for i in range(4):
            stages[first + i][at] = new[i]

    wide = cw.shape[1]
    for c in range(16):
        if c % 4 == 0:
            par_in(c // 4).wait()
        lanes = slice(c * 256, min(c * 256 + 256, wide))
        at = (slice(None), lanes)
        grad = par[c // 4, c % 4 * 64 : c % 4 * 64 + 64, 0 : lanes.stop - lanes.start]
        update(0, at, cw[at], cm[at], cv[at], grad, 0.05)
    for i in range(4):
        out_copies[i].start()

    def unpair(v):
        both = jnp.stack([v[:, :, 0:128], v[:, :, 128:256]], axis=1).reshape(rows * 2, cols, 128)
        tmp[:, pl.ds(0, cols, stride=2), :] = both
        tmp[:, pl.ds(1, cols, stride=2), :] = swap(both)
        return tmp[:, :, 0:64]

    def frame_copies(f):
        return (
            pltpu.make_async_copy(fs.at[f], fg_out.at[f], fg_sem.at[f]),
            pltpu.make_async_copy(rs.at[f], res_out.at[f], out_sem.at[f]),
        )

    def put_frames(f, carry):
        frame_in(frames + f).wait()
        fs[f] = unpair(io[frames + f])
        frame_copies(f)[0].start()
        return carry

    lax.fori_loop(0, frames, put_frames, 0)

    def put_result(f, carry):
        frame_in(f).wait()
        rs[f] = unpair(io[f]).astype(BF16)
        frame_copies(f)[1].start()
        return carry

    lax.fori_loop(0, frames, put_result, 0)

    for e in range(4, 7):
        par_in(e).wait()
    for k in range(4):
        lane = k % 2 * 128
        gmap[0:256, k, :] = par[4 + k // 2, :, lane : lane + 128]
        gmap[256, k : k + 1, :] = par[6, 128 + k // 2 : 129 + k // 2, lane : lane + 128]
    at = slice(None)
    update(4, at, nm[...], nmo[...], nsq[...], gmap[...], 0.04)
    for i in range(4, 8):
        out_copies[i].start()
    update(8, at, tab[...], tmo[...], tsq[...], par[6, 0 : tab.shape[0]], 0.5)
    for i in range(8, 12):
        out_copies[i].start()
    for f in range(frames):
        for copy in frame_copies(f):
            copy.wait()
    for copy in out_copies:
        copy.wait()


def run_finish(shape, io, par, conv, norm, table):
    count, strip, breadth, _ = shape
    hbm = pl.BlockSpec(memory_space=pl.ANY)
    vmem = pl.BlockSpec(memory_space=pltpu.VMEM)
    params = [
        jax.ShapeDtypeStruct(v[0].shape, dtype)
        for v in (conv, norm, table)
        for dtype in (F32, F32, F32, BF16)
    ]
    return pl.pallas_call(
        finish_kernel,
        out_shape=(
            jax.ShapeDtypeStruct(shape, BF16),
            jax.ShapeDtypeStruct(shape, F32),
            *params,
        ),
        in_specs=[hbm, hbm] + [vmem] * 9,
        out_specs=(hbm,) * 14,
        scratch_shapes=[VM(v.shape, v.dtype) for v in params]
        + [
            VM(io.shape, F32),
            VM(par.shape, F32),
            VM((strip, breadth, 128), F32),
            VM(shape, BF16),
            VM(shape, F32),
            VM(norm[0].shape, F32),
            pltpu.SemaphoreType.DMA((2 * count,)),
            pltpu.SemaphoreType.DMA((7,)),
            pltpu.SemaphoreType.DMA((count,)),
            pltpu.SemaphoreType.DMA((count,)),
            pltpu.SemaphoreType.DMA((12,)),
        ],
        compiler_params=pltpu.CompilerParams(vmem_limit_bytes=48 * 1024 * 1024),
        name="finish",
    )(io, par, *conv, *norm, *table)


def local(
    nd,
    ns,
    frames,
    cotangent,
    actions,
    noise_ids,
    games,
    live_counts,
    conv_weight,
    conv_moment,
    conv_square,
    norm_map,
    norm_moment,
    norm_square,
    emb_table,
    table_moment,
    table_square,
):
    conv = [v.T for v in (conv_weight, conv_moment, conv_square)]
    norm = [jnp.transpose(v, (1, 0, 2)) for v in (norm_map, norm_moment, norm_square)]
    table = (emb_table, table_moment, table_square)
    io, par = run_step(
        nd,
        ns,
        frames,
        cotangent,
        actions,
        noise_ids,
        games,
        live_counts,
        conv[0],
        norm[0],
        emb_table,
    )
    result, frames_grad, *new = run_finish(
        frames.shape, io, par, conv, norm, table
    )
    conv_out = [v.T for v in new[0:4]]
    norm_out = [jnp.transpose(v, (1, 0, 2)) for v in new[4:8]]
    return (result, frames_grad, *conv_out, *norm_out, *new[8:12])


def solution(mesh):
    split = P("dp", "space", None, None)
    in_specs = (split, split) + (P("dp"),) * 4 + (P(),) * 9
    out_specs = (split, split) + (P(),) * 12
    sizes = dict(mesh.shape)
    return jax.shard_map(
        functools.partial(local, sizes["dp"], sizes["space"]),
        mesh=mesh,
        in_specs=in_specs,
        out_specs=out_specs,
        check_vma=False,
    )
```

```python
import functools

import jax
import jax.numpy as jnp
from jax import lax
from jax.experimental import pallas as pl
from jax.experimental.pallas import tpu as pltpu
from jax.sharding import PartitionSpec as P

ACTIONS = 18
NOISE_LEVELS = 64
ADAM_STEP = 4
NORM_EPSILON = 1e-05
ADAM_EPS = 1e-08
BETA_ONE = 0.5
BETA_TWO = 0.5
DECAY = 0.01
HIGH = lax.Precision.HIGHEST
F32 = jnp.float32
BF16 = jnp.bfloat16
MESH = pl.DeviceIdType.MESH
VM = pltpu.VMEM

ALPHA, BETA, RSTD, NMR, GAIN, SHIFT, COEF, BIAS = range(8)


def dot_nn(a, b):
    return lax.dot_general(a, b, (((1,), (0,)), ((), ())), preferred_element_type=F32)


def dot_nt(a, b):
    return lax.dot_general(a, b, (((1,), (1,)), ((), ())), preferred_element_type=F32)


def dot_tn(a, b):
    return lax.dot_general(a, b, (((0,), (0,)), ((), ())), preferred_element_type=F32)


def dot_high(a, b):
    return lax.dot_general(
        a, b, (((1,), (0,)), ((), ())), precision=HIGH, preferred_element_type=F32
    )


def logistic(z):
    return 0.5 * jnp.tanh(0.5 * z) + 0.5


def lane_iota(shape):
    return lax.broadcasted_iota(jnp.int32, shape, len(shape) - 1)


def swap(v):
    return pltpu.roll(v, 64, len(v.shape) - 1)


def join(lo, hi):
    return jnp.where(lane_iota(lo.shape) < 64, lo, hi)


def twice(row):
    return jnp.concatenate([row, row], axis=-1)


def step_kernel(
    nd,
    n,
    x_hbm,
    cot_hbm,
    act_ref,
    noise_ref,
    game_ref,
    live_ref,
    cw_hbm,
    nm_hbm,
    tab_hbm,
    io_hbm,
    par_hbm,
    raw,
    cw_ref,
    tab_ref,
    tmp,
    xs,
    gs,
    e1,
    e2,
    esk,
    eg,
    c1,
    gsa,
    gz,
    dv,
    c3,
    gh4,
    gzc,
    gco,
    ec3,
    ec4,
    ecg,
    ecg3,
    ecy,
    ed,
    w1f,
    w1b,
    w2f,
    w2b,
    wsf,
    wsb,
    wup,
    wco,
    wdf,
    wdb,
    w3f,
    w3b,
    w4f,
    w4b,
    acc,
    prm,
    tabp,
    stat,
    hal,
    hout,
    hfull,
    hfout,
    nmv,
    nmb,
    gt_ref,
    rbuf,
    part,
    zbuf,
    zfull,
    zwhole,
    gall,
    packs,
    local_sem,
    out_sem,
    fg_sem,
    stat_send,
    stat_recv,
    halo_send,
    halo_recv,
    dp_send,
    dp_recv,
    sp_send,
    sp_recv,
):
    frames, strip = raw.shape[0], raw.shape[1]
    breadth = raw.shape[2]
    half = frames // 2
    rows = strip // 2
    cols = breadth // 2
    me = lax.axis_index("space")
    dp = lax.axis_index("dp")
    full_cells = float(strip * n * breadth * 32)
    coarse_cells = full_cells / 4.0
    owned = rows * cols
    ext = (rows + 2) * cols

    x_copy = pltpu.make_async_copy(x_hbm, raw, local_sem.at[0])
    x_copy.start()
    g_copy = pltpu.make_async_copy(cot_hbm, raw, local_sem.at[1])
    map_copies = [
        pltpu.make_async_copy(nm_hbm.at[pl.ds(0, 256), k], nmv.at[k], local_sem.at[2 + k])
        for k in range(4)
    ]
    map_copies.append(pltpu.make_async_copy(nm_hbm.at[256], nmb, local_sem.at[6]))
    map_copies.append(pltpu.make_async_copy(tab_hbm, tab_ref, local_sem.at[7]))
    weight_copy = pltpu.make_async_copy(cw_hbm, cw_ref, local_sem.at[8])
    weight_copy.start()
    for copy in map_copies:
        copy.start()

    barrier = pltpu.get_barrier_semaphore()
    for off in range(1, n):
        pl.semaphore_signal(
            barrier,
            inc=1,
            device_id={"space": lax.rem(me + off, n)},
            device_id_type=MESH,
        )
    for off in range(1, nd):
        pl.semaphore_signal(
            barrier,
            inc=1,
            device_id={"dp": lax.rem(dp + off, nd)},
            device_id_type=MESH,
        )

    def halo_copies(k, first, last, to_up, to_down):
        up = pltpu.make_async_remote_copy(
            src_ref=first,
            dst_ref=to_up,
            send_sem=halo_send.at[k, 0],
            recv_sem=halo_recv.at[k, 0],
            device_id={"space": lax.rem(me + n - 1, n)},
            device_id_type=MESH,
        )
        down = pltpu.make_async_remote_copy(
            src_ref=last,
            dst_ref=to_down,
            send_sem=halo_send.at[k, 1],
            recv_sem=halo_recv.at[k, 1],
            device_id={"space": lax.rem(me + 1, n)},
            device_id_type=MESH,
        )
        return up, down

    def halo_start(copies):
        @pl.when(me > 0)
        def _():
            copies[0].start()

        @pl.when(me < n - 1)
        def _():
            copies[1].start()

    def halo_wait(copies):
        @pl.when(me < n - 1)
        def _():
            copies[0].wait_recv()

        @pl.when(me > 0)
        def _():
            copies[1].wait_recv()

    def halo_finish(copies):
        @pl.when(me > 0)
        def _():
            copies[0].wait_send()

        @pl.when(me < n - 1)
        def _():
            copies[1].wait_send()

    def stat_copy(k, off, slots):
        return pltpu.make_async_remote_copy(
            src_ref=stat.at[k, slots],
            dst_ref=stat.at[k, slots],
            send_sem=stat_send.at[k],
            recv_sem=stat_recv.at[k],
            device_id={"space": lax.rem(me + off, n)},
            device_id_type=MESH,
        )

    def stat_start(k, value):
        stat[k, me] = value
        for off in range(1, n):
            stat_copy(k, off, me).start()

    def stat_total(k):
        peers = stat_copy(k, 1, pl.ds(0, n - 1))
        peers.wait_recv()
        total = stat[k, 0]
        for i in range(1, n):
            total = total + stat[k, i]
        peers.wait_send()
        return total

    def wide_halos(k, v):
        both = halo_copies(
            k, v.at[:, 2], v.at[:, rows + 1], v.at[:, rows + 2], v.at[:, 1]
        )
        third = halo_copies(
            k + 1,
            v.at[:, 3, :, pl.ds(0, 128)],
            v.at[:, rows, :, pl.ds(128, 128)],
            v.at[:, rows + 3, :, pl.ds(0, 128)],
            v.at[:, 0, :, pl.ds(128, 128)],
        )
        return both, third

    x_halos = wide_halos(0, xs)
    g_halos = wide_halos(8, gs)

    def coarse_halo(k):
        return halo_copies(
            k, hout.at[k - 2, 0], hout.at[k - 2, 1], hal.at[k - 2, 1], hal.at[k - 2, 0]
        )

    g_h4_halo, d_halo, c3_halo, y_halo, g_h3_halo = [coarse_halo(k) for k in range(2, 7)]
    g_h2_halo = halo_copies(7, hfout.at[0], hfout.at[1], hfull.at[1], hfull.at[0])

    def block_mask(shape, pad):
        blocks = shape[0]
        b = lax.broadcasted_iota(jnp.int32, shape, 0)
        low = jnp.where(me > 0, 0, pad)
        high = jnp.where(me < n - 1, blocks, blocks - pad)
        return (b >= low) & (b < high)

    def param(k, which, f):
        return prm[k * 8 + which, pl.ds(f, 1), :]

    def wide(k, which, f):
        return twice(param(k, which, f))

    def put_row(carry, f, value):
        row = lax.broadcasted_iota(jnp.int32, carry.shape, 0)
        return jnp.where(row == f, value, carry)

    def full_sum(v):
        s = jnp.sum(v.reshape(-1, 256), axis=0, keepdims=True)
        return s[:, :128] + s[:, 128:]

    def paired(raw_rows):
        count = raw_rows.shape[0]
        tmp[0:count, :, 0:64] = raw_rows.astype(F32)
        even = tmp[0:count, pl.ds(0, cols, stride=2), :]
        odd = tmp[0:count, pl.ds(1, cols, stride=2), :]
        return join(even, swap(odd))

    def pair_halves(p):
        count = p.shape[0] // 2
        p = p.reshape(count, 2, cols, 128)
        return p[:, 0], p[:, 1]

    def neighbours(v):
        count = v.shape[0]
        flat = v.reshape(count * cols, 128)
        up = pltpu.roll(flat, count * cols - 1, 0).reshape(v.shape)
        down = pltpu.roll(flat, 1, 0).reshape(v.shape)
        return up, down

    def put_e(e, f, start, h):
        count = h.shape[0]
        for part in range(2):
            v = h[:, :, part * 128 : (part + 1) * 128]
            up, down = neighbours(v)
            lane = lane_iota(v.shape)
            q = lax.broadcasted_iota(jnp.int32, v.shape, 1)
            near = jnp.where(
                lane < 64, jnp.where(q == cols - 1, 0.0, up), jnp.where(q == 0, 0.0, down)
            )
            e[f, start : start + count, :, part * 256 : part * 256 + 128] = v.astype(BF16)
            e[f, start : start + count, :, part * 256 + 128 : part * 256 + 256] = near.astype(BF16)

    def window(e, f, start, count):
        return jnp.concatenate(
            [
                e[f, start - 1 : start - 1 + count, :, 256:512],
                e[f, start : start + count, :, :],
                e[f, start + 1 : start + 1 + count, :, 0:256],
            ],
            axis=-1,
        ).reshape(count * cols, 1024)

    def own_pixels(e, f, start, count):
        return jnp.concatenate(
            [
                e[f, start : start + count, :, 0:128],
                e[f, start : start + count, :, 256:384],
            ],
            axis=-1,
        ).reshape(count * cols, 256)

    def put_ec(ec, hf, v):
        up, down = neighbours(v)
        q = lax.broadcasted_iota(jnp.int32, v.shape, 1)
        ec[hf, :, :, 0:128] = jnp.where(q == 0, 0.0, down).astype(BF16)
        ec[hf, :, :, 128:256] = v.astype(BF16)
        ec[hf, :, :, 256:384] = jnp.where(q == cols - 1, 0.0, up).astype(BF16)

    def coarse_window(ec, hf):
        return jnp.concatenate([ec[hf, a : a + rows] for a in range(3)], axis=-1).reshape(
            owned, 1152
        )

    def coarse_sum(v):
        return jnp.sum(v.reshape(-1, 128), axis=0, keepdims=True)

    def with_halo(ref, hf, k):
        ref[hf, 0] = hal[k, 0, hf].astype(F32)
        ref[hf, rows + 1] = hal[k, 1, hf].astype(F32)

    def border(ref_out, k, hf, v):
        ref_out[k, 0, hf] = v[0].astype(BF16)
        ref_out[k, 1, hf] = v[rows - 1].astype(BF16)

    def group_matrix(coarse):
        r = lax.broadcasted_iota(jnp.int32, (128, 128), 0) // 32
        c = lax.broadcasted_iota(jnp.int32, (128, 128), 1) // 32
        same = (r == c) if coarse else (r % 2 == c % 2)
        return jnp.where(same, 1.0, 0.0)

    def norm_forward(k, total, coarse):
        cells = coarse_cells if coarse else full_cells
        count = half if coarse else frames
        moments = dot_high(total, group_matrix(coarse)) / cells
        mean = moments[0:count]
        var = moments[count : 2 * count] - mean * mean
        rstd = lax.rsqrt(var + NORM_EPSILON)
        gain = prm[k * 8 + GAIN, 0:count, :]
        alpha = rstd * gain
        prm[k * 8 + ALPHA, 0:count, :] = alpha
        prm[k * 8 + BETA, 0:count, :] = prm[k * 8 + SHIFT, 0:count, :] - mean * alpha
        prm[k * 8 + RSTD, 0:count, :] = rstd
        prm[k * 8 + NMR, 0:count, :] = -mean * rstd

    def norm_backward(k, total, coarse):
        cells = coarse_cells if coarse else full_cells
        count = half if coarse else frames
        gain = prm[k * 8 + GAIN, 0:count, :]
        shift_grad = total[0:count]
        scale_grad = total[count : 2 * count]
        means = (
            dot_high(
                jnp.concatenate([shift_grad * gain, scale_grad * gain], axis=0),
                group_matrix(coarse),
            )
            / cells
        )
        rstd = prm[k * 8 + RSTD, 0:count, :]
        factor = -rstd * means[count : 2 * count]
        prm[k * 8 + COEF, 0:count, :] = rstd * factor
        prm[k * 8 + BIAS, 0:count, :] = (
            prm[k * 8 + NMR, 0:count, :] * factor - rstd * means[0:count]
        )
        if coarse:
            scale_all = jnp.concatenate([scale_grad, swap(scale_grad)], axis=0)
            shift_all = jnp.concatenate([shift_grad, swap(shift_grad)], axis=0)
        else:
            scale_all = scale_grad + swap(scale_grad)
            shift_all = shift_grad + swap(shift_grad)
        packs[dp, :, k * 128 : (k + 1) * 128] = join(scale_all, swap(shift_all))

    slots = 32 // nd
    share = 64 // n
    early = max(1, 16 // nd)
    stages = (0, 1, 2) if early > 1 else (0, 2)
    stage_slots = [pl.ds(early, slots - early), pl.ds(1, 1), pl.ds(0, 1)]

    def dp_copy(which, src, dst, off):
        return pltpu.make_async_remote_copy(
            src_ref=src,
            dst_ref=dst,
            send_sem=dp_send.at[which],
            recv_sem=dp_recv.at[which],
            device_id={"dp": lax.rem(dp + off, nd)},
            device_id_type=MESH,
        )

    def sp_copy(which, src, dst, off):
        return pltpu.make_async_remote_copy(
            src_ref=src,
            dst_ref=dst,
            send_sem=sp_send.at[which],
            recv_sem=sp_recv.at[which],
            device_id={"space": lax.rem(me + off, n)},
            device_id_type=MESH,
        )

    dp_peers, sp_peers = pl.ds(0, nd - 1), pl.ds(0, n - 1)

    def first_all(stage):
        ref = rbuf.at[dp_peers, stage_slots[stage]]
        return dp_copy(stage, ref, ref, 1)

    def last_all(stage):
        ref = gall.at[dp_peers, stage_slots[stage]]
        return dp_copy(3 + stage, ref, ref, 1)

    def pack_lanes(which):
        return pl.ds(0, 128) if which else pl.ds(128, 768)

    def pack_all(which):
        ref = packs.at[dp_peers, :, pack_lanes(which)]
        return dp_copy(6 + which, ref, ref, 1)

    def pack_start(which):
        ref = packs.at[dp, :, pack_lanes(which)]
        for off in range(1, nd):
            dp_copy(6 + which, ref, ref, off).start()

    def space_all(which):
        if which >= 2:
            ref = zwhole.at[which - 2, sp_peers]
        else:
            ref = zbuf.at[sp_peers, stage_slots[0]]
        return sp_copy(which, ref, ref, 1)

    def gather_start(stage):
        if stage not in stages:
            return
        where = stage_slots[stage]
        for off in range(1, nd):
            owner = lax.rem(dp + off, nd)
            dp_copy(stage, gt_ref.at[where, owner], rbuf.at[dp, where], off).start()

    def gather_space(stage):
        if stage not in stages:
            return
        where = stage_slots[stage]
        first_all(stage).wait_recv()
        rbuf[dp, where] = gt_ref[where, dp]
        total = rbuf[0, where].astype(F32)
        for i in range(1, nd):
            total = total + rbuf[i, where].astype(F32)
        if stage > 0:
            zwhole[stage - 1, me] = total[0]
            ref = zwhole.at[stage - 1, me]
            for off in range(1, n):
                sp_copy(stage + 1, ref, ref, off).start()
            return
        for z in range(n):
            part[z, where] = total[:, z * share : (z + 1) * share]
        for off in range(1, n):
            row = lax.rem(me + off, n)
            sp_copy(0, part.at[row, where], zbuf.at[me, where], off).start()

    def gather_spread():
        where = stage_slots[0]
        space_all(0).wait_recv()
        zbuf[me, where] = part[me, where]
        total = zbuf[0, where]
        for i in range(1, n):
            total = total + zbuf[i, where]
        zfull[me, where] = total
        for off in range(1, n):
            sp_copy(1, zfull.at[me, where], zfull.at[me, where], off).start()

    def gather_all(stage):
        if stage not in stages:
            return
        where = stage_slots[stage]
        if stage > 0:
            space_all(stage + 1).wait_recv()
            total = zwhole[stage - 1, 0]
            for i in range(1, n):
                total = total + zwhole[stage - 1, i]
            gall[dp, where] = total[None].astype(BF16)
        else:
            space_all(1).wait_recv()
            whole = jnp.concatenate([zfull[z, where] for z in range(n)], axis=1)
            gall[dp, where] = whole.astype(BF16)
        for off in range(1, nd):
            dp_copy(3 + stage, gall.at[dp, where], gall.at[dp, where], off).start()

    def gather_finish(stage):
        last_all(stage).wait_recv()
        first_all(stage).wait_send()
        last_all(stage).wait_send()
        for which in (stage + 1,) if stage > 0 else (0, 1):
            space_all(which).wait_send()

    x_copy.wait()

    def load_x(f, carry):
        total, square = carry
        even, odd = pair_halves(paired(raw[f]))
        both = jnp.concatenate([even, odd], axis=-1)
        xs[f, 2 : 2 + rows] = both.astype(BF16)
        return put_row(total, f, full_sum(both)), put_row(square, f, full_sum(both * both))

    zero_rows = jnp.zeros((frames, 128), F32)
    sums = lax.fori_loop(0, frames, load_x, (zero_rows, zero_rows), unroll=4)
    g_copy.start()
    pl.semaphore_wait(barrier, n + nd - 2)
    stat_start(0, jnp.concatenate(sums, axis=0))
    for copies in x_halos:
        halo_start(copies)

    @pl.when(me == 0)
    def _():
        for v in (xs, gs):
            v[:, 0:2] = jnp.zeros((frames, 2, cols, 256), BF16)
        for which in range(hal.shape[0]):
            hal[which, 0] = jnp.zeros(hal.shape[2:], BF16)
        hfull[0] = jnp.zeros(hfull.shape[1:], BF16)

    @pl.when(me == n - 1)
    def _():
        for v in (xs, gs):
            v[:, rows + 2 : rows + 4] = jnp.zeros((frames, 2, cols, 256), BF16)
        for which in range(hal.shape[0]):
            hal[which, 1] = jnp.zeros(hal.shape[2:], BF16)
        hfull[1] = jnp.zeros(hfull.shape[1:], BF16)

    for v in (xs, gs):
        v[:, 0, :, 0:128] = jnp.zeros((frames, cols, 128), BF16)
        v[:, rows + 3, :, 128:256] = jnp.zeros((frames, cols, 128), BF16)

    def conditioning():
        entry = lax.broadcasted_iota(jnp.int32, (frames, 128), 1)
        row = lax.broadcasted_iota(jnp.int32, (frames, 128), 0)
        hot = jnp.zeros((frames, 128), F32)
        for f in range(frames):
            hit = (
                (entry == act_ref[f])
                | (entry == noise_ref[f] + ACTIONS)
                | (entry == game_ref[f] + ACTIONS + NOISE_LEVELS)
            )
            hot = jnp.where((row == f) & hit, 1.0, hot)
        for copy in map_copies:
            copy.wait()
        table_rows = tab_ref.shape[0]
        tabp[...] = jnp.zeros(tabp.shape, F32)
        tabp[0:table_rows, :] = tab_ref[...]
        embedded = dot_high(hot, tabp[...])
        packs[dp, :, 512:768] = embedded
        packs[dp, :, 768:896] = hot
        for k in range(4):
            mod = dot_high(embedded, nmv[k]) + nmb[k : k + 1, :]
            scale = join(mod, swap(mod)) + 1.0
            shift = join(swap(mod), mod)
            if k < 2:
                prm[k * 8 + GAIN] = scale
                prm[k * 8 + SHIFT] = shift
            else:
                prm[k * 8 + GAIN, 0:half, :] = join(scale[0:half], scale[half:])
                prm[k * 8 + SHIFT, 0:half, :] = join(shift[0:half], shift[half:])

    conditioning()

    g_copy.wait()

    def load_cotangent(f, carry):
        live = jnp.where(f < live_ref[0], 1.0, 0.0)
        even, odd = pair_halves(paired(raw[f]))
        both = jnp.concatenate([even, odd], axis=-1)
        gs[f, 2 : 2 + rows] = (both * live).astype(BF16)
        return carry

    lax.fori_loop(0, frames, load_cotangent, 0, unroll=4)
    for copies in g_halos:
        halo_start(copies)


    def tap(index):
        first = (index // 2) * 128
        last = min(first + 128, cw_ref.shape[1])
        tile = cw_ref[:, first:last].astype(BF16).astype(F32)
        if last - first < 128:
            tile = jnp.concatenate([tile, jnp.zeros((64, 128 - last + first), F32)], axis=-1)
        return tile, index % 2

    def low_half(index):
        tile, odd = tap(index)
        return swap(tile) if odd else tile

    def high_half(index):
        tile, odd = tap(index)
        return tile if odd else swap(tile)

    def lane_pair(low_index, high_index):
        zero = jnp.zeros((64, 128), F32)
        low = zero if low_index is None else low_half(low_index)
        high = zero if high_index is None else high_half(high_index)
        return join(low, high).astype(BF16)

    def fine_weights(index, forward_w, backward_w):
        zero = jnp.zeros((64, 128), BF16)
        pairs = []
        for t in range(3):
            p12 = lane_pair(index(t, 1), index(t, 2))
            p01 = lane_pair(index(t, 0), index(t, 1))
            pz0 = lane_pair(None, index(t, 0))
            p2z = lane_pair(index(t, 2), None)
            pairs.append((p12, p01, pz0, p2z))
        for a in range(4):
            for dr in range(2):
                t = a - dr
                ok = 0 <= t <= 2
                for dq in range(2):
                    r = (dr * 2 + dq) * 64
                    first = pairs[t][0 if dq == 0 else 1] if ok else zero
                    second = pairs[t][2 if dq == 0 else 3] if ok else zero
                    forward_w[r : r + 64, a * 256 : a * 256 + 128] = first
                    forward_w[r : r + 64, a * 256 + 128 : a * 256 + 256] = second
                t = 2 - a + dr
                ok = 0 <= t <= 2
                for g in range(4):
                    r = a * 256 + g * 64
                    backward_w[r : r + 64, dr * 128 : dr * 128 + 128] = (
                        pairs[t][g] if ok else zero
                    )

    def coarse_weights(index, forward_w, backward_w):
        for a in range(3):
            for j in range(3):
                lane = (a * 3 + j) * 128
                low = lane_pair(index(a, j), None)
                high = lane_pair(None, index(a, j))
                forward_w[0:64, lane : lane + 128] = low
                forward_w[64:128, lane : lane + 128] = high
                lane = ((2 - a) * 3 + (2 - j)) * 128
                backward_w[lane : lane + 64, :] = low
                backward_w[lane + 64 : lane + 128, :] = high

    def down_weights(index):
        zero = jnp.zeros((64, 128), BF16)
        wdf[...] = jnp.zeros(wdf.shape, BF16)
        wdb[...] = jnp.zeros(wdb.shape, BF16)
        for t in range(3):
            p12 = lane_pair(index(t, 1), index(t, 2))
            pz0 = lane_pair(None, index(t, 0))
            for hi in range(2):
                lane = hi * 768 + t * 256
                wdf[hi * 64 : hi * 64 + 64, lane : lane + 128] = p12
                wdf[hi * 64 : hi * 64 + 64, lane + 128 : lane + 256] = pz0
                i, dr = ((1, 1), (0, 0), (0, 1))[t]
                lane = hi * 256 + dr * 128
                for j in range(2):
                    r = (i * 2 + j) * 128 + hi * 64
                    wdb[r : r + 64, lane : lane + 128] = p12 if j == 0 else pz0

    def up_weights():
        def up_tap(ta, tb):
            return low_half(45 + (ta * 3 + tb) * 2 + 1)

        taps = [[up_tap(ta, tb) for tb in range(3)] for ta in range(3)]
        members = {(0, 0): (0,), (0, 1): (1, 2), (1, 1): (0, 1), (1, 2): (2,)}
        wup[...] = jnp.zeros(wup.shape, BF16)
        for (dr, i), in_rows in members.items():
            for (dq, j), in_cols in members.items():
                total = sum(taps[ta][tb] for ta in in_rows for tb in in_cols)
                zero = jnp.zeros_like(total)
                r = (dr * 2 + dq) * 64
                lane = (i * 3 + j) * 128
                wup[r : r + 64, lane : lane + 128] = join(total, zero).astype(BF16)
                wup[256 + r : 256 + r + 64, lane : lane + 128] = join(zero, swap(total)).astype(
                    BF16
                )
        for a in range(4):
            for g, off in enumerate((0, 1, 2, -1)):
                chosen = [
                    taps[2 - a + dr][1 - off + dq]
                    for dr in range(2)
                    for dq in range(2)
                    if 0 <= 2 - a + dr <= 2 and 0 <= 1 - off + dq <= 2
                ]
                total = sum(chosen[1:], chosen[0])
                zero = jnp.zeros_like(total)
                r = a * 256 + g * 64
                wco[0, r : r + 64, :] = join(total, zero).astype(BF16)
                wco[1, r : r + 64, :] = join(zero, swap(total)).astype(BF16)

    def stacked(k):
        return lambda t, s: k * 9 + t * 3 + s

    weight_copy.wait()
    fine_weights(stacked(0), w1f, w1b)
    fine_weights(stacked(1), w2f, w2b)
    fine_weights(lambda t, s: 45 + (t * 3 + s) * 2, wsf, wsb)
    up_weights()
    down_weights(stacked(2))
    coarse_weights(stacked(3), w3f, w3b)
    coarse_weights(stacked(4), w4f, w4b)

    for copies in x_halos:
        halo_wait(copies)
    norm_forward(0, stat_total(0), False)

    def first_layer(f, carry):
        total, square = carry
        x = xs[f].astype(F32)
        z = x * wide(0, ALPHA, f) + wide(0, BETA, f)
        h = z * logistic(z)
        h = jnp.where(block_mask(h.shape, 2), h, 0.0)
        put_e(e1, f, 0, h)
        out = dot_nt(window(e1, f, 1, rows + 2), w1f[...]).reshape(rows + 2, cols, 256)
        c1[f] = out
        own = out[1 : rows + 1]
        return put_row(total, f, full_sum(own)), put_row(square, f, full_sum(own * own))

    sums = lax.fori_loop(0, frames, first_layer, (zero_rows, zero_rows), unroll=4)
    stat_start(1, jnp.concatenate(sums, axis=0))

    for copies in g_halos:
        halo_wait(copies)

    def load_g(f, carry):
        g = gs[f].astype(F32)
        put_e(eg, f, 0, jnp.where(block_mask(g.shape, 2), g, 0.0))
        gsa[f] = dot_nn(window(eg, f, 1, rows + 2), wsb[...]).reshape(rows + 2, cols, 256)
        return carry

    lax.fori_loop(0, frames, load_g, 0, unroll=4)

    norm_forward(1, stat_total(1), False)

    def second_layer(f, carry):
        z = c1[f] * wide(1, ALPHA, f) + wide(1, BETA, f)
        h = z * logistic(z)
        h = jnp.where(block_mask(h.shape, 1), h, 0.0)
        edge = jnp.zeros((cols, 512), BF16)
        e2[f, 0] = edge
        e2[f, rows + 3] = edge
        put_e(e2, f, 1, h)
        out = dot_nt(window(e2, f, 1, rows + 2), w2f[...]).reshape(rows + 2, cols, 256)
        skip = out + xs[f, 1 : rows + 3].astype(F32)
        skip = jnp.where(block_mask(skip.shape, 1), skip, 0.0)
        put_e(esk, f, 1, skip)
        return carry

    lax.fori_loop(0, frames, second_layer, 0, unroll=4)

    def down_window(f):
        return jnp.concatenate(
            [esk[f, 1 : 1 + rows, :, 256:512], esk[f, 2 : 2 + rows]], axis=-1
        ).reshape(owned, 768)

    zero_coarse = jnp.zeros((half, 128), F32)
    pad_rows = [jnp.zeros((2 * frames - 2 * half, 128), F32)]

    def down_layer(hf, carry):
        total, square = carry
        d = dot_nt(down_window(hf), wdf[:, 0:768]) + dot_nt(
            down_window(hf + half), wdf[:, 768:1536]
        )
        d = d.reshape(rows, cols, 128)
        dv[hf, 1 : rows + 1] = d
        border(hout, 1, hf, d)
        return put_row(total, hf, coarse_sum(d)), put_row(square, hf, coarse_sum(d * d))

    sums = lax.fori_loop(0, half, down_layer, (zero_coarse, zero_coarse), unroll=4)
    stat_start(2, jnp.concatenate(list(sums) + pad_rows, axis=0))
    halo_start(d_halo)

    def coarse_gradient(hf, carry):
        g = dot_nn(window(eg, hf, 1, rows + 2), wco[0]) + dot_nn(
            window(eg, hf + half, 1, rows + 2), wco[1]
        )
        g = g.reshape(rows + 2, cols, 128)
        g = jnp.where(block_mask(g.shape, 1), g, 0.0).astype(BF16).astype(F32)
        gco[hf] = g
        put_ec(ecg, hf, g)
        back = dot_nn(coarse_window(ecg, hf), w4b[...]).reshape(rows, cols, 128)
        gh4[hf, 1 : rows + 1] = back
        border(hout, 0, hf, back)
        return carry

    lax.fori_loop(0, half, coarse_gradient, 0, unroll=4)
    halo_start(g_h4_halo)

    def put_half(index, value):
        slot, owner = index // 2 // nd, index // 2 % nd
        current = gt_ref[slot, owner].astype(F32)
        value = join(current, swap(value)) if index % 2 else join(value, current)
        gt_ref[slot, owner] = value.astype(BF16)

    gt_ref[...] = jnp.zeros(gt_ref.shape, BF16)

    def fine_kernel_grad(index, e, start, gradient, gradient_start):
        acc[0, :, 0:1024] = jnp.zeros((256, 1024), F32)

        def add(f, carry):
            g = own_pixels(gradient, f, gradient_start, rows)
            acc[0, :, 0:1024] += dot_tn(g, window(e, f, start, rows))
            return carry

        lax.fori_loop(0, frames, add, 0, unroll=4)
        for t in range(3):
            u = []
            for dq in range(2):
                parts = [
                    acc[0, (dr * 2 + dq) * 64 : (dr * 2 + dq) * 64 + 64, pl.ds((t + dr) * 256, 256)]
                    for dr in range(2)
                ]
                u.append(parts[0] + parts[1])
            near, far = [v[:, 0:128] for v in u], [v[:, 128:256] for v in u]
            put_half(index(t, 0), swap(far[0]) + near[1])
            put_half(index(t, 1), near[0] + swap(near[1]))
            put_half(index(t, 2), swap(near[0]) + far[1])

    def coarse_kernel_grad(index, ec, gradient):
        acc[0, 0:128, :] = jnp.zeros((128, 1152), F32)

        def add(hf, carry):
            g = gradient[hf, 1 : rows + 1, :, 128:256].reshape(owned, 128)
            acc[0, 0:128, :] += dot_tn(g, coarse_window(ec, hf))
            return carry

        lax.fori_loop(0, half, add, 0, unroll=4)
        for a in range(3):
            for j in range(3):
                lanes = pl.ds((a * 3 + j) * 128, 128)
                put_half(index(a, j), acc[0, 0:64, lanes] + swap(acc[0, 64:128, lanes]))

    def down_kernel_grad(index):
        acc[:, 0:128, 0:768] = jnp.zeros((2, 128, 768), F32)

        def add(hf, carry):
            g = ed[hf, 1 : rows + 1, :, 0:128].reshape(owned, 128)
            acc[0, 0:128, 0:768] += dot_tn(g, down_window(hf))
            acc[1, 0:128, 0:768] += dot_tn(g, down_window(hf + half))
            return carry

        lax.fori_loop(0, half, add, 0, unroll=4)
        for a in range(3):
            near = acc[0, 0:64, pl.ds(a * 256, 128)] + acc[1, 64:128, pl.ds(a * 256, 128)]
            far = (
                acc[0, 0:64, pl.ds(a * 256 + 128, 128)] + acc[1, 64:128, pl.ds(a * 256 + 128, 128)]
            )
            put_half(index(a, 0), swap(far))
            put_half(index(a, 1), near)
            put_half(index(a, 2), swap(near))

    def up_kernel_grad():
        acc[...] = jnp.zeros(acc.shape, F32)

        def add(hf, carry):
            v = coarse_window(ecy, hf)
            acc[0] += dot_tn(own_pixels(eg, hf, 2, rows), v)
            acc[1] += dot_tn(own_pixels(eg, hf + half, 2, rows), v)
            return carry

        lax.fori_loop(0, half, add, 0, unroll=4)

        def block(dr, dq, i, j):
            r = (dr * 2 + dq) * 64
            lanes = pl.ds((i * 3 + j) * 128, 128)
            return acc[0, r : r + 64, lanes] + swap(acc[1, r : r + 64, lanes])

        place = {(0, 0): 0, (0, 1): 1, (0, 2): 1, (1, 0): 1, (1, 1): 1, (1, 2): 2}
        for ta in range(3):
            for tb in range(3):
                total = sum(
                    block(dr, dq, place[dr, ta], place[dq, tb])
                    for dr in range(2)
                    for dq in range(2)
                )
                put_half(45 + (ta * 3 + tb) * 2 + 1, total)


    halo_wait(d_halo)
    norm_forward(2, stat_total(2), True)

    def third_layer(hf, carry):
        total, square = carry
        with_halo(dv, hf, 1)
        z = dv[hf] * param(2, ALPHA, hf) + param(2, BETA, hf)
        h = z * logistic(z)
        put_ec(ec3, hf, jnp.where(block_mask(h.shape, 1), h, 0.0))
        out = dot_nt(coarse_window(ec3, hf), w3f[...]).reshape(rows, cols, 128)
        c3[hf, 1 : rows + 1] = out
        border(hout, 2, hf, out)
        return put_row(total, hf, coarse_sum(out)), put_row(square, hf, coarse_sum(out * out))

    sums = lax.fori_loop(0, half, third_layer, (zero_coarse, zero_coarse), unroll=4)
    stat_start(3, jnp.concatenate(list(sums) + pad_rows, axis=0))
    halo_start(c3_halo)

    def result_copy(f):
        return pltpu.make_async_copy(gz.at[f, pl.ds(1, rows)], io_hbm.at[f], out_sem.at[f])

    def merge_skip(f, carry):
        out = dot_nt(window(esk, f, 2, rows), wsf[...])
        gz[f, 1 : rows + 1] = out.reshape(rows, cols, 256)
        return carry

    lax.fori_loop(0, half, merge_skip, 0, unroll=4)
    fine_kernel_grad(lambda t, s: 45 + (t * 3 + s) * 2, esk, 2, eg, 2)

    halo_wait(c3_halo)
    halo_wait(g_h4_halo)
    norm_forward(3, stat_total(3), True)

    def fourth_layer(hf, carry):
        shift, scale = carry
        with_halo(c3, hf, 2)
        with_halo(gh4, hf, 0)
        v = c3[hf]
        z = v * param(3, ALPHA, hf) + param(3, BETA, hf)
        gate = logistic(z)
        h = z * gate
        put_ec(ec4, hf, jnp.where(block_mask(h.shape, 1), h, 0.0))
        g = gh4[hf] * (gate + h * (1.0 - gate))
        gzc[hf] = g
        own = g[1 : rows + 1]
        xhat = v[1 : rows + 1] * param(3, RSTD, hf) + param(3, NMR, hf)
        return put_row(shift, hf, coarse_sum(own)), put_row(scale, hf, coarse_sum(own * xhat))

    sums = lax.fori_loop(0, half, fourth_layer, (zero_coarse, zero_coarse), unroll=4)
    stat_start(4, jnp.concatenate(list(sums) + pad_rows, axis=0))

    def coarse_output(hf, carry):
        out = dot_nt(coarse_window(ec4, hf), w4f[...]).reshape(rows, cols, 128)
        y = dv[hf, 1 : rows + 1] + out
        border(hout, 3, hf, y)
        edge = jnp.zeros((1, cols, 128), F32)
        put_ec(ecy, hf, jnp.concatenate([edge, y, edge], axis=0))
        return carry

    lax.fori_loop(0, half, coarse_output, 0, unroll=4)
    halo_start(y_halo)
    coarse_kernel_grad(stacked(4), ec4, ecg)
    lax.fori_loop(half, frames, merge_skip, 0, unroll=4)

    norm_backward(3, stat_total(4), True)

    def third_back(hf, carry):
        shift, scale = carry
        g = (
            gzc[hf] * param(3, ALPHA, hf)
            + c3[hf] * param(3, COEF, hf)
            + param(3, BIAS, hf)
        )
        put_ec(ecg3, hf, jnp.where(block_mask(g.shape, 1), g, 0.0))
        back = dot_nn(coarse_window(ecg3, hf), w3b[...]).reshape(rows, cols, 128)
        border(hout, 4, hf, back)
        v = dv[hf, 1 : rows + 1]
        z = v * param(2, ALPHA, hf) + param(2, BETA, hf)
        gate = logistic(z)
        own = back * (gate + z * gate * (1.0 - gate))
        gzc[hf, 1 : rows + 1] = own
        xhat = v * param(2, RSTD, hf) + param(2, NMR, hf)
        return put_row(shift, hf, coarse_sum(own)), put_row(scale, hf, coarse_sum(own * xhat))

    sums = lax.fori_loop(0, half, third_back, (zero_coarse, zero_coarse), unroll=4)
    stat_start(5, jnp.concatenate(list(sums) + pad_rows, axis=0))
    halo_start(g_h3_halo)

    halo_wait(y_halo)

    def merge(hf, carry):
        for side, row in ((0, 0), (1, rows + 1)):
            line = hal[3, side, hf].astype(F32)[None]
            up, down = neighbours(line)
            q = lax.broadcasted_iota(jnp.int32, line.shape, 1)
            ecy[hf, row, :, 0:128] = jnp.where(q == 0, 0.0, down)[0].astype(BF16)
            ecy[hf, row, :, 128:256] = line[0].astype(BF16)
            ecy[hf, row, :, 256:384] = jnp.where(q == cols - 1, 0.0, up)[0].astype(BF16)
        both = dot_nt(coarse_window(ecy, hf), wup[...])
        for hi in range(2):
            f = hf + hi * half
            up = both[:, hi * 256 : hi * 256 + 256].reshape(rows, cols, 256)
            gz[f, 1 : rows + 1] = gz[f, 1 : rows + 1] + up
            result_copy(f).start()
        return carry

    lax.fori_loop(0, half, merge, 0, unroll=4)
    coarse_kernel_grad(stacked(3), ec3, ecg3)
    up_kernel_grad()
    gather_start(0)

    halo_wait(g_h3_halo)
    norm_backward(2, stat_total(5), True)

    def down_back(hf, carry):
        for side, row in ((0, 0), (1, rows + 1)):
            v = dv[hf, row]
            z = v * param(2, ALPHA, hf) + param(2, BETA, hf)
            gate = logistic(z)
            gzc[hf, row] = hal[4, side, hf].astype(F32) * (gate + z * gate * (1.0 - gate))
        g = (
            gco[hf]
            + gzc[hf] * param(2, ALPHA, hf)
            + dv[hf] * param(2, COEF, hf)
            + param(2, BIAS, hf)
        )
        g = jnp.where(block_mask(g.shape, 1), g, 0.0)
        up, _ = neighbours(g)
        q = lax.broadcasted_iota(jnp.int32, g.shape, 1)
        ed[hf, 0 : rows + 2, :, 0:128] = g.astype(BF16)
        ed[hf, 0 : rows + 2, :, 128:256] = jnp.where(q == cols - 1, 0.0, up).astype(BF16)
        ed[hf, rows + 2] = jnp.zeros((cols, 256), BF16)
        lhs = jnp.concatenate([ed[hf, 0 : rows + 2], ed[hf, 1 : rows + 3]], axis=-1)
        back = dot_nn(lhs.reshape(ext, 512), wdb[...])
        back = back.astype(BF16).astype(F32).reshape(rows + 2, cols, 512)
        for hi in range(2):
            f = hf + hi * half
            total = gsa[f] + back[:, :, hi * 256 : hi * 256 + 256]
            gsa[f] = total
            put_e(eg, f, 0, jnp.where(block_mask(total.shape, 1), total, 0.0))
        return carry

    lax.fori_loop(0, half, down_back, 0, unroll=4)

    def second_back(f, carry):
        shift, scale = carry
        back = dot_nn(window(eg, f, 1, rows), w2b[...]).reshape(rows, cols, 256)
        hfout[0, f] = back[0, :, 0:128].astype(BF16)
        hfout[1, f] = back[rows - 1, :, 128:256].astype(BF16)
        v = c1[f, 1 : rows + 1]
        z = v * wide(1, ALPHA, f) + wide(1, BETA, f)
        gate = logistic(z)
        own = back * (gate + z * gate * (1.0 - gate))
        gz[f, 1 : rows + 1] = own
        xhat = v * wide(1, RSTD, f) + wide(1, NMR, f)
        return put_row(shift, f, full_sum(own)), put_row(scale, f, full_sum(own * xhat))

    for f in range(frames):
        result_copy(f).wait()
    sums = lax.fori_loop(0, frames, second_back, (zero_rows, zero_rows), unroll=4)
    stat_start(6, jnp.concatenate(sums, axis=0))
    halo_start(g_h2_halo)
    down_kernel_grad(stacked(2))
    gather_space(0)
    fine_kernel_grad(stacked(1), e2, 2, eg, 1)
    gather_start(1)
    gather_spread()
    halo_wait(g_h2_halo)
    norm_backward(1, stat_total(6), False)

    def first_gradient(f, carry):
        for side, row in ((0, 0), (1, rows + 1)):
            v = c1[f, row]
            lanes = slice(128, 256) if side == 0 else slice(0, 128)
            z = v[:, lanes] * param(1, ALPHA, f) + param(1, BETA, f)
            gate = logistic(z)
            g = hfull[side, f].astype(F32) * (gate + z * gate * (1.0 - gate))
            blank = jnp.zeros_like(g)
            gz[f, row] = jnp.concatenate([blank, g] if side == 0 else [g, blank], axis=-1)
        g = gz[f] * wide(1, ALPHA, f) + c1[f] * wide(1, COEF, f) + wide(1, BIAS, f)
        put_e(eg, f, 0, jnp.where(block_mask(g.shape, 1), g, 0.0))
        return carry

    lax.fori_loop(0, frames, first_gradient, 0, unroll=4)
    fine_kernel_grad(stacked(0), e1, 2, eg, 1)
    gather_start(2)
    gather_all(0)
    gather_space(1)

    def first_back(f, carry):
        shift, scale = carry
        back = dot_nn(window(eg, f, 1, rows), w1b[...]).reshape(rows, cols, 256)
        v = xs[f, 2 : rows + 2].astype(F32)
        z = v * wide(0, ALPHA, f) + wide(0, BETA, f)
        gate = logistic(z)
        own = back * (gate + z * gate * (1.0 - gate))
        gz[f, 1 : rows + 1] = own
        xhat = v * wide(0, RSTD, f) + wide(0, NMR, f)
        return put_row(shift, f, full_sum(own)), put_row(scale, f, full_sum(own * xhat))

    pack_start(0)
    sums = lax.fori_loop(0, frames, first_back, (zero_rows, zero_rows), unroll=4)
    stat_start(7, jnp.concatenate(sums, axis=0))
    gather_all(1)
    gather_space(2)
    norm_backward(0, stat_total(7), False)
    pack_start(1)
    gather_all(2)

    def frames_copy(f):
        return pltpu.make_async_copy(
            gz.at[f, pl.ds(1, rows)], io_hbm.at[frames + f], fg_sem.at[f]
        )

    def frames_back(f, carry):
        gz[f, 1 : rows + 1] = (
            gsa[f, 1 : rows + 1]
            + gz[f, 1 : rows + 1] * wide(0, ALPHA, f)
            + xs[f, 2 : rows + 2].astype(F32) * wide(0, COEF, f)
            + wide(0, BIAS, f)
        )
        frames_copy(f).start()
        return carry

    lax.fori_loop(0, frames, frames_back, 0, unroll=4)
    for which in range(2):
        pack_all(which).wait_recv()
        pack_all(which).wait_send()
    total_frames = nd * frames
    every = packs[...].reshape(total_frames, 896)
    embedded, hot = every[:, 512:768], every[:, 768:896]
    g_embed = 0.0
    for k in range(4):
        dmod = every[:, k * 128 : (k + 1) * 128]
        acc[1, :, k * 128 : k * 128 + 128] = lax.dot_general(
            embedded, dmod, (((0,), (0,)), ((), ())), precision=HIGH, preferred_element_type=F32
        )
        lane = 512 + k % 2 * 128
        acc[1, 128 + k // 2 : 129 + k // 2, lane : lane + 128] = jnp.sum(
            dmod, axis=0, keepdims=True
        )
        g_embed = g_embed + lax.dot_general(
            dmod, nmv[k], (((1,), (1,)), ((), ())), precision=HIGH, preferred_element_type=F32
        )
    acc[1, 0:128, 512:768] = lax.dot_general(
        hot, g_embed, (((0,), (0,)), ((), ())), precision=HIGH, preferred_element_type=F32
    )

    def par_copy(e):
        return pltpu.make_async_copy(
            acc.at[e // 4, :, pl.ds(e % 4 * 256, 256)], par_hbm.at[e], local_sem.at[e]
        )

    for e in range(4, 7):
        par_copy(e).start()
    for stage in stages:
        gather_finish(stage)
    for tile in range(32):
        row, lane = tile // 2 % 4 * 64, tile // 8 * 256 + tile % 2 * 128
        acc[0, row : row + 64, lane : lane + 128] = gall[tile % nd, tile // nd].astype(F32)
    for e in range(4):
        par_copy(e).start()

    for e in range(7):
        par_copy(e).wait()
    for f in range(frames):
        frames_copy(f).wait()
    for copies in (*x_halos, *g_halos, g_h4_halo, d_halo, c3_halo, y_halo, g_h3_halo, g_h2_halo):
        halo_finish(copies)


def run_step(nd, n, frames, cotangent, actions, noise_ids, games, live_counts, cw, nm, table):
    count, strip, breadth, _ = frames.shape
    half, rows, cols = count // 2, strip // 2, breadth // 2
    fine = (count, rows + 4, cols, 512)
    coarse = (half, rows + 2, cols, 128)
    coarse_e = (half, rows + 2, cols, 384)
    scratch = [
        VM((count, strip, breadth, 64), BF16),
        VM(cw.shape, F32),
        VM(table.shape, F32),
        VM((strip, breadth, 128), F32),
        VM((count, rows + 4, cols, 256), BF16),
        VM((count, rows + 4, cols, 256), BF16),
        VM(fine, BF16),
        VM(fine, BF16),
        VM(fine, BF16),
        VM(fine, BF16),
        VM((count, rows + 2, cols, 256), F32),
        VM((count, rows + 2, cols, 256), F32),
        VM((count, rows + 2, cols, 256), F32),
        VM(coarse, F32),
        VM(coarse, F32),
        VM(coarse, F32),
        VM(coarse, F32),
        VM(coarse, F32),
        VM(coarse_e, BF16),
        VM(coarse_e, BF16),
        VM(coarse_e, BF16),
        VM(coarse_e, BF16),
        VM(coarse_e, BF16),
        VM((half, rows + 3, cols, 256), BF16),
        VM((256, 1024), BF16),
        VM((1024, 256), BF16),
        VM((256, 1024), BF16),
        VM((1024, 256), BF16),
        VM((256, 1024), BF16),
        VM((1024, 256), BF16),
        VM((512, 1152), BF16),
        VM((2, 1024, 128), BF16),
        VM((128, 1536), BF16),
        VM((512, 512), BF16),
        VM((128, 1152), BF16),
        VM((1152, 128), BF16),
        VM((128, 1152), BF16),
        VM((1152, 128), BF16),
        VM((2, 256, 1152), F32),
        VM((32, count, 128), F32),
        VM((128, 256), F32),
        VM((8, n, 2 * count, 128), F32),
        VM((5, 2, half, cols, 128), BF16),
        VM((5, 2, half, cols, 128), BF16),
        VM((2, count, cols, 128), BF16),
        VM((2, count, cols, 128), BF16),
        VM((4, 256, 128), F32),
        VM((4, 128), F32),
        VM((32 // nd, nd, 64, 128), BF16),
        VM((nd, 32 // nd, 64, 128), BF16),
        VM((n, 32 // nd, 64 // n, 128), F32),
        VM((n, 32 // nd, 64 // n, 128), F32),
        VM((n, 32 // nd, 64 // n, 128), F32),
        VM((2, n, 64, 128), F32),
        VM((nd, 32 // nd, 64, 128), BF16),
        VM((nd, count, 896), F32),
        pltpu.SemaphoreType.DMA((9,)),
        pltpu.SemaphoreType.DMA((count,)),
        pltpu.SemaphoreType.DMA((count,)),
        pltpu.SemaphoreType.DMA((8,)),
        pltpu.SemaphoreType.DMA((8,)),
        pltpu.SemaphoreType.DMA((10, 2)),
        pltpu.SemaphoreType.DMA((10, 2)),
        pltpu.SemaphoreType.DMA((8,)),
        pltpu.SemaphoreType.DMA((8,)),
        pltpu.SemaphoreType.DMA((4,)),
        pltpu.SemaphoreType.DMA((4,)),
    ]
    smem = pl.BlockSpec(memory_space=pltpu.SMEM)
    vmem = pl.BlockSpec(memory_space=pltpu.VMEM)
    hbm = pl.BlockSpec(memory_space=pltpu.HBM)
    return pl.pallas_call(
        functools.partial(step_kernel, nd, n),
        out_shape=(
            jax.ShapeDtypeStruct((2 * count, rows, cols, 256), F32),
            jax.ShapeDtypeStruct((7, 256, 256), F32),
        ),
        in_specs=[hbm, hbm, smem, smem, smem, smem, hbm, hbm, hbm],
        out_specs=(hbm, hbm),
        scratch_shapes=scratch,
        compiler_params=pltpu.CompilerParams(
            collective_id=0, has_side_effects=True, vmem_limit_bytes=55 * 1024 * 1024
        ),
        name="step",
    )(frames, cotangent, actions, noise_ids, games, live_counts, cw, nm, table)


def adamw(weight, moment, square, grad_value, rate):
    fix_one = 1.0 - BETA_ONE**ADAM_STEP
    fix_two = 1.0 - BETA_TWO**ADAM_STEP
    moment_new = BETA_ONE * moment + (1.0 - BETA_ONE) * grad_value
    square_new = BETA_TWO * square + (1.0 - BETA_TWO) * grad_value * grad_value
    fixed_m = moment_new / fix_one
    fixed_v = square_new / fix_two
    weight_new = weight - rate * (fixed_m / (jnp.sqrt(fixed_v) + ADAM_EPS) + DECAY * weight)
    return (moment_new, square_new, weight_new, weight_new.astype(BF16))


def finish_kernel(
    io_hbm,
    par_hbm,
    cw,
    cm,
    cv,
    nm,
    nmo,
    nsq,
    tab,
    tmo,
    tsq,
    res_out,
    fg_out,
    *refs,
):
    outs, refs = refs[:12], refs[12:]
    stages, refs = refs[:12], refs[12:]
    io, par, tmp, rs, fs, gmap, in_sem, pin_sem, fg_sem, out_sem, par_sem = refs
    frames, rows, cols = rs.shape[0], io.shape[1], io.shape[2]

    def frame_in(f):
        return pltpu.make_async_copy(io_hbm.at[f], io.at[f], in_sem.at[f])

    def par_in(e):
        return pltpu.make_async_copy(par_hbm.at[e], par.at[e], pin_sem.at[e])

    for e in range(7):
        par_in(e).start()
    for f in range(2 * frames):
        frame_in((f + frames) % (2 * frames)).start()
    out_copies = [
        pltpu.make_async_copy(stages[i], outs[i], par_sem.at[i]) for i in range(12)
    ]

    def update(first, at, weight, moment, square, grad, rate):
        new = adamw(weight, moment, square, grad, rate)
        for i in range(4):
            stages[first + i][at] = new[i]

    wide = cw.shape[1]
    for c in range(16):
        if c % 4 == 0:
            par_in(c // 4).wait()
        lanes = slice(c * 256, min(c * 256 + 256, wide))
        at = (slice(None), lanes)
        grad = par[c // 4, c % 4 * 64 : c % 4 * 64 + 64, 0 : lanes.stop - lanes.start]
        update(0, at, cw[at], cm[at], cv[at], grad, 0.05)
    for i in range(4):
        out_copies[i].start()

    def unpair(v):
        both = jnp.stack([v[:, :, 0:128], v[:, :, 128:256]], axis=1).reshape(rows * 2, cols, 128)
        tmp[:, pl.ds(0, cols, stride=2), :] = both
        tmp[:, pl.ds(1, cols, stride=2), :] = swap(both)
        return tmp[:, :, 0:64]

    def frame_copies(f):
        return (
            pltpu.make_async_copy(fs.at[f], fg_out.at[f], fg_sem.at[f]),
            pltpu.make_async_copy(rs.at[f], res_out.at[f], out_sem.at[f]),
        )

    def put_frames(f, carry):
        frame_in(frames + f).wait()
        fs[f] = unpair(io[frames + f])
        frame_copies(f)[0].start()
        return carry

    lax.fori_loop(0, frames, put_frames, 0)

    def put_result(f, carry):
        frame_in(f).wait()
        rs[f] = unpair(io[f]).astype(BF16)
        frame_copies(f)[1].start()
        return carry

    lax.fori_loop(0, frames, put_result, 0)

    for e in range(4, 7):
        par_in(e).wait()
    for k in range(4):
        lane = k % 2 * 128
        gmap[0:256, k, :] = par[4 + k // 2, :, lane : lane + 128]
        gmap[256, k : k + 1, :] = par[6, 128 + k // 2 : 129 + k // 2, lane : lane + 128]
    at = slice(None)
    update(4, at, nm[...], nmo[...], nsq[...], gmap[...], 0.04)
    for i in range(4, 8):
        out_copies[i].start()
    update(8, at, tab[...], tmo[...], tsq[...], par[6, 0 : tab.shape[0]], 0.5)
    for i in range(8, 12):
        out_copies[i].start()
    for f in range(frames):
        for copy in frame_copies(f):
            copy.wait()
    for copy in out_copies:
        copy.wait()


def run_finish(shape, io, par, conv, norm, table):
    count, strip, breadth, _ = shape
    hbm = pl.BlockSpec(memory_space=pl.ANY)
    vmem = pl.BlockSpec(memory_space=pltpu.VMEM)
    params = [
        jax.ShapeDtypeStruct(v[0].shape, dtype)
        for v in (conv, norm, table)
        for dtype in (F32, F32, F32, BF16)
    ]
    return pl.pallas_call(
        finish_kernel,
        out_shape=(
            jax.ShapeDtypeStruct(shape, BF16),
            jax.ShapeDtypeStruct(shape, F32),
            *params,
        ),
        in_specs=[hbm, hbm] + [vmem] * 9,
        out_specs=(hbm,) * 14,
        scratch_shapes=[VM(v.shape, v.dtype) for v in params]
        + [
            VM(io.shape, F32),
            VM(par.shape, F32),
            VM((strip, breadth, 128), F32),
            VM(shape, BF16),
            VM(shape, F32),
            VM(norm[0].shape, F32),
            pltpu.SemaphoreType.DMA((2 * count,)),
            pltpu.SemaphoreType.DMA((7,)),
            pltpu.SemaphoreType.DMA((count,)),
            pltpu.SemaphoreType.DMA((count,)),
            pltpu.SemaphoreType.DMA((12,)),
        ],
        compiler_params=pltpu.CompilerParams(vmem_limit_bytes=48 * 1024 * 1024),
        name="finish",
    )(io, par, *conv, *norm, *table)


def local(
    nd,
    ns,
    frames,
    cotangent,
    actions,
    noise_ids,
    games,
    live_counts,
    conv_weight,
    conv_moment,
    conv_square,
    norm_map,
    norm_moment,
    norm_square,
    emb_table,
    table_moment,
    table_square,
):
    conv = [v.T for v in (conv_weight, conv_moment, conv_square)]
    norm = [jnp.transpose(v, (1, 0, 2)) for v in (norm_map, norm_moment, norm_square)]
    table = (emb_table, table_moment, table_square)
    io, par = run_step(
        nd,
        ns,
        frames,
        cotangent,
        actions,
        noise_ids,
        games,
        live_counts,
        conv[0],
        norm[0],
        emb_table,
    )
    result, frames_grad, *new = run_finish(
        frames.shape, io, par, conv, norm, table
    )
    conv_out = [v.T for v in new[0:4]]
    norm_out = [jnp.transpose(v, (1, 0, 2)) for v in new[4:8]]
    return (result, frames_grad, *conv_out, *norm_out, *new[8:12])


def solution(mesh):
    split = P("dp", "space", None, None)
    in_specs = (split, split) + (P("dp"),) * 4 + (P(),) * 9
    out_specs = (split, split) + (P(),) * 12
    sizes = dict(mesh.shape)
    return jax.shard_map(
        functools.partial(local, sizes["dp"], sizes["space"]),
        mesh=mesh,
        in_specs=in_specs,
        out_specs=out_specs,
        check_vma=False,
    )
```

```python
import functools

import jax
import jax.numpy as jnp
from jax import lax
from jax.experimental import pallas as pl
from jax.experimental.pallas import tpu as pltpu
from jax.sharding import PartitionSpec as P

ACTIONS = 18
NOISE_LEVELS = 64
ADAM_STEP = 4
NORM_EPSILON = 1e-05
ADAM_EPS = 1e-08
BETA_ONE = 0.5
BETA_TWO = 0.5
DECAY = 0.01
HIGH = lax.Precision.HIGHEST
F32 = jnp.float32
BF16 = jnp.bfloat16
MESH = pl.DeviceIdType.MESH
VM = pltpu.VMEM

ALPHA, BETA, RSTD, NMR, GAIN, SHIFT, COEF, BIAS = range(8)


def dot_nn(a, b):
    return lax.dot_general(a, b, (((1,), (0,)), ((), ())), preferred_element_type=F32)


def dot_nt(a, b):
    return lax.dot_general(a, b, (((1,), (1,)), ((), ())), preferred_element_type=F32)


def dot_tn(a, b):
    return lax.dot_general(a, b, (((0,), (0,)), ((), ())), preferred_element_type=F32)


def dot_high(a, b):
    return lax.dot_general(
        a, b, (((1,), (0,)), ((), ())), precision=HIGH, preferred_element_type=F32
    )


def logistic(z):
    return 0.5 * jnp.tanh(0.5 * z) + 0.5


def lane_iota(shape):
    return lax.broadcasted_iota(jnp.int32, shape, len(shape) - 1)


def swap(v):
    return pltpu.roll(v, 64, len(v.shape) - 1)


def join(lo, hi):
    return jnp.where(lane_iota(lo.shape) < 64, lo, hi)


def twice(row):
    return jnp.concatenate([row, row], axis=-1)


def step_kernel(
    nd,
    n,
    x_hbm,
    cot_hbm,
    act_hbm,
    noise_hbm,
    game_hbm,
    live_hbm,
    cw_hbm,
    nm_hbm,
    tab_hbm,
    io_hbm,
    par_hbm,
    gall_hbm,
    act_ref,
    noise_ref,
    game_ref,
    live_ref,
    raw,
    cw_ref,
    tab_ref,
    tmp,
    xs,
    gs,
    e1,
    e2,
    esk,
    eg,
    c1,
    gsa,
    gz,
    dv,
    c3,
    gh4,
    gzc,
    gco,
    ec3,
    ec4,
    ecg,
    ecg3,
    ecy,
    ed,
    w1f,
    w1b,
    w2f,
    w2b,
    wsf,
    wsb,
    wup,
    wco,
    wdf,
    wdb,
    w3f,
    w3b,
    w4f,
    w4b,
    acc,
    prm,
    tabp,
    stat,
    hal,
    hout,
    hfull,
    hfout,
    nmv,
    nmb,
    gt_ref,
    rbuf,
    part,
    zbuf,
    zfull,
    zwhole,
    gown,
    packs,
    local_sem,
    out_sem,
    fg_sem,
    stat_send,
    stat_recv,
    halo_send,
    halo_recv,
    dp_send,
    dp_recv,
    sp_send,
    sp_recv,
    own_sem,
):
    frames, strip = raw.shape[0], raw.shape[1]
    breadth = raw.shape[2]
    half = frames // 2
    rows = strip // 2
    cols = breadth // 2
    me = lax.axis_index("space")
    dp = lax.axis_index("dp")
    full_cells = float(strip * n * breadth * 32)
    coarse_cells = full_cells / 4.0
    owned = rows * cols
    ext = (rows + 2) * cols

    x_copy = pltpu.make_async_copy(x_hbm, raw, local_sem.at[0])
    x_copy.start()
    g_copy = pltpu.make_async_copy(cot_hbm, raw, local_sem.at[1])
    map_copies = [
        pltpu.make_async_copy(nm_hbm.at[pl.ds(0, 256), k], nmv.at[k], local_sem.at[2 + k])
        for k in range(4)
    ]
    map_copies.append(pltpu.make_async_copy(nm_hbm.at[256], nmb, local_sem.at[6]))
    map_copies.append(pltpu.make_async_copy(tab_hbm, tab_ref, local_sem.at[7]))
    ids = ((act_hbm, act_ref), (noise_hbm, noise_ref), (game_hbm, game_ref), (live_hbm, live_ref))
    for i, (there, here) in enumerate(ids):
        map_copies.append(pltpu.make_async_copy(there, here, local_sem.at[9 + i]))
    weight_copy = pltpu.make_async_copy(cw_hbm, cw_ref, local_sem.at[8])
    weight_copy.start()
    for copy in map_copies:
        copy.start()

    barrier = pltpu.get_barrier_semaphore()
    for off in range(1, n):
        pl.semaphore_signal(
            barrier,
            inc=1,
            device_id={"space": lax.rem(me + off, n)},
            device_id_type=MESH,
        )
    for off in range(1, nd):
        pl.semaphore_signal(
            barrier,
            inc=1,
            device_id={"dp": lax.rem(dp + off, nd)},
            device_id_type=MESH,
        )

    def halo_copies(k, first, last, to_up, to_down):
        up = pltpu.make_async_remote_copy(
            src_ref=first,
            dst_ref=to_up,
            send_sem=halo_send.at[k, 0],
            recv_sem=halo_recv.at[k, 0],
            device_id={"space": lax.rem(me + n - 1, n)},
            device_id_type=MESH,
        )
        down = pltpu.make_async_remote_copy(
            src_ref=last,
            dst_ref=to_down,
            send_sem=halo_send.at[k, 1],
            recv_sem=halo_recv.at[k, 1],
            device_id={"space": lax.rem(me + 1, n)},
            device_id_type=MESH,
        )
        return up, down

    def halo_start(copies):
        @pl.when(me > 0)
        def _():
            copies[0].start()

        @pl.when(me < n - 1)
        def _():
            copies[1].start()

    def halo_wait(copies):
        @pl.when(me < n - 1)
        def _():
            copies[0].wait_recv()

        @pl.when(me > 0)
        def _():
            copies[1].wait_recv()

    def halo_finish(copies):
        @pl.when(me > 0)
        def _():
            copies[0].wait_send()

        @pl.when(me < n - 1)
        def _():
            copies[1].wait_send()

    def stat_copy(k, off, slots):
        return pltpu.make_async_remote_copy(
            src_ref=stat.at[k, slots],
            dst_ref=stat.at[k, slots],
            send_sem=stat_send.at[k],
            recv_sem=stat_recv.at[k],
            device_id={"space": lax.rem(me + off, n)},
            device_id_type=MESH,
        )

    def stat_start(k, value):
        stat[k, me] = value
        for off in range(1, n):
            stat_copy(k, off, me).start()

    def stat_total(k):
        peers = stat_copy(k, 1, pl.ds(0, n - 1))
        peers.wait_recv()
        total = stat[k, 0]
        for i in range(1, n):
            total = total + stat[k, i]
        peers.wait_send()
        return total

    def wide_halos(k, v):
        both = halo_copies(
            k, v.at[:, 2], v.at[:, rows + 1], v.at[:, rows + 2], v.at[:, 1]
        )
        third = halo_copies(
            k + 1,
            v.at[:, 3, :, pl.ds(0, 128)],
            v.at[:, rows, :, pl.ds(128, 128)],
            v.at[:, rows + 3, :, pl.ds(0, 128)],
            v.at[:, 0, :, pl.ds(128, 128)],
        )
        return both, third

    x_halos = wide_halos(0, xs)
    g_halos = wide_halos(8, gs)

    def coarse_halo(k):
        return halo_copies(
            k, hout.at[k - 2, 0], hout.at[k - 2, 1], hal.at[k - 2, 1], hal.at[k - 2, 0]
        )

    g_h4_halo, d_halo, c3_halo, y_halo, g_h3_halo = [coarse_halo(k) for k in range(2, 7)]
    g_h2_halo = halo_copies(7, hfout.at[0], hfout.at[1], hfull.at[1], hfull.at[0])

    def block_mask(shape, pad):
        blocks = shape[0]
        b = lax.broadcasted_iota(jnp.int32, shape, 0)
        low = jnp.where(me > 0, 0, pad)
        high = jnp.where(me < n - 1, blocks, blocks - pad)
        return (b >= low) & (b < high)

    def param(k, which, f):
        return prm[k * 8 + which, pl.ds(f, 1), :]

    def wide(k, which, f):
        return twice(param(k, which, f))

    def put_row(carry, f, value):
        row = lax.broadcasted_iota(jnp.int32, carry.shape, 0)
        return jnp.where(row == f, value, carry)

    def full_sum(v):
        s = jnp.sum(v.reshape(-1, 256), axis=0, keepdims=True)
        return s[:, :128] + s[:, 128:]

    def paired(raw_rows):
        count = raw_rows.shape[0]
        tmp[0:count, :, 0:64] = raw_rows.astype(F32)
        even = tmp[0:count, pl.ds(0, cols, stride=2), :]
        odd = tmp[0:count, pl.ds(1, cols, stride=2), :]
        return join(even, swap(odd))

    def pair_halves(p):
        count = p.shape[0] // 2
        p = p.reshape(count, 2, cols, 128)
        return p[:, 0], p[:, 1]

    def neighbours(v):
        count = v.shape[0]
        flat = v.reshape(count * cols, 128)
        up = pltpu.roll(flat, count * cols - 1, 0).reshape(v.shape)
        down = pltpu.roll(flat, 1, 0).reshape(v.shape)
        return up, down

    def put_e(e, f, start, h):
        count = h.shape[0]
        for part in range(2):
            v = h[:, :, part * 128 : (part + 1) * 128]
            up, down = neighbours(v)
            lane = lane_iota(v.shape)
            q = lax.broadcasted_iota(jnp.int32, v.shape, 1)
            near = jnp.where(
                lane < 64, jnp.where(q == cols - 1, 0.0, up), jnp.where(q == 0, 0.0, down)
            )
            e[f, start : start + count, :, part * 256 : part * 256 + 128] = v.astype(BF16)
            e[f, start : start + count, :, part * 256 + 128 : part * 256 + 256] = near.astype(BF16)

    def window(e, f, start, count):
        return jnp.concatenate(
            [
                e[f, start - 1 : start - 1 + count, :, 256:512],
                e[f, start : start + count, :, :],
                e[f, start + 1 : start + 1 + count, :, 0:256],
            ],
            axis=-1,
        ).reshape(count * cols, 1024)

    def own_pixels(e, f, start, count):
        return jnp.concatenate(
            [
                e[f, start : start + count, :, 0:128],
                e[f, start : start + count, :, 256:384],
            ],
            axis=-1,
        ).reshape(count * cols, 256)

    def put_ec(ec, hf, v):
        up, down = neighbours(v)
        q = lax.broadcasted_iota(jnp.int32, v.shape, 1)
        ec[hf, :, :, 0:128] = jnp.where(q == 0, 0.0, down).astype(BF16)
        ec[hf, :, :, 128:256] = v.astype(BF16)
        ec[hf, :, :, 256:384] = jnp.where(q == cols - 1, 0.0, up).astype(BF16)

    def coarse_window(ec, hf):
        return jnp.concatenate([ec[hf, a : a + rows] for a in range(3)], axis=-1).reshape(
            owned, 1152
        )

    def coarse_sum(v):
        return jnp.sum(v.reshape(-1, 128), axis=0, keepdims=True)

    def with_halo(ref, hf, k):
        ref[hf, 0] = hal[k, 0, hf].astype(F32)
        ref[hf, rows + 1] = hal[k, 1, hf].astype(F32)

    def border(ref_out, k, hf, v):
        ref_out[k, 0, hf] = v[0].astype(BF16)
        ref_out[k, 1, hf] = v[rows - 1].astype(BF16)

    def group_matrix(coarse):
        r = lax.broadcasted_iota(jnp.int32, (128, 128), 0) // 32
        c = lax.broadcasted_iota(jnp.int32, (128, 128), 1) // 32
        same = (r == c) if coarse else (r % 2 == c % 2)
        return jnp.where(same, 1.0, 0.0)

    def norm_forward(k, total, coarse):
        cells = coarse_cells if coarse else full_cells
        count = half if coarse else frames
        moments = dot_high(total, group_matrix(coarse)) / cells
        mean = moments[0:count]
        var = moments[count : 2 * count] - mean * mean
        rstd = lax.rsqrt(var + NORM_EPSILON)
        gain = prm[k * 8 + GAIN, 0:count, :]
        alpha = rstd * gain
        prm[k * 8 + ALPHA, 0:count, :] = alpha
        prm[k * 8 + BETA, 0:count, :] = prm[k * 8 + SHIFT, 0:count, :] - mean * alpha
        prm[k * 8 + RSTD, 0:count, :] = rstd
        prm[k * 8 + NMR, 0:count, :] = -mean * rstd

    def norm_backward(k, total, coarse):
        cells = coarse_cells if coarse else full_cells
        count = half if coarse else frames
        gain = prm[k * 8 + GAIN, 0:count, :]
        shift_grad = total[0:count]
        scale_grad = total[count : 2 * count]
        means = (
            dot_high(
                jnp.concatenate([shift_grad * gain, scale_grad * gain], axis=0),
                group_matrix(coarse),
            )
            / cells
        )
        rstd = prm[k * 8 + RSTD, 0:count, :]
        factor = -rstd * means[count : 2 * count]
        prm[k * 8 + COEF, 0:count, :] = rstd * factor
        prm[k * 8 + BIAS, 0:count, :] = (
            prm[k * 8 + NMR, 0:count, :] * factor - rstd * means[0:count]
        )
        if coarse:
            scale_all = jnp.concatenate([scale_grad, swap(scale_grad)], axis=0)
            shift_all = jnp.concatenate([shift_grad, swap(shift_grad)], axis=0)
        else:
            scale_all = scale_grad + swap(scale_grad)
            shift_all = shift_grad + swap(shift_grad)
        packs[dp, :, k * 128 : (k + 1) * 128] = join(scale_all, swap(shift_all))

    slots = 32 // nd
    share = 64 // n
    early = max(1, 16 // nd)
    stages = (0, 1, 2) if early > 1 else (0, 2)
    stage_slots = [pl.ds(early, slots - early), pl.ds(1, 1), pl.ds(0, 1)]

    def dp_copy(which, src, dst, off):
        return pltpu.make_async_remote_copy(
            src_ref=src,
            dst_ref=dst,
            send_sem=dp_send.at[which],
            recv_sem=dp_recv.at[which],
            device_id={"dp": lax.rem(dp + off, nd)},
            device_id_type=MESH,
        )

    def sp_copy(which, src, dst, off):
        return pltpu.make_async_remote_copy(
            src_ref=src,
            dst_ref=dst,
            send_sem=sp_send.at[which],
            recv_sem=sp_recv.at[which],
            device_id={"space": lax.rem(me + off, n)},
            device_id_type=MESH,
        )

    dp_peers, sp_peers = pl.ds(0, nd - 1), pl.ds(0, n - 1)

    def first_all(stage):
        ref = rbuf.at[dp_peers, stage_slots[stage]]
        return dp_copy(stage, ref, ref, 1)

    def last_all(stage):
        ref = gall_hbm.at[dp_peers, stage_slots[stage]]
        return dp_copy(3 + stage, ref, ref, 1)

    def pack_lanes(which):
        return pl.ds(0, 128) if which else pl.ds(128, 768)

    def pack_all(which):
        ref = packs.at[dp_peers, :, pack_lanes(which)]
        return dp_copy(6 + which, ref, ref, 1)

    def pack_start(which):
        ref = packs.at[dp, :, pack_lanes(which)]
        for off in range(1, nd):
            dp_copy(6 + which, ref, ref, off).start()

    def space_all(which):
        if which >= 2:
            ref = zwhole.at[which - 2, sp_peers]
        else:
            ref = zbuf.at[sp_peers, stage_slots[0]]
        return sp_copy(which, ref, ref, 1)

    def gather_start(stage):
        if stage not in stages:
            return
        where = stage_slots[stage]
        for off in range(1, nd):
            owner = lax.rem(dp + off, nd)
            dp_copy(stage, gt_ref.at[where, owner], rbuf.at[dp, where], off).start()

    def gather_space(stage):
        if stage not in stages:
            return
        where = stage_slots[stage]
        first_all(stage).wait_recv()
        rbuf[dp, where] = gt_ref[where, dp]
        total = rbuf[0, where].astype(F32)
        for i in range(1, nd):
            total = total + rbuf[i, where].astype(F32)
        if stage > 0:
            zwhole[stage - 1, me] = total[0]
            ref = zwhole.at[stage - 1, me]
            for off in range(1, n):
                sp_copy(stage + 1, ref, ref, off).start()
            return
        for z in range(n):
            part[z, where] = total[:, z * share : (z + 1) * share]
        for off in range(1, n):
            row = lax.rem(me + off, n)
            sp_copy(0, part.at[row, where], zbuf.at[me, where], off).start()

    def gather_spread():
        where = stage_slots[0]
        space_all(0).wait_recv()
        zbuf[me, where] = part[me, where]
        total = zbuf[0, where]
        for i in range(1, n):
            total = total + zbuf[i, where]
        zfull[me, where] = total
        for off in range(1, n):
            sp_copy(1, zfull.at[me, where], zfull.at[me, where], off).start()

    def own_copy(stage):
        where = stage_slots[stage]
        return pltpu.make_async_copy(gown.at[where], gall_hbm.at[dp, where], own_sem.at[stage])

    def gather_all(stage):
        if stage not in stages:
            return
        where = stage_slots[stage]
        if stage > 0:
            space_all(stage + 1).wait_recv()
            total = zwhole[stage - 1, 0]
            for i in range(1, n):
                total = total + zwhole[stage - 1, i]
            gown[where] = total[None].astype(BF16)
        else:
            space_all(1).wait_recv()
            whole = jnp.concatenate([zfull[z, where] for z in range(n)], axis=1)
            gown[where] = whole.astype(BF16)
        for off in range(1, nd):
            dp_copy(3 + stage, gown.at[where], gall_hbm.at[dp, where], off).start()
        own_copy(stage).start()

    def gather_finish(stage):
        last_all(stage).wait_recv()
        first_all(stage).wait_send()
        last_all(stage).wait_send()
        own_copy(stage).wait()
        for which in (stage + 1,) if stage > 0 else (0, 1):
            space_all(which).wait_send()

    x_copy.wait()

    def load_x(f, carry):
        total, square = carry
        even, odd = pair_halves(paired(raw[f]))
        both = jnp.concatenate([even, odd], axis=-1)
        xs[f, 2 : 2 + rows] = both.astype(BF16)
        return put_row(total, f, full_sum(both)), put_row(square, f, full_sum(both * both))

    zero_rows = jnp.zeros((frames, 128), F32)
    sums = lax.fori_loop(0, frames, load_x, (zero_rows, zero_rows), unroll=4)
    g_copy.start()
    pl.semaphore_wait(barrier, n + nd - 2)
    stat_start(0, jnp.concatenate(sums, axis=0))
    for copies in x_halos:
        halo_start(copies)

    @pl.when(me == 0)
    def _():
        for v in (xs, gs):
            v[:, 0:2] = jnp.zeros((frames, 2, cols, 256), BF16)
        for which in range(hal.shape[0]):
            hal[which, 0] = jnp.zeros(hal.shape[2:], BF16)
        hfull[0] = jnp.zeros(hfull.shape[1:], BF16)

    @pl.when(me == n - 1)
    def _():
        for v in (xs, gs):
            v[:, rows + 2 : rows + 4] = jnp.zeros((frames, 2, cols, 256), BF16)
        for which in range(hal.shape[0]):
            hal[which, 1] = jnp.zeros(hal.shape[2:], BF16)
        hfull[1] = jnp.zeros(hfull.shape[1:], BF16)

    for v in (xs, gs):
        v[:, 0, :, 0:128] = jnp.zeros((frames, cols, 128), BF16)
        v[:, rows + 3, :, 128:256] = jnp.zeros((frames, cols, 128), BF16)

    def conditioning():
        entry = lax.broadcasted_iota(jnp.int32, (frames, 128), 1)
        row = lax.broadcasted_iota(jnp.int32, (frames, 128), 0)
        hot = jnp.zeros((frames, 128), F32)
        for copy in map_copies:
            copy.wait()
        for f in range(frames):
            hit = (
                (entry == act_ref[f])
                | (entry == noise_ref[f] + ACTIONS)
                | (entry == game_ref[f] + ACTIONS + NOISE_LEVELS)
            )
            hot = jnp.where((row == f) & hit, 1.0, hot)
        table_rows = tab_ref.shape[0]
        tabp[...] = jnp.zeros(tabp.shape, F32)
        tabp[0:table_rows, :] = tab_ref[...]
        embedded = dot_high(hot, tabp[...])
        packs[dp, :, 512:768] = embedded
        packs[dp, :, 768:896] = hot
        for k in range(4):
            mod = dot_high(embedded, nmv[k]) + nmb[k : k + 1, :]
            scale = join(mod, swap(mod)) + 1.0
            shift = join(swap(mod), mod)
            if k < 2:
                prm[k * 8 + GAIN] = scale
                prm[k * 8 + SHIFT] = shift
            else:
                prm[k * 8 + GAIN, 0:half, :] = join(scale[0:half], scale[half:])
                prm[k * 8 + SHIFT, 0:half, :] = join(shift[0:half], shift[half:])

    conditioning()

    g_copy.wait()

    def load_cotangent(f, carry):
        live = jnp.where(f < live_ref[0], 1.0, 0.0)
        even, odd = pair_halves(paired(raw[f]))
        both = jnp.concatenate([even, odd], axis=-1)
        gs[f, 2 : 2 + rows] = (both * live).astype(BF16)
        return carry

    lax.fori_loop(0, frames, load_cotangent, 0, unroll=4)
    for copies in g_halos:
        halo_start(copies)


    def tap(index):
        first = (index // 2) * 128
        last = min(first + 128, cw_ref.shape[1])
        tile = cw_ref[:, first:last].astype(BF16).astype(F32)
        if last - first < 128:
            tile = jnp.concatenate([tile, jnp.zeros((64, 128 - last + first), F32)], axis=-1)
        return tile, index % 2

    def low_half(index):
        tile, odd = tap(index)
        return swap(tile) if odd else tile

    def high_half(index):
        tile, odd = tap(index)
        return tile if odd else swap(tile)

    def lane_pair(low_index, high_index):
        zero = jnp.zeros((64, 128), F32)
        low = zero if low_index is None else low_half(low_index)
        high = zero if high_index is None else high_half(high_index)
        return join(low, high).astype(BF16)

    def fine_weights(index, forward_w, backward_w):
        zero = jnp.zeros((64, 128), BF16)
        pairs = []
        for t in range(3):
            p12 = lane_pair(index(t, 1), index(t, 2))
            p01 = lane_pair(index(t, 0), index(t, 1))
            pz0 = lane_pair(None, index(t, 0))
            p2z = lane_pair(index(t, 2), None)
            pairs.append((p12, p01, pz0, p2z))
        for a in range(4):
            for dr in range(2):
                t = a - dr
                ok = 0 <= t <= 2
                for dq in range(2):
                    r = (dr * 2 + dq) * 64
                    first = pairs[t][0 if dq == 0 else 1] if ok else zero
                    second = pairs[t][2 if dq == 0 else 3] if ok else zero
                    forward_w[r : r + 64, a * 256 : a * 256 + 128] = first
                    forward_w[r : r + 64, a * 256 + 128 : a * 256 + 256] = second
                t = 2 - a + dr
                ok = 0 <= t <= 2
                for g in range(4):
                    r = a * 256 + g * 64
                    backward_w[r : r + 64, dr * 128 : dr * 128 + 128] = (
                        pairs[t][g] if ok else zero
                    )

    def coarse_weights(index, forward_w, backward_w):
        for a in range(3):
            for j in range(3):
                lane = (a * 3 + j) * 128
                low = lane_pair(index(a, j), None)
                high = lane_pair(None, index(a, j))
                forward_w[0:64, lane : lane + 128] = low
                forward_w[64:128, lane : lane + 128] = high
                lane = ((2 - a) * 3 + (2 - j)) * 128
                backward_w[lane : lane + 64, :] = low
                backward_w[lane + 64 : lane + 128, :] = high

    def down_weights(index):
        zero = jnp.zeros((64, 128), BF16)
        wdf[...] = jnp.zeros(wdf.shape, BF16)
        wdb[...] = jnp.zeros(wdb.shape, BF16)
        for t in range(3):
            p12 = lane_pair(index(t, 1), index(t, 2))
            pz0 = lane_pair(None, index(t, 0))
            for hi in range(2):
                lane = hi * 768 + t * 256
                wdf[hi * 64 : hi * 64 + 64, lane : lane + 128] = p12
                wdf[hi * 64 : hi * 64 + 64, lane + 128 : lane + 256] = pz0
                i, dr = ((1, 1), (0, 0), (0, 1))[t]
                lane = hi * 256 + dr * 128
                for j in range(2):
                    r = (i * 2 + j) * 128 + hi * 64
                    wdb[r : r + 64, lane : lane + 128] = p12 if j == 0 else pz0

    def up_weights():
        def up_tap(ta, tb):
            return low_half(45 + (ta * 3 + tb) * 2 + 1)

        taps = [[up_tap(ta, tb) for tb in range(3)] for ta in range(3)]
        members = {(0, 0): (0,), (0, 1): (1, 2), (1, 1): (0, 1), (1, 2): (2,)}
        wup[...] = jnp.zeros(wup.shape, BF16)
        for (dr, i), in_rows in members.items():
            for (dq, j), in_cols in members.items():
                total = sum(taps[ta][tb] for ta in in_rows for tb in in_cols)
                zero = jnp.zeros_like(total)
                r = (dr * 2 + dq) * 64
                lane = (i * 3 + j) * 128
                wup[r : r + 64, lane : lane + 128] = join(total, zero).astype(BF16)
                wup[256 + r : 256 + r + 64, lane : lane + 128] = join(zero, swap(total)).astype(
                    BF16
                )
        for a in range(4):
            for g, off in enumerate((0, 1, 2, -1)):
                chosen = [
                    taps[2 - a + dr][1 - off + dq]
                    for dr in range(2)
                    for dq in range(2)
                    if 0 <= 2 - a + dr <= 2 and 0 <= 1 - off + dq <= 2
                ]
                total = sum(chosen[1:], chosen[0])
                zero = jnp.zeros_like(total)
                r = a * 256 + g * 64
                wco[0, r : r + 64, :] = join(total, zero).astype(BF16)
                wco[1, r : r + 64, :] = join(zero, swap(total)).astype(BF16)

    def stacked(k):
        return lambda t, s: k * 9 + t * 3 + s

    weight_copy.wait()
    fine_weights(stacked(0), w1f, w1b)
    fine_weights(stacked(1), w2f, w2b)
    fine_weights(lambda t, s: 45 + (t * 3 + s) * 2, wsf, wsb)
    up_weights()
    down_weights(stacked(2))
    coarse_weights(stacked(3), w3f, w3b)
    coarse_weights(stacked(4), w4f, w4b)

    for copies in x_halos:
        halo_wait(copies)
    norm_forward(0, stat_total(0), False)

    def first_layer(f, carry):
        total, square = carry
        x = xs[f].astype(F32)
        z = x * wide(0, ALPHA, f) + wide(0, BETA, f)
        h = z * logistic(z)
        h = jnp.where(block_mask(h.shape, 2), h, 0.0)
        put_e(e1, f, 0, h)
        out = dot_nt(window(e1, f, 1, rows + 2), w1f[...]).reshape(rows + 2, cols, 256)
        c1[f] = out
        own = out[1 : rows + 1]
        return put_row(total, f, full_sum(own)), put_row(square, f, full_sum(own * own))

    sums = lax.fori_loop(0, frames, first_layer, (zero_rows, zero_rows), unroll=4)
    stat_start(1, jnp.concatenate(sums, axis=0))

    for copies in g_halos:
        halo_wait(copies)

    def load_g(f, carry):
        g = gs[f].astype(F32)
        put_e(eg, f, 0, jnp.where(block_mask(g.shape, 2), g, 0.0))
        gsa[f] = dot_nn(window(eg, f, 1, rows + 2), wsb[...]).reshape(rows + 2, cols, 256)
        return carry

    lax.fori_loop(0, frames, load_g, 0, unroll=4)

    norm_forward(1, stat_total(1), False)

    def second_layer(f, carry):
        z = c1[f] * wide(1, ALPHA, f) + wide(1, BETA, f)
        h = z * logistic(z)
        h = jnp.where(block_mask(h.shape, 1), h, 0.0)
        edge = jnp.zeros((cols, 512), BF16)
        e2[f, 0] = edge
        e2[f, rows + 3] = edge
        put_e(e2, f, 1, h)
        out = dot_nt(window(e2, f, 1, rows + 2), w2f[...]).reshape(rows + 2, cols, 256)
        skip = out + xs[f, 1 : rows + 3].astype(F32)
        skip = jnp.where(block_mask(skip.shape, 1), skip, 0.0)
        put_e(esk, f, 1, skip)
        return carry

    lax.fori_loop(0, frames, second_layer, 0, unroll=4)

    def down_window(f):
        return jnp.concatenate(
            [esk[f, 1 : 1 + rows, :, 256:512], esk[f, 2 : 2 + rows]], axis=-1
        ).reshape(owned, 768)

    zero_coarse = jnp.zeros((half, 128), F32)
    pad_rows = [jnp.zeros((2 * frames - 2 * half, 128), F32)]

    def down_layer(hf, carry):
        total, square = carry
        d = dot_nt(down_window(hf), wdf[:, 0:768]) + dot_nt(
            down_window(hf + half), wdf[:, 768:1536]
        )
        d = d.reshape(rows, cols, 128)
        dv[hf, 1 : rows + 1] = d
        border(hout, 1, hf, d)
        return put_row(total, hf, coarse_sum(d)), put_row(square, hf, coarse_sum(d * d))

    sums = lax.fori_loop(0, half, down_layer, (zero_coarse, zero_coarse), unroll=4)
    stat_start(2, jnp.concatenate(list(sums) + pad_rows, axis=0))
    halo_start(d_halo)

    def coarse_gradient(hf, carry):
        g = dot_nn(window(eg, hf, 1, rows + 2), wco[0]) + dot_nn(
            window(eg, hf + half, 1, rows + 2), wco[1]
        )
        g = g.reshape(rows + 2, cols, 128)
        g = jnp.where(block_mask(g.shape, 1), g, 0.0).astype(BF16).astype(F32)
        gco[hf] = g
        put_ec(ecg, hf, g)
        back = dot_nn(coarse_window(ecg, hf), w4b[...]).reshape(rows, cols, 128)
        gh4[hf, 1 : rows + 1] = back
        border(hout, 0, hf, back)
        return carry

    lax.fori_loop(0, half, coarse_gradient, 0, unroll=4)
    halo_start(g_h4_halo)

    def put_half(index, value):
        slot, owner = index // 2 // nd, index // 2 % nd
        current = gt_ref[slot, owner].astype(F32)
        value = join(current, swap(value)) if index % 2 else join(value, current)
        gt_ref[slot, owner] = value.astype(BF16)

    gt_ref[...] = jnp.zeros(gt_ref.shape, BF16)

    def fine_kernel_grad(index, e, start, gradient, gradient_start):
        acc[0, :, 0:1024] = jnp.zeros((256, 1024), F32)

        def add(f, carry):
            g = own_pixels(gradient, f, gradient_start, rows)
            acc[0, :, 0:1024] += dot_tn(g, window(e, f, start, rows))
            return carry

        lax.fori_loop(0, frames, add, 0, unroll=4)
        for t in range(3):
            u = []
            for dq in range(2):
                parts = [
                    acc[0, (dr * 2 + dq) * 64 : (dr * 2 + dq) * 64 + 64, pl.ds((t + dr) * 256, 256)]
                    for dr in range(2)
                ]
                u.append(parts[0] + parts[1])
            near, far = [v[:, 0:128] for v in u], [v[:, 128:256] for v in u]
            put_half(index(t, 0), swap(far[0]) + near[1])
            put_half(index(t, 1), near[0] + swap(near[1]))
            put_half(index(t, 2), swap(near[0]) + far[1])

    def coarse_kernel_grad(index, ec, gradient):
        acc[0, 0:128, :] = jnp.zeros((128, 1152), F32)

        def add(hf, carry):
            g = gradient[hf, 1 : rows + 1, :, 128:256].reshape(owned, 128)
            acc[0, 0:128, :] += dot_tn(g, coarse_window(ec, hf))
            return carry

        lax.fori_loop(0, half, add, 0, unroll=4)
        for a in range(3):
            for j in range(3):
                lanes = pl.ds((a * 3 + j) * 128, 128)
                put_half(index(a, j), acc[0, 0:64, lanes] + swap(acc[0, 64:128, lanes]))

    def down_kernel_grad(index):
        acc[:, 0:128, 0:768] = jnp.zeros((2, 128, 768), F32)

        def add(hf, carry):
            g = ed[hf, 1 : rows + 1, :, 0:128].reshape(owned, 128)
            acc[0, 0:128, 0:768] += dot_tn(g, down_window(hf))
            acc[1, 0:128, 0:768] += dot_tn(g, down_window(hf + half))
            return carry

        lax.fori_loop(0, half, add, 0, unroll=4)
        for a in range(3):
            near = acc[0, 0:64, pl.ds(a * 256, 128)] + acc[1, 64:128, pl.ds(a * 256, 128)]
            far = (
                acc[0, 0:64, pl.ds(a * 256 + 128, 128)] + acc[1, 64:128, pl.ds(a * 256 + 128, 128)]
            )
            put_half(index(a, 0), swap(far))
            put_half(index(a, 1), near)
            put_half(index(a, 2), swap(near))

    def up_kernel_grad():
        acc[...] = jnp.zeros(acc.shape, F32)

        def add(hf, carry):
            v = coarse_window(ecy, hf)
            acc[0] += dot_tn(own_pixels(eg, hf, 2, rows), v)
            acc[1] += dot_tn(own_pixels(eg, hf + half, 2, rows), v)
            return carry

        lax.fori_loop(0, half, add, 0, unroll=4)

        def block(dr, dq, i, j):
            r = (dr * 2 + dq) * 64
            lanes = pl.ds((i * 3 + j) * 128, 128)
            return acc[0, r : r + 64, lanes] + swap(acc[1, r : r + 64, lanes])

        place = {(0, 0): 0, (0, 1): 1, (0, 2): 1, (1, 0): 1, (1, 1): 1, (1, 2): 2}
        for ta in range(3):
            for tb in range(3):
                total = sum(
                    block(dr, dq, place[dr, ta], place[dq, tb])
                    for dr in range(2)
                    for dq in range(2)
                )
                put_half(45 + (ta * 3 + tb) * 2 + 1, total)


    halo_wait(d_halo)
    norm_forward(2, stat_total(2), True)

    def third_layer(hf, carry):
        total, square = carry
        with_halo(dv, hf, 1)
        z = dv[hf] * param(2, ALPHA, hf) + param(2, BETA, hf)
        h = z * logistic(z)
        put_ec(ec3, hf, jnp.where(block_mask(h.shape, 1), h, 0.0))
        out = dot_nt(coarse_window(ec3, hf), w3f[...]).reshape(rows, cols, 128)
        c3[hf, 1 : rows + 1] = out
        border(hout, 2, hf, out)
        return put_row(total, hf, coarse_sum(out)), put_row(square, hf, coarse_sum(out * out))

    sums = lax.fori_loop(0, half, third_layer, (zero_coarse, zero_coarse), unroll=4)
    stat_start(3, jnp.concatenate(list(sums) + pad_rows, axis=0))
    halo_start(c3_halo)

    def result_copy(f):
        return pltpu.make_async_copy(gz.at[f, pl.ds(1, rows)], io_hbm.at[f], out_sem.at[f])

    def merge_skip(f, carry):
        out = dot_nt(window(esk, f, 2, rows), wsf[...])
        gz[f, 1 : rows + 1] = out.reshape(rows, cols, 256)
        return carry

    lax.fori_loop(0, half, merge_skip, 0, unroll=4)
    fine_kernel_grad(lambda t, s: 45 + (t * 3 + s) * 2, esk, 2, eg, 2)

    halo_wait(c3_halo)
    halo_wait(g_h4_halo)
    norm_forward(3, stat_total(3), True)

    def fourth_layer(hf, carry):
        shift, scale = carry
        with_halo(c3, hf, 2)
        with_halo(gh4, hf, 0)
        v = c3[hf]
        z = v * param(3, ALPHA, hf) + param(3, BETA, hf)
        gate = logistic(z)
        h = z * gate
        put_ec(ec4, hf, jnp.where(block_mask(h.shape, 1), h, 0.0))
        g = gh4[hf] * (gate + h * (1.0 - gate))
        gzc[hf] = g
        own = g[1 : rows + 1]
        xhat = v[1 : rows + 1] * param(3, RSTD, hf) + param(3, NMR, hf)
        return put_row(shift, hf, coarse_sum(own)), put_row(scale, hf, coarse_sum(own * xhat))

    sums = lax.fori_loop(0, half, fourth_layer, (zero_coarse, zero_coarse), unroll=4)
    stat_start(4, jnp.concatenate(list(sums) + pad_rows, axis=0))

    def coarse_output(hf, carry):
        out = dot_nt(coarse_window(ec4, hf), w4f[...]).reshape(rows, cols, 128)
        y = dv[hf, 1 : rows + 1] + out
        border(hout, 3, hf, y)
        edge = jnp.zeros((1, cols, 128), F32)
        put_ec(ecy, hf, jnp.concatenate([edge, y, edge], axis=0))
        return carry

    lax.fori_loop(0, half, coarse_output, 0, unroll=4)
    halo_start(y_halo)
    coarse_kernel_grad(stacked(4), ec4, ecg)
    lax.fori_loop(half, frames, merge_skip, 0, unroll=4)

    norm_backward(3, stat_total(4), True)

    def third_back(hf, carry):
        shift, scale = carry
        g = (
            gzc[hf] * param(3, ALPHA, hf)
            + c3[hf] * param(3, COEF, hf)
            + param(3, BIAS, hf)
        )
        put_ec(ecg3, hf, jnp.where(block_mask(g.shape, 1), g, 0.0))
        back = dot_nn(coarse_window(ecg3, hf), w3b[...]).reshape(rows, cols, 128)
        border(hout, 4, hf, back)
        v = dv[hf, 1 : rows + 1]
        z = v * param(2, ALPHA, hf) + param(2, BETA, hf)
        gate = logistic(z)
        own = back * (gate + z * gate * (1.0 - gate))
        gzc[hf, 1 : rows + 1] = own
        xhat = v * param(2, RSTD, hf) + param(2, NMR, hf)
        return put_row(shift, hf, coarse_sum(own)), put_row(scale, hf, coarse_sum(own * xhat))

    sums = lax.fori_loop(0, half, third_back, (zero_coarse, zero_coarse), unroll=4)
    stat_start(5, jnp.concatenate(list(sums) + pad_rows, axis=0))
    halo_start(g_h3_halo)

    halo_wait(y_halo)

    def merge(hf, carry):
        for side, row in ((0, 0), (1, rows + 1)):
            line = hal[3, side, hf].astype(F32)[None]
            up, down = neighbours(line)
            q = lax.broadcasted_iota(jnp.int32, line.shape, 1)
            ecy[hf, row, :, 0:128] = jnp.where(q == 0, 0.0, down)[0].astype(BF16)
            ecy[hf, row, :, 128:256] = line[0].astype(BF16)
            ecy[hf, row, :, 256:384] = jnp.where(q == cols - 1, 0.0, up)[0].astype(BF16)
        both = dot_nt(coarse_window(ecy, hf), wup[...])
        for hi in range(2):
            f = hf + hi * half
            up = both[:, hi * 256 : hi * 256 + 256].reshape(rows, cols, 256)
            gz[f, 1 : rows + 1] = gz[f, 1 : rows + 1] + up
            result_copy(f).start()
        return carry

    lax.fori_loop(0, half, merge, 0, unroll=4)
    coarse_kernel_grad(stacked(3), ec3, ecg3)
    up_kernel_grad()
    gather_start(0)

    halo_wait(g_h3_halo)
    norm_backward(2, stat_total(5), True)

    def down_back(hf, carry):
        for side, row in ((0, 0), (1, rows + 1)):
            v = dv[hf, row]
            z = v * param(2, ALPHA, hf) + param(2, BETA, hf)
            gate = logistic(z)
            gzc[hf, row] = hal[4, side, hf].astype(F32) * (gate + z * gate * (1.0 - gate))
        g = (
            gco[hf]
            + gzc[hf] * param(2, ALPHA, hf)
            + dv[hf] * param(2, COEF, hf)
            + param(2, BIAS, hf)
        )
        g = jnp.where(block_mask(g.shape, 1), g, 0.0)
        up, _ = neighbours(g)
        q = lax.broadcasted_iota(jnp.int32, g.shape, 1)
        ed[hf, 0 : rows + 2, :, 0:128] = g.astype(BF16)
        ed[hf, 0 : rows + 2, :, 128:256] = jnp.where(q == cols - 1, 0.0, up).astype(BF16)
        ed[hf, rows + 2] = jnp.zeros((cols, 256), BF16)
        lhs = jnp.concatenate([ed[hf, 0 : rows + 2], ed[hf, 1 : rows + 3]], axis=-1)
        back = dot_nn(lhs.reshape(ext, 512), wdb[...])
        back = back.astype(BF16).astype(F32).reshape(rows + 2, cols, 512)
        for hi in range(2):
            f = hf + hi * half
            total = gsa[f] + back[:, :, hi * 256 : hi * 256 + 256]
            gsa[f] = total
            put_e(eg, f, 0, jnp.where(block_mask(total.shape, 1), total, 0.0))
        return carry

    lax.fori_loop(0, half, down_back, 0, unroll=4)

    def second_back(f, carry):
        shift, scale = carry
        back = dot_nn(window(eg, f, 1, rows), w2b[...]).reshape(rows, cols, 256)
        hfout[0, f] = back[0, :, 0:128].astype(BF16)
        hfout[1, f] = back[rows - 1, :, 128:256].astype(BF16)
        v = c1[f, 1 : rows + 1]
        z = v * wide(1, ALPHA, f) + wide(1, BETA, f)
        gate = logistic(z)
        own = back * (gate + z * gate * (1.0 - gate))
        gz[f, 1 : rows + 1] = own
        xhat = v * wide(1, RSTD, f) + wide(1, NMR, f)
        return put_row(shift, f, full_sum(own)), put_row(scale, f, full_sum(own * xhat))

    for f in range(frames):
        result_copy(f).wait()
    sums = lax.fori_loop(0, frames, second_back, (zero_rows, zero_rows), unroll=4)
    stat_start(6, jnp.concatenate(sums, axis=0))
    halo_start(g_h2_halo)
    down_kernel_grad(stacked(2))
    gather_space(0)
    fine_kernel_grad(stacked(1), e2, 2, eg, 1)
    gather_start(1)
    gather_spread()
    halo_wait(g_h2_halo)
    norm_backward(1, stat_total(6), False)

    def first_gradient(f, carry):
        for side, row in ((0, 0), (1, rows + 1)):
            v = c1[f, row]
            lanes = slice(128, 256) if side == 0 else slice(0, 128)
            z = v[:, lanes] * param(1, ALPHA, f) + param(1, BETA, f)
            gate = logistic(z)
            g = hfull[side, f].astype(F32) * (gate + z * gate * (1.0 - gate))
            blank = jnp.zeros_like(g)
            gz[f, row] = jnp.concatenate([blank, g] if side == 0 else [g, blank], axis=-1)
        g = gz[f] * wide(1, ALPHA, f) + c1[f] * wide(1, COEF, f) + wide(1, BIAS, f)
        put_e(eg, f, 0, jnp.where(block_mask(g.shape, 1), g, 0.0))
        return carry

    lax.fori_loop(0, frames, first_gradient, 0, unroll=4)
    fine_kernel_grad(stacked(0), e1, 2, eg, 1)
    gather_start(2)
    gather_all(0)
    gather_space(1)

    def first_back(f, carry):
        shift, scale = carry
        back = dot_nn(window(eg, f, 1, rows), w1b[...]).reshape(rows, cols, 256)
        v = xs[f, 2 : rows + 2].astype(F32)
        z = v * wide(0, ALPHA, f) + wide(0, BETA, f)
        gate = logistic(z)
        own = back * (gate + z * gate * (1.0 - gate))
        gz[f, 1 : rows + 1] = own
        xhat = v * wide(0, RSTD, f) + wide(0, NMR, f)
        return put_row(shift, f, full_sum(own)), put_row(scale, f, full_sum(own * xhat))

    pack_start(0)
    sums = lax.fori_loop(0, frames, first_back, (zero_rows, zero_rows), unroll=4)
    stat_start(7, jnp.concatenate(sums, axis=0))
    gather_all(1)
    gather_space(2)
    norm_backward(0, stat_total(7), False)
    pack_start(1)
    gather_all(2)

    def frames_copy(f):
        return pltpu.make_async_copy(
            gz.at[f, pl.ds(1, rows)], io_hbm.at[frames + f], fg_sem.at[f]
        )

    def frames_back(f, carry):
        gz[f, 1 : rows + 1] = (
            gsa[f, 1 : rows + 1]
            + gz[f, 1 : rows + 1] * wide(0, ALPHA, f)
            + xs[f, 2 : rows + 2].astype(F32) * wide(0, COEF, f)
            + wide(0, BIAS, f)
        )
        frames_copy(f).start()
        return carry

    lax.fori_loop(0, frames, frames_back, 0, unroll=4)
    for which in range(2):
        pack_all(which).wait_recv()
        pack_all(which).wait_send()
    total_frames = nd * frames
    every = packs[...].reshape(total_frames, 896)
    embedded, hot = every[:, 512:768], every[:, 768:896]
    g_embed = 0.0
    for k in range(4):
        dmod = every[:, k * 128 : (k + 1) * 128]
        acc[1, :, k * 128 : k * 128 + 128] = lax.dot_general(
            embedded, dmod, (((0,), (0,)), ((), ())), precision=HIGH, preferred_element_type=F32
        )
        lane = 512 + k % 2 * 128
        acc[1, 128 + k // 2 : 129 + k // 2, lane : lane + 128] = jnp.sum(
            dmod, axis=0, keepdims=True
        )
        g_embed = g_embed + lax.dot_general(
            dmod, nmv[k], (((1,), (1,)), ((), ())), precision=HIGH, preferred_element_type=F32
        )
    acc[1, 0:128, 512:768] = lax.dot_general(
        hot, g_embed, (((0,), (0,)), ((), ())), precision=HIGH, preferred_element_type=F32
    )

    def par_copy(e):
        return pltpu.make_async_copy(
            acc.at[1, :, pl.ds(e * 256, 256)], par_hbm.at[e], local_sem.at[e]
        )

    for e in range(3):
        par_copy(e).start()
    for stage in stages:
        gather_finish(stage)

    for e in range(3):
        par_copy(e).wait()
    for f in range(frames):
        frames_copy(f).wait()
    for copies in (*x_halos, *g_halos, g_h4_halo, d_halo, c3_halo, y_halo, g_h3_halo, g_h2_halo):
        halo_finish(copies)


def run_step(nd, n, frames, cotangent, actions, noise_ids, games, live_counts, cw, nm, table):
    count, strip, breadth, _ = frames.shape
    half, rows, cols = count // 2, strip // 2, breadth // 2
    fine = (count, rows + 4, cols, 512)
    coarse = (half, rows + 2, cols, 128)
    coarse_e = (half, rows + 2, cols, 384)
    scratch = [
        pltpu.SMEM(actions.shape, jnp.int32),
        pltpu.SMEM(noise_ids.shape, jnp.int32),
        pltpu.SMEM(games.shape, jnp.int32),
        pltpu.SMEM(live_counts.shape, jnp.int32),
        VM((count, strip, breadth, 64), BF16),
        VM(cw.shape, F32),
        VM(table.shape, F32),
        VM((strip, breadth, 128), F32),
        VM((count, rows + 4, cols, 256), BF16),
        VM((count, rows + 4, cols, 256), BF16),
        VM(fine, BF16),
        VM(fine, BF16),
        VM(fine, BF16),
        VM(fine, BF16),
        VM((count, rows + 2, cols, 256), F32),
        VM((count, rows + 2, cols, 256), F32),
        VM((count, rows + 2, cols, 256), F32),
        VM(coarse, F32),
        VM(coarse, F32),
        VM(coarse, F32),
        VM(coarse, F32),
        VM(coarse, F32),
        VM(coarse_e, BF16),
        VM(coarse_e, BF16),
        VM(coarse_e, BF16),
        VM(coarse_e, BF16),
        VM(coarse_e, BF16),
        VM((half, rows + 3, cols, 256), BF16),
        VM((256, 1024), BF16),
        VM((1024, 256), BF16),
        VM((256, 1024), BF16),
        VM((1024, 256), BF16),
        VM((256, 1024), BF16),
        VM((1024, 256), BF16),
        VM((512, 1152), BF16),
        VM((2, 1024, 128), BF16),
        VM((128, 1536), BF16),
        VM((512, 512), BF16),
        VM((128, 1152), BF16),
        VM((1152, 128), BF16),
        VM((128, 1152), BF16),
        VM((1152, 128), BF16),
        VM((2, 256, 1152), F32),
        VM((32, count, 128), F32),
        VM((128, 256), F32),
        VM((8, n, 2 * count, 128), F32),
        VM((5, 2, half, cols, 128), BF16),
        VM((5, 2, half, cols, 128), BF16),
        VM((2, count, cols, 128), BF16),
        VM((2, count, cols, 128), BF16),
        VM((4, 256, 128), F32),
        VM((4, 128), F32),
        VM((32 // nd, nd, 64, 128), BF16),
        VM((nd, 32 // nd, 64, 128), BF16),
        VM((n, 32 // nd, 64 // n, 128), F32),
        VM((n, 32 // nd, 64 // n, 128), F32),
        VM((n, 32 // nd, 64 // n, 128), F32),
        VM((2, n, 64, 128), F32),
        VM((32 // nd, 64, 128), BF16),
        VM((nd, count, 896), F32),
        pltpu.SemaphoreType.DMA((13,)),
        pltpu.SemaphoreType.DMA((count,)),
        pltpu.SemaphoreType.DMA((count,)),
        pltpu.SemaphoreType.DMA((8,)),
        pltpu.SemaphoreType.DMA((8,)),
        pltpu.SemaphoreType.DMA((10, 2)),
        pltpu.SemaphoreType.DMA((10, 2)),
        pltpu.SemaphoreType.DMA((8,)),
        pltpu.SemaphoreType.DMA((8,)),
        pltpu.SemaphoreType.DMA((4,)),
        pltpu.SemaphoreType.DMA((4,)),
        pltpu.SemaphoreType.DMA((3,)),
    ]
    hbm = pl.BlockSpec(memory_space=pltpu.HBM)
    return pl.pallas_call(
        functools.partial(step_kernel, nd, n),
        out_shape=(
            jax.ShapeDtypeStruct((2 * count, rows, cols, 256), F32),
            jax.ShapeDtypeStruct((8, 256, 256), F32),
            jax.ShapeDtypeStruct((4 * nd, 32 // nd, 64, 128), BF16),
        ),
        in_specs=[hbm] * 9,
        out_specs=(hbm, hbm, hbm),
        scratch_shapes=scratch,
        compiler_params=pltpu.CompilerParams(
            collective_id=0, has_side_effects=True, vmem_limit_bytes=55 * 1024 * 1024
        ),
        name="step",
    )(frames, cotangent, actions, noise_ids, games, live_counts, cw, nm, table)


def adamw(weight, moment, square, grad_value, rate):
    fix_one = 1.0 - BETA_ONE**ADAM_STEP
    fix_two = 1.0 - BETA_TWO**ADAM_STEP
    moment_new = BETA_ONE * moment + (1.0 - BETA_ONE) * grad_value
    square_new = BETA_TWO * square + (1.0 - BETA_TWO) * grad_value * grad_value
    fixed_m = moment_new / fix_one
    fixed_v = square_new / fix_two
    weight_new = weight - rate * (fixed_m / (jnp.sqrt(fixed_v) + ADAM_EPS) + DECAY * weight)
    return (moment_new, square_new, weight_new, weight_new.astype(BF16))


def finish_kernel(
    io_hbm,
    par_hbm,
    gall_hbm,
    cw,
    cm,
    cv,
    nm,
    nmo,
    nsq,
    tab,
    tmo,
    tsq,
    res_out,
    fg_out,
    *refs,
):
    outs, refs = refs[:12], refs[12:]
    stages, refs = refs[:12], refs[12:]
    io, par, gall, tmp, rs, fs, gmap, in_sem, pin_sem, fg_sem, out_sem, par_sem = refs
    frames, rows, cols = rs.shape[0], io.shape[1], io.shape[2]

    def frame_in(f):
        return pltpu.make_async_copy(io_hbm.at[f], io.at[f], in_sem.at[f])

    def par_in(e):
        return pltpu.make_async_copy(par_hbm.at[e], par.at[e], pin_sem.at[e])

    gall_in = pltpu.make_async_copy(
        gall_hbm.at[pl.ds(0, gall.shape[0])], gall, pin_sem.at[3]
    )
    gall_in.start()
    for e in range(3):
        par_in(e).start()
    for f in range(2 * frames):
        frame_in((f + frames) % (2 * frames)).start()
    out_copies = [
        pltpu.make_async_copy(stages[i], outs[i], par_sem.at[i]) for i in range(12)
    ]

    def update(first, at, weight, moment, square, grad, rate):
        new = adamw(weight, moment, square, grad, rate)
        for i in range(4):
            stages[first + i][at] = new[i]

    wide = cw.shape[1]
    gall_in.wait()
    for tile in range(32):
        lanes = slice(tile * 128, min(tile * 128 + 128, wide))
        at = (slice(None), lanes)
        owner, slot = tile % gall.shape[0], tile // gall.shape[0]
        grad = gall[owner, slot, :, 0 : lanes.stop - lanes.start].astype(F32)
        update(0, at, cw[at], cm[at], cv[at], grad, 0.05)
    for i in range(4):
        out_copies[i].start()

    def unpair(v):
        both = jnp.stack([v[:, :, 0:128], v[:, :, 128:256]], axis=1).reshape(rows * 2, cols, 128)
        tmp[:, pl.ds(0, cols, stride=2), :] = both
        tmp[:, pl.ds(1, cols, stride=2), :] = swap(both)
        return tmp[:, :, 0:64]

    def frame_copies(f):
        return (
            pltpu.make_async_copy(fs.at[f], fg_out.at[f], fg_sem.at[f]),
            pltpu.make_async_copy(rs.at[f], res_out.at[f], out_sem.at[f]),
        )

    def put_frames(f, carry):
        frame_in(frames + f).wait()
        fs[f] = unpair(io[frames + f])
        frame_copies(f)[0].start()
        return carry

    lax.fori_loop(0, frames, put_frames, 0)

    def put_result(f, carry):
        frame_in(f).wait()
        rs[f] = unpair(io[f]).astype(BF16)
        frame_copies(f)[1].start()
        return carry

    lax.fori_loop(0, frames, put_result, 0)

    for e in range(3):
        par_in(e).wait()
    for k in range(4):
        lane = k % 2 * 128
        gmap[0:256, k, :] = par[k // 2, :, lane : lane + 128]
        gmap[256, k : k + 1, :] = par[2, 128 + k // 2 : 129 + k // 2, lane : lane + 128]
    at = slice(None)
    update(4, at, nm[...], nmo[...], nsq[...], gmap[...], 0.04)
    for i in range(4, 8):
        out_copies[i].start()
    update(8, at, tab[...], tmo[...], tsq[...], par[2, 0 : tab.shape[0]], 0.5)
    for i in range(8, 12):
        out_copies[i].start()
    for f in range(frames):
        for copy in frame_copies(f):
            copy.wait()
    for copy in out_copies:
        copy.wait()


def run_finish(shape, io, par, gall, conv, norm, table):
    count, strip, breadth, _ = shape
    hbm = pl.BlockSpec(memory_space=pl.ANY)
    vmem = pl.BlockSpec(memory_space=pltpu.VMEM)
    params = [
        jax.ShapeDtypeStruct(v[0].shape, dtype)
        for v in (conv, norm, table)
        for dtype in (F32, F32, F32, BF16)
    ]
    return pl.pallas_call(
        finish_kernel,
        out_shape=(
            jax.ShapeDtypeStruct(shape, BF16),
            jax.ShapeDtypeStruct(shape, F32),
            *params,
        ),
        in_specs=[hbm] * 3 + [vmem] * 9,
        out_specs=(hbm,) * 14,
        scratch_shapes=[VM(v.shape, v.dtype) for v in params]
        + [
            VM(io.shape, F32),
            VM((3,) + par.shape[1:], F32),
            VM((gall.shape[0] // 4,) + gall.shape[1:], BF16),
            VM((strip, breadth, 128), F32),
            VM(shape, BF16),
            VM(shape, F32),
            VM(norm[0].shape, F32),
            pltpu.SemaphoreType.DMA((2 * count,)),
            pltpu.SemaphoreType.DMA((4,)),
            pltpu.SemaphoreType.DMA((count,)),
            pltpu.SemaphoreType.DMA((count,)),
            pltpu.SemaphoreType.DMA((12,)),
        ],
        compiler_params=pltpu.CompilerParams(vmem_limit_bytes=48 * 1024 * 1024),
        name="finish",
    )(io, par, gall, *conv, *norm, *table)


def local(
    nd,
    ns,
    frames,
    cotangent,
    actions,
    noise_ids,
    games,
    live_counts,
    conv_weight,
    conv_moment,
    conv_square,
    norm_map,
    norm_moment,
    norm_square,
    emb_table,
    table_moment,
    table_square,
):
    conv = [v.T for v in (conv_weight, conv_moment, conv_square)]
    norm = [jnp.transpose(v, (1, 0, 2)) for v in (norm_map, norm_moment, norm_square)]
    table = (emb_table, table_moment, table_square)
    io, par, gall = run_step(
        nd,
        ns,
        frames,
        cotangent,
        actions,
        noise_ids,
        games,
        live_counts,
        conv[0],
        norm[0],
        emb_table,
    )
    result, frames_grad, *new = run_finish(
        frames.shape, io, par, gall, conv, norm, table
    )
    conv_out = [v.T for v in new[0:4]]
    norm_out = [jnp.transpose(v, (1, 0, 2)) for v in new[4:8]]
    return (result, frames_grad, *conv_out, *norm_out, *new[8:12])


def solution(mesh):
    split = P("dp", "space", None, None)
    in_specs = (split, split) + (P("dp"),) * 4 + (P(),) * 9
    out_specs = (split, split) + (P(),) * 12
    sizes = dict(mesh.shape)
    return jax.shard_map(
        functools.partial(local, sizes["dp"], sizes["space"]),
        mesh=mesh,
        in_specs=in_specs,
        out_specs=out_specs,
        check_vma=False,
    )
```

```python
import functools

import jax
import jax.numpy as jnp
from jax import lax
from jax.experimental import pallas as pl
from jax.experimental.pallas import tpu as pltpu
from jax.sharding import PartitionSpec as P

ACTIONS = 18
NOISE_LEVELS = 64
ADAM_STEP = 4
NORM_EPSILON = 1e-05
ADAM_EPS = 1e-08
BETA_ONE = 0.5
BETA_TWO = 0.5
DECAY = 0.01
HIGH = lax.Precision.HIGHEST
F32 = jnp.float32
BF16 = jnp.bfloat16
MESH = pl.DeviceIdType.MESH
VM = pltpu.VMEM

ALPHA, BETA, RSTD, NMR, GAIN, SHIFT, COEF, BIAS = range(8)


def dot_nn(a, b):
    return lax.dot_general(a, b, (((1,), (0,)), ((), ())), preferred_element_type=F32)


def dot_nt(a, b):
    return lax.dot_general(a, b, (((1,), (1,)), ((), ())), preferred_element_type=F32)


def dot_tn(a, b):
    return lax.dot_general(a, b, (((0,), (0,)), ((), ())), preferred_element_type=F32)


def dot_high(a, b):
    return lax.dot_general(
        a, b, (((1,), (0,)), ((), ())), precision=HIGH, preferred_element_type=F32
    )


def logistic(z):
    return 0.5 * jnp.tanh(0.5 * z) + 0.5


def lane_iota(shape):
    return lax.broadcasted_iota(jnp.int32, shape, len(shape) - 1)


def swap(v):
    return pltpu.roll(v, 64, len(v.shape) - 1)


def join(lo, hi):
    return jnp.where(lane_iota(lo.shape) < 64, lo, hi)


def twice(row):
    return jnp.concatenate([row, row], axis=-1)


def step_kernel(
    nd,
    n,
    x_hbm,
    cot_hbm,
    act_hbm,
    noise_hbm,
    game_hbm,
    live_hbm,
    cw_hbm,
    nm_hbm,
    tab_hbm,
    io_hbm,
    par_hbm,
    gall_hbm,
    act_ref,
    noise_ref,
    game_ref,
    live_ref,
    raw,
    cw_ref,
    tab_ref,
    tmp,
    xs,
    gs,
    e1,
    e2,
    esk,
    eg,
    c1,
    gsa,
    gz,
    dv,
    c3,
    gh4,
    gzc,
    gco,
    ec3,
    ec4,
    ecg,
    ecg3,
    ecy,
    ed,
    w1f,
    w1b,
    w2f,
    w2b,
    wsf,
    wsb,
    wup,
    wco,
    wdf,
    wdb,
    w3f,
    w3b,
    w4f,
    w4b,
    acc,
    prm,
    tabp,
    stat,
    hal,
    hout,
    hfull,
    hfout,
    nmv,
    nmb,
    gt_ref,
    rbuf,
    part,
    zbuf,
    zfull,
    zwhole,
    gown,
    packs,
    local_sem,
    out_sem,
    fg_sem,
    stat_send,
    stat_recv,
    halo_send,
    halo_recv,
    dp_send,
    dp_recv,
    sp_send,
    sp_recv,
    own_sem,
):
    frames, strip = raw.shape[0], raw.shape[1]
    breadth = raw.shape[2]
    half = frames // 2
    rows = strip // 2
    cols = breadth // 2
    me = lax.axis_index("space")
    dp = lax.axis_index("dp")
    full_cells = float(strip * n * breadth * 32)
    coarse_cells = full_cells / 4.0
    owned = rows * cols
    ext = (rows + 2) * cols

    x_copies = []
    for piece in range(2):
        at = pl.ds(piece * half, half)
        x_copies.append(
            pltpu.make_async_copy(x_hbm.at[at], raw.at[at], local_sem.at[13 * piece])
        )
    for copy in x_copies:
        copy.start()
    g_copy = pltpu.make_async_copy(cot_hbm, raw, local_sem.at[1])
    map_copies = [
        pltpu.make_async_copy(nm_hbm.at[pl.ds(0, 256), k], nmv.at[k], local_sem.at[2 + k])
        for k in range(4)
    ]
    map_copies.append(pltpu.make_async_copy(nm_hbm.at[256], nmb, local_sem.at[6]))
    map_copies.append(pltpu.make_async_copy(tab_hbm, tab_ref, local_sem.at[7]))
    ids = ((act_hbm, act_ref), (noise_hbm, noise_ref), (game_hbm, game_ref), (live_hbm, live_ref))
    for i, (there, here) in enumerate(ids):
        map_copies.append(pltpu.make_async_copy(there, here, local_sem.at[9 + i]))
    weight_copy = pltpu.make_async_copy(cw_hbm, cw_ref, local_sem.at[8])
    weight_copy.start()
    for copy in map_copies:
        copy.start()

    barrier = pltpu.get_barrier_semaphore()
    for off in range(1, n):
        pl.semaphore_signal(
            barrier,
            inc=1,
            device_id={"space": lax.rem(me + off, n)},
            device_id_type=MESH,
        )
    for off in range(1, nd):
        pl.semaphore_signal(
            barrier,
            inc=1,
            device_id={"dp": lax.rem(dp + off, nd)},
            device_id_type=MESH,
        )

    def halo_copies(k, first, last, to_up, to_down):
        up = pltpu.make_async_remote_copy(
            src_ref=first,
            dst_ref=to_up,
            send_sem=halo_send.at[k, 0],
            recv_sem=halo_recv.at[k, 0],
            device_id={"space": lax.rem(me + n - 1, n)},
            device_id_type=MESH,
        )
        down = pltpu.make_async_remote_copy(
            src_ref=last,
            dst_ref=to_down,
            send_sem=halo_send.at[k, 1],
            recv_sem=halo_recv.at[k, 1],
            device_id={"space": lax.rem(me + 1, n)},
            device_id_type=MESH,
        )
        return up, down

    def halo_start(copies):
        @pl.when(me > 0)
        def _():
            copies[0].start()

        @pl.when(me < n - 1)
        def _():
            copies[1].start()

    def halo_wait(copies):
        @pl.when(me < n - 1)
        def _():
            copies[0].wait_recv()

        @pl.when(me > 0)
        def _():
            copies[1].wait_recv()

    def halo_finish(copies):
        @pl.when(me > 0)
        def _():
            copies[0].wait_send()

        @pl.when(me < n - 1)
        def _():
            copies[1].wait_send()

    def stat_copy(k, off, slots):
        return pltpu.make_async_remote_copy(
            src_ref=stat.at[k, slots],
            dst_ref=stat.at[k, slots],
            send_sem=stat_send.at[k],
            recv_sem=stat_recv.at[k],
            device_id={"space": lax.rem(me + off, n)},
            device_id_type=MESH,
        )

    def stat_start(k, value):
        stat[k, me] = value
        for off in range(1, n):
            stat_copy(k, off, me).start()

    def stat_total(k):
        peers = stat_copy(k, 1, pl.ds(0, n - 1))
        peers.wait_recv()
        total = stat[k, 0]
        for i in range(1, n):
            total = total + stat[k, i]
        peers.wait_send()
        return total

    def wide_halos(k, v):
        both = halo_copies(
            k, v.at[:, 2], v.at[:, rows + 1], v.at[:, rows + 2], v.at[:, 1]
        )
        third = halo_copies(
            k + 1,
            v.at[:, 3, :, pl.ds(0, 128)],
            v.at[:, rows, :, pl.ds(128, 128)],
            v.at[:, rows + 3, :, pl.ds(0, 128)],
            v.at[:, 0, :, pl.ds(128, 128)],
        )
        return both, third

    x_halos = wide_halos(0, xs)
    g_halos = wide_halos(8, gs)

    def coarse_halo(k):
        return halo_copies(
            k, hout.at[k - 2, 0], hout.at[k - 2, 1], hal.at[k - 2, 1], hal.at[k - 2, 0]
        )

    g_h4_halo, d_halo, c3_halo, y_halo, g_h3_halo = [coarse_halo(k) for k in range(2, 7)]
    g_h2_halo = halo_copies(7, hfout.at[0], hfout.at[1], hfull.at[1], hfull.at[0])

    def block_mask(shape, pad):
        blocks = shape[0]
        b = lax.broadcasted_iota(jnp.int32, shape, 0)
        low = jnp.where(me > 0, 0, pad)
        high = jnp.where(me < n - 1, blocks, blocks - pad)
        return (b >= low) & (b < high)

    def param(k, which, f):
        return prm[k * 8 + which, pl.ds(f, 1), :]

    def wide(k, which, f):
        return twice(param(k, which, f))

    def put_row(carry, f, value):
        row = lax.broadcasted_iota(jnp.int32, carry.shape, 0)
        return jnp.where(row == f, value, carry)

    def full_sum(v):
        s = jnp.sum(v.reshape(-1, 256), axis=0, keepdims=True)
        return s[:, :128] + s[:, 128:]

    def paired(raw_rows):
        count = raw_rows.shape[0]
        tmp[0:count, :, 0:64] = raw_rows.astype(F32)
        even = tmp[0:count, pl.ds(0, cols, stride=2), :]
        odd = tmp[0:count, pl.ds(1, cols, stride=2), :]
        return join(even, swap(odd))

    def pair_halves(p):
        count = p.shape[0] // 2
        p = p.reshape(count, 2, cols, 128)
        return p[:, 0], p[:, 1]

    def neighbours(v):
        count = v.shape[0]
        flat = v.reshape(count * cols, 128)
        up = pltpu.roll(flat, count * cols - 1, 0).reshape(v.shape)
        down = pltpu.roll(flat, 1, 0).reshape(v.shape)
        return up, down

    def put_e(e, f, start, h):
        count = h.shape[0]
        for part in range(2):
            v = h[:, :, part * 128 : (part + 1) * 128]
            up, down = neighbours(v)
            lane = lane_iota(v.shape)
            q = lax.broadcasted_iota(jnp.int32, v.shape, 1)
            near = jnp.where(
                lane < 64, jnp.where(q == cols - 1, 0.0, up), jnp.where(q == 0, 0.0, down)
            )
            e[f, start : start + count, :, part * 256 : part * 256 + 128] = v.astype(BF16)
            e[f, start : start + count, :, part * 256 + 128 : part * 256 + 256] = near.astype(BF16)

    def window(e, f, start, count):
        return jnp.concatenate(
            [
                e[f, start - 1 : start - 1 + count, :, 256:512],
                e[f, start : start + count, :, :],
                e[f, start + 1 : start + 1 + count, :, 0:256],
            ],
            axis=-1,
        ).reshape(count * cols, 1024)

    def own_pixels(e, f, start, count):
        return jnp.concatenate(
            [
                e[f, start : start + count, :, 0:128],
                e[f, start : start + count, :, 256:384],
            ],
            axis=-1,
        ).reshape(count * cols, 256)

    def put_ec(ec, hf, v):
        up, down = neighbours(v)
        q = lax.broadcasted_iota(jnp.int32, v.shape, 1)
        ec[hf, :, :, 0:128] = jnp.where(q == 0, 0.0, down).astype(BF16)
        ec[hf, :, :, 128:256] = v.astype(BF16)
        ec[hf, :, :, 256:384] = jnp.where(q == cols - 1, 0.0, up).astype(BF16)

    def coarse_window(ec, hf):
        return jnp.concatenate([ec[hf, a : a + rows] for a in range(3)], axis=-1).reshape(
            owned, 1152
        )

    def coarse_sum(v):
        return jnp.sum(v.reshape(-1, 128), axis=0, keepdims=True)

    def with_halo(ref, hf, k):
        ref[hf, 0] = hal[k, 0, hf].astype(F32)
        ref[hf, rows + 1] = hal[k, 1, hf].astype(F32)

    def border(ref_out, k, hf, v):
        ref_out[k, 0, hf] = v[0].astype(BF16)
        ref_out[k, 1, hf] = v[rows - 1].astype(BF16)

    def group_matrix(coarse):
        r = lax.broadcasted_iota(jnp.int32, (128, 128), 0) // 32
        c = lax.broadcasted_iota(jnp.int32, (128, 128), 1) // 32
        same = (r == c) if coarse else (r % 2 == c % 2)
        return jnp.where(same, 1.0, 0.0)

    def norm_forward(k, total, coarse):
        cells = coarse_cells if coarse else full_cells
        count = half if coarse else frames
        moments = dot_high(total, group_matrix(coarse)) / cells
        mean = moments[0:count]
        var = moments[count : 2 * count] - mean * mean
        rstd = lax.rsqrt(var + NORM_EPSILON)
        gain = prm[k * 8 + GAIN, 0:count, :]
        alpha = rstd * gain
        prm[k * 8 + ALPHA, 0:count, :] = alpha
        prm[k * 8 + BETA, 0:count, :] = prm[k * 8 + SHIFT, 0:count, :] - mean * alpha
        prm[k * 8 + RSTD, 0:count, :] = rstd
        prm[k * 8 + NMR, 0:count, :] = -mean * rstd

    def norm_backward(k, total, coarse):
        cells = coarse_cells if coarse else full_cells
        count = half if coarse else frames
        gain = prm[k * 8 + GAIN, 0:count, :]
        shift_grad = total[0:count]
        scale_grad = total[count : 2 * count]
        means = (
            dot_high(
                jnp.concatenate([shift_grad * gain, scale_grad * gain], axis=0),
                group_matrix(coarse),
            )
            / cells
        )
        rstd = prm[k * 8 + RSTD, 0:count, :]
        factor = -rstd * means[count : 2 * count]
        prm[k * 8 + COEF, 0:count, :] = rstd * factor
        prm[k * 8 + BIAS, 0:count, :] = (
            prm[k * 8 + NMR, 0:count, :] * factor - rstd * means[0:count]
        )
        if coarse:
            scale_all = jnp.concatenate([scale_grad, swap(scale_grad)], axis=0)
            shift_all = jnp.concatenate([shift_grad, swap(shift_grad)], axis=0)
        else:
            scale_all = scale_grad + swap(scale_grad)
            shift_all = shift_grad + swap(shift_grad)
        packs[dp, :, k * 128 : (k + 1) * 128] = join(scale_all, swap(shift_all))

    slots = 32 // nd
    share = 64 // n
    early = max(1, 16 // nd)
    stages = (0, 1, 2) if early > 1 else (0, 2)
    stage_slots = [pl.ds(early, slots - early), pl.ds(1, 1), pl.ds(0, 1)]

    def dp_copy(which, src, dst, off):
        return pltpu.make_async_remote_copy(
            src_ref=src,
            dst_ref=dst,
            send_sem=dp_send.at[which],
            recv_sem=dp_recv.at[which],
            device_id={"dp": lax.rem(dp + off, nd)},
            device_id_type=MESH,
        )

    def sp_copy(which, src, dst, off):
        return pltpu.make_async_remote_copy(
            src_ref=src,
            dst_ref=dst,
            send_sem=sp_send.at[which],
            recv_sem=sp_recv.at[which],
            device_id={"space": lax.rem(me + off, n)},
            device_id_type=MESH,
        )

    dp_peers, sp_peers = pl.ds(0, nd - 1), pl.ds(0, n - 1)

    def first_all(stage):
        ref = rbuf.at[dp_peers, stage_slots[stage]]
        return dp_copy(stage, ref, ref, 1)

    def last_all(stage):
        ref = gall_hbm.at[dp_peers, stage_slots[stage]]
        return dp_copy(3 + stage, ref, ref, 1)

    def pack_lanes(which):
        return pl.ds(0, 128) if which else pl.ds(128, 768)

    def pack_all(which):
        ref = packs.at[dp_peers, :, pack_lanes(which)]
        return dp_copy(6 + which, ref, ref, 1)

    def pack_start(which):
        ref = packs.at[dp, :, pack_lanes(which)]
        for off in range(1, nd):
            dp_copy(6 + which, ref, ref, off).start()

    def space_all(which):
        if which >= 2:
            ref = zwhole.at[which - 2, sp_peers]
        else:
            ref = zbuf.at[sp_peers, stage_slots[0]]
        return sp_copy(which, ref, ref, 1)

    def gather_start(stage):
        if stage not in stages:
            return
        where = stage_slots[stage]
        for off in range(1, nd):
            owner = lax.rem(dp + off, nd)
            dp_copy(stage, gt_ref.at[where, owner], rbuf.at[dp, where], off).start()

    def gather_space(stage):
        if stage not in stages:
            return
        where = stage_slots[stage]
        first_all(stage).wait_recv()
        rbuf[dp, where] = gt_ref[where, dp]
        total = rbuf[0, where].astype(F32)
        for i in range(1, nd):
            total = total + rbuf[i, where].astype(F32)
        if stage > 0:
            zwhole[stage - 1, me] = total[0]
            ref = zwhole.at[stage - 1, me]
            for off in range(1, n):
                sp_copy(stage + 1, ref, ref, off).start()
            return
        for z in range(n):
            part[z, where] = total[:, z * share : (z + 1) * share]
        for off in range(1, n):
            row = lax.rem(me + off, n)
            sp_copy(0, part.at[row, where], zbuf.at[me, where], off).start()

    def gather_spread():
        where = stage_slots[0]
        space_all(0).wait_recv()
        zbuf[me, where] = part[me, where]
        total = zbuf[0, where]
        for i in range(1, n):
            total = total + zbuf[i, where]
        zfull[me, where] = total
        for off in range(1, n):
            sp_copy(1, zfull.at[me, where], zfull.at[me, where], off).start()

    def own_copy(stage):
        where = stage_slots[stage]
        return pltpu.make_async_copy(gown.at[where], gall_hbm.at[dp, where], own_sem.at[stage])

    def gather_all(stage):
        if stage not in stages:
            return
        where = stage_slots[stage]
        if stage > 0:
            space_all(stage + 1).wait_recv()
            total = zwhole[stage - 1, 0]
            for i in range(1, n):
                total = total + zwhole[stage - 1, i]
            gown[where] = total[None].astype(BF16)
        else:
            space_all(1).wait_recv()
            whole = jnp.concatenate([zfull[z, where] for z in range(n)], axis=1)
            gown[where] = whole.astype(BF16)
        for off in range(1, nd):
            dp_copy(3 + stage, gown.at[where], gall_hbm.at[dp, where], off).start()
        own_copy(stage).start()

    def gather_finish(stage):
        last_all(stage).wait_recv()
        first_all(stage).wait_send()
        last_all(stage).wait_send()
        own_copy(stage).wait()
        for which in (stage + 1,) if stage > 0 else (0, 1):
            space_all(which).wait_send()

    def load_x(f, carry):
        total, square = carry
        even, odd = pair_halves(paired(raw[f]))
        both = jnp.concatenate([even, odd], axis=-1)
        xs[f, 2 : 2 + rows] = both.astype(BF16)
        return put_row(total, f, full_sum(both)), put_row(square, f, full_sum(both * both))

    zero_rows = jnp.zeros((frames, 128), F32)
    sums = (zero_rows, zero_rows)
    for piece in range(2):
        x_copies[piece].wait()
        sums = lax.fori_loop(piece * half, piece * half + half, load_x, sums, unroll=4)
    g_copy.start()
    pl.semaphore_wait(barrier, n + nd - 2)
    stat_start(0, jnp.concatenate(sums, axis=0))
    for copies in x_halos:
        halo_start(copies)

    @pl.when(me == 0)
    def _():
        for v in (xs, gs):
            v[:, 0:2] = jnp.zeros((frames, 2, cols, 256), BF16)
        for which in range(hal.shape[0]):
            hal[which, 0] = jnp.zeros(hal.shape[2:], BF16)
        hfull[0] = jnp.zeros(hfull.shape[1:], BF16)

    @pl.when(me == n - 1)
    def _():
        for v in (xs, gs):
            v[:, rows + 2 : rows + 4] = jnp.zeros((frames, 2, cols, 256), BF16)
        for which in range(hal.shape[0]):
            hal[which, 1] = jnp.zeros(hal.shape[2:], BF16)
        hfull[1] = jnp.zeros(hfull.shape[1:], BF16)

    for v in (xs, gs):
        v[:, 0, :, 0:128] = jnp.zeros((frames, cols, 128), BF16)
        v[:, rows + 3, :, 128:256] = jnp.zeros((frames, cols, 128), BF16)

    def conditioning():
        entry = lax.broadcasted_iota(jnp.int32, (frames, 128), 1)
        row = lax.broadcasted_iota(jnp.int32, (frames, 128), 0)
        hot = jnp.zeros((frames, 128), F32)
        for copy in map_copies:
            copy.wait()
        for f in range(frames):
            hit = (
                (entry == act_ref[f])
                | (entry == noise_ref[f] + ACTIONS)
                | (entry == game_ref[f] + ACTIONS + NOISE_LEVELS)
            )
            hot = jnp.where((row == f) & hit, 1.0, hot)
        table_rows = tab_ref.shape[0]
        tabp[...] = jnp.zeros(tabp.shape, F32)
        tabp[0:table_rows, :] = tab_ref[...]
        embedded = dot_high(hot, tabp[...])
        packs[dp, :, 512:768] = embedded
        packs[dp, :, 768:896] = hot
        for k in range(4):
            mod = dot_high(embedded, nmv[k]) + nmb[k : k + 1, :]
            scale = join(mod, swap(mod)) + 1.0
            shift = join(swap(mod), mod)
            if k < 2:
                prm[k * 8 + GAIN] = scale
                prm[k * 8 + SHIFT] = shift
            else:
                prm[k * 8 + GAIN, 0:half, :] = join(scale[0:half], scale[half:])
                prm[k * 8 + SHIFT, 0:half, :] = join(shift[0:half], shift[half:])

    conditioning()

    g_copy.wait()

    def load_cotangent(f, carry):
        live = jnp.where(f < live_ref[0], 1.0, 0.0)
        even, odd = pair_halves(paired(raw[f]))
        both = jnp.concatenate([even, odd], axis=-1)
        gs[f, 2 : 2 + rows] = (both * live).astype(BF16)
        return carry

    lax.fori_loop(0, frames, load_cotangent, 0, unroll=4)
    for copies in g_halos:
        halo_start(copies)


    def tap(index):
        first = (index // 2) * 128
        last = min(first + 128, cw_ref.shape[1])
        tile = cw_ref[:, first:last].astype(BF16).astype(F32)
        if last - first < 128:
            tile = jnp.concatenate([tile, jnp.zeros((64, 128 - last + first), F32)], axis=-1)
        return tile, index % 2

    def low_half(index):
        tile, odd = tap(index)
        return swap(tile) if odd else tile

    def high_half(index):
        tile, odd = tap(index)
        return tile if odd else swap(tile)

    def lane_pair(low_index, high_index):
        zero = jnp.zeros((64, 128), F32)
        low = zero if low_index is None else low_half(low_index)
        high = zero if high_index is None else high_half(high_index)
        return join(low, high).astype(BF16)

    def fine_weights(index, forward_w, backward_w):
        zero = jnp.zeros((64, 128), BF16)
        pairs = []
        for t in range(3):
            p12 = lane_pair(index(t, 1), index(t, 2))
            p01 = lane_pair(index(t, 0), index(t, 1))
            pz0 = lane_pair(None, index(t, 0))
            p2z = lane_pair(index(t, 2), None)
            pairs.append((p12, p01, pz0, p2z))
        for a in range(4):
            for dr in range(2):
                t = a - dr
                ok = 0 <= t <= 2
                for dq in range(2):
                    r = (dr * 2 + dq) * 64
                    first = pairs[t][0 if dq == 0 else 1] if ok else zero
                    second = pairs[t][2 if dq == 0 else 3] if ok else zero
                    forward_w[r : r + 64, a * 256 : a * 256 + 128] = first
                    forward_w[r : r + 64, a * 256 + 128 : a * 256 + 256] = second
                t = 2 - a + dr
                ok = 0 <= t <= 2
                for g in range(4):
                    r = a * 256 + g * 64
                    backward_w[r : r + 64, dr * 128 : dr * 128 + 128] = (
                        pairs[t][g] if ok else zero
                    )

    def coarse_weights(index, forward_w, backward_w):
        for a in range(3):
            for j in range(3):
                lane = (a * 3 + j) * 128
                low = lane_pair(index(a, j), None)
                high = lane_pair(None, index(a, j))
                forward_w[0:64, lane : lane + 128] = low
                forward_w[64:128, lane : lane + 128] = high
                lane = ((2 - a) * 3 + (2 - j)) * 128
                backward_w[lane : lane + 64, :] = low
                backward_w[lane + 64 : lane + 128, :] = high

    def down_weights(index):
        zero = jnp.zeros((64, 128), BF16)
        wdf[...] = jnp.zeros(wdf.shape, BF16)
        wdb[...] = jnp.zeros(wdb.shape, BF16)
        for t in range(3):
            p12 = lane_pair(index(t, 1), index(t, 2))
            pz0 = lane_pair(None, index(t, 0))
            for hi in range(2):
                lane = hi * 768 + t * 256
                wdf[hi * 64 : hi * 64 + 64, lane : lane + 128] = p12
                wdf[hi * 64 : hi * 64 + 64, lane + 128 : lane + 256] = pz0
                i, dr = ((1, 1), (0, 0), (0, 1))[t]
                lane = hi * 256 + dr * 128
                for j in range(2):
                    r = (i * 2 + j) * 128 + hi * 64
                    wdb[r : r + 64, lane : lane + 128] = p12 if j == 0 else pz0

    def up_weights():
        def up_tap(ta, tb):
            return low_half(45 + (ta * 3 + tb) * 2 + 1)

        taps = [[up_tap(ta, tb) for tb in range(3)] for ta in range(3)]
        members = {(0, 0): (0,), (0, 1): (1, 2), (1, 1): (0, 1), (1, 2): (2,)}
        wup[...] = jnp.zeros(wup.shape, BF16)
        for (dr, i), in_rows in members.items():
            for (dq, j), in_cols in members.items():
                total = sum(taps[ta][tb] for ta in in_rows for tb in in_cols)
                zero = jnp.zeros_like(total)
                r = (dr * 2 + dq) * 64
                lane = (i * 3 + j) * 128
                wup[r : r + 64, lane : lane + 128] = join(total, zero).astype(BF16)
                wup[256 + r : 256 + r + 64, lane : lane + 128] = join(zero, swap(total)).astype(
                    BF16
                )
        for a in range(4):
            for g, off in enumerate((0, 1, 2, -1)):
                chosen = [
                    taps[2 - a + dr][1 - off + dq]
                    for dr in range(2)
                    for dq in range(2)
                    if 0 <= 2 - a + dr <= 2 and 0 <= 1 - off + dq <= 2
                ]
                total = sum(chosen[1:], chosen[0])
                zero = jnp.zeros_like(total)
                r = a * 256 + g * 64
                wco[0, r : r + 64, :] = join(total, zero).astype(BF16)
                wco[1, r : r + 64, :] = join(zero, swap(total)).astype(BF16)

    def stacked(k):
        return lambda t, s: k * 9 + t * 3 + s

    weight_copy.wait()
    fine_weights(stacked(0), w1f, w1b)
    fine_weights(stacked(1), w2f, w2b)
    fine_weights(lambda t, s: 45 + (t * 3 + s) * 2, wsf, wsb)
    up_weights()
    down_weights(stacked(2))
    coarse_weights(stacked(3), w3f, w3b)
    coarse_weights(stacked(4), w4f, w4b)

    for copies in x_halos:
        halo_wait(copies)
    norm_forward(0, stat_total(0), False)

    def first_layer(f, carry):
        total, square = carry
        x = xs[f].astype(F32)
        z = x * wide(0, ALPHA, f) + wide(0, BETA, f)
        h = z * logistic(z)
        h = jnp.where(block_mask(h.shape, 2), h, 0.0)
        put_e(e1, f, 0, h)
        out = dot_nt(window(e1, f, 1, rows + 2), w1f[...]).reshape(rows + 2, cols, 256)
        c1[f] = out
        own = out[1 : rows + 1]
        return put_row(total, f, full_sum(own)), put_row(square, f, full_sum(own * own))

    sums = lax.fori_loop(0, frames, first_layer, (zero_rows, zero_rows), unroll=4)
    stat_start(1, jnp.concatenate(sums, axis=0))

    for copies in g_halos:
        halo_wait(copies)

    def load_g(f, carry):
        g = gs[f].astype(F32)
        put_e(eg, f, 0, jnp.where(block_mask(g.shape, 2), g, 0.0))
        gsa[f] = dot_nn(window(eg, f, 1, rows + 2), wsb[...]).reshape(rows + 2, cols, 256)
        return carry

    lax.fori_loop(0, frames, load_g, 0, unroll=4)

    norm_forward(1, stat_total(1), False)

    def second_layer(f, carry):
        z = c1[f] * wide(1, ALPHA, f) + wide(1, BETA, f)
        h = z * logistic(z)
        h = jnp.where(block_mask(h.shape, 1), h, 0.0)
        edge = jnp.zeros((cols, 512), BF16)
        e2[f, 0] = edge
        e2[f, rows + 3] = edge
        put_e(e2, f, 1, h)
        out = dot_nt(window(e2, f, 1, rows + 2), w2f[...]).reshape(rows + 2, cols, 256)
        skip = out + xs[f, 1 : rows + 3].astype(F32)
        skip = jnp.where(block_mask(skip.shape, 1), skip, 0.0)
        put_e(esk, f, 1, skip)
        return carry

    lax.fori_loop(0, frames, second_layer, 0, unroll=4)

    def down_window(f):
        return jnp.concatenate(
            [esk[f, 1 : 1 + rows, :, 256:512], esk[f, 2 : 2 + rows]], axis=-1
        ).reshape(owned, 768)

    zero_coarse = jnp.zeros((half, 128), F32)
    pad_rows = [jnp.zeros((2 * frames - 2 * half, 128), F32)]

    def down_layer(hf, carry):
        total, square = carry
        d = dot_nt(down_window(hf), wdf[:, 0:768]) + dot_nt(
            down_window(hf + half), wdf[:, 768:1536]
        )
        d = d.reshape(rows, cols, 128)
        dv[hf, 1 : rows + 1] = d
        border(hout, 1, hf, d)
        return put_row(total, hf, coarse_sum(d)), put_row(square, hf, coarse_sum(d * d))

    sums = lax.fori_loop(0, half, down_layer, (zero_coarse, zero_coarse), unroll=4)
    stat_start(2, jnp.concatenate(list(sums) + pad_rows, axis=0))
    halo_start(d_halo)

    def coarse_gradient(hf, carry):
        g = dot_nn(window(eg, hf, 1, rows + 2), wco[0]) + dot_nn(
            window(eg, hf + half, 1, rows + 2), wco[1]
        )
        g = g.reshape(rows + 2, cols, 128)
        g = jnp.where(block_mask(g.shape, 1), g, 0.0).astype(BF16).astype(F32)
        gco[hf] = g
        put_ec(ecg, hf, g)
        back = dot_nn(coarse_window(ecg, hf), w4b[...]).reshape(rows, cols, 128)
        gh4[hf, 1 : rows + 1] = back
        border(hout, 0, hf, back)
        return carry

    lax.fori_loop(0, half, coarse_gradient, 0, unroll=4)
    halo_start(g_h4_halo)

    def put_half(index, value):
        slot, owner = index // 2 // nd, index // 2 % nd
        current = gt_ref[slot, owner].astype(F32)
        value = join(current, swap(value)) if index % 2 else join(value, current)
        gt_ref[slot, owner] = value.astype(BF16)

    gt_ref[...] = jnp.zeros(gt_ref.shape, BF16)

    def fine_kernel_grad(index, e, start, gradient, gradient_start):
        acc[0, :, 0:1024] = jnp.zeros((256, 1024), F32)

        def add(f, carry):
            g = own_pixels(gradient, f, gradient_start, rows)
            acc[0, :, 0:1024] += dot_tn(g, window(e, f, start, rows))
            return carry

        lax.fori_loop(0, frames, add, 0, unroll=4)
        for t in range(3):
            u = []
            for dq in range(2):
                parts = [
                    acc[0, (dr * 2 + dq) * 64 : (dr * 2 + dq) * 64 + 64, pl.ds((t + dr) * 256, 256)]
                    for dr in range(2)
                ]
                u.append(parts[0] + parts[1])
            near, far = [v[:, 0:128] for v in u], [v[:, 128:256] for v in u]
            put_half(index(t, 0), swap(far[0]) + near[1])
            put_half(index(t, 1), near[0] + swap(near[1]))
            put_half(index(t, 2), swap(near[0]) + far[1])

    def coarse_kernel_grad(index, ec, gradient):
        acc[0, 0:128, :] = jnp.zeros((128, 1152), F32)

        def add(hf, carry):
            g = gradient[hf, 1 : rows + 1, :, 128:256].reshape(owned, 128)
            acc[0, 0:128, :] += dot_tn(g, coarse_window(ec, hf))
            return carry

        lax.fori_loop(0, half, add, 0, unroll=4)
        for a in range(3):
            for j in range(3):
                lanes = pl.ds((a * 3 + j) * 128, 128)
                put_half(index(a, j), acc[0, 0:64, lanes] + swap(acc[0, 64:128, lanes]))

    def down_kernel_grad(index):
        acc[:, 0:128, 0:768] = jnp.zeros((2, 128, 768), F32)

        def add(hf, carry):
            g = ed[hf, 1 : rows + 1, :, 0:128].reshape(owned, 128)
            acc[0, 0:128, 0:768] += dot_tn(g, down_window(hf))
            acc[1, 0:128, 0:768] += dot_tn(g, down_window(hf + half))
            return carry

        lax.fori_loop(0, half, add, 0, unroll=4)
        for a in range(3):
            near = acc[0, 0:64, pl.ds(a * 256, 128)] + acc[1, 64:128, pl.ds(a * 256, 128)]
            far = (
                acc[0, 0:64, pl.ds(a * 256 + 128, 128)] + acc[1, 64:128, pl.ds(a * 256 + 128, 128)]
            )
            put_half(index(a, 0), swap(far))
            put_half(index(a, 1), near)
            put_half(index(a, 2), swap(near))

    def up_kernel_grad():
        acc[...] = jnp.zeros(acc.shape, F32)

        def add(hf, carry):
            v = coarse_window(ecy, hf)
            acc[0] += dot_tn(own_pixels(eg, hf, 2, rows), v)
            acc[1] += dot_tn(own_pixels(eg, hf + half, 2, rows), v)
            return carry

        lax.fori_loop(0, half, add, 0, unroll=4)

        def block(dr, dq, i, j):
            r = (dr * 2 + dq) * 64
            lanes = pl.ds((i * 3 + j) * 128, 128)
            return acc[0, r : r + 64, lanes] + swap(acc[1, r : r + 64, lanes])

        place = {(0, 0): 0, (0, 1): 1, (0, 2): 1, (1, 0): 1, (1, 1): 1, (1, 2): 2}
        for ta in range(3):
            for tb in range(3):
                total = sum(
                    block(dr, dq, place[dr, ta], place[dq, tb])
                    for dr in range(2)
                    for dq in range(2)
                )
                put_half(45 + (ta * 3 + tb) * 2 + 1, total)


    halo_wait(d_halo)
    norm_forward(2, stat_total(2), True)

    def third_layer(hf, carry):
        total, square = carry
        with_halo(dv, hf, 1)
        z = dv[hf] * param(2, ALPHA, hf) + param(2, BETA, hf)
        h = z * logistic(z)
        put_ec(ec3, hf, jnp.where(block_mask(h.shape, 1), h, 0.0))
        out = dot_nt(coarse_window(ec3, hf), w3f[...]).reshape(rows, cols, 128)
        c3[hf, 1 : rows + 1] = out
        border(hout, 2, hf, out)
        return put_row(total, hf, coarse_sum(out)), put_row(square, hf, coarse_sum(out * out))

    sums = lax.fori_loop(0, half, third_layer, (zero_coarse, zero_coarse), unroll=4)
    stat_start(3, jnp.concatenate(list(sums) + pad_rows, axis=0))
    halo_start(c3_halo)

    def result_copy(f):
        return pltpu.make_async_copy(gz.at[f, pl.ds(1, rows)], io_hbm.at[f], out_sem.at[f])

    def merge_skip(f, carry):
        out = dot_nt(window(esk, f, 2, rows), wsf[...])
        gz[f, 1 : rows + 1] = out.reshape(rows, cols, 256)
        return carry

    lax.fori_loop(0, half, merge_skip, 0, unroll=4)
    fine_kernel_grad(lambda t, s: 45 + (t * 3 + s) * 2, esk, 2, eg, 2)

    halo_wait(c3_halo)
    halo_wait(g_h4_halo)
    norm_forward(3, stat_total(3), True)

    def fourth_layer(hf, carry):
        shift, scale = carry
        with_halo(c3, hf, 2)
        with_halo(gh4, hf, 0)
        v = c3[hf]
        z = v * param(3, ALPHA, hf) + param(3, BETA, hf)
        gate = logistic(z)
        h = z * gate
        put_ec(ec4, hf, jnp.where(block_mask(h.shape, 1), h, 0.0))
        g = gh4[hf] * (gate + h * (1.0 - gate))
        gzc[hf] = g
        own = g[1 : rows + 1]
        xhat = v[1 : rows + 1] * param(3, RSTD, hf) + param(3, NMR, hf)
        return put_row(shift, hf, coarse_sum(own)), put_row(scale, hf, coarse_sum(own * xhat))

    sums = lax.fori_loop(0, half, fourth_layer, (zero_coarse, zero_coarse), unroll=4)
    stat_start(4, jnp.concatenate(list(sums) + pad_rows, axis=0))

    def coarse_output(hf, carry):
        out = dot_nt(coarse_window(ec4, hf), w4f[...]).reshape(rows, cols, 128)
        y = dv[hf, 1 : rows + 1] + out
        border(hout, 3, hf, y)
        edge = jnp.zeros((1, cols, 128), F32)
        put_ec(ecy, hf, jnp.concatenate([edge, y, edge], axis=0))
        return carry

    lax.fori_loop(0, half, coarse_output, 0, unroll=4)
    halo_start(y_halo)
    coarse_kernel_grad(stacked(4), ec4, ecg)
    lax.fori_loop(half, frames, merge_skip, 0, unroll=4)

    norm_backward(3, stat_total(4), True)

    def third_back(hf, carry):
        shift, scale = carry
        g = (
            gzc[hf] * param(3, ALPHA, hf)
            + c3[hf] * param(3, COEF, hf)
            + param(3, BIAS, hf)
        )
        put_ec(ecg3, hf, jnp.where(block_mask(g.shape, 1), g, 0.0))
        back = dot_nn(coarse_window(ecg3, hf), w3b[...]).reshape(rows, cols, 128)
        border(hout, 4, hf, back)
        v = dv[hf, 1 : rows + 1]
        z = v * param(2, ALPHA, hf) + param(2, BETA, hf)
        gate = logistic(z)
        own = back * (gate + z * gate * (1.0 - gate))
        gzc[hf, 1 : rows + 1] = own
        xhat = v * param(2, RSTD, hf) + param(2, NMR, hf)
        return put_row(shift, hf, coarse_sum(own)), put_row(scale, hf, coarse_sum(own * xhat))

    sums = lax.fori_loop(0, half, third_back, (zero_coarse, zero_coarse), unroll=4)
    stat_start(5, jnp.concatenate(list(sums) + pad_rows, axis=0))
    halo_start(g_h3_halo)

    halo_wait(y_halo)

    def merge(hf, carry):
        for side, row in ((0, 0), (1, rows + 1)):
            line = hal[3, side, hf].astype(F32)[None]
            up, down = neighbours(line)
            q = lax.broadcasted_iota(jnp.int32, line.shape, 1)
            ecy[hf, row, :, 0:128] = jnp.where(q == 0, 0.0, down)[0].astype(BF16)
            ecy[hf, row, :, 128:256] = line[0].astype(BF16)
            ecy[hf, row, :, 256:384] = jnp.where(q == cols - 1, 0.0, up)[0].astype(BF16)
        both = dot_nt(coarse_window(ecy, hf), wup[...])
        for hi in range(2):
            f = hf + hi * half
            up = both[:, hi * 256 : hi * 256 + 256].reshape(rows, cols, 256)
            gz[f, 1 : rows + 1] = gz[f, 1 : rows + 1] + up
            result_copy(f).start()
        return carry

    lax.fori_loop(0, half, merge, 0, unroll=4)
    coarse_kernel_grad(stacked(3), ec3, ecg3)
    up_kernel_grad()
    gather_start(0)

    halo_wait(g_h3_halo)
    norm_backward(2, stat_total(5), True)

    def down_back(hf, carry):
        for side, row in ((0, 0), (1, rows + 1)):
            v = dv[hf, row]
            z = v * param(2, ALPHA, hf) + param(2, BETA, hf)
            gate = logistic(z)
            gzc[hf, row] = hal[4, side, hf].astype(F32) * (gate + z * gate * (1.0 - gate))
        g = (
            gco[hf]
            + gzc[hf] * param(2, ALPHA, hf)
            + dv[hf] * param(2, COEF, hf)
            + param(2, BIAS, hf)
        )
        g = jnp.where(block_mask(g.shape, 1), g, 0.0)
        up, _ = neighbours(g)
        q = lax.broadcasted_iota(jnp.int32, g.shape, 1)
        ed[hf, 0 : rows + 2, :, 0:128] = g.astype(BF16)
        ed[hf, 0 : rows + 2, :, 128:256] = jnp.where(q == cols - 1, 0.0, up).astype(BF16)
        ed[hf, rows + 2] = jnp.zeros((cols, 256), BF16)
        lhs = jnp.concatenate([ed[hf, 0 : rows + 2], ed[hf, 1 : rows + 3]], axis=-1)
        back = dot_nn(lhs.reshape(ext, 512), wdb[...])
        back = back.astype(BF16).astype(F32).reshape(rows + 2, cols, 512)
        for hi in range(2):
            f = hf + hi * half
            total = gsa[f] + back[:, :, hi * 256 : hi * 256 + 256]
            gsa[f] = total
            put_e(eg, f, 0, jnp.where(block_mask(total.shape, 1), total, 0.0))
        return carry

    lax.fori_loop(0, half, down_back, 0, unroll=4)

    def second_back(f, carry):
        shift, scale = carry
        back = dot_nn(window(eg, f, 1, rows), w2b[...]).reshape(rows, cols, 256)
        hfout[0, f] = back[0, :, 0:128].astype(BF16)
        hfout[1, f] = back[rows - 1, :, 128:256].astype(BF16)
        v = c1[f, 1 : rows + 1]
        z = v * wide(1, ALPHA, f) + wide(1, BETA, f)
        gate = logistic(z)
        own = back * (gate + z * gate * (1.0 - gate))
        gz[f, 1 : rows + 1] = own
        xhat = v * wide(1, RSTD, f) + wide(1, NMR, f)
        return put_row(shift, f, full_sum(own)), put_row(scale, f, full_sum(own * xhat))

    for f in range(frames):
        result_copy(f).wait()
    sums = lax.fori_loop(0, frames, second_back, (zero_rows, zero_rows), unroll=4)
    stat_start(6, jnp.concatenate(sums, axis=0))
    halo_start(g_h2_halo)
    down_kernel_grad(stacked(2))
    gather_space(0)
    fine_kernel_grad(stacked(1), e2, 2, eg, 1)
    gather_start(1)
    gather_spread()
    halo_wait(g_h2_halo)
    norm_backward(1, stat_total(6), False)

    def first_gradient(f, carry):
        for side, row in ((0, 0), (1, rows + 1)):
            v = c1[f, row]
            lanes = slice(128, 256) if side == 0 else slice(0, 128)
            z = v[:, lanes] * param(1, ALPHA, f) + param(1, BETA, f)
            gate = logistic(z)
            g = hfull[side, f].astype(F32) * (gate + z * gate * (1.0 - gate))
            blank = jnp.zeros_like(g)
            gz[f, row] = jnp.concatenate([blank, g] if side == 0 else [g, blank], axis=-1)
        g = gz[f] * wide(1, ALPHA, f) + c1[f] * wide(1, COEF, f) + wide(1, BIAS, f)
        put_e(eg, f, 0, jnp.where(block_mask(g.shape, 1), g, 0.0))
        return carry

    lax.fori_loop(0, frames, first_gradient, 0, unroll=4)
    fine_kernel_grad(stacked(0), e1, 2, eg, 1)
    gather_start(2)
    gather_all(0)
    gather_space(1)

    def first_back(f, carry):
        shift, scale = carry
        back = dot_nn(window(eg, f, 1, rows), w1b[...]).reshape(rows, cols, 256)
        v = xs[f, 2 : rows + 2].astype(F32)
        z = v * wide(0, ALPHA, f) + wide(0, BETA, f)
        gate = logistic(z)
        own = back * (gate + z * gate * (1.0 - gate))
        gz[f, 1 : rows + 1] = own
        xhat = v * wide(0, RSTD, f) + wide(0, NMR, f)
        return put_row(shift, f, full_sum(own)), put_row(scale, f, full_sum(own * xhat))

    pack_start(0)
    sums = lax.fori_loop(0, frames, first_back, (zero_rows, zero_rows), unroll=4)
    stat_start(7, jnp.concatenate(sums, axis=0))
    gather_all(1)
    gather_space(2)
    norm_backward(0, stat_total(7), False)
    pack_start(1)
    gather_all(2)

    def frames_copy(f):
        return pltpu.make_async_copy(
            gz.at[f, pl.ds(1, rows)], io_hbm.at[frames + f], fg_sem.at[f]
        )

    def frames_back(f, carry):
        gz[f, 1 : rows + 1] = (
            gsa[f, 1 : rows + 1]
            + gz[f, 1 : rows + 1] * wide(0, ALPHA, f)
            + xs[f, 2 : rows + 2].astype(F32) * wide(0, COEF, f)
            + wide(0, BIAS, f)
        )
        frames_copy(f).start()
        return carry

    lax.fori_loop(0, frames, frames_back, 0, unroll=4)
    for which in range(2):
        pack_all(which).wait_recv()
        pack_all(which).wait_send()
    total_frames = nd * frames
    every = packs[...].reshape(total_frames, 896)
    embedded, hot = every[:, 512:768], every[:, 768:896]
    g_embed = 0.0
    for k in range(4):
        dmod = every[:, k * 128 : (k + 1) * 128]
        acc[1, :, k * 128 : k * 128 + 128] = lax.dot_general(
            embedded, dmod, (((0,), (0,)), ((), ())), precision=HIGH, preferred_element_type=F32
        )
        lane = 512 + k % 2 * 128
        acc[1, 128 + k // 2 : 129 + k // 2, lane : lane + 128] = jnp.sum(
            dmod, axis=0, keepdims=True
        )
        g_embed = g_embed + lax.dot_general(
            dmod, nmv[k], (((1,), (1,)), ((), ())), precision=HIGH, preferred_element_type=F32
        )
    acc[1, 0:128, 512:768] = lax.dot_general(
        hot, g_embed, (((0,), (0,)), ((), ())), precision=HIGH, preferred_element_type=F32
    )

    def par_copy(e):
        return pltpu.make_async_copy(
            acc.at[1, :, pl.ds(e * 256, 256)], par_hbm.at[e], local_sem.at[e]
        )

    for e in range(3):
        par_copy(e).start()
    for stage in stages:
        gather_finish(stage)

    for e in range(3):
        par_copy(e).wait()
    for f in range(frames):
        frames_copy(f).wait()
    for copies in (*x_halos, *g_halos, g_h4_halo, d_halo, c3_halo, y_halo, g_h3_halo, g_h2_halo):
        halo_finish(copies)


def run_step(nd, n, frames, cotangent, actions, noise_ids, games, live_counts, cw, nm, table):
    count, strip, breadth, _ = frames.shape
    half, rows, cols = count // 2, strip // 2, breadth // 2
    fine = (count, rows + 4, cols, 512)
    coarse = (half, rows + 2, cols, 128)
    coarse_e = (half, rows + 2, cols, 384)
    scratch = [
        pltpu.SMEM(actions.shape, jnp.int32),
        pltpu.SMEM(noise_ids.shape, jnp.int32),
        pltpu.SMEM(games.shape, jnp.int32),
        pltpu.SMEM(live_counts.shape, jnp.int32),
        VM((count, strip, breadth, 64), BF16),
        VM(cw.shape, F32),
        VM(table.shape, F32),
        VM((strip, breadth, 128), F32),
        VM((count, rows + 4, cols, 256), BF16),
        VM((count, rows + 4, cols, 256), BF16),
        VM(fine, BF16),
        VM(fine, BF16),
        VM(fine, BF16),
        VM(fine, BF16),
        VM((count, rows + 2, cols, 256), F32),
        VM((count, rows + 2, cols, 256), F32),
        VM((count, rows + 2, cols, 256), F32),
        VM(coarse, F32),
        VM(coarse, F32),
        VM(coarse, F32),
        VM(coarse, F32),
        VM(coarse, F32),
        VM(coarse_e, BF16),
        VM(coarse_e, BF16),
        VM(coarse_e, BF16),
        VM(coarse_e, BF16),
        VM(coarse_e, BF16),
        VM((half, rows + 3, cols, 256), BF16),
        VM((256, 1024), BF16),
        VM((1024, 256), BF16),
        VM((256, 1024), BF16),
        VM((1024, 256), BF16),
        VM((256, 1024), BF16),
        VM((1024, 256), BF16),
        VM((512, 1152), BF16),
        VM((2, 1024, 128), BF16),
        VM((128, 1536), BF16),
        VM((512, 512), BF16),
        VM((128, 1152), BF16),
        VM((1152, 128), BF16),
        VM((128, 1152), BF16),
        VM((1152, 128), BF16),
        VM((2, 256, 1152), F32),
        VM((32, count, 128), F32),
        VM((128, 256), F32),
        VM((8, n, 2 * count, 128), F32),
        VM((5, 2, half, cols, 128), BF16),
        VM((5, 2, half, cols, 128), BF16),
        VM((2, count, cols, 128), BF16),
        VM((2, count, cols, 128), BF16),
        VM((4, 256, 128), F32),
        VM((4, 128), F32),
        VM((32 // nd, nd, 64, 128), BF16),
        VM((nd, 32 // nd, 64, 128), BF16),
        VM((n, 32 // nd, 64 // n, 128), F32),
        VM((n, 32 // nd, 64 // n, 128), F32),
        VM((n, 32 // nd, 64 // n, 128), F32),
        VM((2, n, 64, 128), F32),
        VM((32 // nd, 64, 128), BF16),
        VM((nd, count, 896), F32),
        pltpu.SemaphoreType.DMA((14,)),
        pltpu.SemaphoreType.DMA((count,)),
        pltpu.SemaphoreType.DMA((count,)),
        pltpu.SemaphoreType.DMA((8,)),
        pltpu.SemaphoreType.DMA((8,)),
        pltpu.SemaphoreType.DMA((10, 2)),
        pltpu.SemaphoreType.DMA((10, 2)),
        pltpu.SemaphoreType.DMA((8,)),
        pltpu.SemaphoreType.DMA((8,)),
        pltpu.SemaphoreType.DMA((4,)),
        pltpu.SemaphoreType.DMA((4,)),
        pltpu.SemaphoreType.DMA((3,)),
    ]
    hbm = pl.BlockSpec(memory_space=pltpu.HBM)
    return pl.pallas_call(
        functools.partial(step_kernel, nd, n),
        out_shape=(
            jax.ShapeDtypeStruct((2 * count, rows, cols, 256), F32),
            jax.ShapeDtypeStruct((8, 256, 256), F32),
            jax.ShapeDtypeStruct((4 * nd, 32 // nd, 64, 128), BF16),
        ),
        in_specs=[hbm] * 9,
        out_specs=(hbm, hbm, hbm),
        scratch_shapes=scratch,
        compiler_params=pltpu.CompilerParams(
            collective_id=0, has_side_effects=True, vmem_limit_bytes=55 * 1024 * 1024
        ),
        name="step",
    )(frames, cotangent, actions, noise_ids, games, live_counts, cw, nm, table)


def adamw(weight, moment, square, grad_value, rate):
    fix_one = 1.0 - BETA_ONE**ADAM_STEP
    fix_two = 1.0 - BETA_TWO**ADAM_STEP
    moment_new = BETA_ONE * moment + (1.0 - BETA_ONE) * grad_value
    square_new = BETA_TWO * square + (1.0 - BETA_TWO) * grad_value * grad_value
    fixed_m = moment_new / fix_one
    fixed_v = square_new / fix_two
    weight_new = weight - rate * (fixed_m / (jnp.sqrt(fixed_v) + ADAM_EPS) + DECAY * weight)
    return (moment_new, square_new, weight_new, weight_new.astype(BF16))


def finish_kernel(
    io_hbm,
    par_hbm,
    gall_hbm,
    cw,
    cm,
    cv,
    nm,
    nmo,
    nsq,
    tab,
    tmo,
    tsq,
    res_out,
    fg_out,
    *refs,
):
    outs, refs = refs[:12], refs[12:]
    stages, refs = refs[:12], refs[12:]
    io, par, gall, tmp, rs, fs, gmap, in_sem, pin_sem, fg_sem, out_sem, par_sem = refs
    frames, rows, cols = rs.shape[0], io.shape[1], io.shape[2]

    def frame_in(f):
        return pltpu.make_async_copy(io_hbm.at[f], io.at[f], in_sem.at[f])

    def par_in(e):
        return pltpu.make_async_copy(par_hbm.at[e], par.at[e], pin_sem.at[e])

    gall_in = pltpu.make_async_copy(
        gall_hbm.at[pl.ds(0, gall.shape[0])], gall, pin_sem.at[3]
    )
    gall_in.start()
    for e in range(3):
        par_in(e).start()
    for f in range(2 * frames):
        frame_in((f + frames) % (2 * frames)).start()
    out_copies = [
        pltpu.make_async_copy(stages[i], outs[i], par_sem.at[i]) for i in range(12)
    ]

    def update(first, at, weight, moment, square, grad, rate):
        new = adamw(weight, moment, square, grad, rate)
        for i in range(4):
            stages[first + i][at] = new[i]

    wide = cw.shape[1]
    gall_in.wait()
    for tile in range(32):
        lanes = slice(tile * 128, min(tile * 128 + 128, wide))
        at = (slice(None), lanes)
        owner, slot = tile % gall.shape[0], tile // gall.shape[0]
        grad = gall[owner, slot, :, 0 : lanes.stop - lanes.start].astype(F32)
        update(0, at, cw[at], cm[at], cv[at], grad, 0.05)
    for i in range(4):
        out_copies[i].start()

    def unpair(v):
        both = jnp.stack([v[:, :, 0:128], v[:, :, 128:256]], axis=1).reshape(rows * 2, cols, 128)
        tmp[:, pl.ds(0, cols, stride=2), :] = both
        tmp[:, pl.ds(1, cols, stride=2), :] = swap(both)
        return tmp[:, :, 0:64]

    def frame_copies(f):
        return (
            pltpu.make_async_copy(fs.at[f], fg_out.at[f], fg_sem.at[f]),
            pltpu.make_async_copy(rs.at[f], res_out.at[f], out_sem.at[f]),
        )

    def put_frames(f, carry):
        frame_in(frames + f).wait()
        fs[f] = unpair(io[frames + f])
        frame_copies(f)[0].start()
        return carry

    lax.fori_loop(0, frames, put_frames, 0)

    def put_result(f, carry):
        frame_in(f).wait()
        rs[f] = unpair(io[f]).astype(BF16)
        frame_copies(f)[1].start()
        return carry

    lax.fori_loop(0, frames, put_result, 0)

    for e in range(3):
        par_in(e).wait()
    for k in range(4):
        lane = k % 2 * 128
        gmap[0:256, k, :] = par[k // 2, :, lane : lane + 128]
        gmap[256, k : k + 1, :] = par[2, 128 + k // 2 : 129 + k // 2, lane : lane + 128]
    at = slice(None)
    update(4, at, nm[...], nmo[...], nsq[...], gmap[...], 0.04)
    for i in range(4, 8):
        out_copies[i].start()
    update(8, at, tab[...], tmo[...], tsq[...], par[2, 0 : tab.shape[0]], 0.5)
    for i in range(8, 12):
        out_copies[i].start()
    for f in range(frames):
        for copy in frame_copies(f):
            copy.wait()
    for copy in out_copies:
        copy.wait()


def run_finish(shape, io, par, gall, conv, norm, table):
    count, strip, breadth, _ = shape
    hbm = pl.BlockSpec(memory_space=pl.ANY)
    vmem = pl.BlockSpec(memory_space=pltpu.VMEM)
    params = [
        jax.ShapeDtypeStruct(v[0].shape, dtype)
        for v in (conv, norm, table)
        for dtype in (F32, F32, F32, BF16)
    ]
    return pl.pallas_call(
        finish_kernel,
        out_shape=(
            jax.ShapeDtypeStruct(shape, BF16),
            jax.ShapeDtypeStruct(shape, F32),
            *params,
        ),
        in_specs=[hbm] * 3 + [vmem] * 9,
        out_specs=(hbm,) * 14,
        scratch_shapes=[VM(v.shape, v.dtype) for v in params]
        + [
            VM(io.shape, F32),
            VM((3,) + par.shape[1:], F32),
            VM((gall.shape[0] // 4,) + gall.shape[1:], BF16),
            VM((strip, breadth, 128), F32),
            VM(shape, BF16),
            VM(shape, F32),
            VM(norm[0].shape, F32),
            pltpu.SemaphoreType.DMA((2 * count,)),
            pltpu.SemaphoreType.DMA((4,)),
            pltpu.SemaphoreType.DMA((count,)),
            pltpu.SemaphoreType.DMA((count,)),
            pltpu.SemaphoreType.DMA((12,)),
        ],
        compiler_params=pltpu.CompilerParams(vmem_limit_bytes=48 * 1024 * 1024),
        name="finish",
    )(io, par, gall, *conv, *norm, *table)


def local(
    nd,
    ns,
    frames,
    cotangent,
    actions,
    noise_ids,
    games,
    live_counts,
    conv_weight,
    conv_moment,
    conv_square,
    norm_map,
    norm_moment,
    norm_square,
    emb_table,
    table_moment,
    table_square,
):
    conv = [v.T for v in (conv_weight, conv_moment, conv_square)]
    norm = [jnp.transpose(v, (1, 0, 2)) for v in (norm_map, norm_moment, norm_square)]
    table = (emb_table, table_moment, table_square)
    io, par, gall = run_step(
        nd,
        ns,
        frames,
        cotangent,
        actions,
        noise_ids,
        games,
        live_counts,
        conv[0],
        norm[0],
        emb_table,
    )
    result, frames_grad, *new = run_finish(
        frames.shape, io, par, gall, conv, norm, table
    )
    conv_out = [v.T for v in new[0:4]]
    norm_out = [jnp.transpose(v, (1, 0, 2)) for v in new[4:8]]
    return (result, frames_grad, *conv_out, *norm_out, *new[8:12])


def solution(mesh):
    split = P("dp", "space", None, None)
    in_specs = (split, split) + (P("dp"),) * 4 + (P(),) * 9
    out_specs = (split, split) + (P(),) * 12
    sizes = dict(mesh.shape)
    return jax.shard_map(
        functools.partial(local, sizes["dp"], sizes["space"]),
        mesh=mesh,
        in_specs=in_specs,
        out_specs=out_specs,
        check_vma=False,
    )
```
